32 devices in a mesh: section: 2 (over core), pts: 16 (over z, y, x).
Axes of the slice: x: 2, y: 2, z: 4, core: 2. Of those that a mesh axis runs over, the one named last changes fastest.
Arguments:
- node_features: float32 [4, 32768, 128], P(None, 'pts'), may hold values from -6 to 6
- cotangent: float32 [4, 32768, 128], P(None, 'pts'), may hold values from -6 to 6
- lengths: int32 [4, 8], replicated, may hold values from 1 to 32761, as said below
- attention_weight: float32 [2, 4, 128, 128], P('section'), may hold values from -0.5 to 0.5
- inner_weight: float32 [2, 128, 256], P('section'), may hold values from -0.5 to 0.5
- outer_weight: float32 [2, 256, 128], P('section'), may hold values from -0.375 to 0.375
- vectors: float32 [2, 11, 128], P('section'), may hold values from -3 to 3
- momentum_attention: float32 [2, 4, 128, 128], P('section'), may hold values from -0.006 to 0.006
- variance_attention: float32 [2, 4, 128, 128], P('section'), may hold values from 1e-07 to 1e-05
- momentum_inner: float32 [2, 128, 256], P('section'), may hold values from -0.006 to 0.006
- variance_inner: float32 [2, 128, 256], P('section'), may hold values from 1e-07 to 1e-05
- momentum_outer: float32 [2, 256, 128], P('section'), may hold values from -0.006 to 0.006
- variance_outer: float32 [2, 256, 128], P('section'), may hold values from 1e-07 to 1e-05
- momentum_vectors: float32 [2, 11, 128], P('section'), may hold values from -0.006 to 0.006
- variance_vectors: float32 [2, 11, 128], P('section'), may hold values from 1e-07 to 1e-05
Outputs:
- activations: float32 [2, 4, 32768, 128], P('section', None, 'pts')
- input_gradient: float32 [2, 4, 32768, 128], P('section', None, 'pts')
- attention_gradient: float32 [2, 4, 128, 128], P('section')
- attention_momentum: float32 [2, 4, 128, 128], P('section')
- attention_variance: float32 [2, 4, 128, 128], P('section')
- attention_updated: float32 [2, 4, 128, 128], P('section')
- inner_gradient: float32 [2, 128, 256], P('section')
- inner_momentum: float32 [2, 128, 256], P('section')
- inner_variance: float32 [2, 128, 256], P('section')
- inner_updated: float32 [2, 128, 256], P('section')
- outer_gradient: float32 [2, 256, 128], P('section')
- outer_momentum: float32 [2, 256, 128], P('section')
- outer_variance: float32 [2, 256, 128], P('section')
- outer_updated: float32 [2, 256, 128], P('section')
- vectors_gradient: float32 [2, 11, 128], P('section')
- vectors_momentum: float32 [2, 11, 128], P('section')
- vectors_variance: float32 [2, 11, 128], P('section')
- vectors_updated: float32 [2, 11, 128], P('section')
The draws below stay inside these ranges and needn't reach their ends.
Inputs may be any that keep to these rules, and one draw needn't show every extreme that they name: Each row of lengths sums to 32768; in each row one mesh starts among the first 2048 nodes and ends among the last 2048.
All inputs are finite; a program needn't handle non-finite values.
Results may differ from the reference program's by a relative error of at most 0.0003.
Values sent between devices are 32-bit elements; how exact they have to be, the bound alone decides.
A program may use at most 192 MiB of HBM per device.

```python
import math
import jax
import jax.numpy as jnp
from jax import lax

D = 128
HEADS = 4
FF = 256
VROWS = 11
TOK_DEV = 2048
SEGS = 8
MICRO = 4
STEP = 1200
TOTAL_STEPS = 4000
TOKENS = 32768


def draw_lengths(key, part):
    key = jax.random.fold_in(key, 11)
    short_key, pick_key, row_key = jax.random.split(key, 3)
    bound_short = (TOK_DEV - 1) // SEGS
    short_lengths = jax.random.randint(short_key, (MICRO, SEGS), 1, bound_short + 1)
    full_row = jax.random.randint(row_key, (), 0, MICRO)
    short_lengths = jnp.where(jnp.arange(MICRO)[:, None] == full_row, 1, short_lengths)
    chosen = jax.random.randint(pick_key, (MICRO,), 0, SEGS)
    is_chosen = jnp.arange(SEGS)[None, :] == chosen[:, None]
    others_total = jnp.sum(jnp.where(is_chosen, 0, short_lengths), axis=1, keepdims=True)
    return jnp.where(is_chosen, TOKENS - others_total, short_lengths).astype(jnp.int32)


def block_levels(own_key, dims, pieces, smallest, top_value):
    level, own = 1.0, jax.random.fold_in(own_key, 6)
    for axis_at, parts in pieces:
        heights = jnp.exp(jax.random.uniform(jax.random.fold_in(own, axis_at), (parts,), jnp.float32, smallest / len(pieces), top_value / len(pieces)))
        level = level * jnp.repeat(heights, dims[axis_at] // parts).reshape([-1 if axis == axis_at else 1 for axis in range(len(dims))])
    return level


def gaussian(own_key, shape, deviation, limit, cuts=(), kind=jnp.bfloat16):
    values = jax.random.normal(own_key, shape, jnp.float32) * deviation
    if len(cuts) > 0:
        values = block_levels(own_key, shape, cuts, -0.22, 0.18) * values
    return jnp.clip(values, min=-limit, max=limit).astype(kind)


def setup_inputs(seed: int = 0) -> dict:
    keys = jax.random.split(jax.random.key(seed), 16)
    return {
        "node_features": gaussian(keys[0], (MICRO, TOKENS, D), 1.0, 6.0, ((1, 16),), jnp.float32),
        "cotangent": gaussian(keys[1], (MICRO, TOKENS, D), 1.0, 6.0, ((1, 16),), jnp.float32),
        "lengths": draw_lengths(jax.random.fold_in(keys[15], 71), 0),
        "attention_weight": gaussian(keys[3], (2, 4, D, D), D ** -0.5, 0.5, ((0, 2),), jnp.float32),
        "inner_weight": gaussian(keys[4], (2, D, FF), D ** -0.5, 0.5, ((0, 2),), jnp.float32),
        "outer_weight": gaussian(keys[5], (2, FF, D), FF ** -0.5, 0.375, ((0, 2),), jnp.float32),
        "vectors": gaussian(keys[6], (2, VROWS, D), 0.5, 3.0, ((0, 2),), jnp.float32),
        "momentum_attention": gaussian(keys[7], (2, 4, D, D), 0.001, 0.006, ((0, 2),), jnp.float32),
        "variance_attention": jnp.clip(jnp.exp(math.log(9.999999747378752e-06) - 4.6051701 * jax.random.uniform(keys[8], (2, 4, D, D), jnp.float32) ** block_levels(keys[8], (2, 4, D, D), ((0, 2),), -0.2, 0.2)), 1.0000000116860974e-07, 9.999999747378752e-06),
        "momentum_inner": gaussian(keys[9], (2, D, FF), 0.001, 0.006, ((0, 2),), jnp.float32),
        "variance_inner": jnp.clip(jnp.exp(math.log(9.999999747378752e-06) - 4.6051701 * jax.random.uniform(keys[10], (2, D, FF), jnp.float32) ** block_levels(keys[10], (2, D, FF), ((0, 2),), -0.2, 0.2)), 1.0000000116860974e-07, 9.999999747378752e-06),
        "momentum_outer": gaussian(keys[11], (2, FF, D), 0.001, 0.006, ((0, 2),), jnp.float32),
        "variance_outer": jnp.clip(jnp.exp(math.log(9.999999747378752e-06) - 4.6051701 * jax.random.uniform(keys[12], (2, FF, D), jnp.float32) ** block_levels(keys[12], (2, FF, D), ((0, 2),), -0.2, 0.2)), 1.0000000116860974e-07, 9.999999747378752e-06),
        "momentum_vectors": gaussian(keys[13], (2, VROWS, D), 0.001, 0.006, ((0, 2),), jnp.float32),
        "variance_vectors": jnp.clip(jnp.exp(math.log(9.999999747378752e-06) - 4.6051701 * jax.random.uniform(keys[14], (2, VROWS, D), jnp.float32) ** block_levels(keys[14], (2, VROWS, D), ((0, 2),), -0.2, 0.2)), 1.0000000116860974e-07, 9.999999747378752e-06),
    }


@jax.custom_vjp
def low(v):
    return lax.optimization_barrier(v.astype(jnp.bfloat16)).astype(jnp.float32)

@jax.custom_vjp
def low_back(v):
    return v

def low_keep(v):
    return (low(v), None)

def low_pass(kept, grad):
    return (grad,)

def back_keep(v):
    return (v, None)

def back_low(kept, grad):
    return (low(grad),)
low.defvjp(low_keep, low_pass)
low_back.defvjp(back_keep, back_low)
HIGH = lax.Precision.HIGHEST
EPS_NORM = 1e-05

def dense(left, right):
    return jnp.dot(left, right, precision=HIGH, preferred_element_type=jnp.float32)

def head_norm(field, gain, shift):
    rows = field.shape[0]
    grouped = field.reshape(rows, HEADS, -1)
    centre = lax.optimization_barrier(jnp.mean(grouped, axis=2, keepdims=True))
    spread = lax.optimization_barrier(jnp.mean(jnp.square(grouped - centre), axis=2, keepdims=True))
    normed = ((grouped - centre) * lax.rsqrt(spread + EPS_NORM)).reshape(rows, -1)
    return normed * (1.0 + gain) + shift

def project(inputs, weights, params):
    queries = dense(inputs, weights[0]) + params[0]
    keyed = head_norm(dense(inputs, weights[1]) + params[1], params[4], params[5])
    valued = head_norm(dense(inputs, weights[2]) + params[2], params[6], params[7])
    return (queries, keyed, valued)

def finish(inputs, mixed, weights, inner, outer, params):
    middle = inputs + dense(mixed, weights[3]) + params[3]
    hidden = jax.nn.gelu(dense(middle, inner) + params[9:].reshape(-1), approximate=True)
    return middle + dense(hidden, outer) + params[8]

def plan():
    warm = 0.3 * TOTAL_STEPS
    top = 0.001
    start = top / 25.0
    bottom = start / 10000.0
    if STEP <= warm:
        return start + (top - start) * (1.0 - math.cos(math.pi * STEP / warm)) / 2.0
    return bottom + (top - bottom) * (1.0 + math.cos(math.pi * (STEP - warm) / (TOTAL_STEPS - warm))) / 2.0

def adamw(weight, gradient, momentum, variance, scale):
    average = gradient * scale
    new_momentum = 0.9 * momentum + 0.1 * average
    new_variance = 0.999 * variance + 0.001 * average * average
    unbiased_mean = new_momentum / (1.0 - 0.9 ** STEP)
    unbiased_square = new_variance / (1.0 - 0.999 ** STEP)
    updated = weight - plan() * (unbiased_mean / (jnp.sqrt(unbiased_square) + 1e-08) + 0.01 * weight)
    return (new_momentum, new_variance, updated)

def layer(inputs, weights, inner, outer, params, lengths_row):
    queries, keyed, valued = project(inputs, weights, params)
    rows = inputs.shape[0]
    ends = jnp.cumsum(lengths_row).astype(jnp.int32)
    starts = (ends - lengths_row).astype(jnp.int32)
    position = jnp.arange(rows, dtype=jnp.int32)
    member = ((position[:, None] >= starts[None, :]) & (position[:, None] < ends[None, :])).astype(jnp.float32)
    counts = lengths_row.astype(jnp.float32)
    queries3 = queries.reshape(rows, HEADS, -1)
    keyed3 = keyed.reshape(rows, HEADS, -1)
    valued3 = valued.reshape(rows, HEADS, -1)

    def segment_moment(index):
        column = lax.dynamic_index_in_dim(member, index, 1, keepdims=False)
        total = jnp.einsum('the,thf->hef', keyed3 * column[:, None, None], valued3, precision=HIGH)
        return total / counts[index]
    moments = lax.map(segment_moment, jnp.arange(SEGS, dtype=jnp.int32))

    def accumulate(total, index):
        column = lax.dynamic_index_in_dim(member, index, 1, keepdims=False)
        table = lax.dynamic_index_in_dim(moments, index, 0, keepdims=False)
        piece = jnp.einsum('the,hef->thf', queries3, table, precision=HIGH)
        return (total + column[:, None, None] * piece, None)
    mixed3, _ = lax.scan(accumulate, jnp.zeros_like(queries3), jnp.arange(SEGS, dtype=jnp.int32))
    return finish(inputs, mixed3.reshape(rows, -1), weights, inner, outer, params)

def reference(node_features, cotangent, lengths, attention_weight, inner_weight, outer_weight, vectors, momentum_attention, variance_attention, momentum_inner, variance_inner, momentum_outer, variance_outer, momentum_vectors, variance_vectors):
    params = [(attention_weight[level], inner_weight[level], outer_weight[level], vectors[level]) for level in range(2)]
    totals = [[jnp.zeros_like(piece) for piece in params[level]] for level in range(2)]
    first_outs, second_outs, first_grads, second_grads = ([], [], [], [])
    for batch in range(MICRO):
        lengths_row = lengths[batch]

        def section_layer(inputs, weights, inner, outer, table):
            return layer(inputs, weights, inner, outer, table, lengths_row)
        first_out, first_back = jax.vjp(section_layer, node_features[batch], *params[0])
        second_out, second_back = jax.vjp(section_layer, first_out, *params[1])
        second_terms = second_back(cotangent[batch])
        first_terms = first_back(second_terms[0])
        first_outs.append(first_out)
        second_outs.append(second_out)
        first_grads.append(first_terms[0])
        second_grads.append(second_terms[0])
        for index in range(4):
            totals[0][index] = totals[0][index] + first_terms[index + 1]
            totals[1][index] = totals[1][index] + second_terms[index + 1]
    activations = jnp.stack([jnp.stack(first_outs), jnp.stack(second_outs)])
    input_gradient = jnp.stack([jnp.stack(first_grads), jnp.stack(second_grads)])
    scale = 1.0 / (MICRO * TOKENS)
    gradients = [jnp.stack([totals[0][index], totals[1][index]]) for index in range(4)]
    weights_all = [attention_weight, inner_weight, outer_weight, vectors]
    momenta = [momentum_attention, momentum_inner, momentum_outer, momentum_vectors]
    variances = [variance_attention, variance_inner, variance_outer, variance_vectors]
    results = []
    for index in range(4):
        new_momentum, new_variance, updated = adamw(weights_all[index], gradients[index], momenta[index], variances[index], scale)
        results.append((gradients[index], new_momentum, new_variance, updated))
    return (activations, input_gradient, results[0][0], results[0][1], results[0][2], results[0][3], results[1][0], results[1][1], results[1][2], results[1][3], results[2][0], results[2][1], results[2][2], results[2][3], results[3][0], results[3][1], results[3][2], results[3][3])
```

```python
import functools
import math

import jax
import jax.numpy as jnp
from jax import lax
from jax.experimental import pallas as pl
from jax.experimental.pallas import tpu as pltpu
from jax.sharding import PartitionSpec as P

HEADS = 4
STEP = 1200
TOTAL_STEPS = 4000
EPS_NORM = 1e-05
SUB = 256
UNROLL = 2
PAY = 40

MESH = pl.DeviceIdType.MESH
HIGH = lax.Precision.HIGH
HIGHEST = lax.Precision.HIGHEST
F32 = jnp.float32
BF16 = jnp.bfloat16


def plan():
    warm = 0.3 * TOTAL_STEPS
    top = 0.001
    start = top / 25.0
    low = start / 10000.0
    if STEP <= warm:
        return start + (top - start) * (1.0 - math.cos(math.pi * STEP / warm)) / 2.0
    return low + (top - low) * (1.0 + math.cos(math.pi * (STEP - warm) / (TOTAL_STEPS - warm))) / 2.0


def cat(parts, axis=0):
    return jnp.concatenate(parts, axis=axis)


def split(value):
    high = value.astype(BF16)
    return high, (value - high.astype(F32)).astype(BF16)


def pack3(weight):
    high, low = split(weight)
    return cat([high, high, low], 1)


def dot16(left, right):
    return jnp.dot(left, right, preferred_element_type=F32)


def outer16(left, right):
    full = lax.dot_general(left, right, (((1,), (1,)), ((), ())), preferred_element_type=F32)
    m, n = full.shape[0] // 2, full.shape[1] // 2
    return full[:m, :n] + full[m:, :n] + full[:m, n:]


def mm(left, right, precision=HIGH):
    return jnp.dot(left, right, precision=precision, preferred_element_type=F32)


def mm_nt(left, right, precision=HIGHEST):
    return lax.dot_general(left, right, (((1,), (1,)), ((), ())), precision=precision, preferred_element_type=F32)


def mm_tn(left, right, precision=HIGHEST):
    return lax.dot_general(left, right, (((0,), (0,)), ((), ())), precision=precision, preferred_element_type=F32)


def wide(table, width):
    return cat([table] * (width // 128), 1)


def fold(value):
    total = value[:, :128]
    for at in range(128, value.shape[1], 128):
        total = total + value[:, at : at + 128]
    return total


def digits_of(places):
    found, stride = [], 1
    while stride < places:
        radix = 4 if (places // stride) % 4 == 0 else 2
        found.append((stride, radix))
        stride *= radix
    return found


def mega(cfg, x_hbm, cot_hbm, len_s, att_hbm, inn_hbm, out_hbm, vec_hbm, act_hbm, grd_hbm, gsum_hbm, *scratch):
    sm = dict(zip(cfg["names"], scratch))
    places, segs, micro, nsub = cfg["places"], cfg["segs"], cfg["micro"], cfg["nsub"]
    rows = nsub * SUB
    tokens = rows * places
    per = micro // 2
    D = cfg["D"]
    FF = cfg["FF"]
    group = D // HEADS
    digits = digits_of(places)
    c = lax.axis_index("section")
    place = lax.axis_index("pts")
    other = 1 - c
    edge = (place == 0) | (place == places - 1)

    stage = sm["stage"]

    dma_in = sm["dma_in"]
    watt, winn, wout, wvec = sm["watt"], sm["winn"], sm["wout"], sm["wvec"]

    def x_copy(bb):
        return pltpu.make_async_copy(x_hbm.at[c * per + bb], stage.at[0, bb], dma_in.at[bb])

    def cot_copy(bb):
        return pltpu.make_async_copy(cot_hbm.at[c * per + bb], stage.at[1, bb], dma_in.at[per + bb])

    weights = [(att_hbm, watt), (inn_hbm, winn), (out_hbm, wout), (vec_hbm, wvec)]

    def weight_copy(k):
        source, held = weights[k]
        return pltpu.make_async_copy(source.at[0], held.at[c], dma_in.at[2 * per + k])

    def weight_send(k):
        source, held = weights[k]
        return pltpu.make_async_remote_copy(
            src_ref=source.at[0], dst_ref=held.at[c], send_sem=sm["w_send"].at[k], recv_sem=sm["w_recv"].at[k],
            device_id={"section": other}, device_id_type=MESH,
        )

    def weight_arrival(k):
        source, held = weights[k]
        return pltpu.make_async_remote_copy(
            src_ref=source.at[0], dst_ref=held.at[other], send_sem=sm["w_send"].at[k], recv_sem=sm["w_recv"].at[k],
            device_id={"section": other}, device_id_type=MESH,
        )

    for k in range(4):
        weight_copy(k).start()
    for bb in range(per):
        x_copy(bb).start()
    for bb in range(per):
        cot_copy(bb).start()

    def partner(digit, offset):
        stride, radix = digits[digit]
        mine = (place // stride) % radix
        theirs = (mine + offset) % radix
        return place + (theirs - mine) * stride

    def digit_at(digit, offset=0):
        stride, radix = digits[digit]
        return ((place // stride) % radix + offset) % radix

    barrier = pltpu.get_barrier_semaphore()
    greeted = 1
    pl.semaphore_signal(barrier, inc=1, device_id={"section": other}, device_id_type=MESH)
    for digit, (stride, radix) in enumerate(digits):
        for offset in range(1, radix):
            pl.semaphore_signal(barrier, inc=1, device_id={"pts": partner(digit, offset)}, device_id_type=MESH)
            greeted += 1

    tab = sm["tab"]
    T_SLOT, T_END, T_ZI, T_KEEP = 0, nsub, 2 * nsub, 3 * nsub
    T_C = 4 * nsub
    T_LO, T_HI, T_CS, T_ZK = T_C + segs, T_C + 2 * segs, T_C + 3 * segs, T_C + 4 * segs
    T_LAST, T_CIDX, T_NLOC, T_CNT = T_C + 5 * segs, T_C + 6 * segs, T_C + 7 * segs, T_C + 8 * segs
    base = place * rows
    zero = jnp.int32(0)

    def pick(values, at):
        total = zero
        for s, value in enumerate(values):
            total = total + jnp.where(at == s, value, 0)
        return total

    for bb in range(per):
        batch = c * per + bb
        lens = [len_s[batch, s] for s in range(segs)]
        ends, run = [], zero
        for s in range(segs):
            run = run + lens[s]
            ends.append(run)
        starts = [ends[s] - lens[s] for s in range(segs)]
        big = zero
        for s in range(segs):
            big = big + jnp.where((starts[s] <= rows - 1) & (ends[s] > tokens - rows), s, 0)

        def slot_of(s):
            return jnp.where(s == big, 0, jnp.where(s < big, s + 1, s))

        slots = [slot_of(jnp.int32(s)) for s in range(segs)]
        local_start = [jnp.clip(starts[s] - base, -1, rows) for s in range(segs)]
        local_end = [jnp.clip(ends[s] - base, 0, rows) for s in range(segs)]
        before = None
        sub_slots = []
        for sub in range(nsub):
            row = sub * SUB
            seg = zero
            for s in range(segs - 1):
                seg = seg + jnp.where(local_end[s] <= row, 1, 0)
            sub_slots.append(pick(slots, seg))
            tab[bb, T_SLOT + sub] = sub_slots[-1]
            tab[bb, T_END + sub] = jnp.minimum(pick(local_end, seg) - row, SUB)
            tab[bb, T_KEEP + sub] = zero if before is None else jnp.where(seg == before, 1, 0)
            before = seg
        cells, valid = [zero], [zero]
        tab[bb, T_C] = zero
        for s in range(1, segs):
            at = local_start[s]
            inside = jnp.maximum(at, 0)
            cell = jnp.minimum(inside // SUB, nsub - 1)
            low = inside - cell * SUB
            ok = jnp.where((at > 0) & (at < rows) & (low > 0), 1, 0)
            cells.append(cell)
            valid.append(ok)
            tab[bb, T_C + s] = cell
            tab[bb, T_LO + s] = jnp.where(ok == 1, low, SUB)
            tab[bb, T_HI + s] = jnp.where(ok == 1, jnp.minimum(local_end[s] - cell * SUB, SUB), 0)
            tab[bb, T_CS + s] = slots[s]
            tab[bb, T_ZK + s] = ok * valid[s - 1] * jnp.where(cell == cells[s - 1], 1, 0)
        for sub in range(nsub):
            found = zero
            for s in range(1, segs):
                found = jnp.where((valid[s] == 1) & (cells[s] == sub), s, found)
            tab[bb, T_ZI + sub] = found
        for j in range(segs):
            last = jnp.int32(nsub)
            for sub in range(nsub):
                last = jnp.where(sub_slots[sub] == j, sub, last)
            tab[bb, T_LAST + j] = last
            index, count, local = zero, zero, zero
            for s in range(segs):
                mine = slots[s] == j
                index = index + jnp.where(mine, s * valid[s], 0)
                count = count + jnp.where(mine, lens[s], 0)
                local = local + jnp.where(mine, local_end[s] - jnp.maximum(local_start[s], 0), 0)
            tab[bb, T_CIDX + j] = index
            tab[bb, T_NLOC + j] = local
            tab[bb, T_CNT + j] = count

    lane_head = lax.broadcasted_iota(jnp.int32, (group, D), 1) // group
    block_mask = (
        lax.broadcasted_iota(jnp.int32, (D, D), 0) // group == lax.broadcasted_iota(jnp.int32, (D, D), 1) // group
    ).astype(F32)
    ones8 = jnp.ones((8, 128), F32)
    row8 = lax.broadcasted_iota(jnp.int32, (8, D), 0)

    def lanes():
        return lax.broadcasted_iota(jnp.int32, (1, SUB), 1)

    def compact(square):
        total = None
        for j in range(HEADS):
            piece = jnp.where(lane_head == j, square[group * j : group * (j + 1), :], 0.0)
            total = piece if total is None else total + piece
        return total

    def expand(packed):
        return cat([packed] * HEADS, 0) * block_mask

    def centred(matrix):
        grouped = matrix.reshape(matrix.shape[0] // group, group, matrix.shape[1])
        return (grouped - jnp.mean(grouped, axis=1, keepdims=True)).reshape(matrix.shape)

    for name in ("zm", "zk", "zv", "corr_c", "corr_n", "corr_g", "corr_d"):
        sm[name][0] = jnp.zeros(sm[name].shape[1:], F32)
    for name in ("acc_c", "acc_n", "acc_g", "acc_d"):
        sm[name][nsub] = jnp.zeros(sm[name].shape[1:], F32)
    for name in ("d_outer", "d_inner", "d_kv", "s_du", "s_g", "s_dz"):
        sm[name][...] = jnp.zeros(sm[name].shape, F32)
    gb = sm["gb"]
    gb[...] = jnp.zeros(gb.shape, F32)
    R_Q, R_K, R_V, R_3, R_I, R_O = 0, D, 2 * D, 3 * D, 4 * D, 4 * D + FF
    R_VEC = 4 * D + 2 * FF

    pl.semaphore_wait(barrier, greeted)
    for k in range(4):
        weight_send(k).start()

    tables = sm["tables"]

    def prepare(layer):
        @pl.when(c == layer)
        def _():
            for k in range(4):
                weight_copy(k).wait()

        @pl.when(c != layer)
        def _():
            for k in range(4):
                weight_arrival(k).wait_recv()

        def column(row):
            return jnp.broadcast_to(wvec[layer, row : row + 1, :], (128, D)).T

        for row in (0, 3, 5, 7, 8, 9, 10):
            tables[layer, row] = column(row)
        for row in (1, 2):
            tables[layer, row] = centred(column(row))
        for row in (4, 6):
            tables[layer, row] = 1.0 + column(row)
        sm["wq_t"][layer] = watt[layer, 0].T
        sm["w3_t"][layer] = watt[layer, 3].T
        sm["kvw"][layer] = pack3(cat([centred(watt[layer, 1].T), centred(watt[layer, 2].T)], 0))
        sm["kvw_back"][layer] = cat([pack3(watt[layer, 1]), pack3(watt[layer, 2])], 1)
        inner = winn[layer]
        sm["inn_t"][layer] = pack3(cat([inner[:, at : at + D].T for at in range(0, FF, D)], 0))
        sm["inn"][layer] = pack3(inner)
        outer = wout[layer]
        sm["out_t"][layer] = pack3(cat([outer[at : at + D, :].T for at in range(0, FF, D)], 1))
        sm["out"][layer] = pack3(outer)

    ar = sm["ar"]

    def ar_copy(k, digit, offset):
        spot = ar.at[k, digit, digit_at(digit)]
        return pltpu.make_async_remote_copy(
            src_ref=spot, dst_ref=spot, send_sem=sm["ar_send"].at[k, digit, offset - 1],
            recv_sem=sm["ar_recv"].at[k, digit, offset - 1],
            device_id={"pts": partner(digit, offset)}, device_id_type=MESH,
        )

    def ar_arrival(k, digit, offset):
        radix = digits[digit][1]
        spot = ar.at[k, digit, digit_at(digit, radix - offset)]
        return pltpu.make_async_remote_copy(
            src_ref=spot, dst_ref=spot, send_sem=sm["ar_send"].at[k, digit, offset - 1],
            recv_sem=sm["ar_recv"].at[k, digit, offset - 1],
            device_id={"pts": partner(digit, offset)}, device_id_type=MESH,
        )

    def ar_launch(k, digit, payload):
        ar[k, digit, digit_at(digit)] = payload
        for offset in range(1, digits[digit][1]):
            ar_copy(k, digit, offset).start()

    def ar_land(k, digit):
        radix = digits[digit][1]
        for offset in range(1, radix):
            ar_arrival(k, digit, offset).wait_recv()
        total = ar[k, digit, 0]
        for at in range(1, radix):
            total = total + ar[k, digit, at]
        return total

    def ar_step(k, digit):
        if digit < len(digits):
            ar_launch(k, digit, ar_land(k, digit - 1))

    def ar_finish(k):
        for digit in range(2, len(digits)):
            ar_step(k, digit)
        return ar_land(k, len(digits) - 1)

    def ar_drain(k):
        for digit in range(len(digits)):
            for offset in range(1, digits[digit][1]):
                ar_copy(k, digit, offset).wait_send()

    hs, kvs, rst, dms = sm["hs"], sm["kvs"], sm["rst"], sm["dms"]
    mids, hids, gps = sm["mids"], sm["hids"], sm["gps"]

    def three(pair, at=0, size=D):
        high = pair[at : at + size]
        return [high, pair[at + size : at + 2 * size], high]

    def joined(pairs):
        whole = pairs.astype(F32)
        return cat([whole[:D] + whole[D : 2 * D], whole[2 * D : 3 * D] + whole[3 * D :]])

    def keys_and_values(layer, bb, sub, pair):
        bias = cat([wide(tables[layer, 1], SUB), wide(tables[layer, 2], SUB)], 0)
        field = dot16(sm["kvw"][layer], cat(three(pair))) + bias
        grouped = field.reshape(2 * HEADS, group, SUB)
        spread = jnp.mean(grouped * grouped, axis=1, keepdims=True)
        scale = lax.rsqrt(spread + EPS_NORM)
        normed = (grouped * scale).reshape(2 * D, SUB)
        rst[layer, bb, sub] = scale.reshape(2 * HEADS, SUB)
        k_high, k_low = split(normed[:D])
        v_high, v_low = split(normed[D:])
        keys, values = cat([k_high, k_low]), cat([v_high, v_low])
        kvs[layer, bb, sub] = cat([keys, values])
        inside = lanes() < tab[bb, T_END + sub]
        product = compact(outer16(keys * inside.astype(BF16), values))
        sums = fold(jnp.where(inside, normed, 0.0))
        keep = tab[bb, T_KEEP + sub] == 1
        past = jnp.maximum(sub - 1, 0)
        sm["acc_c"][sub] = product + jnp.where(keep, sm["acc_c"][past], 0.0)
        sm["acc_n"][sub] = sums + jnp.where(keep, sm["acc_n"][past], 0.0)

    def feed_forward(layer, bb, sub):
        pair = hs[layer, bb, sub]
        slot = tab[bb, T_SLOT + sub]
        inside = lanes() < tab[bb, T_END + sub]
        middle = dot16(sm["fwd_mat"][slot], cat(three(pair))) + wide(sm["fwd_add"][slot], SUB)
        middle = jnp.where(inside, middle, sm["zm"][tab[bb, T_ZI + sub]])
        m_high, m_low = split(middle)
        mid_pair = cat([m_high, m_low])
        u = dot16(sm["inn_t"][layer], cat(three(mid_pair)))
        u = u + cat([wide(tables[layer, 9], SUB), wide(tables[layer, 10], SUB)], 0)
        k0 = 0.7978845608
        square = u * u
        t = jnp.tanh(u * (k0 + (k0 * 0.044715) * square))
        half = 0.5 + 0.5 * t
        hidden = u * half
        slope = half + hidden * (1.0 - t) * (k0 + (3.0 * k0 * 0.044715) * square)
        h_high, h_low = split(hidden)
        hid_pair = cat([h_high, h_low])
        out = middle + dot16(sm["out_t"][layer], cat(three(hid_pair, 0, FF))) + wide(tables[layer, 8], SUB)
        return out, mid_pair, hid_pair, slope

    def feed_back(layer, bb, sub, upstream, mid_pair, hid_pair, slope):
        g_high, g_low = split(upstream)
        g_pair = cat([g_high, g_low])
        du = dot16(sm["out"][layer], cat(three(g_pair))) * slope
        u_high, u_low = split(du)
        u_pair = cat([u_high, u_low])
        d_mid = upstream + dot16(sm["inn"][layer], cat(three(u_pair, 0, FF)))
        q_high, q_low = split(d_mid)
        q_pair = cat([q_high, q_low])
        dms[bb, sub] = q_pair
        inside = lanes() < tab[bb, T_END + sub]
        product = outer16(hs[layer, bb, sub], q_pair * inside.astype(BF16))
        sums = fold(jnp.where(inside, d_mid, 0.0))
        keep = tab[bb, T_KEEP + sub] == 1
        past = jnp.maximum(sub - 1, 0)
        sm["acc_g"][sub] = product + jnp.where(keep, sm["acc_g"][past], 0.0)
        sm["acc_d"][sub] = sums + jnp.where(keep, sm["acc_d"][past], 0.0)
        sm["d_outer"][layer] += outer16(hid_pair, g_pair)
        sm["d_inner"][layer] += outer16(u_pair, mid_pair)
        sm["s_du"][layer] += fold(du)
        sm["s_g"][layer] += fold(upstream)

    def attention_back(layer, bb, sub):
        pairs = kvs[layer, bb, sub]
        normed = joined(pairs)
        slot = tab[bb, T_SLOT + sub]
        zi = tab[bb, T_ZI + sub]
        inside = lanes() < tab[bb, T_END + sub]
        e_k = dot16(sm["key_mat"][slot], cat(three(pairs, 2 * D))) + wide(sm["key_add"][slot], SUB)
        e_v = dot16(sm["val_mat"][slot], cat(three(pairs))) + wide(sm["val_add"][slot], SUB)
        e = cat([jnp.where(inside, e_k, sm["zk"][zi]), jnp.where(inside, e_v, sm["zv"][zi])])
        shape = (2 * HEADS, group, SUB)
        e3, n3 = e.reshape(shape), normed.reshape(shape)
        scale = rst[layer, bb, sub].reshape(2 * HEADS, 1, SUB)
        along = jnp.mean(e3 * n3, axis=1, keepdims=True)
        dz = ((e3 - n3 * along) * scale).reshape(2 * D, SUB)
        z_high, z_low = split(dz)
        sm["d_kv"][layer] += outer16(cat([z_high, z_low]), hs[layer, bb, sub])
        sm["s_dz"][layer] += fold(dz)
        q_pair = dms[bb, sub] * inside.astype(BF16)
        left = cat([sm["back_mat"][layer, bb, slot], sm["kvw_back"][layer]], 1)
        right = three(q_pair) + [z_high[:D], z_low[:D], z_high[:D], z_high[D:], z_low[D:], z_high[D:]]
        return dot16(left, cat(right)) + sm["zm"][zi]

    def over(low, high, stage):
        def body(i, carry):
            for j in range(UNROLL):
                stage(i * UNROLL + j)
            return carry

        lax.fori_loop(low // UNROLL, high // UNROLL, body, 0)

    half_way = max(UNROLL, (nsub // 2) // UNROLL * UNROLL)

    def loop(stage, between):
        over(0, half_way, stage)
        between()
        over(half_way, nsub, stage)

    def span(bb, s):
        at = lanes()
        return (at >= tab[bb, T_LO + s]) & (at < tab[bb, T_HI + s])

    def fill(name, bb, s, inside, value):
        before = jnp.where(tab[bb, T_ZK + s] == 1, sm[name][s - 1], 0.0)
        sm[name][s] = jnp.where(inside, value, before)

    def corrections_mid(layer, bb):
        @pl.when(edge)
        def _():
            for s in range(1, segs):
                pair = hs[layer, bb, tab[bb, T_C + s]]
                slot = tab[bb, T_CS + s]
                value = dot16(sm["fwd_mat"][slot], cat(three(pair))) + wide(sm["fwd_add"][slot], SUB)
                fill("zm", bb, s, span(bb, s), value)

    def corrections_back(layer, bb):
        @pl.when(edge)
        def _():
            for s in range(1, segs):
                cell, slot, inside = tab[bb, T_C + s], tab[bb, T_CS + s], span(bb, s)
                pairs = kvs[layer, bb, cell]
                e_k = dot16(sm["key_mat"][slot], cat(three(pairs, 2 * D))) + wide(sm["key_add"][slot], SUB)
                e_v = dot16(sm["val_mat"][slot], cat(three(pairs))) + wide(sm["val_add"][slot], SUB)
                e_d = dot16(sm["back_mat"][layer, bb, slot], cat(three(dms[bb, cell])))
                fill("zk", bb, s, inside, e_k)
                fill("zv", bb, s, inside, e_v)
                fill("zm", bb, s, inside, e_d)

    def corrections_moments(layer, bb):
        @pl.when(edge)
        def _():
            for s in range(1, segs):
                cell, inside = tab[bb, T_C + s], span(bb, s)
                pairs = kvs[layer, bb, cell]
                product = outer16(pairs[: 2 * D] * inside.astype(BF16), pairs[2 * D :])
                sm["corr_c"][s] = compact(product)
                sm["corr_n"][s] = fold(jnp.where(inside, joined(pairs), 0.0))

    def corrections_grams(layer, bb):
        @pl.when(edge)
        def _():
            for s in range(1, segs):
                cell, inside = tab[bb, T_C + s], span(bb, s)
                q_pair = dms[bb, cell] * inside.astype(BF16)
                sm["corr_g"][s] = outer16(hs[layer, bb, cell], q_pair)
                sm["corr_d"][s] = fold(q_pair[:D].astype(F32) + q_pair[D:].astype(F32))

    sl = sm["sl"]
    vec = sm["vec"]

    def total_of(name, bb, j):
        return sm["acc_" + name][tab[bb, T_LAST + j]] + sm["corr_" + name][tab[bb, T_CIDX + j]]

    def vec_rows(layer):
        return wvec[layer]

    def moments_of(layer, bb, j):
        sums = mm_nt(ones8, total_of("n", bb, j))
        sl[layer, bb, j] = cat([total_of("c", bb, j), jnp.where(row8 == 0, sums[:, :D], sums[:, D:])], 0)

    def mixing_of(layer, bb, j, pay):
        params = vec_rows(layer)
        key_gain, key_shift = 1.0 + params[4:5], params[5:6]
        value_gain, value_shift = 1.0 + params[6:7], params[7:8]
        count = tab[bb, T_CNT + j].astype(F32)
        keys, values = pay[group : group + 1], pay[group + 1 : group + 2]
        left = jnp.where(row8 == 0, keys * key_gain, jnp.where(row8 == 1, key_shift, 0.0))
        right = jnp.where(row8 == 0, value_shift, jnp.where(row8 == 1, values * value_gain + count * value_shift, 0.0))
        full = tables[layer, 4] * expand(pay[:group]) * value_gain + mm_tn(left, right)
        moments_t = (full * block_mask / count).T
        sm["mt"][layer, bb, j] = moments_t
        mixed = mm(moments_t, cat([sm["wq_t"][layer], tables[layer, 0]], 1))
        through = mm(sm["w3_t"][layer], mixed)
        eye = (
            lax.broadcasted_iota(jnp.int32, (D, D), 0) == lax.broadcasted_iota(jnp.int32, (D, D), 1)
        ).astype(F32)
        forward = through[:, :D] + eye
        sm["fwd_mat"][j] = pack3(forward)
        sm["fwd_add"][j] = through[:, D:] + tables[layer, 3]
        sm["back_mat"][layer, bb, j] = pack3(forward.T)

    def gram_of(layer, bb, j):
        gram = total_of("g", bb, j)
        sums = mm_nt(ones8, total_of("d", bb, j))
        onto = mm(cat([gram, sums], 0), sm["w3_t"][layer])
        both = mm(sm["wq_t"][layer], cat([onto[:D], gram], 1))
        query_bias = tables[layer, 0]
        d_moments = both[:, :D] + query_bias * onto[D : D + 1]
        return compact(d_moments), onto, both[:, D:] + query_bias * sums[0:1], sums

    def projections_of(layer, bb, j, onto, through, sums):
        moments_t = sm["mt"][layer, bb, j]
        d_query = mm(onto, moments_t)
        gb[layer, R_Q : R_Q + D] += d_query[:D]
        gb[layer, R_3 : R_3 + D] += mm(moments_t, through)
        vec[layer, 0] += d_query[D:]
        vec[layer, 3] += sums

    def back_of(layer, bb, j, packed):
        params = vec_rows(layer)
        key_gain, key_shift = 1.0 + params[4:5], params[5:6]
        value_gain, value_shift = 1.0 + params[6:7], params[7:8]
        count = tab[bb, T_CNT + j].astype(F32)
        local = tab[bb, T_NLOC + j].astype(F32)
        d_m = expand(packed) / count
        d_mt = d_m.T
        sm["key_mat"][j] = pack3(centred(tables[layer, 4] * d_m * value_gain))
        sm["key_add"][j] = centred(tables[layer, 4] * mm(d_m, tables[layer, 7]))
        sm["val_mat"][j] = pack3(centred(tables[layer, 6] * d_mt * key_gain))
        sm["val_add"][j] = centred(tables[layer, 6] * mm(d_mt, tables[layer, 5]))
        pay = sl[layer, bb, j]
        keys, values = pay[group : group + 1], pay[group + 1 : group + 2]
        product = d_m * expand(pay[:group])
        from_values = mm_nt(jnp.where(row8 == 0, value_shift, values * value_gain + local * value_shift), d_m)
        from_keys = mm(jnp.where(row8 == 0, key_shift, keys * key_gain + local * key_shift), d_m, HIGHEST)
        vec[layer, 4] += mm_nt(ones8, product * value_gain) + keys * from_values[0:1]
        vec[layer, 5] += jnp.broadcast_to(from_values[1:2], (8, D))
        column_sums = jnp.sum(tables[layer, 4] * product, axis=0, keepdims=True)
        vec[layer, 6] += jnp.broadcast_to(column_sums + values * from_keys[0:1], (8, D))
        vec[layer, 7] += jnp.broadcast_to(from_keys[1:2], (8, D))

    def key_of(stage, bb):
        return stage * per + bb

    def moments_out(layer, bb, k):
        corrections_moments(layer, bb)
        moments_of(layer, bb, 0)
        ar_launch(k, 0, sl[layer, bb, 0])

        @pl.when(edge)
        def _():
            for j in range(1, segs):
                moments_of(layer, bb, j)

    def mixing_in(layer, bb, k):
        @pl.when(edge)
        def _():
            for j in range(1, segs):
                mixing_of(layer, bb, j, sl[layer, bb, j])

        mixing_of(layer, bb, 0, ar_finish(k))
        corrections_mid(layer, bb)

    back_small = sm["back_small"]

    def grams_out(layer, bb, k):
        corrections_grams(layer, bb)
        packed, onto, through, sums = gram_of(layer, bb, 0)
        ar_launch(k, 0, cat([packed, jnp.zeros((PAY - group, D), F32)], 0))
        projections_of(layer, bb, 0, onto, through, sums)

        @pl.when(edge)
        def _():
            for j in range(1, segs):
                packed, onto, through, sums = gram_of(layer, bb, j)
                back_small[bb, j] = packed
                projections_of(layer, bb, j, onto, through, sums)

    def grams_in(layer, bb, k):
        @pl.when(edge)
        def _():
            for j in range(1, segs):
                back_of(layer, bb, j, back_small[bb, j])

        back_of(layer, bb, 0, ar_finish(k)[:group])
        corrections_back(layer, bb)

    vec[...] = jnp.zeros(vec.shape, F32)

    targets = (act_hbm, grd_hbm)

    def kept(kind, layer, bb):
        return pltpu.make_async_copy(
            stage.at[layer, bb], targets[kind].at[c * per + bb], sm["o_local"].at[kind, bb]
        )

    def sent(kind, layer, bb):
        return pltpu.make_async_remote_copy(
            src_ref=stage.at[layer, bb], dst_ref=targets[kind].at[c * per + bb], send_sem=sm["o_send"].at[kind, bb],
            recv_sem=sm["o_recv"].at[kind, bb], device_id={"section": other}, device_id_type=MESH,
        )

    def came(kind, layer, bb):
        return pltpu.make_async_remote_copy(
            src_ref=stage.at[layer, bb], dst_ref=targets[kind].at[other * per + bb], send_sem=sm["o_send"].at[kind, bb],
            recv_sem=sm["o_recv"].at[kind, bb], device_id={"section": other}, device_id_type=MESH,
        )

    def ship(kind, layer, bb):
        @pl.when(c == layer)
        def _():
            kept(kind, layer, bb).start()

        @pl.when(c != layer)
        def _():
            sent(kind, layer, bb).start()

    def shipped(kind, layer, bb):
        @pl.when(c == layer)
        def _():
            kept(kind, layer, bb).wait()

        @pl.when(c != layer)
        def _():
            sent(kind, layer, bb).wait_send()

    def start_stage(bb, sub):
        high, low = split(stage[0, bb, sub].T)
        pair = cat([high, low])
        hs[0, bb, sub] = pair
        keys_and_values(0, bb, sub, pair)

    def first_stage(bb, sub):
        out, mid_pair, hid_pair, slope = feed_forward(0, bb, sub)
        mids[bb, sub] = mid_pair
        hids[bb, sub] = hid_pair
        gps[bb, sub] = slope
        stage[0, bb, sub] = out.T
        high, low = split(out)
        pair = cat([high, low])
        hs[1, bb, sub] = pair
        keys_and_values(1, bb, sub, pair)

    def second_stage(bb, sub):
        out, mid_pair, hid_pair, slope = feed_forward(1, bb, sub)
        upstream = stage[1, bb, sub].T
        stage[1, bb, sub] = out.T
        feed_back(1, bb, sub, upstream, mid_pair, hid_pair, slope)

    def third_stage(bb, sub):
        upstream = attention_back(1, bb, sub)
        stage[1, bb, sub] = upstream.T
        feed_back(0, bb, sub, upstream, mids[bb, sub], hids[bb, sub], gps[bb, sub])

    def fourth_stage(bb, sub):
        stage[0, bb, sub] = attention_back(0, bb, sub).T

    prepare(0)
    for bb in range(per):
        x_copy(bb).wait()
        loop(functools.partial(start_stage, bb), lambda bb=bb: ar_step(key_of(0, bb - 1), 1) if bb > 0 else None)
        moments_out(0, bb, key_of(0, bb))
    prepare(1)
    ar_step(key_of(0, per - 1), 1)

    def in_flight(stage, bb):
        if bb > 0:
            return lambda: ar_step(key_of(stage, bb - 1), 1)
        return lambda: None

    def late(stage):
        ar_step(key_of(stage, per - 1), 1)

    for bb in range(per):
        mixing_in(0, bb, key_of(0, bb))
        loop(functools.partial(first_stage, bb), in_flight(1, bb))
        ship(0, 0, bb)
        moments_out(1, bb, key_of(1, bb))
    for bb in range(per):
        cot_copy(bb).wait()
        mixing_in(1, bb, key_of(1, bb))
        loop(functools.partial(second_stage, bb), in_flight(2, bb) if bb > 0 else lambda: late(1))
        ship(0, 1, bb)
        grams_out(1, bb, key_of(2, bb))
    for bb in range(per):
        grams_in(1, bb, key_of(2, bb))
        shipped(0, 1, bb)
        loop(functools.partial(third_stage, bb), in_flight(3, bb) if bb > 0 else lambda: late(2))
        ship(1, 1, bb)
        grams_out(0, bb, key_of(3, bb))
    for bb in range(per):
        grams_in(0, bb, key_of(3, bb))
        shipped(0, 0, bb)
        loop(functools.partial(fourth_stage, bb), (lambda: None) if bb > 0 else (lambda: late(3)))
        ship(1, 0, bb)

    for layer in range(2):
        d_kv = sm["d_kv"][layer]
        gb[layer, R_K : R_K + D] = d_kv[:D].T
        gb[layer, R_V : R_V + D] = d_kv[D:].T
        d_inner = sm["d_inner"][layer]
        for at in range(0, FF, D):
            gb[layer, R_I + at : R_I + at + D] = d_inner[at : at + D].T
        gb[layer, R_O : R_O + FF] = sm["d_outer"][layer]
        s_dz = mm_nt(ones8, sm["s_dz"][layer])
        s_du = mm_nt(ones8, sm["s_du"][layer])
        s_g = mm_nt(ones8, sm["s_g"][layer])
        pieces = [vec[layer, 0], s_dz[:, :D], s_dz[:, D:]] + [vec[layer, at] for at in range(3, 8)]
        lines = pieces + [s_g, s_du[:, :D], s_du[:, D:]]
        block = jnp.zeros((16, D), F32)
        row16 = lax.broadcasted_iota(jnp.int32, (16, D), 0)
        for at, line in enumerate(lines):
            block = jnp.where(row16 == at, line[0:1], block)
        gb[layer, R_VEC : R_VEC + 16] = block

    cross = pltpu.make_async_remote_copy(
        src_ref=gb.at[other], dst_ref=sm["xb"], send_sem=sm["x_send"].at[0], recv_sem=sm["x_recv"].at[0],
        device_id={"section": other}, device_id_type=MESH,
    )
    cross.start()
    cross.wait_recv()
    gb[c] = gb[c] + sm["xb"][...]

    total_rows = gb.shape[1]
    rb, og = sm["rb"], sm["og"]
    offset_rows, size, at_rb = 0, total_rows, 0
    spans = []
    for digit, (stride, radix) in enumerate(digits):
        piece = size // radix
        spans.append((offset_rows, piece, at_rb))
        mine = offset_rows + digit_at(digit) * piece

        def scatter(offset):
            theirs = pl.multiple_of(offset_rows + digit_at(digit, offset) * piece, 8)
            return pltpu.make_async_remote_copy(
                src_ref=gb.at[c, pl.ds(theirs, piece)],
                dst_ref=rb.at[pl.ds(at_rb + (offset - 1) * piece, piece)],
                send_sem=sm["g_send"].at[0, digit, offset - 1], recv_sem=sm["g_recv"].at[0, digit, offset - 1],
                device_id={"pts": partner(digit, offset)}, device_id_type=MESH,
            )

        copies = [scatter(offset) for offset in range(1, radix)]
        for copy in copies:
            copy.start()
        for copy in copies:
            copy.wait_recv()
        start = pl.multiple_of(mine, 8)
        total = gb[c, pl.ds(start, piece)]
        for offset in range(1, radix):
            total = total + rb[pl.ds(at_rb + (offset - 1) * piece, piece)]
        if digit < len(digits) - 1:
            gb[c, pl.ds(start, piece)] = total
        else:
            og[pl.ds(start, piece)] = total
        for copy in copies:
            copy.wait_send()
        offset_rows, size = mine, piece
        at_rb += (radix - 1) * piece
    for digit in reversed(range(len(digits))):
        stride, radix = digits[digit]
        low, piece, _ = spans[digit]

        def gather(offset, at):
            spot = og.at[pl.ds(pl.multiple_of(low + digit_at(digit, at) * piece, 8), piece)]
            return pltpu.make_async_remote_copy(
                src_ref=spot, dst_ref=spot,
                send_sem=sm["g_send"].at[1, digit, offset - 1], recv_sem=sm["g_recv"].at[1, digit, offset - 1],
                device_id={"pts": partner(digit, offset)}, device_id_type=MESH,
            )

        for offset in range(1, radix):
            gather(offset, 0).start()
        for offset in range(1, radix):
            gather(offset, radix - offset).wait_recv()
        for offset in range(1, radix):
            gather(offset, 0).wait_send()
    out_copy = pltpu.make_async_copy(og, gsum_hbm, dma_in.at[0])
    out_copy.start()

    cross.wait_send()
    for k in range(4):
        weight_send(k).wait_send()
    for k in range(4 * per):
        ar_drain(k)
    for bb in range(per):
        for layer in range(2):
            shipped(1, layer, bb)
        for layer in range(2):
            @pl.when(c == layer)
            def _():
                came(0, layer, bb).wait_recv()
                came(1, layer, bb).wait_recv()
    out_copy.wait()


def finishing(scale, D, FF, gsum, att, inn, out, vec, m_att, v_att, m_inn, v_inn, m_out, v_out, m_vec, v_vec, *results):
    rate = plan()

    def step(weight, gradient, momentum, variance):
        average = gradient * scale
        new_momentum = 0.9 * momentum + 0.1 * average
        new_variance = 0.999 * variance + 0.001 * average * average
        mean = new_momentum / (1.0 - 0.9**STEP)
        square = new_variance / (1.0 - 0.999**STEP)
        updated = weight - rate * (mean / (jnp.sqrt(square) + 1e-08) + 0.01 * weight)
        return gradient, new_momentum, new_variance, updated

    def store(refs, index, values):
        for ref, value in zip(refs, values):
            ref[index] = value

    for part in range(4):
        at = (0, part)
        store(results[0:4], at, step(att[at], gsum[part * D : (part + 1) * D], m_att[at], v_att[at]))
    low = 4 * D
    for part in range(0, FF, D):
        at = (0, slice(None), slice(part, part + D))
        store(results[4:8], at, step(inn[at], gsum[low + part : low + part + D], m_inn[at], v_inn[at]))
    low = 4 * D + FF
    store(results[8:12], 0, step(out[0], gsum[low : low + FF], m_out[0], v_out[0]))
    low = 4 * D + 2 * FF
    lines = vec.shape[1]
    store(results[12:16], 0, step(vec[0], gsum[low : low + lines], m_vec[0], v_vec[0]))


def per_device(
    node_features, cotangent, lengths, attention_weight, inner_weight, outer_weight, vectors,
    momentum_attention, variance_attention, momentum_inner, variance_inner,
    momentum_outer, variance_outer, momentum_vectors, variance_vectors,
):
    places = lax.axis_size("pts")
    micro, rows, D = node_features.shape
    FF = inner_weight.shape[-1]
    segs = lengths.shape[1]
    lines = vectors.shape[1]
    nsub = rows // SUB
    per = micro // 2
    digits = digits_of(places)
    group = D // HEADS
    grad_rows = 4 * D + 2 * FF + 16
    chunk = -(-grad_rows // (8 * places)) * 8
    total_rows = chunk * places
    landing, size = 0, total_rows
    for _, radix in digits:
        size //= radix
        landing += (radix - 1) * size
    nar = 4 * per

    def f32(*shape):
        return pltpu.VMEM(shape, F32)

    def b16(*shape):
        return pltpu.VMEM(shape, BF16)

    def dma(*shape):
        return pltpu.SemaphoreType.DMA(shape)

    scratch = dict(
        watt=f32(2, 4, D, D), winn=f32(2, D, FF), wout=f32(2, FF, D), wvec=f32(2, lines, D),
        tab=pltpu.SMEM((per, 4 * nsub + 9 * segs), jnp.int32),
        tables=f32(2, 11, D, 128), wq_t=f32(2, D, D), w3_t=f32(2, D, D),
        kvw=b16(2, 2 * D, 3 * D), kvw_back=b16(2, D, 6 * D),
        inn_t=b16(2, FF, 3 * D), inn=b16(2, D, 3 * FF), out_t=b16(2, D, 3 * FF), out=b16(2, FF, 3 * D),
        hs=b16(2, per, nsub, 2 * D, SUB), kvs=b16(2, per, nsub, 4 * D, SUB),
        rst=f32(2, per, nsub, 2 * HEADS, SUB), dms=b16(per, nsub, 2 * D, SUB),
        mids=b16(per, nsub, 2 * D, SUB), hids=b16(per, nsub, 2 * FF, SUB), gps=f32(per, nsub, FF, SUB),
        stage=f32(2, per, nsub, SUB, D),
        zm=f32(segs, D, SUB), zk=f32(segs, D, SUB), zv=f32(segs, D, SUB),
        acc_c=f32(nsub + 1, group, D), acc_n=f32(nsub + 1, 2 * D, 128),
        acc_g=f32(nsub + 1, D, D), acc_d=f32(nsub + 1, D, 128),
        corr_c=f32(segs, group, D), corr_n=f32(segs, 2 * D, 128), corr_g=f32(segs, D, D), corr_d=f32(segs, D, 128),
        sl=f32(2, per, segs, PAY, D), back_small=f32(per, segs, group, D), mt=f32(2, per, segs, D, D),
        fwd_mat=b16(segs, D, 3 * D), fwd_add=f32(segs, D, 128), back_mat=b16(2, per, segs, D, 3 * D),
        key_mat=b16(segs, D, 3 * D), key_add=f32(segs, D, 128),
        val_mat=b16(segs, D, 3 * D), val_add=f32(segs, D, 128),
        d_outer=f32(2, FF, D), d_inner=f32(2, FF, D), d_kv=f32(2, 2 * D, D),
        s_du=f32(2, FF, 128), s_g=f32(2, D, 128), s_dz=f32(2, 2 * D, 128),
        vec=f32(2, 8, 8, D), gb=f32(2, total_rows, D), xb=f32(total_rows, D), rb=f32(landing, D), og=f32(total_rows, D),
        ar=f32(nar, len(digits), 4, PAY, D),
        dma_in=dma(2 * per + 4), w_send=dma(4), w_recv=dma(4),
        ar_send=dma(nar, len(digits), 3), ar_recv=dma(nar, len(digits), 3),
        o_local=dma(2, per), o_send=dma(2, per), o_recv=dma(2, per),
        x_send=dma(1), x_recv=dma(1), g_send=dma(2, len(digits), 3), g_recv=dma(2, len(digits), 3),
    )
    cfg = dict(names=list(scratch), places=places, segs=segs, micro=micro, nsub=nsub, D=D, FF=FF)
    anywhere = pl.BlockSpec(memory_space=pl.ANY)
    tiled = (micro, nsub, SUB, D)
    act, grd, gsum = pl.pallas_call(
        functools.partial(mega, cfg),
        out_shape=(
            jax.ShapeDtypeStruct(tiled, F32), jax.ShapeDtypeStruct(tiled, F32),
            jax.ShapeDtypeStruct((total_rows, D), F32),
        ),
        in_specs=[anywhere, anywhere, pl.BlockSpec(memory_space=pltpu.SMEM)] + [anywhere] * 4,
        out_specs=(anywhere, anywhere, anywhere),
        scratch_shapes=list(scratch.values()),
        compiler_params=pltpu.CompilerParams(
            collective_id=0, has_side_effects=True, vmem_limit_bytes=63 * 2**20
        ),
        name="layers",
    )(
        node_features.reshape(tiled), cotangent.reshape(tiled), lengths,
        attention_weight, inner_weight, outer_weight, vectors,
    )
    scale = 1.0 / (micro * rows * places)
    held = [attention_weight, inner_weight, outer_weight, vectors]
    moments = [
        momentum_attention, variance_attention, momentum_inner, variance_inner,
        momentum_outer, variance_outer, momentum_vectors, variance_vectors,
    ]
    small = pl.pallas_call(
        functools.partial(finishing, scale, D, FF),
        out_shape=tuple(jax.ShapeDtypeStruct(piece.shape, F32) for piece in held for _ in range(4)),
        compiler_params=pltpu.CompilerParams(vmem_limit_bytes=32 * 2**20),
        name="adamw",
    )(gsum, *held, *moments)
    whole = (1, micro, rows, D)
    return (act.reshape(whole), grd.reshape(whole)) + tuple(small)


def solution(mesh):
    first = P("section", None, None)
    attention = P("section", None, None, None)
    nodes = P(None, "pts", None)
    return jax.shard_map(
        per_device,
        mesh=mesh,
        in_specs=(nodes, nodes, P(), attention, first, first, first, attention, attention) + (first,) * 6,
        out_specs=(P("section", None, "pts", None),) * 2 + (attention,) * 4 + (first,) * 12,
        check_vma=False,
    )
```

```python
import functools
import math

import jax
import jax.numpy as jnp
from jax import lax
from jax.experimental import pallas as pl
from jax.experimental.pallas import tpu as pltpu
from jax.sharding import PartitionSpec as P

HEADS = 4
STEP = 1200
TOTAL_STEPS = 4000
EPS_NORM = 1e-05
SUB = 256
TILE = 512

MESH = pl.DeviceIdType.MESH
HIGHEST = lax.Precision.HIGHEST
F32 = jnp.float32
BF16 = jnp.bfloat16


def plan():
    warm = 0.3 * TOTAL_STEPS
    top = 0.001
    start = top / 25.0
    low = start / 10000.0
    if STEP <= warm:
        return start + (top - start) * (1.0 - math.cos(math.pi * STEP / warm)) / 2.0
    return low + (top - low) * (1.0 + math.cos(math.pi * (STEP - warm) / (TOTAL_STEPS - warm))) / 2.0


def cat(parts, axis=0):
    return jnp.concatenate(parts, axis=axis)


def split(value):
    high = value.astype(BF16)
    return high, (value - high.astype(F32)).astype(BF16)


def pack3(weight):
    high, low = split(weight)
    return cat([high, high, low], 1)


def pack2(weight):
    return cat(list(split(weight)), 1)


def left3(pack):
    size = pack.shape[1] // 2
    return cat([pack[:, :size], pack], 1)


def right3(value):
    high, low = split(value)
    return cat([high, low, high])


def dot16(left, right):
    return jnp.dot(left, right, preferred_element_type=F32)


def outer16(left, right):
    full = lax.dot_general(left, right, (((1,), (1,)), ((), ())), preferred_element_type=F32)
    m, n = full.shape[0] // 2, full.shape[1] // 2
    return full[:m, :n] + full[m:, :n] + full[:m, n:]


def outer16_sums(left, right):
    ones = jnp.ones((16, left.shape[1]), BF16)
    full = lax.dot_general(cat([left, ones]), right, (((1,), (1,)), ((), ())), preferred_element_type=F32)
    m, n = left.shape[0] // 2, full.shape[1] // 2
    return cat([full[:m, :n] + full[m : 2 * m, :n] + full[:m, n:], full[2 * m :, :n] + full[2 * m :, n:]])


def mm_nt(left, right, precision=HIGHEST):
    return lax.dot_general(left, right, (((1,), (1,)), ((), ())), precision=precision, preferred_element_type=F32)


def wide(table, width):
    return cat([table] * (width // 128), 1)


def fold(value):
    total = value[:, :128]
    for at in range(128, value.shape[1], 128):
        total = total + value[:, at : at + 128]
    return total


def digits_of(places):
    found, stride = [], 1
    while stride < places:
        radix = 4 if (places // stride) % 4 == 0 else 2
        found.append((stride, radix))
        stride *= radix
    return found


def mega(cfg, x_hbm, cot_hbm, len_s, att_hbm, inn_hbm, out_hbm, vec_hbm, act_hbm, grd_hbm, gsum_hbm, *scratch):
    sm = dict(zip(cfg["names"], scratch))
    places, segs, micro, nsub = cfg["places"], cfg["segs"], cfg["micro"], cfg["nsub"]
    rows = nsub * SUB
    tokens = rows * places
    per = micro // 2
    D = cfg["D"]
    FF = cfg["FF"]
    group = D // HEADS
    digits = digits_of(places)
    c = lax.axis_index("section")
    place = lax.axis_index("pts")
    other = 1 - c
    edge = (place == 0) | (place == places - 1)

    stage = sm["stage"]

    dma_in = sm["dma_in"]
    watt, winn, wout, wvec = sm["watt"], sm["winn"], sm["wout"], sm["wvec"]

    def x_copy(bb):
        return pltpu.make_async_copy(x_hbm.at[c * per + bb], stage.at[0, bb], dma_in.at[bb])

    def cot_copy(bb):
        return pltpu.make_async_copy(cot_hbm.at[c * per + bb], stage.at[1, bb], dma_in.at[per + bb])

    weights = [(att_hbm.at[0], watt), (inn_hbm.at[0], winn), (out_hbm.at[0], wout), (vec_hbm, wvec)]

    def weight_copy(k):
        source, held = weights[k]
        return pltpu.make_async_copy(source, held.at[c], dma_in.at[2 * per + k])

    def weight_send(k):
        source, held = weights[k]
        return pltpu.make_async_remote_copy(
            src_ref=source, dst_ref=held.at[c], send_sem=sm["w_send"].at[k], recv_sem=sm["w_recv"].at[k],
            device_id={"section": other}, device_id_type=MESH,
        )

    def weight_arrival(k):
        source, held = weights[k]
        return pltpu.make_async_remote_copy(
            src_ref=source, dst_ref=held.at[other], send_sem=sm["w_send"].at[k], recv_sem=sm["w_recv"].at[k],
            device_id={"section": other}, device_id_type=MESH,
        )

    for k in range(4):
        weight_copy(k).start()
    for bb in range(per):
        x_copy(bb).start()
    for bb in range(per):
        cot_copy(bb).start()

    def partner(digit, offset):
        stride, radix = digits[digit]
        mine = (place // stride) % radix
        theirs = (mine + offset) % radix
        return place + (theirs - mine) * stride

    def digit_at(digit, offset=0):
        stride, radix = digits[digit]
        return ((place // stride) % radix + offset) % radix

    barrier = pltpu.get_barrier_semaphore()
    greeted = 1
    pl.semaphore_signal(barrier, inc=1, device_id={"section": other}, device_id_type=MESH)
    for digit, (stride, radix) in enumerate(digits):
        for offset in range(1, radix):
            pl.semaphore_signal(barrier, inc=1, device_id={"pts": partner(digit, offset)}, device_id_type=MESH)
            greeted += 1

    tab = sm["tab"]
    T_SLOT, T_END, T_ZI, T_KEEP = 0, nsub, 2 * nsub, 3 * nsub
    T_C, T_LO, T_HI, T_CS, T_ZK, T_LAST, T_CIDX, T_NLOC, T_CNT, T_LS, T_LE, T_OK = (
        4 * nsub + at * segs for at in range(12)
    )
    base = place * rows
    zero = jnp.int32(0)

    for bb in range(per):
        batch = c * per + bb
        lens = [len_s[batch, s] for s in range(segs)]
        ends, run = [], zero
        for s in range(segs):
            run = run + lens[s]
            ends.append(run)
        starts = [zero] + ends[:-1]
        big = zero
        for s in range(1, segs):
            big = big + jnp.where(starts[s] <= rows - 1, 1, 0)
        before = zero
        for s in range(segs):
            before = before + jnp.where(ends[s] <= tokens - rows, 1, 0)
        big = jnp.minimum(big, before)
        local_start = [jnp.clip(starts[s] - base, -1, rows) for s in range(segs)]
        local_end = [jnp.clip(ends[s] - base, 0, rows) for s in range(segs)]
        cells, valid = [zero], [zero]
        tab[bb, T_C] = zero
        tab[bb, T_OK] = zero
        for s in range(segs):
            tab[bb, T_LS + s] = local_start[s]
            tab[bb, T_LE + s] = local_end[s]
            slot = jnp.where(s == big, 0, jnp.where(s < big, s + 1, s))
            tab[bb, T_CS + s] = slot
            if s > 0:
                at = local_start[s]
                inside = jnp.maximum(at, 0)
                cell = jnp.minimum(inside // SUB, nsub - 1)
                low = inside - cell * SUB
                ok = jnp.where((at > 0) & (at < rows) & (low > 0), 1, 0)
                cells.append(cell)
                valid.append(ok)
                tab[bb, T_C + s] = cell
                tab[bb, T_OK + s] = ok
                tab[bb, T_LO + s] = jnp.where(ok == 1, low, SUB)
                tab[bb, T_HI + s] = jnp.where(ok == 1, jnp.minimum(local_end[s] - cell * SUB, SUB), 0)
                tab[bb, T_ZK + s] = ok * valid[s - 1] * jnp.where(cell == cells[s - 1], 1, 0)
        past = None
        for sub in range(nsub):
            row = sub * SUB
            first, final = zero, zero
            for s in range(segs - 1):
                first = first + jnp.where(local_end[s] <= row, 1, 0)
                final = final + jnp.where(local_end[s] <= row + SUB - 1, 1, 0)
            tab[bb, T_SLOT + sub] = tab[bb, T_CS + first]
            tab[bb, T_END + sub] = jnp.minimum(tab[bb, T_LE + first] - row, SUB)
            tab[bb, T_KEEP + sub] = zero if past is None else jnp.where(first == past, 1, 0)
            tab[bb, T_ZI + sub] = jnp.where(final == first, 0, final)
            past = first
        for j in range(segs):
            s = big if j == 0 else jnp.where(j - 1 < big, j - 1, j)
            low, high = tab[bb, T_LS + s], tab[bb, T_LE + s]
            cell = jnp.maximum(high - 1, 0) // SUB
            tab[bb, T_LAST + j] = jnp.where((high > 0) & (low < rows) & (cell * SUB >= low), cell, nsub)
            tab[bb, T_CIDX + j] = jnp.where(tab[bb, T_OK + s] == 1, s, 0)
            tab[bb, T_NLOC + j] = high - jnp.maximum(low, 0)
            tab[bb, T_CNT + j] = len_s[batch, s]

    lane_head = lax.broadcasted_iota(jnp.int32, (group, D), 1) // group
    block_mask = (
        lax.broadcasted_iota(jnp.int32, (D, D), 0) // group == lax.broadcasted_iota(jnp.int32, (D, D), 1) // group
    ).astype(F32)
    ones8 = jnp.ones((8, 128), F32)
    row8 = lax.broadcasted_iota(jnp.int32, (8, D), 0)

    def lanes():
        return lax.broadcasted_iota(jnp.int32, (1, SUB), 1)

    def compact(square):
        total = None
        for j in range(HEADS):
            piece = jnp.where(lane_head == j, square[group * j : group * (j + 1), :], 0.0)
            total = piece if total is None else total + piece
        return total

    def moment_rows(product):
        return cat([compact(product[:D]), product[D : D + 8]])

    def expand(packed):
        return cat([packed] * HEADS, 0) * block_mask

    def centred(matrix):
        grouped = matrix.reshape(matrix.shape[0] // group, group, matrix.shape[1])
        return (grouped - jnp.mean(grouped, axis=1, keepdims=True)).reshape(matrix.shape)

    for name in ("zm", "zk", "zv", "corr_c", "corr_n", "corr_g"):
        sm[name][0] = jnp.zeros(sm[name].shape[1:], F32)
    for name in ("acc_c", "acc_n", "acc_g"):
        sm[name][nsub] = jnp.zeros(sm[name].shape[1:], F32)
    for name in ("d_outer", "d_inner", "d_kv", "s_du", "s_g", "s_dz"):
        sm[name][...] = jnp.zeros(sm[name].shape, F32)
    gb = sm["gb"]
    gb[...] = jnp.zeros(gb.shape, F32)
    R_Q, R_K, R_V, R_3, R_I, R_O = 0, D, 2 * D, 3 * D, 4 * D, 4 * D + FF
    R_VEC = 4 * D + 2 * FF

    pl.semaphore_wait(barrier, greeted)
    for k in range(4):
        weight_send(k).start()

    tables = sm["tables"]

    def prepare(layer):
        @pl.when(c == layer)
        def _():
            for k in range(4):
                weight_copy(k).wait()

        @pl.when(c != layer)
        def _():
            for k in range(4):
                weight_arrival(k).wait_recv()

        def column(row):
            return jnp.broadcast_to(wvec[layer, row], (128, D)).T

        for row in (0, 3, 8, 9, 10):
            tables[layer, row] = column(row)
        for row in (1, 2):
            tables[layer, row] = centred(column(row))
        packed = sm["packed"]
        packed[layer, 0] = compact(1.0 + column(4))
        packed[layer, 1] = compact(column(5))
        packed[layer, 2] = compact(1.0 + column(6))
        query_t, output_t = watt[layer, 0].T, watt[layer, 3].T
        sm["wq_t"][layer] = pack3(query_t)
        sm["w3_t"][layer] = pack3(output_t)
        sm["wq_right"][layer] = right3(cat([query_t, tables[layer, 0]], 1))
        sm["w3_right"][layer] = right3(output_t)
        sm["kvw"][layer] = pack3(cat([centred(watt[layer, 1].T), centred(watt[layer, 2].T)], 0))
        sm["kvw_back"][layer] = cat([pack3(watt[layer, 1]), pack3(watt[layer, 2])], 1)
        inner = winn[layer]
        sm["inn_t"][layer] = pack3(cat([inner[:, at : at + D].T for at in range(0, FF, D)], 0))
        sm["inn"][layer] = pack3(inner)
        outer = wout[layer]
        sm["out_t"][layer] = pack3(cat([outer[at : at + D, :].T for at in range(0, FF, D)], 1))
        sm["out"][layer] = pack3(outer)

    ar = sm["ar"]

    def ar_copy(k, digit, offset):
        spot = ar.at[k, digit, digit_at(digit)]
        return pltpu.make_async_remote_copy(
            src_ref=spot, dst_ref=spot, send_sem=sm["ar_send"].at[k, digit, offset - 1],
            recv_sem=sm["ar_recv"].at[k, digit, offset - 1],
            device_id={"pts": partner(digit, offset)}, device_id_type=MESH,
        )

    def ar_arrival(k, digit, offset):
        radix = digits[digit][1]
        spot = ar.at[k, digit, digit_at(digit, radix - offset)]
        return pltpu.make_async_remote_copy(
            src_ref=spot, dst_ref=spot, send_sem=sm["ar_send"].at[k, digit, offset - 1],
            recv_sem=sm["ar_recv"].at[k, digit, offset - 1],
            device_id={"pts": partner(digit, offset)}, device_id_type=MESH,
        )

    def ar_launch(k, digit, payload):
        ar[k, digit, digit_at(digit)] = payload
        for offset in range(1, digits[digit][1]):
            ar_copy(k, digit, offset).start()

    def ar_land(k, digit):
        radix = digits[digit][1]
        for offset in range(1, radix):
            ar_arrival(k, digit, offset).wait_recv()
        total = ar[k, digit, 0]
        for at in range(1, radix):
            total = total + ar[k, digit, at]
        return total

    def ar_step(k, digit):
        if digit < len(digits):
            ar_launch(k, digit, ar_land(k, digit - 1))

    def ar_finish(k):
        for digit in range(2, len(digits)):
            ar_step(k, digit)
        return ar_land(k, len(digits) - 1)

    def ar_drain(k):
        for digit in range(len(digits)):
            for offset in range(1, digits[digit][1]):
                ar_copy(k, digit, offset).wait_send()

    hs, kvs, rst, dms = sm["hs"], sm["kvs"], sm["rst"], sm["dms"]
    mids, hids, gps = sm["mids"], sm["hids"], sm["gps"]

    def three(pair, at=0, size=D):
        high = pair[at : at + size]
        return [high, pair[at + size : at + 2 * size], high]

    def joined(pairs):
        whole = pairs.astype(F32)
        return cat([whole[:D] + whole[D : 2 * D], whole[2 * D : 3 * D] + whole[3 * D :]])

    def load(ref, lead, subs):
        return cat([ref[(*lead, sub)] for sub in subs], 1)

    def save(ref, lead, subs, value):
        for at, sub in enumerate(subs):
            ref[(*lead, sub)] = value[:, SUB * at : SUB * (at + 1)]

    def part(value, at):
        return value[:, SUB * at : SUB * (at + 1)]

    def inside_of(bb, sub):
        return lanes() < tab[bb, T_END + sub]

    def keys_and_values(layer, bb, subs, pair):
        width = SUB * len(subs)
        bias = cat([wide(tables[layer, 1], width), wide(tables[layer, 2], width)], 0)
        field = dot16(sm["kvw"][layer], cat(three(pair))) + bias
        grouped = field.reshape(2 * HEADS, group, width)
        spread = jnp.mean(grouped * grouped, axis=1, keepdims=True)
        scale = lax.rsqrt(spread + EPS_NORM)
        normed = (grouped * scale).reshape(2 * D, width)
        save(rst, (layer, bb), subs, scale.reshape(2 * HEADS, width))
        k_high, k_low = split(normed[:D])
        v_high, v_low = split(normed[D:])
        keys, values = cat([k_high, k_low]), cat([v_high, v_low])
        save(kvs, (layer, bb), subs, cat([keys, values]))
        for at, sub in enumerate(subs):
            inside = inside_of(bb, sub)
            product = moment_rows(outer16_sums(part(keys, at), part(values, at) * inside.astype(BF16)))
            sums = fold(jnp.where(inside, part(normed, at)[:D], 0.0))
            keep = tab[bb, T_KEEP + sub] == 1
            past = jnp.maximum(sub - 1, 0)
            sm["acc_c"][sub] = product + jnp.where(keep, sm["acc_c"][past], 0.0)
            sm["acc_n"][sub] = sums + jnp.where(keep, sm["acc_n"][past], 0.0)

    def feed_forward(layer, bb, subs):
        width = SUB * len(subs)
        middles = []
        for sub in subs:
            slot = tab[bb, T_SLOT + sub]
            value = dot16(left3(sm["fwd_mat"][slot]), cat(three(hs[layer, bb, sub]))) + wide(sm["fwd_add"][slot], SUB)
            middles.append(jnp.where(inside_of(bb, sub), value, sm["zm"][tab[bb, T_ZI + sub]]))
        middle = cat(middles, 1)
        m_high, m_low = split(middle)
        mid_pair = cat([m_high, m_low])
        u = dot16(sm["inn_t"][layer], cat(three(mid_pair)))
        u = u + cat([wide(tables[layer, 9], width), wide(tables[layer, 10], width)], 0)
        k0 = 0.7978845608
        square = u * u
        t = jnp.tanh(u * (k0 + (k0 * 0.044715) * square))
        half = 0.5 + 0.5 * t
        hidden = u * half
        slope = half + hidden * (1.0 - t) * (k0 + (3.0 * k0 * 0.044715) * square)
        h_high, h_low = split(hidden)
        hid_pair = cat([h_high, h_low])
        out = middle + dot16(sm["out_t"][layer], cat(three(hid_pair, 0, FF))) + wide(tables[layer, 8], width)
        return out, mid_pair, hid_pair, slope

    def feed_back(layer, bb, subs, upstream, mid_pair, hid_pair, slope):
        g_high, g_low = split(upstream)
        g_pair = cat([g_high, g_low])
        du = dot16(sm["out"][layer], cat(three(g_pair))) * slope
        u_high, u_low = split(du)
        u_pair = cat([u_high, u_low])
        d_mid = upstream + dot16(sm["inn"][layer], cat(three(u_pair, 0, FF)))
        q_high, q_low = split(d_mid)
        q_pair = cat([q_high, q_low])
        save(dms, (bb,), subs, q_pair)
        for at, sub in enumerate(subs):
            q_inside = part(q_pair, at) * inside_of(bb, sub).astype(BF16)
            product = outer16_sums(hs[layer, bb, sub], q_inside)
            keep = tab[bb, T_KEEP + sub] == 1
            past = jnp.maximum(sub - 1, 0)
            sm["acc_g"][sub] = product + jnp.where(keep, sm["acc_g"][past], 0.0)
        sm["d_outer"][layer] += outer16(hid_pair, g_pair)
        sm["d_inner"][layer] += outer16(u_pair, mid_pair)
        sm["s_du"][layer] += fold(du)
        sm["s_g"][layer] += fold(upstream)

    def attention_back(layer, bb, subs):
        width = SUB * len(subs)
        pairs = load(kvs, (layer, bb), subs)
        normed = joined(pairs)
        e_ks, e_vs, q_pairs = [], [], []
        for at, sub in enumerate(subs):
            slot, zi, inside = tab[bb, T_SLOT + sub], tab[bb, T_ZI + sub], inside_of(bb, sub)
            own = part(pairs, at)
            e_k = dot16(left3(sm["key_mat"][slot]), cat(three(own, 2 * D))) + wide(sm["key_add"][slot], SUB)
            e_v = dot16(left3(sm["val_mat"][slot]), cat(three(own))) + wide(sm["val_add"][slot], SUB)
            e_ks.append(jnp.where(inside, e_k, sm["zk"][zi]))
            e_vs.append(jnp.where(inside, e_v, sm["zv"][zi]))
            q_pairs.append(dms[bb, sub] * inside.astype(BF16))
        e = cat([cat(e_ks, 1), cat(e_vs, 1)])
        shape = (2 * HEADS, group, width)
        e3, n3 = e.reshape(shape), normed.reshape(shape)
        scale = load(rst, (layer, bb), subs).reshape(2 * HEADS, 1, width)
        along = jnp.mean(e3 * n3, axis=1, keepdims=True)
        dz = ((e3 - n3 * along) * scale).reshape(2 * D, width)
        z_high, z_low = split(dz)
        sm["d_kv"][layer] += outer16(cat([z_high, z_low]), load(hs, (layer, bb), subs))
        sm["s_dz"][layer] += fold(dz)
        through = [z_high[:D], z_low[:D], z_high[:D], z_high[D:], z_low[D:], z_high[D:]]
        backs = []
        for at, sub in enumerate(subs):
            slot, zi = tab[bb, T_SLOT + sub], tab[bb, T_ZI + sub]
            left = cat([left3(sm["back_mat"][layer, bb, slot]), sm["kvw_back"][layer]], 1)
            right = three(q_pairs[at]) + [part(one, at) for one in through]
            backs.append(dot16(left, cat(right)) + sm["zm"][zi])
        return cat(backs, 1)

    count = TILE // SUB

    def over(low, high, stage):
        def body(i, carry):
            stage([i * count + at for at in range(count)])
            return carry

        lax.fori_loop(low, high, body, 0)

    steps = nsub // count

    def loop(stage, between):
        over(0, (steps + 1) // 2, stage)
        between()
        over((steps + 1) // 2, steps, stage)

    def span(bb, s):
        at = lanes()
        return (at >= tab[bb, T_LO + s]) & (at < tab[bb, T_HI + s])

    def fill(name, bb, s, inside, value):
        before = jnp.where(tab[bb, T_ZK + s] == 1, sm[name][s - 1], 0.0)
        sm[name][s] = jnp.where(inside, value, before)

    def corrections_mid(layer, bb):
        @pl.when(edge)
        def _():
            for s in range(1, segs):
                pair = hs[layer, bb, tab[bb, T_C + s]]
                slot = tab[bb, T_CS + s]
                value = dot16(left3(sm["fwd_mat"][slot]), cat(three(pair))) + wide(sm["fwd_add"][slot], SUB)
                fill("zm", bb, s, span(bb, s), value)

    def corrections_back(layer, bb):
        @pl.when(edge)
        def _():
            for s in range(1, segs):
                cell, slot, inside = tab[bb, T_C + s], tab[bb, T_CS + s], span(bb, s)
                pairs = kvs[layer, bb, cell]
                e_k = dot16(left3(sm["key_mat"][slot]), cat(three(pairs, 2 * D))) + wide(sm["key_add"][slot], SUB)
                e_v = dot16(left3(sm["val_mat"][slot]), cat(three(pairs))) + wide(sm["val_add"][slot], SUB)
                e_d = dot16(left3(sm["back_mat"][layer, bb, slot]), cat(three(dms[bb, cell])))
                fill("zk", bb, s, inside, e_k)
                fill("zv", bb, s, inside, e_v)
                fill("zm", bb, s, inside, e_d)

    def corrections_moments(layer, bb):
        @pl.when(edge)
        def _():
            for s in range(1, segs):
                cell, inside = tab[bb, T_C + s], span(bb, s)
                pairs = kvs[layer, bb, cell]
                product = outer16_sums(pairs[: 2 * D], pairs[2 * D :] * inside.astype(BF16))
                sm["corr_c"][s] = moment_rows(product)
                keys = pairs[: 2 * D].astype(F32)
                sm["corr_n"][s] = fold(jnp.where(inside, keys[:D] + keys[D:], 0.0))

    def corrections_grams(layer, bb):
        @pl.when(edge)
        def _():
            for s in range(1, segs):
                cell, inside = tab[bb, T_C + s], span(bb, s)
                q_pair = dms[bb, cell] * inside.astype(BF16)
                sm["corr_g"][s] = outer16_sums(hs[layer, bb, cell], q_pair)

    stats, own_c, own_d, vec, vec_c = sm["stats"], sm["own_c"], sm["own_d"], sm["vec"], sm["vec_c"]

    def total_of(name, bb, j):
        return sm["acc_" + name][tab[bb, T_LAST + j]] + sm["corr_" + name][tab[bb, T_CIDX + j]]

    def shifts(layer):
        return 1.0 + wvec[layer, 4], wvec[layer, 5], 1.0 + wvec[layer, 6], wvec[layer, 7]

    def moments_of(layer, bb, j):
        key_gain, key_shift, value_gain, value_shift = shifts(layer)
        gain_c, shift_c = sm["packed"][layer, 0], sm["packed"][layer, 1]
        rows_c = total_of("c", bb, j)
        product, values = rows_c[:group], rows_c[group : group + 1]
        keys = compact(jnp.broadcast_to(jnp.sum(total_of("n", bb, j), axis=1, keepdims=True), (D, 128)))
        stats[layer, bb, j] = cat([product, keys, rows_c[group:]])
        local = tab[bb, T_NLOC + j].astype(F32)
        from_values = values * value_gain + local * value_shift
        return gain_c * (product * value_gain + keys * value_shift) + shift_c * from_values

    def mixing_of(layer, bb, slots, moments):
        packs = []
        for j, moment in zip(slots, moments):
            pack = pack2((expand(moment) / tab[bb, T_CNT + j].astype(F32)).T)
            sm["mt"][layer, bb, j] = pack
            packs.append(left3(pack))
        mixed = dot16(cat(packs), sm["wq_right"][layer])
        rights = [right3(mixed[D * at : D * (at + 1)]) for at in range(len(slots))]
        through = dot16(sm["w3_t"][layer], cat(rights, 1))
        eye = (
            lax.broadcasted_iota(jnp.int32, (D, D), 0) == lax.broadcasted_iota(jnp.int32, (D, D), 1)
        ).astype(F32)
        for at, j in enumerate(slots):
            forward = through[:, 2 * D * at : 2 * D * at + D] + eye
            sm["fwd_mat"][j] = pack2(forward)
            sm["fwd_add"][j] = through[:, 2 * D * at + D : 2 * D * (at + 1)] + tables[layer, 3]
            sm["back_mat"][layer, bb, j] = pack2(forward.T)

    def grams_of(layer, bb, slots):
        grams = [total_of("g", bb, j) for j in slots]
        tall = D + 16
        onto = dot16(cat([pack3(gram) for gram in grams]), sm["w3_right"][layer])
        ontos = [onto[tall * at : tall * (at + 1)] for at in range(len(slots))]
        rights = [right3(cat([one[:D], gram[:D]], 1)) for one, gram in zip(ontos, grams)]
        both = dot16(sm["wq_t"][layer], cat(rights, 1))
        query_bias = tables[layer, 0]
        d_moments, throughs = [], []
        for at, (one, gram) in enumerate(zip(ontos, grams)):
            d_moments.append(compact(both[:, 2 * D * at : 2 * D * at + D] + query_bias * one[D : D + 1]))
            throughs.append(both[:, 2 * D * at + D : 2 * D * (at + 1)] + query_bias * gram[D : D + 1])
        return d_moments, ontos, throughs, grams

    def projections_of(layer, bb, slots, ontos, throughs, grams):
        mts = [sm["mt"][layer, bb, j] for j in slots]
        right = [part for mt in mts for part in (mt[:, :D], mt[:, D:], mt[:, :D])]
        d_query = dot16(cat([pack3(one) for one in ontos], 1), cat(right))
        gb[layer, R_Q : R_Q + D] += d_query[:D]
        gb[layer, R_3 : R_3 + D] += dot16(cat([left3(mt) for mt in mts], 1), cat([right3(through) for through in throughs]))
        vec[layer, 0] += d_query[D : D + 8]
        sums = grams[0][D : D + 8]
        for gram in grams[1:]:
            sums = sums + gram[D : D + 8]
        vec[layer, 1] += sums

    def back_of(layer, bb, slots, d_moments):
        key_gain, key_shift, value_gain, value_shift = shifts(layer)
        gain_c, shift_c, value_gain_c = (sm["packed"][layer, at] for at in range(3))

        def across(packed):
            return jnp.broadcast_to(jnp.sum(expand(centred(packed)), axis=1, keepdims=True), (D, 128))

        for j, d_moment in zip(slots, d_moments):
            d = d_moment / tab[bb, T_CNT + j].astype(F32)
            d_t = compact(expand(d).T)
            sm["key_mat"][j] = pack2(expand(centred(gain_c * d * value_gain)))
            sm["key_add"][j] = across(gain_c * d * value_shift)
            sm["val_mat"][j] = pack2(expand(centred(value_gain_c * d_t * key_gain)))
            sm["val_add"][j] = across(value_gain_c * d_t * key_shift)
            held = stats[layer, bb, j]
            product, keys, values = held[:group], held[group : 2 * group], held[2 * group : 2 * group + 1]
            local = tab[bb, T_NLOC + j].astype(F32)
            vec_c[layer, 0] += d * (product * value_gain + keys * value_shift)
            vec_c[layer, 1] += d * (values * value_gain + local * value_shift)
            vec_c[layer, 2] += d * (gain_c * product + shift_c * values)
            vec_c[layer, 3] += d * (gain_c * keys + shift_c * local)

    small = list(range(1, segs))

    def key_of(stage, bb):
        return stage * per + bb

    def moments_out(layer, bb, k):
        corrections_moments(layer, bb)
        ar_launch(k, 0, moments_of(layer, bb, 0))

        @pl.when(edge)
        def _():
            for j in small:
                own_c[layer, bb, j] = moments_of(layer, bb, j)

    def mixing_in(layer, bb, k):
        @pl.when(edge)
        def _():
            mixing_of(layer, bb, small, [own_c[layer, bb, j] for j in small])

        mixing_of(layer, bb, [0], [ar_finish(k)])
        corrections_mid(layer, bb)

    def grams_out(layer, bb, k):
        corrections_grams(layer, bb)
        d_moments, *rest = grams_of(layer, bb, [0])
        ar_launch(k, 0, d_moments[0])
        projections_of(layer, bb, [0], *rest)

        @pl.when(edge)
        def _():
            d_moments, *rest = grams_of(layer, bb, small)
            for j, d_moment in zip(small, d_moments):
                own_d[bb, j] = d_moment
            projections_of(layer, bb, small, *rest)

    def grams_in(layer, bb, k):
        @pl.when(edge)
        def _():
            back_of(layer, bb, small, [own_d[bb, j] for j in small])

        back_of(layer, bb, [0], [ar_finish(k)])
        corrections_back(layer, bb)

    vec[...] = jnp.zeros(vec.shape, F32)
    vec_c[...] = jnp.zeros(vec_c.shape, F32)

    targets = (act_hbm, grd_hbm)

    def kept(kind, layer, bb):
        return pltpu.make_async_copy(
            stage.at[layer, bb], targets[kind].at[c * per + bb], sm["o_local"].at[kind, bb]
        )

    def sent(kind, layer, bb):
        return pltpu.make_async_remote_copy(
            src_ref=stage.at[layer, bb], dst_ref=targets[kind].at[c * per + bb], send_sem=sm["o_send"].at[kind, bb],
            recv_sem=sm["o_recv"].at[kind, bb], device_id={"section": other}, device_id_type=MESH,
        )

    def came(kind, layer, bb):
        return pltpu.make_async_remote_copy(
            src_ref=stage.at[layer, bb], dst_ref=targets[kind].at[other * per + bb], send_sem=sm["o_send"].at[kind, bb],
            recv_sem=sm["o_recv"].at[kind, bb], device_id={"section": other}, device_id_type=MESH,
        )

    def ship(kind, layer, bb):
        @pl.when(c == layer)
        def _():
            kept(kind, layer, bb).start()

        @pl.when(c != layer)
        def _():
            sent(kind, layer, bb).start()

    def shipped(kind, layer, bb):
        @pl.when(c == layer)
        def _():
            kept(kind, layer, bb).wait()

        @pl.when(c != layer)
        def _():
            sent(kind, layer, bb).wait_send()

    def load_t(layer, bb, subs):
        return cat([stage[layer, bb, sub].T for sub in subs], 1)

    def save_t(layer, bb, subs, value):
        for at, sub in enumerate(subs):
            stage[layer, bb, sub] = part(value, at).T

    def start_stage(bb, subs):
        high, low = split(load_t(0, bb, subs))
        pair = cat([high, low])
        save(hs, (0, bb), subs, pair)
        keys_and_values(0, bb, subs, pair)

    def first_stage(bb, subs):
        out, mid_pair, hid_pair, slope = feed_forward(0, bb, subs)
        save(mids, (bb,), subs, mid_pair)
        save(hids, (bb,), subs, hid_pair)
        save(gps, (bb,), subs, slope)
        save_t(0, bb, subs, out)
        high, low = split(out)
        pair = cat([high, low])
        save(hs, (1, bb), subs, pair)
        keys_and_values(1, bb, subs, pair)

    def second_stage(bb, subs):
        out, mid_pair, hid_pair, slope = feed_forward(1, bb, subs)
        upstream = load_t(1, bb, subs)
        save_t(1, bb, subs, out)
        feed_back(1, bb, subs, upstream, mid_pair, hid_pair, slope)

    def third_stage(bb, subs):
        upstream = attention_back(1, bb, subs)
        save_t(1, bb, subs, upstream)
        held = [load(ref, (bb,), subs) for ref in (mids, hids, gps)]
        feed_back(0, bb, subs, upstream, *held)

    def fourth_stage(bb, subs):
        save_t(0, bb, subs, attention_back(0, bb, subs))

    prepare(0)
    for bb in range(per):
        x_copy(bb).wait()
        loop(functools.partial(start_stage, bb), lambda bb=bb: ar_step(key_of(0, bb - 1), 1) if bb > 0 else None)
        moments_out(0, bb, key_of(0, bb))
    prepare(1)
    ar_step(key_of(0, per - 1), 1)

    def in_flight(stage, bb):
        if bb > 0:
            return lambda: ar_step(key_of(stage, bb - 1), 1)
        return lambda: None

    def late(stage):
        ar_step(key_of(stage, per - 1), 1)

    for bb in range(per):
        mixing_in(0, bb, key_of(0, bb))
        loop(functools.partial(first_stage, bb), in_flight(1, bb))
        ship(0, 0, bb)
        moments_out(1, bb, key_of(1, bb))
    for bb in range(per):
        cot_copy(bb).wait()
        mixing_in(1, bb, key_of(1, bb))
        loop(functools.partial(second_stage, bb), in_flight(2, bb) if bb > 0 else lambda: late(1))
        ship(0, 1, bb)
        grams_out(1, bb, key_of(2, bb))
    for bb in range(per):
        grams_in(1, bb, key_of(2, bb))
        shipped(0, 1, bb)
        loop(functools.partial(third_stage, bb), in_flight(3, bb) if bb > 0 else lambda: late(2))
        ship(1, 1, bb)
        grams_out(0, bb, key_of(3, bb))
    for bb in range(per):
        grams_in(0, bb, key_of(3, bb))
        shipped(0, 0, bb)
        loop(functools.partial(fourth_stage, bb), (lambda: None) if bb > 0 else (lambda: late(3)))
        ship(1, 0, bb)

    for layer in range(2):
        d_kv = sm["d_kv"][layer]
        gb[layer, R_K : R_K + D] = d_kv[:D].T
        gb[layer, R_V : R_V + D] = d_kv[D:].T
        d_inner = sm["d_inner"][layer]
        for at in range(0, FF, D):
            gb[layer, R_I + at : R_I + at + D] = d_inner[at : at + D].T
        gb[layer, R_O : R_O + FF] = sm["d_outer"][layer]
        s_dz = mm_nt(ones8, sm["s_dz"][layer])
        s_du = mm_nt(ones8, sm["s_du"][layer])
        s_g = mm_nt(ones8, sm["s_g"][layer])
        lines = [vec[layer, 0], s_dz[:, :D], s_dz[:, D:], vec[layer, 1]]
        lines += [mm_nt(ones8, expand(vec_c[layer, at])) for at in (0, 1)]
        lines += [jnp.sum(vec_c[layer, at], axis=0, keepdims=True) for at in (2, 3)]
        lines += [s_g, s_du[:, :D], s_du[:, D:]]
        block = jnp.zeros((16, D), F32)
        row16 = lax.broadcasted_iota(jnp.int32, (16, D), 0)
        for at, line in enumerate(lines):
            block = jnp.where(row16 == at, line[0:1], block)
        gb[layer, R_VEC : R_VEC + 16] = block

    cross = pltpu.make_async_remote_copy(
        src_ref=gb.at[other], dst_ref=sm["xb"], send_sem=sm["x_send"].at[0], recv_sem=sm["x_recv"].at[0],
        device_id={"section": other}, device_id_type=MESH,
    )
    cross.start()
    cross.wait_recv()
    gb[c] = gb[c] + sm["xb"][...]

    total_rows = gb.shape[1]
    rb, og = sm["rb"], sm["og"]
    offset_rows, size, at_rb = 0, total_rows, 0
    spans = []
    for digit, (stride, radix) in enumerate(digits):
        piece = size // radix
        spans.append((offset_rows, piece, at_rb))
        mine = offset_rows + digit_at(digit) * piece

        def scatter(offset):
            theirs = pl.multiple_of(offset_rows + digit_at(digit, offset) * piece, 8)
            return pltpu.make_async_remote_copy(
                src_ref=gb.at[c, pl.ds(theirs, piece)],
                dst_ref=rb.at[pl.ds(at_rb + (offset - 1) * piece, piece)],
                send_sem=sm["g_send"].at[0, digit, offset - 1], recv_sem=sm["g_recv"].at[0, digit, offset - 1],
                device_id={"pts": partner(digit, offset)}, device_id_type=MESH,
            )

        copies = [scatter(offset) for offset in range(1, radix)]
        for copy in copies:
            copy.start()
        for copy in copies:
            copy.wait_recv()
        start = pl.multiple_of(mine, 8)
        total = gb[c, pl.ds(start, piece)]
        for offset in range(1, radix):
            total = total + rb[pl.ds(at_rb + (offset - 1) * piece, piece)]
        if digit < len(digits) - 1:
            gb[c, pl.ds(start, piece)] = total
        else:
            og[pl.ds(start, piece)] = total
        for copy in copies:
            copy.wait_send()
        offset_rows, size = mine, piece
        at_rb += (radix - 1) * piece
    for digit in reversed(range(len(digits))):
        stride, radix = digits[digit]
        low, piece, _ = spans[digit]

        def gather(offset, at):
            spot = og.at[pl.ds(pl.multiple_of(low + digit_at(digit, at) * piece, 8), piece)]
            return pltpu.make_async_remote_copy(
                src_ref=spot, dst_ref=spot,
                send_sem=sm["g_send"].at[1, digit, offset - 1], recv_sem=sm["g_recv"].at[1, digit, offset - 1],
                device_id={"pts": partner(digit, offset)}, device_id_type=MESH,
            )

        for offset in range(1, radix):
            gather(offset, 0).start()
        for offset in range(1, radix):
            gather(offset, radix - offset).wait_recv()
        for offset in range(1, radix):
            gather(offset, 0).wait_send()
    out_copy = pltpu.make_async_copy(og, gsum_hbm, dma_in.at[0])
    out_copy.start()

    cross.wait_send()
    for k in range(4):
        weight_send(k).wait_send()
    for k in range(4 * per):
        ar_drain(k)
    for bb in range(per):
        for layer in range(2):
            shipped(1, layer, bb)
        for layer in range(2):
            @pl.when(c == layer)
            def _():
                came(0, layer, bb).wait_recv()
                came(1, layer, bb).wait_recv()
    out_copy.wait()


def finishing(scale, D, FF, act, grd, gsum_hbm, *refs):
    sources, results = refs[:12], refs[12:30]
    gsum, held, made, sem_large, sem_in, sem_out = refs[30], refs[31:43], refs[43:59], *refs[59:]
    large = []
    for kind, (source, target) in enumerate(((act, results[0]), (grd, results[1]))):
        for part in range(source.shape[0]):
            large.append(pltpu.make_async_copy(source.at[part], target.at[part], sem_large.at[kind, part]))
    loads = [pltpu.make_async_copy(gsum_hbm, gsum, sem_in.at[12])]
    loads += [pltpu.make_async_copy(sources[at], held[at], sem_in.at[at]) for at in range(12)]
    for copy in loads:
        copy.start()
    for copy in large:
        copy.start()
    rate = plan()

    def step(weight, gradient, momentum, variance):
        average = gradient * scale
        new_momentum = 0.9 * momentum + 0.1 * average
        new_variance = 0.999 * variance + 0.001 * average * average
        mean = new_momentum / (1.0 - 0.9**STEP)
        square = new_variance / (1.0 - 0.999**STEP)
        updated = weight - rate * (mean / (jnp.sqrt(square) + 1e-08) + 0.01 * weight)
        return gradient, new_momentum, new_variance, updated

    low = 4 * D
    late = low + 2 * FF
    places = [
        [((0, part), slice(part * D, (part + 1) * D)) for part in range(4)],
        [((0, slice(None), slice(at, at + D)), slice(low + at, low + at + D)) for at in range(0, FF, D)],
        [((0,), slice(low + FF, low + 2 * FF))],
        [((line,), slice(late + line, late + line + 1)) for line in range(held[3].shape[0])],
    ]
    loads[0].wait()
    stores = []
    for kind in range(4):
        for at in (kind, 4 + 2 * kind, 5 + 2 * kind):
            loads[1 + at].wait()
        weight, momentum, variance = held[kind], held[4 + 2 * kind], held[5 + 2 * kind]
        for index, lines in places[kind]:
            values = step(weight[index], gsum[lines], momentum[index], variance[index])
            for ref, value in zip(made[4 * kind : 4 * kind + 4], values):
                ref[index] = value
        for at in range(4 * kind, 4 * kind + 4):
            stores.append(pltpu.make_async_copy(made[at], results[2 + at], sem_out.at[at]))
            stores[-1].start()
    for copy in large + stores:
        copy.wait()


def per_device(
    node_features, cotangent, lengths, attention_weight, inner_weight, outer_weight, vectors,
    momentum_attention, variance_attention, momentum_inner, variance_inner,
    momentum_outer, variance_outer, momentum_vectors, variance_vectors,
):
    places = lax.axis_size("pts")
    micro, rows, D = node_features.shape
    FF = inner_weight.shape[-1]
    segs = lengths.shape[1]
    lines = vectors.shape[1]
    nsub = rows // SUB
    per = micro // 2
    digits = digits_of(places)
    group = D // HEADS
    grad_rows = 4 * D + 2 * FF + 16
    chunk = -(-grad_rows // (8 * places)) * 8
    total_rows = chunk * places
    landing, size = 0, total_rows
    for _, radix in digits:
        size //= radix
        landing += (radix - 1) * size
    nar = 4 * per

    def f32(*shape):
        return pltpu.VMEM(shape, F32)

    def b16(*shape):
        return pltpu.VMEM(shape, BF16)

    def dma(*shape):
        return pltpu.SemaphoreType.DMA(shape)

    scratch = dict(
        watt=f32(2, 4, D, D), winn=f32(2, D, FF), wout=f32(2, FF, D), wvec=f32(2, lines, 1, D),
        tab=pltpu.SMEM((per, 4 * nsub + 12 * segs), jnp.int32),
        tables=f32(2, 11, D, 128), packed=f32(2, 3, group, D),
        wq_t=b16(2, D, 3 * D), w3_t=b16(2, D, 3 * D), wq_right=b16(2, 3 * D, 2 * D), w3_right=b16(2, 3 * D, D),
        kvw=b16(2, 2 * D, 3 * D), kvw_back=b16(2, D, 6 * D),
        inn_t=b16(2, FF, 3 * D), inn=b16(2, D, 3 * FF), out_t=b16(2, D, 3 * FF), out=b16(2, FF, 3 * D),
        hs=b16(2, per, nsub, 2 * D, SUB), kvs=b16(2, per, nsub, 4 * D, SUB),
        rst=f32(2, per, nsub, 2 * HEADS, SUB), dms=b16(per, nsub, 2 * D, SUB),
        mids=b16(per, nsub, 2 * D, SUB), hids=b16(per, nsub, 2 * FF, SUB), gps=f32(per, nsub, FF, SUB),
        stage=f32(2, per, nsub, SUB, D),
        zm=f32(segs, D, SUB), zk=f32(segs, D, SUB), zv=f32(segs, D, SUB),
        acc_c=f32(nsub + 1, group + 8, D), acc_n=f32(nsub + 1, D, 128), acc_g=f32(nsub + 1, D + 16, D),
        corr_c=f32(segs, group + 8, D), corr_n=f32(segs, D, 128), corr_g=f32(segs, D + 16, D),
        stats=f32(2, per, segs, 2 * group + 8, D), own_c=f32(2, per, segs, group, D), own_d=f32(per, segs, group, D),
        mt=b16(2, per, segs, D, 2 * D), vec_c=f32(2, 4, group, D),
        fwd_mat=b16(segs, D, 2 * D), fwd_add=f32(segs, D, 128), back_mat=b16(2, per, segs, D, 2 * D),
        key_mat=b16(segs, D, 2 * D), key_add=f32(segs, D, 128),
        val_mat=b16(segs, D, 2 * D), val_add=f32(segs, D, 128),
        d_outer=f32(2, FF, D), d_inner=f32(2, FF, D), d_kv=f32(2, 2 * D, D),
        s_du=f32(2, FF, 128), s_g=f32(2, D, 128), s_dz=f32(2, 2 * D, 128),
        vec=f32(2, 2, 8, D), gb=f32(2, total_rows, D), xb=f32(total_rows, D), rb=f32(landing, D), og=f32(total_rows, D),
        ar=f32(nar, len(digits), 4, group, D),
        dma_in=dma(2 * per + 4), w_send=dma(4), w_recv=dma(4),
        ar_send=dma(nar, len(digits), 3), ar_recv=dma(nar, len(digits), 3),
        o_local=dma(2, per), o_send=dma(2, per), o_recv=dma(2, per),
        x_send=dma(1), x_recv=dma(1), g_send=dma(2, len(digits), 3), g_recv=dma(2, len(digits), 3),
    )
    cfg = dict(names=list(scratch), places=places, segs=segs, micro=micro, nsub=nsub, D=D, FF=FF)

    def lined(piece):
        return jnp.transpose(piece, (1, 0, 2))

    anywhere = pl.BlockSpec(memory_space=pl.ANY)
    tiled = (micro, nsub, SUB, D)
    act, grd, gsum = pl.pallas_call(
        functools.partial(mega, cfg),
        out_shape=(
            jax.ShapeDtypeStruct(tiled, F32), jax.ShapeDtypeStruct(tiled, F32),
            jax.ShapeDtypeStruct((total_rows, D), F32),
        ),
        in_specs=[anywhere, anywhere, pl.BlockSpec(memory_space=pltpu.SMEM)] + [anywhere] * 4,
        out_specs=(anywhere, anywhere, anywhere),
        scratch_shapes=list(scratch.values()),
        compiler_params=pltpu.CompilerParams(
            collective_id=0, has_side_effects=True, vmem_limit_bytes=63 * 2**20
        ),
        name="layers",
    )(
        node_features.reshape(tiled), cotangent.reshape(tiled), lengths,
        attention_weight, inner_weight, outer_weight, lined(vectors),
    )
    scale = 1.0 / (micro * rows * places)
    held = [attention_weight, inner_weight, outer_weight, vectors]
    moments = [
        momentum_attention, variance_attention, momentum_inner, variance_inner,
        momentum_outer, variance_outer, momentum_vectors, variance_vectors,
    ]
    held[3] = lined(vectors)
    moments[6:] = [lined(momentum_vectors), lined(variance_vectors)]
    shapes = [jax.ShapeDtypeStruct(piece.shape, F32) for piece in held for _ in range(4)]
    results = pl.pallas_call(
        functools.partial(finishing, scale, D, FF),
        out_shape=tuple([jax.ShapeDtypeStruct(tiled, F32)] * 2 + shapes),
        in_specs=[anywhere] * 15,
        out_specs=tuple([anywhere] * 18),
        scratch_shapes=[f32(total_rows, D)] + [f32(*piece.shape) for piece in held + moments]
        + [f32(*shape.shape) for shape in shapes] + [dma(2, micro), dma(13), dma(16)],
        compiler_params=pltpu.CompilerParams(vmem_limit_bytes=32 * 2**20),
        name="adamw",
    )(act, grd, gsum, *held, *moments)
    whole = (1, micro, rows, D)
    lines_back = tuple(lined(piece) for piece in results[14:])
    return (results[0].reshape(whole), results[1].reshape(whole)) + tuple(results[2:14]) + lines_back


def solution(mesh):
    first = P("section", None, None)
    attention = P("section", None, None, None)
    nodes = P(None, "pts", None)
    return jax.shard_map(
        per_device,
        mesh=mesh,
        in_specs=(nodes, nodes, P(), attention, first, first, first, attention, attention) + (first,) * 6,
        out_specs=(P("section", None, "pts", None),) * 2 + (attention,) * 4 + (first,) * 12,
        check_vma=False,
    )
```

```python
import functools
import math

import jax
import jax.numpy as jnp
from jax import lax
from jax.experimental import pallas as pl
from jax.experimental.pallas import tpu as pltpu
from jax.sharding import PartitionSpec as P

HEADS = 4
STEP = 1200
TOTAL_STEPS = 4000
EPS_NORM = 1e-05
SUB = 256
TILE = 512

MESH = pl.DeviceIdType.MESH
HIGHEST = lax.Precision.HIGHEST
F32 = jnp.float32
BF16 = jnp.bfloat16


def plan():
    warm = 0.3 * TOTAL_STEPS
    top = 0.001
    start = top / 25.0
    low = start / 10000.0
    if STEP <= warm:
        return start + (top - start) * (1.0 - math.cos(math.pi * STEP / warm)) / 2.0
    return low + (top - low) * (1.0 + math.cos(math.pi * (STEP - warm) / (TOTAL_STEPS - warm))) / 2.0


def cat(parts, axis=0):
    return jnp.concatenate(parts, axis=axis)


def split(value):
    high = value.astype(BF16)
    return high, (value - high.astype(F32)).astype(BF16)


def pack3(weight):
    high, low = split(weight)
    return cat([high, high, low], 1)


def pack2(weight):
    return cat(list(split(weight)), 1)


def left3(pack):
    size = pack.shape[1] // 2
    return cat([pack[:, :size], pack], 1)


def right3(value):
    high, low = split(value)
    return cat([high, low, high])


def dot16(left, right):
    return jnp.dot(left, right, preferred_element_type=F32)


def outer16(left, right):
    full = lax.dot_general(left, right, (((1,), (1,)), ((), ())), preferred_element_type=F32)
    m, n = full.shape[0] // 2, full.shape[1] // 2
    return full[:m, :n] + full[m:, :n] + full[:m, n:]


def outer16_sums(left, right):
    ones = jnp.ones((16, left.shape[1]), BF16)
    full = lax.dot_general(cat([left, ones]), right, (((1,), (1,)), ((), ())), preferred_element_type=F32)
    m, n = left.shape[0] // 2, full.shape[1] // 2
    return cat([full[:m, :n] + full[m : 2 * m, :n] + full[:m, n:], full[2 * m :, :n] + full[2 * m :, n:]])


def mm_nt(left, right, precision=HIGHEST):
    return lax.dot_general(left, right, (((1,), (1,)), ((), ())), precision=precision, preferred_element_type=F32)


def wide(table, width):
    return cat([table] * (width // 128), 1)


def fold(value):
    total = value[:, :128]
    for at in range(128, value.shape[1], 128):
        total = total + value[:, at : at + 128]
    return total


def digits_of(places):
    found, stride = [], 1
    while stride < places:
        radix = 4 if (places // stride) % 4 == 0 else 2
        found.append((stride, radix))
        stride *= radix
    return found


def gradient_rows(D, FF, digits):
    unit = 8
    for _, radix in digits[:2]:
        unit *= radix
    early = -(-(2 * FF + 2 * D) // unit) * unit
    late = -(-(2 * D + 16) // unit) * unit
    first = dict(outer=0, inner=FF, q=2 * FF, o=2 * FF + D, k=early, v=early + D, vec=early + 2 * D)
    return first, (early, late)


def mega(cfg, x_hbm, cot_hbm, len_s, att_hbm, inn_hbm, out_hbm, vec_hbm, act_hbm, grd_hbm, gsum_hbm, *scratch):
    sm = dict(zip(cfg["names"], scratch))
    places, segs, micro, nsub = cfg["places"], cfg["segs"], cfg["micro"], cfg["nsub"]
    rows = nsub * SUB
    tokens = rows * places
    per = micro // 2
    D = cfg["D"]
    FF = cfg["FF"]
    group = D // HEADS
    digits = digits_of(places)
    c = lax.axis_index("section")
    place = lax.axis_index("pts")
    other = 1 - c
    edge = (place == 0) | (place == places - 1)

    stage = sm["stage"]

    dma_in = sm["dma_in"]
    watt, winn, wout, wvec = sm["watt"], sm["winn"], sm["wout"], sm["wvec"]

    def x_copy(bb):
        return pltpu.make_async_copy(x_hbm.at[c * per + bb], stage.at[0, bb], dma_in.at[bb])

    def cot_copy(bb):
        return pltpu.make_async_copy(cot_hbm.at[c * per + bb], stage.at[1, bb], dma_in.at[per + bb])

    weights = [(att_hbm.at[0], watt), (inn_hbm.at[0], winn), (out_hbm.at[0], wout), (vec_hbm, wvec)]

    def weight_copy(k):
        source, held = weights[k]
        return pltpu.make_async_copy(source, held.at[c], dma_in.at[2 * per + k])

    def weight_send(k):
        source, held = weights[k]
        return pltpu.make_async_remote_copy(
            src_ref=source, dst_ref=held.at[c], send_sem=sm["w_send"].at[k], recv_sem=sm["w_recv"].at[k],
            device_id={"section": other}, device_id_type=MESH,
        )

    def weight_arrival(k):
        source, held = weights[k]
        return pltpu.make_async_remote_copy(
            src_ref=source, dst_ref=held.at[other], send_sem=sm["w_send"].at[k], recv_sem=sm["w_recv"].at[k],
            device_id={"section": other}, device_id_type=MESH,
        )

    for k in range(4):
        weight_copy(k).start()
    for bb in range(per):
        x_copy(bb).start()
    for bb in range(per):
        cot_copy(bb).start()

    def partner(digit, offset):
        stride, radix = digits[digit]
        mine = (place // stride) % radix
        theirs = (mine + offset) % radix
        return place + (theirs - mine) * stride

    def digit_at(digit, offset=0):
        stride, radix = digits[digit]
        return ((place // stride) % radix + offset) % radix

    barrier = pltpu.get_barrier_semaphore()
    greeted = 1
    pl.semaphore_signal(barrier, inc=1, device_id={"section": other}, device_id_type=MESH)
    for digit, (stride, radix) in enumerate(digits):
        for offset in range(1, radix):
            pl.semaphore_signal(barrier, inc=1, device_id={"pts": partner(digit, offset)}, device_id_type=MESH)
            greeted += 1

    for offset in range(1, digits[0][1]):
        pl.semaphore_signal(
            barrier, inc=1, device_id={"section": other, "pts": partner(0, offset)}, device_id_type=MESH
        )
        greeted += 1

    tab = sm["tab"]
    T_SLOT, T_END, T_ZI, T_KEEP = 0, nsub, 2 * nsub, 3 * nsub
    T_C, T_LO, T_HI, T_CS, T_ZK, T_LAST, T_CIDX, T_NLOC, T_CNT, T_LS, T_LE, T_OK = (
        4 * nsub + at * segs for at in range(12)
    )
    base = place * rows
    zero = jnp.int32(0)

    for bb in range(per):
        batch = c * per + bb
        lens = [len_s[batch, s] for s in range(segs)]
        ends, run = [], zero
        for s in range(segs):
            run = run + lens[s]
            ends.append(run)
        starts = [zero] + ends[:-1]
        big = zero
        for s in range(1, segs):
            big = big + jnp.where(starts[s] <= rows - 1, 1, 0)
        before = zero
        for s in range(segs):
            before = before + jnp.where(ends[s] <= tokens - rows, 1, 0)
        big = jnp.minimum(big, before)
        local_start = [jnp.clip(starts[s] - base, -1, rows) for s in range(segs)]
        local_end = [jnp.clip(ends[s] - base, 0, rows) for s in range(segs)]
        cells, valid = [zero], [zero]
        tab[bb, T_C] = zero
        tab[bb, T_OK] = zero
        for s in range(segs):
            tab[bb, T_LS + s] = local_start[s]
            tab[bb, T_LE + s] = local_end[s]
            slot = jnp.where(s == big, 0, jnp.where(s < big, s + 1, s))
            tab[bb, T_CS + s] = slot
            if s > 0:
                at = local_start[s]
                inside = jnp.maximum(at, 0)
                cell = jnp.minimum(inside // SUB, nsub - 1)
                low = inside - cell * SUB
                ok = jnp.where((at > 0) & (at < rows) & (low > 0), 1, 0)
                cells.append(cell)
                valid.append(ok)
                tab[bb, T_C + s] = cell
                tab[bb, T_OK + s] = ok
                tab[bb, T_LO + s] = jnp.where(ok == 1, low, SUB)
                tab[bb, T_HI + s] = jnp.where(ok == 1, jnp.minimum(local_end[s] - cell * SUB, SUB), 0)
                tab[bb, T_ZK + s] = ok * valid[s - 1] * jnp.where(cell == cells[s - 1], 1, 0)
        past = None
        for sub in range(nsub):
            row = sub * SUB
            first, final = zero, zero
            for s in range(segs - 1):
                first = first + jnp.where(local_end[s] <= row, 1, 0)
                final = final + jnp.where(local_end[s] <= row + SUB - 1, 1, 0)
            tab[bb, T_SLOT + sub] = tab[bb, T_CS + first]
            tab[bb, T_END + sub] = jnp.minimum(tab[bb, T_LE + first] - row, SUB)
            tab[bb, T_KEEP + sub] = zero if past is None else jnp.where(first == past, 1, 0)
            tab[bb, T_ZI + sub] = jnp.where(final == first, 0, final)
            past = first
        for j in range(segs):
            s = big if j == 0 else jnp.where(j - 1 < big, j - 1, j)
            low, high = tab[bb, T_LS + s], tab[bb, T_LE + s]
            cell = jnp.maximum(high - 1, 0) // SUB
            tab[bb, T_LAST + j] = jnp.where((high > 0) & (low < rows) & (cell * SUB >= low), cell, nsub)
            tab[bb, T_CIDX + j] = jnp.where(tab[bb, T_OK + s] == 1, s, 0)
            tab[bb, T_NLOC + j] = high - jnp.maximum(low, 0)
            tab[bb, T_CNT + j] = len_s[batch, s]

    lane_head = lax.broadcasted_iota(jnp.int32, (group, D), 1) // group
    block_mask = (
        lax.broadcasted_iota(jnp.int32, (D, D), 0) // group == lax.broadcasted_iota(jnp.int32, (D, D), 1) // group
    ).astype(F32)
    ones8 = jnp.ones((8, 128), F32)
    row8 = lax.broadcasted_iota(jnp.int32, (8, D), 0)

    def lanes():
        return lax.broadcasted_iota(jnp.int32, (1, SUB), 1)

    def compact(square):
        total = None
        for j in range(HEADS):
            piece = jnp.where(lane_head == j, square[group * j : group * (j + 1), :], 0.0)
            total = piece if total is None else total + piece
        return total

    def moment_rows(product):
        return cat([compact(product[:D]), product[D : D + 8]])

    def expand(packed):
        return cat([packed] * HEADS, 0) * block_mask

    def centred(matrix):
        grouped = matrix.reshape(matrix.shape[0] // group, group, matrix.shape[1])
        return (grouped - jnp.mean(grouped, axis=1, keepdims=True)).reshape(matrix.shape)

    for name in ("zm", "zk", "zv", "corr_c", "corr_n", "corr_g"):
        sm[name][0] = jnp.zeros(sm[name].shape[1:], F32)
    for name in ("acc_c", "acc_n", "acc_g"):
        sm[name][nsub] = jnp.zeros(sm[name].shape[1:], F32)
    for name in ("d_outer", "d_inner", "d_kv", "s_du", "s_g", "s_dz"):
        sm[name][...] = jnp.zeros(sm[name].shape, F32)
    gb = sm["gb"]
    gb[...] = jnp.zeros(gb.shape, F32)
    first, parts_rows = gradient_rows(D, FF, digits)
    R_Q, R_K, R_V, R_3, R_I, R_O, R_VEC = (first[name] for name in ("q", "k", "v", "o", "inner", "outer", "vec"))

    pl.semaphore_wait(barrier, greeted)
    for k in range(4):
        weight_send(k).start()

    tables = sm["tables"]

    def prepare(layer):
        @pl.when(c == layer)
        def _():
            for k in range(4):
                weight_copy(k).wait()

        @pl.when(c != layer)
        def _():
            for k in range(4):
                weight_arrival(k).wait_recv()

        def column(row):
            return jnp.broadcast_to(wvec[layer, row], (128, D)).T

        for row in (0, 3, 8, 9, 10):
            tables[layer, row] = column(row)
        for row in (1, 2):
            tables[layer, row] = centred(column(row))
        packed = sm["packed"]
        packed[layer, 0] = compact(1.0 + column(4))
        packed[layer, 1] = compact(column(5))
        packed[layer, 2] = compact(1.0 + column(6))
        query_t, output_t = watt[layer, 0].T, watt[layer, 3].T
        sm["wq_t"][layer] = pack3(query_t)
        sm["w3_t"][layer] = pack3(output_t)
        sm["wq_right"][layer] = right3(cat([query_t, tables[layer, 0]], 1))
        sm["w3_right"][layer] = right3(output_t)
        sm["kvw"][layer] = pack3(cat([centred(watt[layer, 1].T), centred(watt[layer, 2].T)], 0))
        sm["kvw_back"][layer] = cat([pack3(watt[layer, 1]), pack3(watt[layer, 2])], 1)
        inner = winn[layer]
        sm["inn_t"][layer] = pack3(cat([inner[:, at : at + D].T for at in range(0, FF, D)], 0))
        sm["inn"][layer] = pack3(inner)
        outer = wout[layer]
        sm["out_t"][layer] = pack3(cat([outer[at : at + D, :].T for at in range(0, FF, D)], 1))
        sm["out"][layer] = pack3(outer)

    ar = sm["ar"]

    def ar_copy(k, digit, offset):
        spot = ar.at[k, digit, digit_at(digit)]
        return pltpu.make_async_remote_copy(
            src_ref=spot, dst_ref=spot, send_sem=sm["ar_send"].at[k, digit, offset - 1],
            recv_sem=sm["ar_recv"].at[k, digit, offset - 1],
            device_id={"pts": partner(digit, offset)}, device_id_type=MESH,
        )

    def ar_arrival(k, digit, offset):
        radix = digits[digit][1]
        spot = ar.at[k, digit, digit_at(digit, radix - offset)]
        return pltpu.make_async_remote_copy(
            src_ref=spot, dst_ref=spot, send_sem=sm["ar_send"].at[k, digit, offset - 1],
            recv_sem=sm["ar_recv"].at[k, digit, offset - 1],
            device_id={"pts": partner(digit, offset)}, device_id_type=MESH,
        )

    def ar_launch(k, digit, payload):
        ar[k, digit, digit_at(digit)] = payload
        for offset in range(1, digits[digit][1]):
            ar_copy(k, digit, offset).start()

    def ar_land(k, digit):
        radix = digits[digit][1]
        for offset in range(1, radix):
            ar_arrival(k, digit, offset).wait_recv()
        total = ar[k, digit, 0]
        for at in range(1, radix):
            total = total + ar[k, digit, at]
        return total

    def ar_step(k, digit):
        if digit < len(digits):
            ar_launch(k, digit, ar_land(k, digit - 1))

    def ar_finish(k):
        for digit in range(2, len(digits)):
            ar_step(k, digit)
        return ar_land(k, len(digits) - 1)

    def ar_drain(k):
        for digit in range(len(digits)):
            for offset in range(1, digits[digit][1]):
                ar_copy(k, digit, offset).wait_send()

    hs, kvs, rst, dms = sm["hs"], sm["kvs"], sm["rst"], sm["dms"]
    mids, hids, gps = sm["mids"], sm["hids"], sm["gps"]

    def three(pair, at=0, size=D):
        high = pair[at : at + size]
        return [high, pair[at + size : at + 2 * size], high]

    def joined(pairs):
        whole = pairs.astype(F32)
        return cat([whole[:D] + whole[D : 2 * D], whole[2 * D : 3 * D] + whole[3 * D :]])

    def load(ref, lead, subs):
        return cat([ref[(*lead, sub)] for sub in subs], 1)

    def save(ref, lead, subs, value):
        for at, sub in enumerate(subs):
            ref[(*lead, sub)] = value[:, SUB * at : SUB * (at + 1)]

    def part(value, at):
        return value[:, SUB * at : SUB * (at + 1)]

    def inside_of(bb, sub):
        return lanes() < tab[bb, T_END + sub]

    def keys_and_values(layer, bb, subs, pair):
        width = SUB * len(subs)
        bias = cat([wide(tables[layer, 1], width), wide(tables[layer, 2], width)], 0)
        field = dot16(sm["kvw"][layer], cat(three(pair))) + bias
        grouped = field.reshape(2 * HEADS, group, width)
        spread = jnp.mean(grouped * grouped, axis=1, keepdims=True)
        scale = lax.rsqrt(spread + EPS_NORM)
        normed = (grouped * scale).reshape(2 * D, width)
        save(rst, (layer, bb), subs, scale.reshape(2 * HEADS, width))
        k_high, k_low = split(normed[:D])
        v_high, v_low = split(normed[D:])
        keys, values = cat([k_high, k_low]), cat([v_high, v_low])
        save(kvs, (layer, bb), subs, cat([keys, values]))
        for at, sub in enumerate(subs):
            inside = inside_of(bb, sub)
            product = moment_rows(outer16_sums(part(keys, at), part(values, at) * inside.astype(BF16)))
            sums = fold(jnp.where(inside, part(normed, at)[:D], 0.0))
            keep = tab[bb, T_KEEP + sub] == 1
            past = jnp.maximum(sub - 1, 0)
            sm["acc_c"][sub] = product + jnp.where(keep, sm["acc_c"][past], 0.0)
            sm["acc_n"][sub] = sums + jnp.where(keep, sm["acc_n"][past], 0.0)

    def feed_forward(layer, bb, subs):
        width = SUB * len(subs)
        middles = []
        for sub in subs:
            slot = tab[bb, T_SLOT + sub]
            value = dot16(left3(sm["fwd_mat"][slot]), cat(three(hs[layer, bb, sub]))) + wide(sm["fwd_add"][slot], SUB)
            middles.append(jnp.where(inside_of(bb, sub), value, sm["zm"][tab[bb, T_ZI + sub]]))
        middle = cat(middles, 1)
        m_high, m_low = split(middle)
        mid_pair = cat([m_high, m_low])
        u = dot16(sm["inn_t"][layer], cat(three(mid_pair)))
        u = u + cat([wide(tables[layer, 9], width), wide(tables[layer, 10], width)], 0)
        k0 = 0.7978845608
        square = u * u
        t = jnp.tanh(u * (k0 + (k0 * 0.044715) * square))
        half = 0.5 + 0.5 * t
        hidden = u * half
        slope = half + hidden * (1.0 - t) * (k0 + (3.0 * k0 * 0.044715) * square)
        h_high, h_low = split(hidden)
        hid_pair = cat([h_high, h_low])
        out = middle + dot16(sm["out_t"][layer], cat(three(hid_pair, 0, FF))) + wide(tables[layer, 8], width)
        return out, mid_pair, hid_pair, slope

    def feed_back(layer, bb, subs, upstream, mid_pair, hid_pair, slope):
        g_high, g_low = split(upstream)
        g_pair = cat([g_high, g_low])
        du = dot16(sm["out"][layer], cat(three(g_pair))) * slope
        u_high, u_low = split(du)
        u_pair = cat([u_high, u_low])
        d_mid = upstream + dot16(sm["inn"][layer], cat(three(u_pair, 0, FF)))
        q_high, q_low = split(d_mid)
        q_pair = cat([q_high, q_low])
        save(dms, (bb,), subs, q_pair)
        for at, sub in enumerate(subs):
            q_inside = part(q_pair, at) * inside_of(bb, sub).astype(BF16)
            product = outer16_sums(hs[layer, bb, sub], q_inside)
            keep = tab[bb, T_KEEP + sub] == 1
            past = jnp.maximum(sub - 1, 0)
            sm["acc_g"][sub] = product + jnp.where(keep, sm["acc_g"][past], 0.0)
        sm["d_outer"][layer] += outer16(hid_pair, g_pair)
        sm["d_inner"][layer] += outer16(u_pair, mid_pair)
        sm["s_du"][layer] += fold(du)
        sm["s_g"][layer] += fold(upstream)

    def norm_back(layer, bb, subs):
        width = SUB * len(subs)
        pairs = load(kvs, (layer, bb), subs)
        normed = joined(pairs)
        e_ks, e_vs = [], []
        for at, sub in enumerate(subs):
            slot, zi, inside = tab[bb, T_SLOT + sub], tab[bb, T_ZI + sub], inside_of(bb, sub)
            own = part(pairs, at)
            e_k = dot16(left3(sm["key_mat"][slot]), cat(three(own, 2 * D))) + wide(sm["key_add"][slot], SUB)
            e_v = dot16(left3(sm["val_mat"][slot]), cat(three(own))) + wide(sm["val_add"][slot], SUB)
            e_ks.append(jnp.where(inside, e_k, sm["zk"][zi]))
            e_vs.append(jnp.where(inside, e_v, sm["zv"][zi]))
        e = cat([cat(e_ks, 1), cat(e_vs, 1)])
        shape = (2 * HEADS, group, width)
        e3, n3 = e.reshape(shape), normed.reshape(shape)
        scale = load(rst, (layer, bb), subs).reshape(2 * HEADS, 1, width)
        along = jnp.mean(e3 * n3, axis=1, keepdims=True)
        dz = ((e3 - n3 * along) * scale).reshape(2 * D, width)
        z_high, z_low = split(dz)
        z_pair = cat([z_high, z_low])
        sm["d_kv"][layer] += outer16(z_pair, load(hs, (layer, bb), subs))
        sm["s_dz"][layer] += fold(dz)
        return z_pair

    def input_back(layer, bb, subs, z_pair):
        z_high, z_low = z_pair[: 2 * D], z_pair[2 * D :]
        through = [z_high[:D], z_low[:D], z_high[:D], z_high[D:], z_low[D:], z_high[D:]]
        backs = []
        for at, sub in enumerate(subs):
            slot, zi = tab[bb, T_SLOT + sub], tab[bb, T_ZI + sub]
            left = cat([left3(sm["back_mat"][layer, bb, slot]), sm["kvw_back"][layer]], 1)
            right = three(dms[bb, sub] * inside_of(bb, sub).astype(BF16)) + [part(one, at) for one in through]
            backs.append(dot16(left, cat(right)) + sm["zm"][zi])
        return cat(backs, 1)

    count = TILE // SUB

    def over(low, high, stage):
        def body(i, carry):
            stage([i * count + at for at in range(count)])
            return carry

        lax.fori_loop(low, high, body, 0)

    steps = nsub // count

    def loop(stage, between):
        over(0, (steps + 1) // 2, stage)
        between()
        over((steps + 1) // 2, steps, stage)

    def span(bb, s):
        at = lanes()
        return (at >= tab[bb, T_LO + s]) & (at < tab[bb, T_HI + s])

    def fill(name, bb, s, inside, value):
        before = jnp.where(tab[bb, T_ZK + s] == 1, sm[name][s - 1], 0.0)
        sm[name][s] = jnp.where(inside, value, before)

    def corrections_mid(layer, bb):
        @pl.when(edge)
        def _():
            for s in range(1, segs):
                pair = hs[layer, bb, tab[bb, T_C + s]]
                slot = tab[bb, T_CS + s]
                value = dot16(left3(sm["fwd_mat"][slot]), cat(three(pair))) + wide(sm["fwd_add"][slot], SUB)
                fill("zm", bb, s, span(bb, s), value)

    def corrections_back(layer, bb):
        @pl.when(edge)
        def _():
            for s in range(1, segs):
                cell, slot, inside = tab[bb, T_C + s], tab[bb, T_CS + s], span(bb, s)
                pairs = kvs[layer, bb, cell]
                e_k = dot16(left3(sm["key_mat"][slot]), cat(three(pairs, 2 * D))) + wide(sm["key_add"][slot], SUB)
                e_v = dot16(left3(sm["val_mat"][slot]), cat(three(pairs))) + wide(sm["val_add"][slot], SUB)
                e_d = dot16(left3(sm["back_mat"][layer, bb, slot]), cat(three(dms[bb, cell])))
                fill("zk", bb, s, inside, e_k)
                fill("zv", bb, s, inside, e_v)
                fill("zm", bb, s, inside, e_d)

    def corrections_moments(layer, bb):
        @pl.when(edge)
        def _():
            for s in range(1, segs):
                cell, inside = tab[bb, T_C + s], span(bb, s)
                pairs = kvs[layer, bb, cell]
                product = outer16_sums(pairs[: 2 * D], pairs[2 * D :] * inside.astype(BF16))
                sm["corr_c"][s] = moment_rows(product)
                keys = pairs[: 2 * D].astype(F32)
                sm["corr_n"][s] = fold(jnp.where(inside, keys[:D] + keys[D:], 0.0))

    def corrections_grams(layer, bb):
        @pl.when(edge)
        def _():
            for s in range(1, segs):
                cell, inside = tab[bb, T_C + s], span(bb, s)
                q_pair = dms[bb, cell] * inside.astype(BF16)
                sm["corr_g"][s] = outer16_sums(hs[layer, bb, cell], q_pair)

    stats, own_c, own_d, vec, vec_c = sm["stats"], sm["own_c"], sm["own_d"], sm["vec"], sm["vec_c"]

    def total_of(name, bb, j):
        return sm["acc_" + name][tab[bb, T_LAST + j]] + sm["corr_" + name][tab[bb, T_CIDX + j]]

    def shifts(layer):
        return 1.0 + wvec[layer, 4], wvec[layer, 5], 1.0 + wvec[layer, 6], wvec[layer, 7]

    def moments_of(layer, bb, j):
        key_gain, key_shift, value_gain, value_shift = shifts(layer)
        gain_c, shift_c = sm["packed"][layer, 0], sm["packed"][layer, 1]
        rows_c = total_of("c", bb, j)
        product, values = rows_c[:group], rows_c[group : group + 1]
        keys = compact(jnp.broadcast_to(jnp.sum(total_of("n", bb, j), axis=1, keepdims=True), (D, 128)))
        stats[layer, bb, j] = cat([product, keys, rows_c[group:]])
        local = tab[bb, T_NLOC + j].astype(F32)
        from_values = values * value_gain + local * value_shift
        return gain_c * (product * value_gain + keys * value_shift) + shift_c * from_values

    def mixing_of(layer, bb, slots, moments):
        packs = []
        for j, moment in zip(slots, moments):
            pack = pack2((expand(moment) / tab[bb, T_CNT + j].astype(F32)).T)
            sm["mt"][layer, bb, j] = pack
            packs.append(left3(pack))
        mixed = dot16(cat(packs), sm["wq_right"][layer])
        rights = [right3(mixed[D * at : D * (at + 1)]) for at in range(len(slots))]
        through = dot16(sm["w3_t"][layer], cat(rights, 1))
        eye = (
            lax.broadcasted_iota(jnp.int32, (D, D), 0) == lax.broadcasted_iota(jnp.int32, (D, D), 1)
        ).astype(F32)
        for at, j in enumerate(slots):
            forward = through[:, 2 * D * at : 2 * D * at + D] + eye
            sm["fwd_mat"][j] = pack2(forward)
            sm["fwd_add"][j] = through[:, 2 * D * at + D : 2 * D * (at + 1)] + tables[layer, 3]
            sm["back_mat"][layer, bb, j] = pack2(forward.T)

    def grams_of(layer, bb, slots):
        grams = [total_of("g", bb, j) for j in slots]
        tall = D + 16
        onto = dot16(cat([pack3(gram) for gram in grams]), sm["w3_right"][layer])
        ontos = [onto[tall * at : tall * (at + 1)] for at in range(len(slots))]
        rights = [right3(cat([one[:D], gram[:D]], 1)) for one, gram in zip(ontos, grams)]
        both = dot16(sm["wq_t"][layer], cat(rights, 1))
        query_bias = tables[layer, 0]
        d_moments, throughs = [], []
        for at, (one, gram) in enumerate(zip(ontos, grams)):
            d_moments.append(compact(both[:, 2 * D * at : 2 * D * at + D] + query_bias * one[D : D + 1]))
            throughs.append(both[:, 2 * D * at + D : 2 * D * (at + 1)] + query_bias * gram[D : D + 1])
        return d_moments, ontos, throughs, grams

    def projections_of(layer, bb, slots, ontos, throughs, grams):
        mts = [sm["mt"][layer, bb, j] for j in slots]
        right = [part for mt in mts for part in (mt[:, :D], mt[:, D:], mt[:, :D])]
        d_query = dot16(cat([pack3(one) for one in ontos], 1), cat(right))
        gb[layer, R_Q : R_Q + D] += d_query[:D]
        gb[layer, R_3 : R_3 + D] += dot16(cat([left3(mt) for mt in mts], 1), cat([right3(through) for through in throughs]))
        vec[layer, 0] += d_query[D : D + 8]
        sums = grams[0][D : D + 8]
        for gram in grams[1:]:
            sums = sums + gram[D : D + 8]
        vec[layer, 1] += sums

    def back_of(layer, bb, slots, d_moments):
        key_gain, key_shift, value_gain, value_shift = shifts(layer)
        gain_c, shift_c, value_gain_c = (sm["packed"][layer, at] for at in range(3))

        def across(packed):
            return jnp.broadcast_to(jnp.sum(expand(centred(packed)), axis=1, keepdims=True), (D, 128))

        for j, d_moment in zip(slots, d_moments):
            d = d_moment / tab[bb, T_CNT + j].astype(F32)
            d_t = compact(expand(d).T)
            sm["key_mat"][j] = pack2(expand(centred(gain_c * d * value_gain)))
            sm["key_add"][j] = across(gain_c * d * value_shift)
            sm["val_mat"][j] = pack2(expand(centred(value_gain_c * d_t * key_gain)))
            sm["val_add"][j] = across(value_gain_c * d_t * key_shift)
            held = stats[layer, bb, j]
            product, keys, values = held[:group], held[group : 2 * group], held[2 * group : 2 * group + 1]
            local = tab[bb, T_NLOC + j].astype(F32)
            vec_c[layer, 0] += d * (product * value_gain + keys * value_shift)
            vec_c[layer, 1] += d * (values * value_gain + local * value_shift)
            vec_c[layer, 2] += d * (gain_c * product + shift_c * values)
            vec_c[layer, 3] += d * (gain_c * keys + shift_c * local)

    small = list(range(1, segs))

    def key_of(stage, bb):
        return stage * per + bb

    def moments_out(layer, bb, k):
        corrections_moments(layer, bb)
        ar_launch(k, 0, moments_of(layer, bb, 0))

        @pl.when(edge)
        def _():
            for j in small:
                own_c[layer, bb, j] = moments_of(layer, bb, j)

    def mixing_in(layer, bb, k):
        @pl.when(edge)
        def _():
            mixing_of(layer, bb, small, [own_c[layer, bb, j] for j in small])

        mixing_of(layer, bb, [0], [ar_finish(k)])
        corrections_mid(layer, bb)

    def grams_out(layer, bb, k):
        corrections_grams(layer, bb)
        d_moments, *rest = grams_of(layer, bb, [0])
        ar_launch(k, 0, d_moments[0])
        projections_of(layer, bb, [0], *rest)

        @pl.when(edge)
        def _():
            d_moments, *rest = grams_of(layer, bb, small)
            for j, d_moment in zip(small, d_moments):
                own_d[bb, j] = d_moment
            projections_of(layer, bb, small, *rest)

    def grams_in(layer, bb, k):
        @pl.when(edge)
        def _():
            back_of(layer, bb, small, [own_d[bb, j] for j in small])

        back_of(layer, bb, [0], [ar_finish(k)])
        corrections_back(layer, bb)

    vec[...] = jnp.zeros(vec.shape, F32)
    vec_c[...] = jnp.zeros(vec_c.shape, F32)

    targets = (act_hbm, grd_hbm)

    def kept(kind, layer, bb):
        return pltpu.make_async_copy(
            stage.at[layer, bb], targets[kind].at[c * per + bb], sm["o_local"].at[kind, bb]
        )

    def sent(kind, layer, bb):
        return pltpu.make_async_remote_copy(
            src_ref=stage.at[layer, bb], dst_ref=targets[kind].at[c * per + bb], send_sem=sm["o_send"].at[kind, bb],
            recv_sem=sm["o_recv"].at[kind, bb], device_id={"section": other}, device_id_type=MESH,
        )

    def came(kind, layer, bb):
        return pltpu.make_async_remote_copy(
            src_ref=stage.at[layer, bb], dst_ref=targets[kind].at[other * per + bb], send_sem=sm["o_send"].at[kind, bb],
            recv_sem=sm["o_recv"].at[kind, bb], device_id={"section": other}, device_id_type=MESH,
        )

    def ship(kind, layer, bb):
        @pl.when(c == layer)
        def _():
            kept(kind, layer, bb).start()

        @pl.when(c != layer)
        def _():
            sent(kind, layer, bb).start()

    def shipped(kind, layer, bb):
        @pl.when(c == layer)
        def _():
            kept(kind, layer, bb).wait()

        @pl.when(c != layer)
        def _():
            sent(kind, layer, bb).wait_send()

    def load_t(layer, bb, subs):
        return cat([stage[layer, bb, sub].T for sub in subs], 1)

    def save_t(layer, bb, subs, value):
        for at, sub in enumerate(subs):
            stage[layer, bb, sub] = part(value, at).T

    def start_stage(bb, subs):
        high, low = split(load_t(0, bb, subs))
        pair = cat([high, low])
        save(hs, (0, bb), subs, pair)
        keys_and_values(0, bb, subs, pair)

    def first_stage(bb, subs):
        out, mid_pair, hid_pair, slope = feed_forward(0, bb, subs)
        save(mids, (bb,), subs, mid_pair)
        save(hids, (bb,), subs, hid_pair)
        save(gps, (bb,), subs, slope)
        save_t(0, bb, subs, out)
        high, low = split(out)
        pair = cat([high, low])
        save(hs, (1, bb), subs, pair)
        keys_and_values(1, bb, subs, pair)

    def second_stage(bb, subs):
        out, mid_pair, hid_pair, slope = feed_forward(1, bb, subs)
        upstream = load_t(1, bb, subs)
        save_t(1, bb, subs, out)
        feed_back(1, bb, subs, upstream, mid_pair, hid_pair, slope)

    def third_stage(bb, subs):
        upstream = input_back(1, bb, subs, norm_back(1, bb, subs))
        save_t(1, bb, subs, upstream)
        held = [load(ref, (bb,), subs) for ref in (mids, hids, gps)]
        feed_back(0, bb, subs, upstream, *held)

    def fourth_stage(bb, subs):
        save_t(0, bb, subs, input_back(0, bb, subs, norm_back(0, bb, subs)))

    def fifth_stage(bb, subs):
        save(kvs, (0, bb), subs, norm_back(0, bb, subs))

    def sixth_stage(bb, subs):
        save_t(0, bb, subs, input_back(0, bb, subs, load(kvs, (0, bb), subs)))

    og = sm["og"]
    summed, widened = digits[:2], digits[2:]
    sizes = []
    for kind in range(2):
        sizes.append([parts_rows[kind]])
        for _, radix in summed:
            sizes[-1].append(sizes[-1][-1] // radix)
    g_send, g_recv = sm["g_send"], sm["g_recv"]

    def early_rows(layer):
        gb[layer, R_O : R_O + FF] = sm["d_outer"][layer]
        d_inner = sm["d_inner"][layer]
        for at in range(0, FF, D):
            gb[layer, R_I + at : R_I + at + D] = d_inner[at : at + D].T

    def late_rows(layer):
        d_kv = sm["d_kv"][layer]
        gb[layer, R_K : R_K + D] = d_kv[:D].T
        gb[layer, R_V : R_V + D] = d_kv[D:].T
        s_dz = mm_nt(ones8, sm["s_dz"][layer])
        s_du = mm_nt(ones8, sm["s_du"][layer])
        s_g = mm_nt(ones8, sm["s_g"][layer])
        lines = [vec[layer, 0], s_dz[:, :D], s_dz[:, D:], vec[layer, 1]]
        lines += [mm_nt(ones8, expand(vec_c[layer, at])) for at in (0, 1)]
        lines += [jnp.sum(vec_c[layer, at], axis=0, keepdims=True) for at in (2, 3)]
        lines += [s_g, s_du[:, :D], s_du[:, D:]]
        block = jnp.zeros((16, D), F32)
        row16 = lax.broadcasted_iota(jnp.int32, (16, D), 0)
        for at, line in enumerate(lines):
            block = jnp.where(row16 == at, line[0:1], block)
        gb[layer, R_VEC : R_VEC + 16] = block

    def block_of(kind, depth, at=None):
        low = 0 if kind == 0 else parts_rows[0]
        for digit in range(depth):
            offset = at if (at is not None and digit == depth - 1) else 0
            low = low + digit_at(digit, offset) * sizes[kind][digit + 1]
        return pl.ds(low if depth == 0 else pl.multiple_of(low, 8), sizes[kind][depth])

    def landing(kind, digit):
        return sm["rb%d%d" % (kind, digit)]

    def scatter_first(layer, kind, offset):
        radix = summed[0][1]
        own = offset - 1
        far = radix - 1 + offset

        def copy(slot, target):
            return pltpu.make_async_remote_copy(
                src_ref=gb.at[layer, block_of(kind, 1, offset)], dst_ref=landing(kind, 0).at[slot],
                send_sem=g_send.at[kind, 0, 0, slot], recv_sem=g_recv.at[kind, 0, 0, slot],
                device_id=target, device_id_type=MESH,
            )

        near = {"pts": partner(0, offset)}
        return copy(own, near), copy(far, {"section": other, "pts": partner(0, offset)})

    def scatter_next(layer, kind, digit, offset):
        return pltpu.make_async_remote_copy(
            src_ref=gb.at[layer, block_of(kind, digit + 1, offset)], dst_ref=landing(kind, digit).at[offset - 1],
            send_sem=g_send.at[kind, 0, digit, offset - 1], recv_sem=g_recv.at[kind, 0, digit, offset - 1],
            device_id={"pts": partner(digit, offset)}, device_id_type=MESH,
        )

    def gather(kind, digit, offset, at):
        spot = og.at[block_of(kind, digit + 1, at)]
        return pltpu.make_async_remote_copy(
            src_ref=spot, dst_ref=spot,
            send_sem=g_send.at[kind, 1, digit, offset - 1], recv_sem=g_recv.at[kind, 1, digit, offset - 1],
            device_id={"pts": partner(digit, offset)}, device_id_type=MESH,
        )

    def exchange(kind, at, offset, back=0):
        digit = len(summed) + at
        spot = sm["wide%d" % kind].at[at, digit_at(digit, back)]
        return pltpu.make_async_remote_copy(
            src_ref=spot, dst_ref=spot,
            send_sem=g_send.at[kind, 0, digit, offset - 1], recv_sem=g_recv.at[kind, 0, digit, offset - 1],
            device_id={"pts": partner(digit, offset)}, device_id_type=MESH,
        )

    def gradient_step(layer, kind, step):
        last = len(summed)
        if step == 0:
            @pl.when(c == layer)
            def _():
                for offset in range(1, summed[0][1]):
                    scatter_first(layer, kind, offset)[0].start()

            @pl.when(c != layer)
            def _():
                for offset in range(summed[0][1]):
                    scatter_first(layer, kind, offset)[1].start()

        elif step <= last:
            digit = step - 1
            radix = summed[digit][1]

            @pl.when(c == layer)
            def _():
                total = gb[layer, block_of(kind, digit + 1)]
                for offset in range(1, radix):
                    if digit == 0:
                        scatter_first(layer, kind, offset)[0].wait_recv()
                    else:
                        scatter_next(layer, kind, digit, offset).wait_recv()
                    total = total + landing(kind, digit)[offset - 1]
                if digit == 0:
                    for offset in range(radix):
                        scatter_first(layer, kind, offset)[1].wait_recv()
                        total = total + landing(kind, 0)[radix - 1 + offset]
                if step < last:
                    gb[layer, block_of(kind, digit + 1)] = total
                    for offset in range(1, summed[step][1]):
                        scatter_next(layer, kind, step, offset).start()
                else:
                    for at, (_, wide_radix) in enumerate(widened):
                        digit_now = last + at
                        sm["wide%d" % kind][at, digit_at(digit_now)] = total
                        for offset in range(1, wide_radix):
                            exchange(kind, at, offset).start()
                        for offset in range(1, wide_radix):
                            exchange(kind, at, offset, wide_radix - offset).wait_recv()
                        total = sm["wide%d" % kind][at, 0]
                        for other_at in range(1, wide_radix):
                            total = total + sm["wide%d" % kind][at, other_at]
                    og[block_of(kind, last)] = total
                    for offset in range(1, radix):
                        gather(kind, digit, offset, 0).start()

        elif step <= 2 * last:
            digit = 2 * last - step

            @pl.when(c == layer)
            def _():
                radix = summed[digit][1]
                for offset in range(1, radix):
                    gather(kind, digit, offset, radix - offset).wait_recv()
                if digit > 0:
                    for offset in range(1, summed[digit - 1][1]):
                        gather(kind, digit - 1, offset, 0).start()

    def drain_gradients():
        for layer in range(2):
            @pl.when(c == layer)
            def _():
                for kind in range(2):
                    for offset in range(1, summed[0][1]):
                        scatter_first(layer, kind, offset)[0].wait_send()
                    for digit in range(1, len(summed)):
                        for offset in range(1, summed[digit][1]):
                            scatter_next(layer, kind, digit, offset).wait_send()
                    for at, (_, wide_radix) in enumerate(widened):
                        for offset in range(1, wide_radix):
                            exchange(kind, at, offset).wait_send()
                    for digit in range(len(summed)):
                        for offset in range(1, summed[digit][1]):
                            gather(kind, digit, offset, 0).wait_send()

            @pl.when(c != layer)
            def _():
                for kind in range(2):
                    for offset in range(summed[0][1]):
                        scatter_first(layer, kind, offset)[1].wait_send()

    EARLY, LATE = 0, 1

    def together(*actions):
        def run():
            for action in actions:
                action()

        return run

    def grad(layer, kind, step):
        return functools.partial(gradient_step, layer, kind, step)

    prepare(0)
    for bb in range(per):
        x_copy(bb).wait()
        loop(functools.partial(start_stage, bb), lambda bb=bb: ar_step(key_of(0, bb - 1), 1) if bb > 0 else None)
        moments_out(0, bb, key_of(0, bb))
    prepare(1)
    ar_step(key_of(0, per - 1), 1)

    def in_flight(stage, bb):
        if bb > 0:
            return lambda: ar_step(key_of(stage, bb - 1), 1)
        return lambda: None

    def late(stage):
        ar_step(key_of(stage, per - 1), 1)

    for bb in range(per):
        mixing_in(0, bb, key_of(0, bb))
        loop(functools.partial(first_stage, bb), in_flight(1, bb))
        ship(0, 0, bb)
        moments_out(1, bb, key_of(1, bb))
    for bb in range(per):
        cot_copy(bb).wait()
        mixing_in(1, bb, key_of(1, bb))
        loop(functools.partial(second_stage, bb), in_flight(2, bb) if bb > 0 else lambda: late(1))
        ship(0, 1, bb)
        grams_out(1, bb, key_of(2, bb))
    early_rows(1)
    gradient_step(1, EARLY, 0)
    for bb in range(per):
        grams_in(1, bb, key_of(2, bb))
        shipped(0, 1, bb)
        beside = together(in_flight(3, bb), grad(1, EARLY, 2)) if bb > 0 else together(functools.partial(late, 2), grad(1, EARLY, 1))
        loop(functools.partial(third_stage, bb), beside)
        ship(1, 1, bb)
        grams_out(0, bb, key_of(3, bb))
    early_rows(0)
    late_rows(1)
    gradient_step(0, EARLY, 0)
    gradient_step(1, LATE, 0)
    gradient_step(1, EARLY, 3)
    for bb in range(per - 1):
        grams_in(0, bb, key_of(3, bb))
        shipped(0, 0, bb)
        beside = together(functools.partial(late, 3), grad(0, EARLY, 1), grad(1, LATE, 1), grad(1, EARLY, 4))
        loop(functools.partial(fourth_stage, bb), beside if bb == 0 else lambda: None)
        ship(1, 0, bb)
    bb = per - 1
    grams_in(0, bb, key_of(3, bb))
    shipped(0, 0, bb)
    loop(functools.partial(fifth_stage, bb), together(grad(0, EARLY, 2), grad(1, LATE, 2)))
    late_rows(0)
    gradient_step(0, LATE, 0)
    gradient_step(0, EARLY, 3)
    gradient_step(1, LATE, 3)
    loop(functools.partial(sixth_stage, bb), grad(0, LATE, 1))
    ship(1, 0, bb)
    gradient_step(0, LATE, 2)
    gradient_step(0, EARLY, 4)
    gradient_step(1, LATE, 4)
    gradient_step(0, LATE, 3)
    gradient_step(0, LATE, 4)
    out_copy = pltpu.make_async_copy(og, gsum_hbm, dma_in.at[0])
    out_copy.start()

    drain_gradients()
    for k in range(4):
        weight_send(k).wait_send()
    for k in range(4 * per):
        ar_drain(k)
    for bb in range(per):
        for layer in range(2):
            shipped(1, layer, bb)
        for layer in range(2):
            @pl.when(c == layer)
            def _():
                came(0, layer, bb).wait_recv()
                came(1, layer, bb).wait_recv()
    out_copy.wait()


def finishing(scale, D, FF, first, act, grd, gsum_hbm, *refs):
    sources, results = refs[:12], refs[12:30]
    gsum, held, made, sem_large, sem_in, sem_out = refs[30], refs[31:43], refs[43:59], *refs[59:]
    large = []
    for kind, (source, target) in enumerate(((act, results[0]), (grd, results[1]))):
        for part in range(source.shape[0]):
            large.append(pltpu.make_async_copy(source.at[part], target.at[part], sem_large.at[kind, part]))
    loads = [pltpu.make_async_copy(gsum_hbm, gsum, sem_in.at[12])]
    loads += [pltpu.make_async_copy(sources[at], held[at], sem_in.at[at]) for at in range(12)]
    for copy in loads:
        copy.start()
    for copy in large:
        copy.start()
    rate = plan()

    def step(weight, gradient, momentum, variance):
        average = gradient * scale
        new_momentum = 0.9 * momentum + 0.1 * average
        new_variance = 0.999 * variance + 0.001 * average * average
        mean = new_momentum / (1.0 - 0.9**STEP)
        square = new_variance / (1.0 - 0.999**STEP)
        updated = weight - rate * (mean / (jnp.sqrt(square) + 1e-08) + 0.01 * weight)
        return gradient, new_momentum, new_variance, updated

    parts = [first[name] for name in ("q", "k", "v", "o")]
    inner, outer, late = first["inner"], first["outer"], first["vec"]
    places = [
        [((0, at), slice(low, low + D)) for at, low in enumerate(parts)],
        [((0, slice(None), slice(at, at + D)), slice(inner + at, inner + at + D)) for at in range(0, FF, D)],
        [((0,), slice(outer, outer + FF))],
        [((line,), slice(late + line, late + line + 1)) for line in range(held[3].shape[0])],
    ]
    loads[0].wait()
    stores = []
    for kind in range(4):
        for at in (kind, 4 + 2 * kind, 5 + 2 * kind):
            loads[1 + at].wait()
        weight, momentum, variance = held[kind], held[4 + 2 * kind], held[5 + 2 * kind]
        for index, lines in places[kind]:
            values = step(weight[index], gsum[lines], momentum[index], variance[index])
            for ref, value in zip(made[4 * kind : 4 * kind + 4], values):
                ref[index] = value
        for at in range(4 * kind, 4 * kind + 4):
            stores.append(pltpu.make_async_copy(made[at], results[2 + at], sem_out.at[at]))
            stores[-1].start()
    for copy in large + stores:
        copy.wait()


def per_device(
    node_features, cotangent, lengths, attention_weight, inner_weight, outer_weight, vectors,
    momentum_attention, variance_attention, momentum_inner, variance_inner,
    momentum_outer, variance_outer, momentum_vectors, variance_vectors,
):
    places = lax.axis_size("pts")
    micro, rows, D = node_features.shape
    FF = inner_weight.shape[-1]
    segs = lengths.shape[1]
    lines = vectors.shape[1]
    nsub = rows // SUB
    per = micro // 2
    digits = digits_of(places)
    group = D // HEADS
    first, parts_rows = gradient_rows(D, FF, digits)
    total_rows = sum(parts_rows)
    nar = 4 * per

    def f32(*shape):
        return pltpu.VMEM(shape, F32)

    def b16(*shape):
        return pltpu.VMEM(shape, BF16)

    def dma(*shape):
        return pltpu.SemaphoreType.DMA(shape)

    scratch = dict(
        watt=f32(2, 4, D, D), winn=f32(2, D, FF), wout=f32(2, FF, D), wvec=f32(2, lines, 1, D),
        tab=pltpu.SMEM((per, 4 * nsub + 12 * segs), jnp.int32),
        tables=f32(2, 11, D, 128), packed=f32(2, 3, group, D),
        wq_t=b16(2, D, 3 * D), w3_t=b16(2, D, 3 * D), wq_right=b16(2, 3 * D, 2 * D), w3_right=b16(2, 3 * D, D),
        kvw=b16(2, 2 * D, 3 * D), kvw_back=b16(2, D, 6 * D),
        inn_t=b16(2, FF, 3 * D), inn=b16(2, D, 3 * FF), out_t=b16(2, D, 3 * FF), out=b16(2, FF, 3 * D),
        hs=b16(2, per, nsub, 2 * D, SUB), kvs=b16(2, per, nsub, 4 * D, SUB),
        rst=f32(2, per, nsub, 2 * HEADS, SUB), dms=b16(per, nsub, 2 * D, SUB),
        mids=b16(per, nsub, 2 * D, SUB), hids=b16(per, nsub, 2 * FF, SUB), gps=f32(per, nsub, FF, SUB),
        stage=f32(2, per, nsub, SUB, D),
        zm=f32(segs, D, SUB), zk=f32(segs, D, SUB), zv=f32(segs, D, SUB),
        acc_c=f32(nsub + 1, group + 8, D), acc_n=f32(nsub + 1, D, 128), acc_g=f32(nsub + 1, D + 16, D),
        corr_c=f32(segs, group + 8, D), corr_n=f32(segs, D, 128), corr_g=f32(segs, D + 16, D),
        stats=f32(2, per, segs, 2 * group + 8, D), own_c=f32(2, per, segs, group, D), own_d=f32(per, segs, group, D),
        mt=b16(2, per, segs, D, 2 * D), vec_c=f32(2, 4, group, D),
        fwd_mat=b16(segs, D, 2 * D), fwd_add=f32(segs, D, 128), back_mat=b16(2, per, segs, D, 2 * D),
        key_mat=b16(segs, D, 2 * D), key_add=f32(segs, D, 128),
        val_mat=b16(segs, D, 2 * D), val_add=f32(segs, D, 128),
        d_outer=f32(2, FF, D), d_inner=f32(2, FF, D), d_kv=f32(2, 2 * D, D),
        s_du=f32(2, FF, 128), s_g=f32(2, D, 128), s_dz=f32(2, 2 * D, 128),
        vec=f32(2, 2, 8, D), gb=f32(2, total_rows, D), og=f32(total_rows, D),
        ar=f32(nar, len(digits), 4, group, D),
        dma_in=dma(2 * per + 4), w_send=dma(4), w_recv=dma(4),
        ar_send=dma(nar, len(digits), 3), ar_recv=dma(nar, len(digits), 3),
        o_local=dma(2, per), o_send=dma(2, per), o_recv=dma(2, per),
        g_send=dma(2, 2, len(digits), 7), g_recv=dma(2, 2, len(digits), 7),
    )
    for kind, size in enumerate(parts_rows):
        for digit, (_, radix) in enumerate(digits[:2]):
            size //= radix
            scratch["rb%d%d" % (kind, digit)] = f32(2 * radix - 1 if digit == 0 else radix - 1, size, D)
        if len(digits) > 2:
            scratch["wide%d" % kind] = f32(len(digits) - 2, 4, size, D)
    cfg = dict(names=list(scratch), places=places, segs=segs, micro=micro, nsub=nsub, D=D, FF=FF)

    def lined(piece):
        return jnp.transpose(piece, (1, 0, 2))

    anywhere = pl.BlockSpec(memory_space=pl.ANY)
    tiled = (micro, nsub, SUB, D)
    act, grd, gsum = pl.pallas_call(
        functools.partial(mega, cfg),
        out_shape=(
            jax.ShapeDtypeStruct(tiled, F32), jax.ShapeDtypeStruct(tiled, F32),
            jax.ShapeDtypeStruct((total_rows, D), F32),
        ),
        in_specs=[anywhere, anywhere, pl.BlockSpec(memory_space=pltpu.SMEM)] + [anywhere] * 4,
        out_specs=(anywhere, anywhere, anywhere),
        scratch_shapes=list(scratch.values()),
        compiler_params=pltpu.CompilerParams(
            collective_id=0, has_side_effects=True, vmem_limit_bytes=63 * 2**20
        ),
        name="layers",
    )(
        node_features.reshape(tiled), cotangent.reshape(tiled), lengths,
        attention_weight, inner_weight, outer_weight, lined(vectors),
    )
    scale = 1.0 / (micro * rows * places)
    held = [attention_weight, inner_weight, outer_weight, vectors]
    moments = [
        momentum_attention, variance_attention, momentum_inner, variance_inner,
        momentum_outer, variance_outer, momentum_vectors, variance_vectors,
    ]
    held[3] = lined(vectors)
    moments[6:] = [lined(momentum_vectors), lined(variance_vectors)]
    shapes = [jax.ShapeDtypeStruct(piece.shape, F32) for piece in held for _ in range(4)]
    results = pl.pallas_call(
        functools.partial(finishing, scale, D, FF, first),
        out_shape=tuple([jax.ShapeDtypeStruct(tiled, F32)] * 2 + shapes),
        in_specs=[pl.BlockSpec(memory_space=pltpu.HBM)] * 15,
        out_specs=tuple([pl.BlockSpec(memory_space=pltpu.HBM)] * 18),
        scratch_shapes=[f32(total_rows, D)] + [f32(*piece.shape) for piece in held + moments]
        + [f32(*shape.shape) for shape in shapes] + [dma(2, micro), dma(13), dma(16)],
        compiler_params=pltpu.CompilerParams(vmem_limit_bytes=60 * 2**20),
        name="adamw",
    )(act, grd, gsum, *held, *moments)
    whole = (1, micro, rows, D)
    lines_back = tuple(lined(piece) for piece in results[14:])
    return (results[0].reshape(whole), results[1].reshape(whole)) + tuple(results[2:14]) + lines_back


def solution(mesh):
    first = P("section", None, None)
    attention = P("section", None, None, None)
    nodes = P(None, "pts", None)
    return jax.shard_map(
        per_device,
        mesh=mesh,
        in_specs=(nodes, nodes, P(), attention, first, first, first, attention, attention) + (first,) * 6,
        out_specs=(P("section", None, "pts", None),) * 2 + (attention,) * 4 + (first,) * 12,
        check_vma=False,
    )
```

```python
import functools
import math

import jax
import jax.numpy as jnp
from jax import lax
from jax.experimental import pallas as pl
from jax.experimental.pallas import tpu as pltpu
from jax.sharding import PartitionSpec as P

HEADS = 4
STEP = 1200
TOTAL_STEPS = 4000
EPS_NORM = 1e-05
SUB = 256
TILE = 512

MESH = pl.DeviceIdType.MESH
HIGHEST = lax.Precision.HIGHEST
F32 = jnp.float32
BF16 = jnp.bfloat16


def plan():
    warm = 0.3 * TOTAL_STEPS
    top = 0.001
    start = top / 25.0
    low = start / 10000.0
    if STEP <= warm:
        return start + (top - start) * (1.0 - math.cos(math.pi * STEP / warm)) / 2.0
    return low + (top - low) * (1.0 + math.cos(math.pi * (STEP - warm) / (TOTAL_STEPS - warm))) / 2.0


def cat(parts, axis=0):
    return jnp.concatenate(parts, axis=axis)


def split(value):
    high = value.astype(BF16)
    return high, (value - high.astype(F32)).astype(BF16)


def pack3(weight):
    high, low = split(weight)
    return cat([high, high, low], 1)


def pack2(weight):
    return cat(list(split(weight)), 1)


def left3(pack):
    size = pack.shape[1] // 2
    return cat([pack[:, :size], pack], 1)


def right3(value):
    high, low = split(value)
    return cat([high, low, high])


def dot16(left, right):
    return jnp.dot(left, right, preferred_element_type=F32)


def outer16(left, right):
    full = lax.dot_general(left, right, (((1,), (1,)), ((), ())), preferred_element_type=F32)
    m, n = full.shape[0] // 2, full.shape[1] // 2
    return full[:m, :n] + full[m:, :n] + full[:m, n:]


def outer16_sums(left, right):
    ones = jnp.ones((16, left.shape[1]), BF16)
    full = lax.dot_general(cat([left, ones]), right, (((1,), (1,)), ((), ())), preferred_element_type=F32)
    m, n = left.shape[0] // 2, full.shape[1] // 2
    return cat([full[:m, :n] + full[m : 2 * m, :n] + full[:m, n:], full[2 * m :, :n] + full[2 * m :, n:]])


def mm_nt(left, right, precision=HIGHEST):
    return lax.dot_general(left, right, (((1,), (1,)), ((), ())), precision=precision, preferred_element_type=F32)


def wide(table, width):
    return cat([table] * (width // 128), 1)


def fold(value):
    total = value[:, :128]
    for at in range(128, value.shape[1], 128):
        total = total + value[:, at : at + 128]
    return total


def digits_of(places):
    found, stride = [], 1
    while stride < places:
        radix = 4 if (places // stride) % 4 == 0 else 2
        found.append((stride, radix))
        stride *= radix
    return found


def gradient_rows(D, FF, digits):
    unit = 8
    for _, radix in digits[:2]:
        unit *= radix
    early = -(-(2 * FF + 2 * D) // unit) * unit
    late = -(-(2 * D + 16) // unit) * unit
    first = dict(outer=0, inner=FF, q=2 * FF, o=2 * FF + D, k=early, v=early + D, vec=early + 2 * D)
    return first, (early, late)


def mega(cfg, x_hbm, cot_hbm, len_s, att_hbm, inn_hbm, out_hbm, vec_hbm, act_hbm, grd_hbm, gsum_hbm, *scratch):
    sm = dict(zip(cfg["names"], scratch))
    places, segs, micro, nsub = cfg["places"], cfg["segs"], cfg["micro"], cfg["nsub"]
    rows = nsub * SUB
    tokens = rows * places
    per = micro // 2
    D = cfg["D"]
    FF = cfg["FF"]
    group = D // HEADS
    digits = digits_of(places)
    c = lax.axis_index("section")
    place = lax.axis_index("pts")
    other = 1 - c
    edge = (place == 0) | (place == places - 1)

    stage = sm["stage"]

    dma_in = sm["dma_in"]
    watt, winn, wout, wvec = sm["watt"], sm["winn"], sm["wout"], sm["wvec"]

    def x_copy(bb):
        return pltpu.make_async_copy(x_hbm.at[c * per + bb], stage.at[0, bb], dma_in.at[bb])

    def cot_copy(bb):
        return pltpu.make_async_copy(cot_hbm.at[c * per + bb], stage.at[1, bb], dma_in.at[per + bb])

    weights = [(att_hbm.at[0], watt), (inn_hbm.at[0], winn), (out_hbm.at[0], wout), (vec_hbm, wvec)]

    def weight_copy(k):
        source, held = weights[k]
        return pltpu.make_async_copy(source, held.at[c], dma_in.at[2 * per + k])

    def weight_send(k):
        source, held = weights[k]
        return pltpu.make_async_remote_copy(
            src_ref=source, dst_ref=held.at[c], send_sem=sm["w_send"].at[k], recv_sem=sm["w_recv"].at[k],
            device_id={"section": other}, device_id_type=MESH,
        )

    def weight_arrival(k):
        source, held = weights[k]
        return pltpu.make_async_remote_copy(
            src_ref=source, dst_ref=held.at[other], send_sem=sm["w_send"].at[k], recv_sem=sm["w_recv"].at[k],
            device_id={"section": other}, device_id_type=MESH,
        )

    for k in range(4):
        weight_copy(k).start()
    for bb in range(per):
        x_copy(bb).start()
    for bb in range(per):
        cot_copy(bb).start()

    def partner(digit, offset):
        stride, radix = digits[digit]
        mine = (place // stride) % radix
        theirs = (mine + offset) % radix
        return place + (theirs - mine) * stride

    def digit_at(digit, offset=0):
        stride, radix = digits[digit]
        return ((place // stride) % radix + offset) % radix

    barrier = pltpu.get_barrier_semaphore()
    greeted = 1
    pl.semaphore_signal(barrier, inc=1, device_id={"section": other}, device_id_type=MESH)
    for digit, (stride, radix) in enumerate(digits):
        for offset in range(1, radix):
            pl.semaphore_signal(barrier, inc=1, device_id={"pts": partner(digit, offset)}, device_id_type=MESH)
            greeted += 1

    for offset in range(1, digits[0][1]):
        pl.semaphore_signal(
            barrier, inc=1, device_id={"section": other, "pts": partner(0, offset)}, device_id_type=MESH
        )
        greeted += 1

    tab = sm["tab"]
    T_SLOT, T_END, T_ZI, T_KEEP = 0, nsub, 2 * nsub, 3 * nsub
    T_C, T_LO, T_HI, T_CS, T_ZK, T_LAST, T_CIDX, T_NLOC, T_CNT, T_LS, T_LE, T_OK = (
        4 * nsub + at * segs for at in range(12)
    )
    base = place * rows
    zero = jnp.int32(0)

    for bb in range(per):
        batch = c * per + bb
        lens = [len_s[batch, s] for s in range(segs)]
        ends, run = [], zero
        for s in range(segs):
            run = run + lens[s]
            ends.append(run)
        starts = [zero] + ends[:-1]
        big = zero
        for s in range(1, segs):
            big = big + jnp.where(starts[s] <= rows - 1, 1, 0)
        before = zero
        for s in range(segs):
            before = before + jnp.where(ends[s] <= tokens - rows, 1, 0)
        big = jnp.minimum(big, before)
        local_start = [jnp.clip(starts[s] - base, -1, rows) for s in range(segs)]
        local_end = [jnp.clip(ends[s] - base, 0, rows) for s in range(segs)]
        cells, valid = [zero], [zero]
        tab[bb, T_C] = zero
        tab[bb, T_OK] = zero
        for s in range(segs):
            tab[bb, T_LS + s] = local_start[s]
            tab[bb, T_LE + s] = local_end[s]
            slot = jnp.where(s == big, 0, jnp.where(s < big, s + 1, s))
            tab[bb, T_CS + s] = slot
            if s > 0:
                at = local_start[s]
                inside = jnp.maximum(at, 0)
                cell = jnp.minimum(inside // SUB, nsub - 1)
                low = inside - cell * SUB
                ok = jnp.where((at > 0) & (at < rows) & (low > 0), 1, 0)
                cells.append(cell)
                valid.append(ok)
                tab[bb, T_C + s] = cell
                tab[bb, T_OK + s] = ok
                tab[bb, T_LO + s] = jnp.where(ok == 1, low, SUB)
                tab[bb, T_HI + s] = jnp.where(ok == 1, jnp.minimum(local_end[s] - cell * SUB, SUB), 0)
                tab[bb, T_ZK + s] = ok * valid[s - 1] * jnp.where(cell == cells[s - 1], 1, 0)
        past = None
        for sub in range(nsub):
            row = sub * SUB
            first, final = zero, zero
            for s in range(segs - 1):
                first = first + jnp.where(local_end[s] <= row, 1, 0)
                final = final + jnp.where(local_end[s] <= row + SUB - 1, 1, 0)
            tab[bb, T_SLOT + sub] = tab[bb, T_CS + first]
            tab[bb, T_END + sub] = jnp.minimum(tab[bb, T_LE + first] - row, SUB)
            tab[bb, T_KEEP + sub] = zero if past is None else jnp.where(first == past, 1, 0)
            tab[bb, T_ZI + sub] = jnp.where(final == first, 0, final)
            past = first
        for j in range(segs):
            s = big if j == 0 else jnp.where(j - 1 < big, j - 1, j)
            low, high = tab[bb, T_LS + s], tab[bb, T_LE + s]
            cell = jnp.maximum(high - 1, 0) // SUB
            tab[bb, T_LAST + j] = jnp.where((high > 0) & (low < rows) & (cell * SUB >= low), cell, nsub)
            tab[bb, T_CIDX + j] = jnp.where(tab[bb, T_OK + s] == 1, s, 0)
            tab[bb, T_NLOC + j] = high - jnp.maximum(low, 0)
            tab[bb, T_CNT + j] = len_s[batch, s]

    lane_head = lax.broadcasted_iota(jnp.int32, (group, D), 1) // group
    block_mask = (
        lax.broadcasted_iota(jnp.int32, (D, D), 0) // group == lax.broadcasted_iota(jnp.int32, (D, D), 1) // group
    ).astype(F32)
    ones8 = jnp.ones((8, 128), F32)
    row8 = lax.broadcasted_iota(jnp.int32, (8, D), 0)

    def lanes():
        return lax.broadcasted_iota(jnp.int32, (1, SUB), 1)

    def compact(square):
        total = None
        for j in range(HEADS):
            piece = jnp.where(lane_head == j, square[group * j : group * (j + 1), :], 0.0)
            total = piece if total is None else total + piece
        return total

    def moment_rows(product):
        return cat([compact(product[:D]), product[D : D + 8]])

    def expand(packed):
        return cat([packed] * HEADS, 0) * block_mask

    def centred(matrix):
        grouped = matrix.reshape(matrix.shape[0] // group, group, matrix.shape[1])
        return (grouped - jnp.mean(grouped, axis=1, keepdims=True)).reshape(matrix.shape)

    for name in ("zm", "zk", "zv", "corr_c", "corr_n", "corr_g"):
        sm[name][0] = jnp.zeros(sm[name].shape[1:], F32)
    for name in ("acc_c", "acc_n", "acc_g"):
        sm[name][nsub] = jnp.zeros(sm[name].shape[1:], F32)
    for name in ("d_outer", "d_inner", "d_kv", "s_du", "s_g", "s_dz"):
        sm[name][...] = jnp.zeros(sm[name].shape, F32)
    gb = sm["gb"]
    gb[...] = jnp.zeros(gb.shape, F32)
    first, parts_rows = gradient_rows(D, FF, digits)
    R_Q, R_K, R_V, R_3, R_I, R_O, R_VEC = (first[name] for name in ("q", "k", "v", "o", "inner", "outer", "vec"))

    pl.semaphore_wait(barrier, greeted)
    for k in range(4):
        weight_send(k).start()

    tables = sm["tables"]

    def prepare(layer):
        @pl.when(c == layer)
        def _():
            for k in range(4):
                weight_copy(k).wait()

        @pl.when(c != layer)
        def _():
            for k in range(4):
                weight_arrival(k).wait_recv()

        def column(row):
            return jnp.broadcast_to(wvec[layer, row], (128, D)).T

        for row in (0, 3, 8, 9, 10):
            tables[layer, row] = column(row)
        for row in (1, 2):
            tables[layer, row] = centred(column(row))
        packed = sm["packed"]
        packed[layer, 0] = compact(1.0 + column(4))
        packed[layer, 1] = compact(column(5))
        packed[layer, 2] = compact(1.0 + column(6))
        query_t, output_t = watt[layer, 0].T, watt[layer, 3].T
        sm["wq_t"][layer] = pack3(query_t)
        sm["w3_t"][layer] = pack3(output_t)
        sm["wq_right"][layer] = right3(cat([query_t, tables[layer, 0]], 1))
        sm["w3_right"][layer] = right3(output_t)
        sm["kvw"][layer] = pack3(cat([centred(watt[layer, 1].T), centred(watt[layer, 2].T)], 0))
        sm["kvw_back"][layer] = cat([pack3(watt[layer, 1]), pack3(watt[layer, 2])], 1)
        inner = winn[layer]
        sm["inn_t"][layer] = pack3(cat([inner[:, at : at + D].T for at in range(0, FF, D)], 0))
        sm["inn"][layer] = pack3(inner)
        outer = wout[layer]
        sm["out_t"][layer] = pack3(cat([outer[at : at + D, :].T for at in range(0, FF, D)], 1))
        sm["out"][layer] = pack3(outer)

    ar = sm["ar"]

    def ar_copy(k, digit, offset):
        spot = ar.at[k, digit, digit_at(digit)]
        return pltpu.make_async_remote_copy(
            src_ref=spot, dst_ref=spot, send_sem=sm["ar_send"].at[k, digit, offset - 1],
            recv_sem=sm["ar_recv"].at[k, digit, offset - 1],
            device_id={"pts": partner(digit, offset)}, device_id_type=MESH,
        )

    def ar_arrival(k, digit, offset):
        radix = digits[digit][1]
        spot = ar.at[k, digit, digit_at(digit, radix - offset)]
        return pltpu.make_async_remote_copy(
            src_ref=spot, dst_ref=spot, send_sem=sm["ar_send"].at[k, digit, offset - 1],
            recv_sem=sm["ar_recv"].at[k, digit, offset - 1],
            device_id={"pts": partner(digit, offset)}, device_id_type=MESH,
        )

    def ar_launch(k, digit, payload):
        ar[k, digit, digit_at(digit)] = payload
        for offset in range(1, digits[digit][1]):
            ar_copy(k, digit, offset).start()

    def ar_land(k, digit):
        radix = digits[digit][1]
        for offset in range(1, radix):
            ar_arrival(k, digit, offset).wait_recv()
        total = ar[k, digit, 0]
        for at in range(1, radix):
            total = total + ar[k, digit, at]
        return total

    def ar_step(k, digit):
        if digit < len(digits):
            ar_launch(k, digit, ar_land(k, digit - 1))

    def ar_finish(k):
        for digit in range(2, len(digits)):
            ar_step(k, digit)
        return ar_land(k, len(digits) - 1)

    def ar_drain(k):
        for digit in range(len(digits)):
            for offset in range(1, digits[digit][1]):
                ar_copy(k, digit, offset).wait_send()

    hs, kvs, rst, dms = sm["hs"], sm["kvs"], sm["rst"], sm["dms"]
    mids, hids, gps = sm["mids"], sm["hids"], sm["gps"]

    def three(pair, at=0, size=D):
        high = pair[at : at + size]
        return [high, pair[at + size : at + 2 * size], high]

    def joined(pairs):
        whole = pairs.astype(F32)
        return cat([whole[:D] + whole[D : 2 * D], whole[2 * D : 3 * D] + whole[3 * D :]])

    def load(ref, lead, subs):
        return cat([ref[(*lead, sub)] for sub in subs], 1)

    def save(ref, lead, subs, value):
        for at, sub in enumerate(subs):
            ref[(*lead, sub)] = value[:, SUB * at : SUB * (at + 1)]

    def part(value, at):
        return value[:, SUB * at : SUB * (at + 1)]

    def inside_of(bb, sub):
        return lanes() < tab[bb, T_END + sub]

    def keys_and_values(layer, bb, subs, pair):
        width = SUB * len(subs)
        bias = cat([wide(tables[layer, 1], width), wide(tables[layer, 2], width)], 0)
        field = dot16(sm["kvw"][layer], cat(three(pair))) + bias
        grouped = field.reshape(2 * HEADS, group, width)
        spread = jnp.mean(grouped * grouped, axis=1, keepdims=True)
        scale = lax.rsqrt(spread + EPS_NORM)
        normed = (grouped * scale).reshape(2 * D, width)
        save(rst, (layer, bb), subs, scale.reshape(2 * HEADS, width))
        k_high, k_low = split(normed[:D])
        v_high, v_low = split(normed[D:])
        keys, values = cat([k_high, k_low]), cat([v_high, v_low])
        save(kvs, (layer, bb), subs, cat([keys, values]))
        for at, sub in enumerate(subs):
            inside = inside_of(bb, sub)
            product = moment_rows(outer16_sums(part(keys, at), part(values, at) * inside.astype(BF16)))
            sums = fold(jnp.where(inside, part(normed, at)[:D], 0.0))
            keep = tab[bb, T_KEEP + sub] == 1
            past = jnp.maximum(sub - 1, 0)
            sm["acc_c"][sub] = product + jnp.where(keep, sm["acc_c"][past], 0.0)
            sm["acc_n"][sub] = sums + jnp.where(keep, sm["acc_n"][past], 0.0)

    def feed_forward(layer, bb, subs):
        width = SUB * len(subs)
        middles = []
        for sub in subs:
            slot = tab[bb, T_SLOT + sub]
            value = dot16(left3(sm["fwd_mat"][slot]), cat(three(hs[layer, bb, sub]))) + wide(sm["fwd_add"][slot], SUB)
            middles.append(jnp.where(inside_of(bb, sub), value, sm["zm"][tab[bb, T_ZI + sub]]))
        middle = cat(middles, 1)
        m_high, m_low = split(middle)
        mid_pair = cat([m_high, m_low])
        u = dot16(sm["inn_t"][layer], cat(three(mid_pair)))
        u = u + cat([wide(tables[layer, 9], width), wide(tables[layer, 10], width)], 0)
        k0 = 0.7978845608
        square = u * u
        t = jnp.tanh(u * (k0 + (k0 * 0.044715) * square))
        half = 0.5 + 0.5 * t
        hidden = u * half
        slope = half + hidden * (1.0 - t) * (k0 + (3.0 * k0 * 0.044715) * square)
        h_high, h_low = split(hidden)
        hid_pair = cat([h_high, h_low])
        out = middle + dot16(sm["out_t"][layer], cat(three(hid_pair, 0, FF))) + wide(tables[layer, 8], width)
        return out, mid_pair, hid_pair, slope

    def feed_back(layer, bb, subs, upstream, mid_pair, hid_pair, slope):
        g_high, g_low = split(upstream)
        g_pair = cat([g_high, g_low])
        du = dot16(sm["out"][layer], cat(three(g_pair))) * slope
        u_high, u_low = split(du)
        u_pair = cat([u_high, u_low])
        d_mid = upstream + dot16(sm["inn"][layer], cat(three(u_pair, 0, FF)))
        q_high, q_low = split(d_mid)
        q_pair = cat([q_high, q_low])
        save(dms, (bb,), subs, q_pair)
        for at, sub in enumerate(subs):
            q_inside = part(q_pair, at) * inside_of(bb, sub).astype(BF16)
            product = outer16_sums(hs[layer, bb, sub], q_inside)
            keep = tab[bb, T_KEEP + sub] == 1
            past = jnp.maximum(sub - 1, 0)
            sm["acc_g"][sub] = product + jnp.where(keep, sm["acc_g"][past], 0.0)
        sm["d_outer"][layer] += outer16(hid_pair, g_pair)
        sm["d_inner"][layer] += outer16(u_pair, mid_pair)
        sm["s_du"][layer] += fold(du)
        sm["s_g"][layer] += fold(upstream)

    def norm_back(layer, bb, subs):
        width = SUB * len(subs)
        pairs = load(kvs, (layer, bb), subs)
        normed = joined(pairs)
        e_ks, e_vs = [], []
        for at, sub in enumerate(subs):
            slot, zi, inside = tab[bb, T_SLOT + sub], tab[bb, T_ZI + sub], inside_of(bb, sub)
            own = part(pairs, at)
            e_k = dot16(left3(sm["key_mat"][slot]), cat(three(own, 2 * D))) + wide(sm["key_add"][slot], SUB)
            e_v = dot16(left3(sm["val_mat"][slot]), cat(three(own))) + wide(sm["val_add"][slot], SUB)
            e_ks.append(jnp.where(inside, e_k, sm["zk"][zi]))
            e_vs.append(jnp.where(inside, e_v, sm["zv"][zi]))
        e = cat([cat(e_ks, 1), cat(e_vs, 1)])
        shape = (2 * HEADS, group, width)
        e3, n3 = e.reshape(shape), normed.reshape(shape)
        scale = load(rst, (layer, bb), subs).reshape(2 * HEADS, 1, width)
        along = jnp.mean(e3 * n3, axis=1, keepdims=True)
        dz = ((e3 - n3 * along) * scale).reshape(2 * D, width)
        z_high, z_low = split(dz)
        z_pair = cat([z_high, z_low])
        sm["d_kv"][layer] += outer16(z_pair, load(hs, (layer, bb), subs))
        sm["s_dz"][layer] += fold(dz)
        return z_pair

    def input_back(layer, bb, subs, z_pair):
        z_high, z_low = z_pair[: 2 * D], z_pair[2 * D :]
        through = [z_high[:D], z_low[:D], z_high[:D], z_high[D:], z_low[D:], z_high[D:]]
        backs = []
        for at, sub in enumerate(subs):
            slot, zi = tab[bb, T_SLOT + sub], tab[bb, T_ZI + sub]
            left = cat([left3(sm["back_mat"][layer, bb, slot]), sm["kvw_back"][layer]], 1)
            right = three(dms[bb, sub] * inside_of(bb, sub).astype(BF16)) + [part(one, at) for one in through]
            backs.append(dot16(left, cat(right)) + sm["zm"][zi])
        return cat(backs, 1)

    count = TILE // SUB

    def over(low, high, stage):
        def body(i, carry):
            stage([i * count + at for at in range(count)])
            return carry

        lax.fori_loop(low, high, body, 0)

    steps = nsub // count

    def loop(stage, between):
        over(0, (steps + 1) // 2, stage)
        between()
        over((steps + 1) // 2, steps, stage)

    def span(bb, s):
        at = lanes()
        return (at >= tab[bb, T_LO + s]) & (at < tab[bb, T_HI + s])

    def fill(name, bb, s, inside, value):
        before = jnp.where(tab[bb, T_ZK + s] == 1, sm[name][s - 1], 0.0)
        sm[name][s] = jnp.where(inside, value, before)

    def corrections_mid(layer, bb):
        @pl.when(edge)
        def _():
            for s in range(1, segs):
                pair = hs[layer, bb, tab[bb, T_C + s]]
                slot = tab[bb, T_CS + s]
                value = dot16(left3(sm["fwd_mat"][slot]), cat(three(pair))) + wide(sm["fwd_add"][slot], SUB)
                fill("zm", bb, s, span(bb, s), value)

    def corrections_back(layer, bb):
        @pl.when(edge)
        def _():
            for s in range(1, segs):
                cell, slot, inside = tab[bb, T_C + s], tab[bb, T_CS + s], span(bb, s)
                pairs = kvs[layer, bb, cell]
                e_k = dot16(left3(sm["key_mat"][slot]), cat(three(pairs, 2 * D))) + wide(sm["key_add"][slot], SUB)
                e_v = dot16(left3(sm["val_mat"][slot]), cat(three(pairs))) + wide(sm["val_add"][slot], SUB)
                e_d = dot16(left3(sm["back_mat"][layer, bb, slot]), cat(three(dms[bb, cell])))
                fill("zk", bb, s, inside, e_k)
                fill("zv", bb, s, inside, e_v)
                fill("zm", bb, s, inside, e_d)

    def corrections_moments(layer, bb):
        @pl.when(edge)
        def _():
            for s in range(1, segs):
                cell, inside = tab[bb, T_C + s], span(bb, s)
                pairs = kvs[layer, bb, cell]
                product = outer16_sums(pairs[: 2 * D], pairs[2 * D :] * inside.astype(BF16))
                sm["corr_c"][s] = moment_rows(product)
                keys = pairs[: 2 * D].astype(F32)
                sm["corr_n"][s] = fold(jnp.where(inside, keys[:D] + keys[D:], 0.0))

    def corrections_grams(layer, bb):
        @pl.when(edge)
        def _():
            for s in range(1, segs):
                cell, inside = tab[bb, T_C + s], span(bb, s)
                q_pair = dms[bb, cell] * inside.astype(BF16)
                sm["corr_g"][s] = outer16_sums(hs[layer, bb, cell], q_pair)

    stats, own_c, own_d, vec, vec_c = sm["stats"], sm["own_c"], sm["own_d"], sm["vec"], sm["vec_c"]

    def total_of(name, bb, j):
        return sm["acc_" + name][tab[bb, T_LAST + j]] + sm["corr_" + name][tab[bb, T_CIDX + j]]

    def shifts(layer):
        return 1.0 + wvec[layer, 4], wvec[layer, 5], 1.0 + wvec[layer, 6], wvec[layer, 7]

    def moments_of(layer, bb, j):
        key_gain, key_shift, value_gain, value_shift = shifts(layer)
        gain_c, shift_c = sm["packed"][layer, 0], sm["packed"][layer, 1]
        rows_c = total_of("c", bb, j)
        product, values = rows_c[:group], rows_c[group : group + 1]
        keys = compact(jnp.broadcast_to(jnp.sum(total_of("n", bb, j), axis=1, keepdims=True), (D, 128)))
        stats[layer, bb, j] = cat([product, keys, rows_c[group:]])
        local = tab[bb, T_NLOC + j].astype(F32)
        from_values = values * value_gain + local * value_shift
        return gain_c * (product * value_gain + keys * value_shift) + shift_c * from_values

    def mixing_of(layer, bb, slots, moments):
        packs = []
        for j, moment in zip(slots, moments):
            pack = pack2((expand(moment) / tab[bb, T_CNT + j].astype(F32)).T)
            sm["mt"][layer, bb, j] = pack
            packs.append(left3(pack))
        mixed = dot16(cat(packs), sm["wq_right"][layer])
        rights = [right3(mixed[D * at : D * (at + 1)]) for at in range(len(slots))]
        through = dot16(sm["w3_t"][layer], cat(rights, 1))
        eye = (
            lax.broadcasted_iota(jnp.int32, (D, D), 0) == lax.broadcasted_iota(jnp.int32, (D, D), 1)
        ).astype(F32)
        for at, j in enumerate(slots):
            forward = through[:, 2 * D * at : 2 * D * at + D] + eye
            sm["fwd_mat"][j] = pack2(forward)
            sm["fwd_add"][j] = through[:, 2 * D * at + D : 2 * D * (at + 1)] + tables[layer, 3]
            sm["back_mat"][layer, bb, j] = pack2(forward.T)

    def grams_of(layer, bb, slots):
        grams = [total_of("g", bb, j) for j in slots]
        tall = D + 16
        onto = dot16(cat([pack3(gram) for gram in grams]), sm["w3_right"][layer])
        ontos = [onto[tall * at : tall * (at + 1)] for at in range(len(slots))]
        rights = [right3(cat([one[:D], gram[:D]], 1)) for one, gram in zip(ontos, grams)]
        both = dot16(sm["wq_t"][layer], cat(rights, 1))
        query_bias = tables[layer, 0]
        d_moments, throughs = [], []
        for at, (one, gram) in enumerate(zip(ontos, grams)):
            d_moments.append(compact(both[:, 2 * D * at : 2 * D * at + D] + query_bias * one[D : D + 1]))
            throughs.append(both[:, 2 * D * at + D : 2 * D * (at + 1)] + query_bias * gram[D : D + 1])
        return d_moments, ontos, throughs, grams

    def projections_of(layer, bb, slots, ontos, throughs, grams):
        mts = [sm["mt"][layer, bb, j] for j in slots]
        right = [part for mt in mts for part in (mt[:, :D], mt[:, D:], mt[:, :D])]
        d_query = dot16(cat([pack3(one) for one in ontos], 1), cat(right))
        gb[layer, R_Q : R_Q + D] += d_query[:D]
        gb[layer, R_3 : R_3 + D] += dot16(cat([left3(mt) for mt in mts], 1), cat([right3(through) for through in throughs]))
        vec[layer, 0] += d_query[D : D + 8]
        sums = grams[0][D : D + 8]
        for gram in grams[1:]:
            sums = sums + gram[D : D + 8]
        vec[layer, 1] += sums

    def back_of(layer, bb, slots, d_moments):
        key_gain, key_shift, value_gain, value_shift = shifts(layer)
        gain_c, shift_c, value_gain_c = (sm["packed"][layer, at] for at in range(3))

        def across(packed):
            return jnp.broadcast_to(jnp.sum(expand(centred(packed)), axis=1, keepdims=True), (D, 128))

        for j, d_moment in zip(slots, d_moments):
            d = d_moment / tab[bb, T_CNT + j].astype(F32)
            d_t = compact(expand(d).T)
            sm["key_mat"][j] = pack2(expand(centred(gain_c * d * value_gain)))
            sm["key_add"][j] = across(gain_c * d * value_shift)
            sm["val_mat"][j] = pack2(expand(centred(value_gain_c * d_t * key_gain)))
            sm["val_add"][j] = across(value_gain_c * d_t * key_shift)
            held = stats[layer, bb, j]
            product, keys, values = held[:group], held[group : 2 * group], held[2 * group : 2 * group + 1]
            local = tab[bb, T_NLOC + j].astype(F32)
            vec_c[layer, 0] += d * (product * value_gain + keys * value_shift)
            vec_c[layer, 1] += d * (values * value_gain + local * value_shift)
            vec_c[layer, 2] += d * (gain_c * product + shift_c * values)
            vec_c[layer, 3] += d * (gain_c * keys + shift_c * local)

    small = list(range(1, segs))

    def key_of(stage, bb):
        return stage * per + bb

    def moments_out(layer, bb, k):
        corrections_moments(layer, bb)
        ar_launch(k, 0, moments_of(layer, bb, 0))

        @pl.when(edge)
        def _():
            for j in small:
                own_c[layer, bb, j] = moments_of(layer, bb, j)

    def mixing_in(layer, bb, k):
        @pl.when(edge)
        def _():
            mixing_of(layer, bb, small, [own_c[layer, bb, j] for j in small])

        mixing_of(layer, bb, [0], [ar_finish(k)])
        corrections_mid(layer, bb)

    def grams_out(layer, bb, k):
        corrections_grams(layer, bb)
        d_moments, *rest = grams_of(layer, bb, [0])
        ar_launch(k, 0, d_moments[0])
        projections_of(layer, bb, [0], *rest)

        @pl.when(edge)
        def _():
            d_moments, *rest = grams_of(layer, bb, small)
            for j, d_moment in zip(small, d_moments):
                own_d[bb, j] = d_moment
            projections_of(layer, bb, small, *rest)

    def grams_in(layer, bb, k):
        @pl.when(edge)
        def _():
            back_of(layer, bb, small, [own_d[bb, j] for j in small])

        back_of(layer, bb, [0], [ar_finish(k)])
        corrections_back(layer, bb)

    vec[...] = jnp.zeros(vec.shape, F32)
    vec_c[...] = jnp.zeros(vec_c.shape, F32)

    targets = (act_hbm, grd_hbm)

    def kept(kind, layer, bb):
        return pltpu.make_async_copy(
            stage.at[layer, bb], targets[kind].at[c * per + bb], sm["o_local"].at[kind, bb]
        )

    def sent(kind, layer, bb):
        return pltpu.make_async_remote_copy(
            src_ref=stage.at[layer, bb], dst_ref=targets[kind].at[c * per + bb], send_sem=sm["o_send"].at[kind, bb],
            recv_sem=sm["o_recv"].at[kind, bb], device_id={"section": other}, device_id_type=MESH,
        )

    def came(kind, layer, bb):
        return pltpu.make_async_remote_copy(
            src_ref=stage.at[layer, bb], dst_ref=targets[kind].at[other * per + bb], send_sem=sm["o_send"].at[kind, bb],
            recv_sem=sm["o_recv"].at[kind, bb], device_id={"section": other}, device_id_type=MESH,
        )

    def ship(kind, layer, bb):
        @pl.when(c == layer)
        def _():
            kept(kind, layer, bb).start()

        @pl.when(c != layer)
        def _():
            sent(kind, layer, bb).start()

    def shipped(kind, layer, bb):
        @pl.when(c == layer)
        def _():
            kept(kind, layer, bb).wait()

        @pl.when(c != layer)
        def _():
            sent(kind, layer, bb).wait_send()

    def load_t(layer, bb, subs):
        return cat([stage[layer, bb, sub].T for sub in subs], 1)

    def save_t(layer, bb, subs, value):
        for at, sub in enumerate(subs):
            stage[layer, bb, sub] = part(value, at).T

    def start_stage(bb, subs):
        high, low = split(load_t(0, bb, subs))
        pair = cat([high, low])
        save(hs, (0, bb), subs, pair)
        keys_and_values(0, bb, subs, pair)

    def first_stage(bb, subs):
        out, mid_pair, hid_pair, slope = feed_forward(0, bb, subs)
        save(mids, (bb,), subs, mid_pair)
        save(hids, (bb,), subs, hid_pair)
        save(gps, (bb,), subs, slope)
        save_t(0, bb, subs, out)
        high, low = split(out)
        pair = cat([high, low])
        save(hs, (1, bb), subs, pair)
        keys_and_values(1, bb, subs, pair)

    def second_stage(bb, subs):
        out, mid_pair, hid_pair, slope = feed_forward(1, bb, subs)
        upstream = load_t(1, bb, subs)
        save_t(1, bb, subs, out)
        feed_back(1, bb, subs, upstream, mid_pair, hid_pair, slope)

    def third_stage(bb, subs):
        upstream = input_back(1, bb, subs, norm_back(1, bb, subs))
        save_t(1, bb, subs, upstream)
        held = [load(ref, (bb,), subs) for ref in (mids, hids, gps)]
        feed_back(0, bb, subs, upstream, *held)

    def fourth_stage(bb, subs):
        save_t(0, bb, subs, input_back(0, bb, subs, norm_back(0, bb, subs)))

    def fifth_stage(bb, subs):
        save(kvs, (0, bb), subs, norm_back(0, bb, subs))

    def sixth_stage(bb, subs):
        save_t(0, bb, subs, input_back(0, bb, subs, load(kvs, (0, bb), subs)))

    og = sm["og"]
    summed, widened = digits[:2], digits[2:]
    sizes = []
    for kind in range(2):
        sizes.append([parts_rows[kind]])
        for _, radix in summed:
            sizes[-1].append(sizes[-1][-1] // radix)
    g_send, g_recv = sm["g_send"], sm["g_recv"]

    def early_rows(layer):
        gb[layer, R_O : R_O + FF] = sm["d_outer"][layer]
        d_inner = sm["d_inner"][layer]
        for at in range(0, FF, D):
            gb[layer, R_I + at : R_I + at + D] = d_inner[at : at + D].T

    def late_rows(layer):
        d_kv = sm["d_kv"][layer]
        gb[layer, R_K : R_K + D] = d_kv[:D].T
        gb[layer, R_V : R_V + D] = d_kv[D:].T
        s_dz = mm_nt(ones8, sm["s_dz"][layer])
        s_du = mm_nt(ones8, sm["s_du"][layer])
        s_g = mm_nt(ones8, sm["s_g"][layer])
        lines = [vec[layer, 0], s_dz[:, :D], s_dz[:, D:], vec[layer, 1]]
        lines += [mm_nt(ones8, expand(vec_c[layer, at])) for at in (0, 1)]
        lines += [jnp.sum(vec_c[layer, at], axis=0, keepdims=True) for at in (2, 3)]
        lines += [s_g, s_du[:, :D], s_du[:, D:]]
        block = jnp.zeros((16, D), F32)
        row16 = lax.broadcasted_iota(jnp.int32, (16, D), 0)
        for at, line in enumerate(lines):
            block = jnp.where(row16 == at, line[0:1], block)
        gb[layer, R_VEC : R_VEC + 16] = block

    def block_of(kind, depth, at=None):
        low = 0 if kind == 0 else parts_rows[0]
        for digit in range(depth):
            offset = at if (at is not None and digit == depth - 1) else 0
            low = low + digit_at(digit, offset) * sizes[kind][digit + 1]
        return pl.ds(low if depth == 0 else pl.multiple_of(low, 8), sizes[kind][depth])

    def landing(kind, digit):
        return sm["rb%d%d" % (kind, digit)]

    def scatter_first(layer, kind, offset):
        radix = summed[0][1]
        own = offset - 1
        far = radix - 1 + offset

        def copy(slot, target):
            return pltpu.make_async_remote_copy(
                src_ref=gb.at[layer, block_of(kind, 1, offset)], dst_ref=landing(kind, 0).at[slot],
                send_sem=g_send.at[kind, 0, 0, slot], recv_sem=g_recv.at[kind, 0, 0, slot],
                device_id=target, device_id_type=MESH,
            )

        near = {"pts": partner(0, offset)}
        return copy(own, near), copy(far, {"section": other, "pts": partner(0, offset)})

    def scatter_next(layer, kind, digit, offset):
        return pltpu.make_async_remote_copy(
            src_ref=gb.at[layer, block_of(kind, digit + 1, offset)], dst_ref=landing(kind, digit).at[offset - 1],
            send_sem=g_send.at[kind, 0, digit, offset - 1], recv_sem=g_recv.at[kind, 0, digit, offset - 1],
            device_id={"pts": partner(digit, offset)}, device_id_type=MESH,
        )

    def gather(kind, digit, offset, at):
        spot = og.at[block_of(kind, digit + 1, at)]
        return pltpu.make_async_remote_copy(
            src_ref=spot, dst_ref=spot,
            send_sem=g_send.at[kind, 1, digit, offset - 1], recv_sem=g_recv.at[kind, 1, digit, offset - 1],
            device_id={"pts": partner(digit, offset)}, device_id_type=MESH,
        )

    def exchange(kind, at, offset, back=0):
        digit = len(summed) + at
        spot = sm["wide%d" % kind].at[at, digit_at(digit, back)]
        return pltpu.make_async_remote_copy(
            src_ref=spot, dst_ref=spot,
            send_sem=g_send.at[kind, 0, digit, offset - 1], recv_sem=g_recv.at[kind, 0, digit, offset - 1],
            device_id={"pts": partner(digit, offset)}, device_id_type=MESH,
        )

    def gradient_step(layer, kind, step):
        last = len(summed)
        if step == 0:
            @pl.when(c == layer)
            def _():
                for offset in range(1, summed[0][1]):
                    scatter_first(layer, kind, offset)[0].start()

            @pl.when(c != layer)
            def _():
                for offset in range(summed[0][1]):
                    scatter_first(layer, kind, offset)[1].start()

        elif step <= last:
            digit = step - 1
            radix = summed[digit][1]

            @pl.when(c == layer)
            def _():
                total = gb[layer, block_of(kind, digit + 1)]
                for offset in range(1, radix):
                    if digit == 0:
                        scatter_first(layer, kind, offset)[0].wait_recv()
                    else:
                        scatter_next(layer, kind, digit, offset).wait_recv()
                    total = total + landing(kind, digit)[offset - 1]
                if digit == 0:
                    for offset in range(radix):
                        scatter_first(layer, kind, offset)[1].wait_recv()
                        total = total + landing(kind, 0)[radix - 1 + offset]
                if step < last:
                    gb[layer, block_of(kind, digit + 1)] = total
                    for offset in range(1, summed[step][1]):
                        scatter_next(layer, kind, step, offset).start()
                else:
                    for at, (_, wide_radix) in enumerate(widened):
                        digit_now = last + at
                        sm["wide%d" % kind][at, digit_at(digit_now)] = total
                        for offset in range(1, wide_radix):
                            exchange(kind, at, offset).start()
                        for offset in range(1, wide_radix):
                            exchange(kind, at, offset, wide_radix - offset).wait_recv()
                        total = sm["wide%d" % kind][at, 0]
                        for other_at in range(1, wide_radix):
                            total = total + sm["wide%d" % kind][at, other_at]
                    og[block_of(kind, last)] = total
                    for offset in range(1, radix):
                        gather(kind, digit, offset, 0).start()

        elif step <= 2 * last:
            digit = 2 * last - step

            @pl.when(c == layer)
            def _():
                radix = summed[digit][1]
                for offset in range(1, radix):
                    gather(kind, digit, offset, radix - offset).wait_recv()
                if digit > 0:
                    for offset in range(1, summed[digit - 1][1]):
                        gather(kind, digit - 1, offset, 0).start()

    def drain_gradients():
        for layer in range(2):
            @pl.when(c == layer)
            def _():
                for kind in range(2):
                    for offset in range(1, summed[0][1]):
                        scatter_first(layer, kind, offset)[0].wait_send()
                    for digit in range(1, len(summed)):
                        for offset in range(1, summed[digit][1]):
                            scatter_next(layer, kind, digit, offset).wait_send()
                    for at, (_, wide_radix) in enumerate(widened):
                        for offset in range(1, wide_radix):
                            exchange(kind, at, offset).wait_send()
                    for digit in range(len(summed)):
                        for offset in range(1, summed[digit][1]):
                            gather(kind, digit, offset, 0).wait_send()

            @pl.when(c != layer)
            def _():
                for kind in range(2):
                    for offset in range(summed[0][1]):
                        scatter_first(layer, kind, offset)[1].wait_send()

    EARLY, LATE = 0, 1

    def together(*actions):
        def run():
            for action in actions:
                action()

        return run

    def grad(layer, kind, step):
        return functools.partial(gradient_step, layer, kind, step)

    prepare(0)
    for bb in range(per):
        x_copy(bb).wait()
        loop(functools.partial(start_stage, bb), lambda bb=bb: ar_step(key_of(0, bb - 1), 1) if bb > 0 else None)
        moments_out(0, bb, key_of(0, bb))
    prepare(1)
    ar_step(key_of(0, per - 1), 1)

    def in_flight(stage, bb):
        if bb > 0:
            return lambda: ar_step(key_of(stage, bb - 1), 1)
        return lambda: None

    def late(stage):
        ar_step(key_of(stage, per - 1), 1)

    for bb in range(per):
        mixing_in(0, bb, key_of(0, bb))
        loop(functools.partial(first_stage, bb), in_flight(1, bb))
        ship(0, 0, bb)
        moments_out(1, bb, key_of(1, bb))
    for bb in range(per):
        cot_copy(bb).wait()
        mixing_in(1, bb, key_of(1, bb))
        loop(functools.partial(second_stage, bb), in_flight(2, bb) if bb > 0 else lambda: late(1))
        ship(0, 1, bb)
        grams_out(1, bb, key_of(2, bb))
    early_rows(1)
    gradient_step(1, EARLY, 0)
    for bb in range(per):
        grams_in(1, bb, key_of(2, bb))
        shipped(0, 1, bb)
        beside = together(in_flight(3, bb), grad(1, EARLY, 2)) if bb > 0 else together(functools.partial(late, 2), grad(1, EARLY, 1))
        loop(functools.partial(third_stage, bb), beside)
        ship(1, 1, bb)
        grams_out(0, bb, key_of(3, bb))
    early_rows(0)
    late_rows(1)
    gradient_step(0, EARLY, 0)
    gradient_step(1, LATE, 0)
    gradient_step(1, EARLY, 3)
    for bb in range(per - 1):
        grams_in(0, bb, key_of(3, bb))
        shipped(0, 0, bb)
        beside = together(functools.partial(late, 3), grad(0, EARLY, 1), grad(1, LATE, 1), grad(1, EARLY, 4))
        loop(functools.partial(fourth_stage, bb), beside if bb == 0 else lambda: None)
        ship(1, 0, bb)
    bb = per - 1
    grams_in(0, bb, key_of(3, bb))
    shipped(0, 0, bb)
    loop(functools.partial(fifth_stage, bb), together(grad(0, EARLY, 2), grad(1, LATE, 2)))
    late_rows(0)
    gradient_step(0, LATE, 0)
    gradient_step(0, EARLY, 3)
    gradient_step(1, LATE, 3)
    loop(functools.partial(sixth_stage, bb), grad(0, LATE, 1))
    ship(1, 0, bb)
    gradient_step(0, LATE, 2)
    gradient_step(0, EARLY, 4)
    gradient_step(1, LATE, 4)
    gradient_step(0, LATE, 3)
    gradient_step(0, LATE, 4)
    out_copy = pltpu.make_async_copy(og, gsum_hbm, dma_in.at[0])
    out_copy.start()

    drain_gradients()
    for k in range(4):
        weight_send(k).wait_send()
    for k in range(4 * per):
        ar_drain(k)
    for bb in range(per):
        for layer in range(2):
            shipped(1, layer, bb)
        for layer in range(2):
            @pl.when(c == layer)
            def _():
                came(0, layer, bb).wait_recv()
                came(1, layer, bb).wait_recv()
    out_copy.wait()


def finishing(scale, D, FF, first, act, grd, gsum_hbm, *refs):
    sources, results = refs[:12], refs[12:30]
    gsum, held, made, through, sem_large, sem_in, sem_out = refs[30], refs[31:43], refs[43:59], *refs[59:]
    large, onward = [], []
    for kind, (source, target) in enumerate(((act, results[0]), (grd, results[1]))):
        for part in range(source.shape[0]):
            spot = through.at[kind, part]
            large.append(pltpu.make_async_copy(source.at[part], spot, sem_large.at[0, kind, part]))
            onward.append(pltpu.make_async_copy(spot, target.at[part], sem_large.at[1, kind, part]))
    loads = [pltpu.make_async_copy(gsum_hbm, gsum, sem_in.at[12])]
    loads += [pltpu.make_async_copy(sources[at], held[at], sem_in.at[at]) for at in range(12)]
    for copy in loads:
        copy.start()
    for copy in large:
        copy.start()
    rate = plan()

    def step(weight, gradient, momentum, variance):
        average = gradient * scale
        new_momentum = 0.9 * momentum + 0.1 * average
        new_variance = 0.999 * variance + 0.001 * average * average
        mean = new_momentum / (1.0 - 0.9**STEP)
        square = new_variance / (1.0 - 0.999**STEP)
        updated = weight - rate * (mean / (jnp.sqrt(square) + 1e-08) + 0.01 * weight)
        return gradient, new_momentum, new_variance, updated

    parts = [first[name] for name in ("q", "k", "v", "o")]
    inner, outer, late = first["inner"], first["outer"], first["vec"]
    places = [
        [((0, at), slice(low, low + D)) for at, low in enumerate(parts)],
        [((0, slice(None), slice(at, at + D)), slice(inner + at, inner + at + D)) for at in range(0, FF, D)],
        [((0,), slice(outer, outer + FF))],
        [((line,), slice(late + line, late + line + 1)) for line in range(held[3].shape[0])],
    ]
    for copy, after in zip(large, onward):
        copy.wait()
        after.start()
    loads[0].wait()
    stores = []
    for kind in range(4):
        for at in (kind, 4 + 2 * kind, 5 + 2 * kind):
            loads[1 + at].wait()
        weight, momentum, variance = held[kind], held[4 + 2 * kind], held[5 + 2 * kind]
        for index, lines in places[kind]:
            values = step(weight[index], gsum[lines], momentum[index], variance[index])
            for ref, value in zip(made[4 * kind : 4 * kind + 4], values):
                ref[index] = value
        for at in range(4 * kind, 4 * kind + 4):
            stores.append(pltpu.make_async_copy(made[at], results[2 + at], sem_out.at[at]))
            stores[-1].start()
    for copy in onward + stores:
        copy.wait()


def per_device(
    node_features, cotangent, lengths, attention_weight, inner_weight, outer_weight, vectors,
    momentum_attention, variance_attention, momentum_inner, variance_inner,
    momentum_outer, variance_outer, momentum_vectors, variance_vectors,
):
    places = lax.axis_size("pts")
    micro, rows, D = node_features.shape
    FF = inner_weight.shape[-1]
    segs = lengths.shape[1]
    lines = vectors.shape[1]
    nsub = rows // SUB
    per = micro // 2
    digits = digits_of(places)
    group = D // HEADS
    first, parts_rows = gradient_rows(D, FF, digits)
    total_rows = sum(parts_rows)
    nar = 4 * per

    def f32(*shape):
        return pltpu.VMEM(shape, F32)

    def b16(*shape):
        return pltpu.VMEM(shape, BF16)

    def dma(*shape):
        return pltpu.SemaphoreType.DMA(shape)

    scratch = dict(
        watt=f32(2, 4, D, D), winn=f32(2, D, FF), wout=f32(2, FF, D), wvec=f32(2, lines, 1, D),
        tab=pltpu.SMEM((per, 4 * nsub + 12 * segs), jnp.int32),
        tables=f32(2, 11, D, 128), packed=f32(2, 3, group, D),
        wq_t=b16(2, D, 3 * D), w3_t=b16(2, D, 3 * D), wq_right=b16(2, 3 * D, 2 * D), w3_right=b16(2, 3 * D, D),
        kvw=b16(2, 2 * D, 3 * D), kvw_back=b16(2, D, 6 * D),
        inn_t=b16(2, FF, 3 * D), inn=b16(2, D, 3 * FF), out_t=b16(2, D, 3 * FF), out=b16(2, FF, 3 * D),
        hs=b16(2, per, nsub, 2 * D, SUB), kvs=b16(2, per, nsub, 4 * D, SUB),
        rst=f32(2, per, nsub, 2 * HEADS, SUB), dms=b16(per, nsub, 2 * D, SUB),
        mids=b16(per, nsub, 2 * D, SUB), hids=b16(per, nsub, 2 * FF, SUB), gps=f32(per, nsub, FF, SUB),
        stage=f32(2, per, nsub, SUB, D),
        zm=f32(segs, D, SUB), zk=f32(segs, D, SUB), zv=f32(segs, D, SUB),
        acc_c=f32(nsub + 1, group + 8, D), acc_n=f32(nsub + 1, D, 128), acc_g=f32(nsub + 1, D + 16, D),
        corr_c=f32(segs, group + 8, D), corr_n=f32(segs, D, 128), corr_g=f32(segs, D + 16, D),
        stats=f32(2, per, segs, 2 * group + 8, D), own_c=f32(2, per, segs, group, D), own_d=f32(per, segs, group, D),
        mt=b16(2, per, segs, D, 2 * D), vec_c=f32(2, 4, group, D),
        fwd_mat=b16(segs, D, 2 * D), fwd_add=f32(segs, D, 128), back_mat=b16(2, per, segs, D, 2 * D),
        key_mat=b16(segs, D, 2 * D), key_add=f32(segs, D, 128),
        val_mat=b16(segs, D, 2 * D), val_add=f32(segs, D, 128),
        d_outer=f32(2, FF, D), d_inner=f32(2, FF, D), d_kv=f32(2, 2 * D, D),
        s_du=f32(2, FF, 128), s_g=f32(2, D, 128), s_dz=f32(2, 2 * D, 128),
        vec=f32(2, 2, 8, D), gb=f32(2, total_rows, D), og=f32(total_rows, D),
        ar=f32(nar, len(digits), 4, group, D),
        dma_in=dma(2 * per + 4), w_send=dma(4), w_recv=dma(4),
        ar_send=dma(nar, len(digits), 3), ar_recv=dma(nar, len(digits), 3),
        o_local=dma(2, per), o_send=dma(2, per), o_recv=dma(2, per),
        g_send=dma(2, 2, len(digits), 7), g_recv=dma(2, 2, len(digits), 7),
    )
    for kind, size in enumerate(parts_rows):
        for digit, (_, radix) in enumerate(digits[:2]):
            size //= radix
            scratch["rb%d%d" % (kind, digit)] = f32(2 * radix - 1 if digit == 0 else radix - 1, size, D)
        if len(digits) > 2:
            scratch["wide%d" % kind] = f32(len(digits) - 2, 4, size, D)
    cfg = dict(names=list(scratch), places=places, segs=segs, micro=micro, nsub=nsub, D=D, FF=FF)

    def lined(piece):
        return jnp.transpose(piece, (1, 0, 2))

    anywhere = pl.BlockSpec(memory_space=pl.ANY)
    tiled = (micro, nsub, SUB, D)
    act, grd, gsum = pl.pallas_call(
        functools.partial(mega, cfg),
        out_shape=(
            jax.ShapeDtypeStruct(tiled, F32), jax.ShapeDtypeStruct(tiled, F32),
            jax.ShapeDtypeStruct((total_rows, D), F32),
        ),
        in_specs=[anywhere, anywhere, pl.BlockSpec(memory_space=pltpu.SMEM)] + [anywhere] * 4,
        out_specs=(anywhere, anywhere, anywhere),
        scratch_shapes=list(scratch.values()),
        compiler_params=pltpu.CompilerParams(
            collective_id=0, has_side_effects=True, vmem_limit_bytes=63 * 2**20
        ),
        name="layers",
    )(
        node_features.reshape(tiled), cotangent.reshape(tiled), lengths,
        attention_weight, inner_weight, outer_weight, lined(vectors),
    )
    scale = 1.0 / (micro * rows * places)
    held = [attention_weight, inner_weight, outer_weight, vectors]
    moments = [
        momentum_attention, variance_attention, momentum_inner, variance_inner,
        momentum_outer, variance_outer, momentum_vectors, variance_vectors,
    ]
    held[3] = lined(vectors)
    moments[6:] = [lined(momentum_vectors), lined(variance_vectors)]
    shapes = [jax.ShapeDtypeStruct(piece.shape, F32) for piece in held for _ in range(4)]
    results = pl.pallas_call(
        functools.partial(finishing, scale, D, FF, first),
        out_shape=tuple([jax.ShapeDtypeStruct(tiled, F32)] * 2 + shapes),
        in_specs=[pl.BlockSpec(memory_space=pltpu.HBM)] * 15,
        out_specs=tuple([pl.BlockSpec(memory_space=pltpu.HBM)] * 18),
        scratch_shapes=[f32(total_rows, D)] + [f32(*piece.shape) for piece in held + moments]
        + [f32(*shape.shape) for shape in shapes] + [f32(2, *tiled), dma(2, 2, micro), dma(13), dma(16)],
        compiler_params=pltpu.CompilerParams(vmem_limit_bytes=60 * 2**20),
        name="adamw",
    )(act, grd, gsum, *held, *moments)
    whole = (1, micro, rows, D)
    lines_back = tuple(lined(piece) for piece in results[14:])
    return (results[0].reshape(whole), results[1].reshape(whole)) + tuple(results[2:14]) + lines_back


def solution(mesh):
    first = P("section", None, None)
    attention = P("section", None, None, None)
    nodes = P(None, "pts", None)
    return jax.shard_map(
        per_device,
        mesh=mesh,
        in_specs=(nodes, nodes, P(), attention, first, first, first, attention, attention) + (first,) * 6,
        out_specs=(P("section", None, "pts", None),) * 2 + (attention,) * 4 + (first,) * 12,
        check_vma=False,
    )
```

```python
import functools
import math

import jax
import jax.numpy as jnp
from jax import lax
from jax.experimental import pallas as pl
from jax.experimental.pallas import tpu as pltpu
from jax.sharding import PartitionSpec as P

HEADS = 4
STEP = 1200
TOTAL_STEPS = 4000
EPS_NORM = 1e-05
SUB = 256
TILE = 1024

MESH = pl.DeviceIdType.MESH
HIGHEST = lax.Precision.HIGHEST
F32 = jnp.float32
BF16 = jnp.bfloat16


def plan():
    warm = 0.3 * TOTAL_STEPS
    top = 0.001
    start = top / 25.0
    low = start / 10000.0
    if STEP <= warm:
        return start + (top - start) * (1.0 - math.cos(math.pi * STEP / warm)) / 2.0
    return low + (top - low) * (1.0 + math.cos(math.pi * (STEP - warm) / (TOTAL_STEPS - warm))) / 2.0


def cat(parts, axis=0):
    return jnp.concatenate(parts, axis=axis)


def split(value):
    high = value.astype(BF16)
    return high, (value - high.astype(F32)).astype(BF16)


def pack3(weight):
    high, low = split(weight)
    return cat([high, high, low], 1)


def pack2(weight):
    return cat(list(split(weight)), 1)


def left3(pack):
    size = pack.shape[1] // 2
    return cat([pack[:, :size], pack], 1)


def right3(value):
    high, low = split(value)
    return cat([high, low, high])


def dot16(left, right):
    return jnp.dot(left, right, preferred_element_type=F32)


def outer16(left, right):
    full = lax.dot_general(left, right, (((1,), (1,)), ((), ())), preferred_element_type=F32)
    m, n = full.shape[0] // 2, full.shape[1] // 2
    return full[:m, :n] + full[m:, :n] + full[:m, n:]


def outer16_sums(left, right):
    ones = jnp.ones((16, left.shape[1]), BF16)
    full = lax.dot_general(cat([left, ones]), right, (((1,), (1,)), ((), ())), preferred_element_type=F32)
    m, n = left.shape[0] // 2, full.shape[1] // 2
    return cat([full[:m, :n] + full[m : 2 * m, :n] + full[:m, n:], full[2 * m :, :n] + full[2 * m :, n:]])


def mm_nt(left, right, precision=HIGHEST):
    return lax.dot_general(left, right, (((1,), (1,)), ((), ())), precision=precision, preferred_element_type=F32)


def wide(table, width):
    return cat([table] * (width // 128), 1)


def fold(value):
    total = value[:, :128]
    for at in range(128, value.shape[1], 128):
        total = total + value[:, at : at + 128]
    return total


def digits_of(places):
    found, stride = [], 1
    while stride < places:
        radix = 4 if (places // stride) % 4 == 0 else 2
        found.append((stride, radix))
        stride *= radix
    return found


def gradient_rows(D, FF, digits):
    unit = 8
    for _, radix in digits[:2]:
        unit *= radix
    early = -(-(2 * FF + 2 * D) // unit) * unit
    late = -(-(2 * D + 16) // unit) * unit
    first = dict(outer=0, inner=FF, q=2 * FF, o=2 * FF + D, k=early, v=early + D, vec=early + 2 * D)
    return first, (early, late)


def mega(cfg, x_hbm, cot_hbm, len_s, att_hbm, inn_hbm, out_hbm, vec_hbm, act_hbm, grd_hbm, gsum_hbm, *scratch):
    sm = dict(zip(cfg["names"], scratch))
    places, segs, micro, nsub = cfg["places"], cfg["segs"], cfg["micro"], cfg["nsub"]
    rows = nsub * SUB
    tokens = rows * places
    per = micro // 2
    D = cfg["D"]
    FF = cfg["FF"]
    group = D // HEADS
    digits = digits_of(places)
    c = lax.axis_index("section")
    place = lax.axis_index("pts")
    other = 1 - c
    edge = (place == 0) | (place == places - 1)

    stage = sm["stage"]

    dma_in = sm["dma_in"]
    watt, winn, wout, wvec = sm["watt"], sm["winn"], sm["wout"], sm["wvec"]

    def x_copy(bb):
        return pltpu.make_async_copy(x_hbm.at[c * per + bb], stage.at[0, bb], dma_in.at[bb])

    def cot_copy(bb):
        return pltpu.make_async_copy(cot_hbm.at[c * per + bb], stage.at[1, bb], dma_in.at[per + bb])

    weights = [(att_hbm.at[0], watt), (inn_hbm.at[0], winn), (out_hbm.at[0], wout), (vec_hbm, wvec)]

    def weight_copy(k):
        source, held = weights[k]
        return pltpu.make_async_copy(source, held.at[c], dma_in.at[2 * per + k])

    def weight_send(k):
        source, held = weights[k]
        return pltpu.make_async_remote_copy(
            src_ref=source, dst_ref=held.at[c], send_sem=sm["w_send"].at[k], recv_sem=sm["w_recv"].at[k],
            device_id={"section": other}, device_id_type=MESH,
        )

    def weight_arrival(k):
        source, held = weights[k]
        return pltpu.make_async_remote_copy(
            src_ref=source, dst_ref=held.at[other], send_sem=sm["w_send"].at[k], recv_sem=sm["w_recv"].at[k],
            device_id={"section": other}, device_id_type=MESH,
        )

    x_copy(0).start()
    for k in (0, 3, 1, 2):
        weight_copy(k).start()
    for bb in range(1, per):
        x_copy(bb).start()
    for bb in range(per):
        cot_copy(bb).start()

    def partner(digit, offset):
        stride, radix = digits[digit]
        mine = (place // stride) % radix
        theirs = (mine + offset) % radix
        return place + (theirs - mine) * stride

    def digit_at(digit, offset=0):
        stride, radix = digits[digit]
        return ((place // stride) % radix + offset) % radix

    barrier = pltpu.get_barrier_semaphore()
    greeted = 1
    pl.semaphore_signal(barrier, inc=1, device_id={"section": other}, device_id_type=MESH)
    for digit, (stride, radix) in enumerate(digits):
        for offset in range(1, radix):
            pl.semaphore_signal(barrier, inc=1, device_id={"pts": partner(digit, offset)}, device_id_type=MESH)
            greeted += 1

    for offset in range(1, digits[0][1]):
        pl.semaphore_signal(
            barrier, inc=1, device_id={"section": other, "pts": partner(0, offset)}, device_id_type=MESH
        )
        greeted += 1

    tab = sm["tab"]
    T_SLOT, T_END, T_ZI, T_KEEP = 0, nsub, 2 * nsub, 3 * nsub
    T_C, T_LO, T_HI, T_CS, T_ZK, T_LAST, T_CIDX, T_NLOC, T_CNT, T_LS, T_LE, T_OK = (
        4 * nsub + at * segs for at in range(12)
    )
    base = place * rows
    zero = jnp.int32(0)

    for bb in range(per):
        batch = c * per + bb
        lens = [len_s[batch, s] for s in range(segs)]
        ends, run = [], zero
        for s in range(segs):
            run = run + lens[s]
            ends.append(run)
        starts = [zero] + ends[:-1]
        big = zero
        for s in range(1, segs):
            big = big + jnp.where(starts[s] <= rows - 1, 1, 0)
        before = zero
        for s in range(segs):
            before = before + jnp.where(ends[s] <= tokens - rows, 1, 0)
        big = jnp.minimum(big, before)
        local_start = [jnp.clip(starts[s] - base, -1, rows) for s in range(segs)]
        local_end = [jnp.clip(ends[s] - base, 0, rows) for s in range(segs)]
        cells, valid = [zero], [zero]
        tab[bb, T_C] = zero
        tab[bb, T_OK] = zero
        for s in range(segs):
            tab[bb, T_LS + s] = local_start[s]
            tab[bb, T_LE + s] = local_end[s]
            slot = jnp.where(s == big, 0, jnp.where(s < big, s + 1, s))
            tab[bb, T_CS + s] = slot
            if s > 0:
                at = local_start[s]
                inside = jnp.maximum(at, 0)
                cell = jnp.minimum(inside // SUB, nsub - 1)
                low = inside - cell * SUB
                ok = jnp.where((at > 0) & (at < rows) & (low > 0), 1, 0)
                cells.append(cell)
                valid.append(ok)
                tab[bb, T_C + s] = cell
                tab[bb, T_OK + s] = ok
                tab[bb, T_LO + s] = jnp.where(ok == 1, low, SUB)
                tab[bb, T_HI + s] = jnp.where(ok == 1, jnp.minimum(local_end[s] - cell * SUB, SUB), 0)
                tab[bb, T_ZK + s] = ok * valid[s - 1] * jnp.where(cell == cells[s - 1], 1, 0)
        past = None
        for sub in range(nsub):
            row = sub * SUB
            first, final = zero, zero
            for s in range(segs - 1):
                first = first + jnp.where(local_end[s] <= row, 1, 0)
                final = final + jnp.where(local_end[s] <= row + SUB - 1, 1, 0)
            tab[bb, T_SLOT + sub] = tab[bb, T_CS + first]
            tab[bb, T_END + sub] = jnp.minimum(tab[bb, T_LE + first] - row, SUB)
            tab[bb, T_KEEP + sub] = zero if past is None else jnp.where(first == past, 1, 0)
            tab[bb, T_ZI + sub] = jnp.where(final == first, 0, final)
            past = first
        for j in range(segs):
            s = big if j == 0 else jnp.where(j - 1 < big, j - 1, j)
            low, high = tab[bb, T_LS + s], tab[bb, T_LE + s]
            cell = jnp.maximum(high - 1, 0) // SUB
            tab[bb, T_LAST + j] = jnp.where((high > 0) & (low < rows) & (cell * SUB >= low), cell, nsub)
            tab[bb, T_CIDX + j] = jnp.where(tab[bb, T_OK + s] == 1, s, 0)
            tab[bb, T_NLOC + j] = high - jnp.maximum(low, 0)
            tab[bb, T_CNT + j] = len_s[batch, s]

    lane_head = lax.broadcasted_iota(jnp.int32, (group, D), 1) // group
    block_mask = (
        lax.broadcasted_iota(jnp.int32, (D, D), 0) // group == lax.broadcasted_iota(jnp.int32, (D, D), 1) // group
    ).astype(F32)
    ones8 = jnp.ones((8, 128), F32)
    row8 = lax.broadcasted_iota(jnp.int32, (8, D), 0)

    def lanes():
        return lax.broadcasted_iota(jnp.int32, (1, SUB), 1)

    def compact(square):
        total = None
        for j in range(HEADS):
            piece = jnp.where(lane_head == j, square[group * j : group * (j + 1), :], 0.0)
            total = piece if total is None else total + piece
        return total

    def moment_rows(product):
        return cat([compact(product[:D]), product[D : D + 8]])

    def expand(packed):
        return cat([packed] * HEADS, 0) * block_mask

    def centred(matrix):
        grouped = matrix.reshape(matrix.shape[0] // group, group, matrix.shape[1])
        return (grouped - jnp.mean(grouped, axis=1, keepdims=True)).reshape(matrix.shape)

    for bb in range(per):
        sm["zm"][bb, 0] = jnp.zeros((D, SUB), F32)
    for name in ("zk", "zv", "corr_c", "corr_n", "corr_g"):
        sm[name][0] = jnp.zeros(sm[name].shape[1:], F32)
    for name in ("acc_c", "acc_n", "acc_g"):
        sm[name][nsub] = jnp.zeros(sm[name].shape[1:], F32)
    for name in ("d_outer", "d_inner", "d_kv", "s_du", "s_g", "s_dz"):
        sm[name][...] = jnp.zeros(sm[name].shape, F32)
    gb = sm["gb"]
    first, parts_rows = gradient_rows(D, FF, digits)
    R_Q, R_K, R_V, R_3, R_I, R_O, R_VEC = (first[name] for name in ("q", "k", "v", "o", "inner", "outer", "vec"))

    pl.semaphore_wait(barrier, greeted)
    for k in (0, 3, 1, 2):
        weight_send(k).start()

    tables = sm["tables"]

    def arrived(layer, k):
        @pl.when(c == layer)
        def _():
            weight_copy(k).wait()

        @pl.when(c != layer)
        def _():
            weight_arrival(k).wait_recv()

    def column(layer, row):
        return jnp.broadcast_to(wvec[layer, row], (128, D)).T

    def prepare_projections(layer):
        arrived(layer, 0)
        arrived(layer, 3)
        for row in (1, 2):
            tables[layer, row] = centred(column(layer, row))
        packed = sm["packed"]
        packed[layer, 0] = compact(1.0 + column(layer, 4))
        packed[layer, 1] = compact(column(layer, 5))
        packed[layer, 2] = compact(1.0 + column(layer, 6))
        sm["kvw"][layer] = pack2(cat([centred(watt[layer, 1].T), centred(watt[layer, 2].T)], 0))

    def prepare(layer):
        arrived(layer, 1)
        arrived(layer, 2)

        for at, row in ((0, 0), (3, 3), (4, 8), (5, 9), (6, 10)):
            tables[layer, at] = column(layer, row)
        query_t, output_t = watt[layer, 0].T, watt[layer, 3].T
        sm["wq_t"][layer] = pack3(query_t)
        sm["w3_t"][layer] = pack3(output_t)
        sm["wq_right"][layer] = right3(cat([query_t, tables[layer, 0]], 1))
        sm["w3_right"][layer] = right3(output_t)
        sm["kvw_back"][layer] = cat([pack2(watt[layer, 1]), pack2(watt[layer, 2])], 1)
        inner = winn[layer]
        sm["inn_t"][layer] = pack2(cat([inner[:, at : at + D].T for at in range(0, FF, D)], 0))
        sm["inn"][layer] = pack2(inner)
        outer = wout[layer]
        sm["out_t"][layer] = pack2(cat([outer[at : at + D, :].T for at in range(0, FF, D)], 1))
        sm["out"][layer] = pack2(outer)

    ar = sm["ar"]

    def ar_copy(k, digit, offset):
        spot = ar.at[k, digit, digit_at(digit)]
        return pltpu.make_async_remote_copy(
            src_ref=spot, dst_ref=spot, send_sem=sm["ar_send"].at[k, digit, offset - 1],
            recv_sem=sm["ar_recv"].at[k, digit, offset - 1],
            device_id={"pts": partner(digit, offset)}, device_id_type=MESH,
        )

    def ar_arrival(k, digit, offset):
        radix = digits[digit][1]
        spot = ar.at[k, digit, digit_at(digit, radix - offset)]
        return pltpu.make_async_remote_copy(
            src_ref=spot, dst_ref=spot, send_sem=sm["ar_send"].at[k, digit, offset - 1],
            recv_sem=sm["ar_recv"].at[k, digit, offset - 1],
            device_id={"pts": partner(digit, offset)}, device_id_type=MESH,
        )

    def ar_launch(k, digit, payload):
        ar[k, digit, digit_at(digit)] = payload
        for offset in range(1, digits[digit][1]):
            ar_copy(k, digit, offset).start()

    def ar_land(k, digit):
        radix = digits[digit][1]
        for offset in range(1, radix):
            ar_arrival(k, digit, offset).wait_recv()
        total = ar[k, digit, 0]
        for at in range(1, radix):
            total = total + ar[k, digit, at]
        return total

    def ar_step(k, digit):
        if digit < len(digits):
            ar_launch(k, digit, ar_land(k, digit - 1))

    def ar_finish(k):
        for digit in range(2, len(digits)):
            ar_step(k, digit)
        return ar_land(k, len(digits) - 1)

    def ar_drain(k):
        for digit in range(len(digits)):
            for offset in range(1, digits[digit][1]):
                ar_copy(k, digit, offset).wait_send()

    hs, kvs, rst, dms = sm["hs"], sm["kvs"], sm["rst"], sm["dms"]
    mids, hids, gps = sm["mids"], sm["hids"], sm["gps"]

    def three(pair, at=0, size=D):
        high = pair[at : at + size]
        return [high, pair[at + size : at + 2 * size], high]

    def joined(pairs):
        whole = pairs.astype(F32)
        return cat([whole[:D] + whole[D : 2 * D], whole[2 * D : 3 * D] + whole[3 * D :]])

    def load(ref, lead, subs):
        return cat([ref[(*lead, sub)] for sub in subs], 1)

    def save(ref, lead, subs, value):
        for at, sub in enumerate(subs):
            ref[(*lead, sub)] = value[:, SUB * at : SUB * (at + 1)]

    def part(value, at):
        return value[:, SUB * at : SUB * (at + 1)]

    def inside_of(bb, sub):
        return lanes() < tab[bb, T_END + sub]

    def keys_and_values(layer, bb, subs, pair):
        width = SUB * len(subs)
        bias = cat([wide(tables[layer, 1], width), wide(tables[layer, 2], width)], 0)
        field = dot16(left3(sm["kvw"][layer]), cat(three(pair))) + bias
        grouped = field.reshape(2 * HEADS, group, width)
        spread = jnp.mean(grouped * grouped, axis=1, keepdims=True)
        scale = lax.rsqrt(spread + EPS_NORM)
        normed = (grouped * scale).reshape(2 * D, width)
        save(rst, (layer, bb), subs, scale.reshape(2 * HEADS, width))
        k_high, k_low = split(normed[:D])
        v_high, v_low = split(normed[D:])
        keys, values = cat([k_high, k_low]), cat([v_high, v_low])
        save(kvs, (layer, bb), subs, cat([keys, values]))
        for at, sub in enumerate(subs):
            inside = inside_of(bb, sub)
            product = moment_rows(outer16_sums(part(keys, at), part(values, at) * inside.astype(BF16)))
            sums = fold(jnp.where(inside, part(normed, at)[:D], 0.0))
            keep = tab[bb, T_KEEP + sub] == 1
            past = jnp.maximum(sub - 1, 0)
            sm["acc_c"][sub] = product + jnp.where(keep, sm["acc_c"][past], 0.0)
            sm["acc_n"][sub] = sums + jnp.where(keep, sm["acc_n"][past], 0.0)

    def feed_forward(layer, bb, subs):
        width = SUB * len(subs)
        middles = []
        for sub in subs:
            slot = tab[bb, T_SLOT + sub]
            value = dot16(left3(sm["fwd_mat"][slot]), cat(three(hs[layer, bb, sub]))) + wide(sm["fwd_add"][slot], SUB)
            middles.append(jnp.where(inside_of(bb, sub), value, sm["zm"][bb, tab[bb, T_ZI + sub]]))
        middle = cat(middles, 1)
        m_high, m_low = split(middle)
        mid_pair = cat([m_high, m_low])
        u = dot16(left3(sm["inn_t"][layer]), cat(three(mid_pair)))
        u = u + cat([wide(tables[layer, 5], width), wide(tables[layer, 6], width)], 0)
        k0 = 0.7978845608
        square = u * u
        t = jnp.tanh(u * (k0 + (k0 * 0.044715) * square))
        half = 0.5 + 0.5 * t
        hidden = u * half
        slope = half + hidden * (1.0 - t) * (k0 + (3.0 * k0 * 0.044715) * square)
        h_high, h_low = split(hidden)
        hid_pair = cat([h_high, h_low])
        out = middle + dot16(left3(sm["out_t"][layer]), cat(three(hid_pair, 0, FF))) + wide(tables[layer, 4], width)
        return out, mid_pair, hid_pair, slope

    def feed_back(layer, bb, subs, upstream, mid_pair, hid_pair, slope):
        g_high, g_low = split(upstream)
        g_pair = cat([g_high, g_low])
        du = dot16(left3(sm["out"][layer]), cat(three(g_pair))) * slope
        u_high, u_low = split(du)
        u_pair = cat([u_high, u_low])
        d_mid = upstream + dot16(left3(sm["inn"][layer]), cat(three(u_pair, 0, FF)))
        q_high, q_low = split(d_mid)
        q_pair = cat([q_high, q_low])
        save(dms, (bb,), subs, q_pair)
        for at, sub in enumerate(subs):
            q_inside = part(q_pair, at) * inside_of(bb, sub).astype(BF16)
            product = outer16_sums(hs[layer, bb, sub], q_inside)
            keep = tab[bb, T_KEEP + sub] == 1
            past = jnp.maximum(sub - 1, 0)
            sm["acc_g"][sub] = product + jnp.where(keep, sm["acc_g"][past], 0.0)
        sm["d_outer"][layer] += outer16(hid_pair, g_pair)
        sm["d_inner"][layer] += outer16(u_pair, mid_pair)
        sm["s_du"][layer] += fold(du)
        sm["s_g"][layer] += fold(upstream)

    def norm_back(layer, bb, subs):
        width = SUB * len(subs)
        pairs = load(kvs, (layer, bb), subs)
        normed = joined(pairs)
        e_ks, e_vs = [], []
        for at, sub in enumerate(subs):
            slot, zi, inside = tab[bb, T_SLOT + sub], tab[bb, T_ZI + sub], inside_of(bb, sub)
            own = part(pairs, at)
            e_k = dot16(left3(sm["key_mat"][slot]), cat(three(own, 2 * D))) + wide(sm["key_add"][slot], SUB)
            e_v = dot16(left3(sm["val_mat"][slot]), cat(three(own))) + wide(sm["val_add"][slot], SUB)
            e_ks.append(jnp.where(inside, e_k, sm["zk"][zi]))
            e_vs.append(jnp.where(inside, e_v, sm["zv"][zi]))
        e = cat([cat(e_ks, 1), cat(e_vs, 1)])
        shape = (2 * HEADS, group, width)
        e3, n3 = e.reshape(shape), normed.reshape(shape)
        scale = load(rst, (layer, bb), subs).reshape(2 * HEADS, 1, width)
        along = jnp.mean(e3 * n3, axis=1, keepdims=True)
        dz = ((e3 - n3 * along) * scale).reshape(2 * D, width)
        z_high, z_low = split(dz)
        z_pair = cat([z_high, z_low])
        sm["d_kv"][layer] += outer16(z_pair, load(hs, (layer, bb), subs))
        sm["s_dz"][layer] += fold(dz)
        return z_pair

    def input_back(layer, bb, subs, z_pair):
        z_high, z_low = z_pair[: 2 * D], z_pair[2 * D :]
        through = [z_high[:D], z_low[:D], z_high[:D], z_high[D:], z_low[D:], z_high[D:]]
        backs = []
        back = sm["kvw_back"][layer]
        for at, sub in enumerate(subs):
            slot, zi = tab[bb, T_SLOT + sub], tab[bb, T_ZI + sub]
            left = cat([left3(sm["back_mat"][layer, bb, slot]), left3(back[:, : 2 * D]), left3(back[:, 2 * D :])], 1)
            right = three(dms[bb, sub] * inside_of(bb, sub).astype(BF16)) + [part(one, at) for one in through]
            backs.append(dot16(left, cat(right)) + sm["zm"][bb, zi])
        return cat(backs, 1)

    count = TILE // SUB

    def over(low, high, stage):
        def body(i, carry):
            stage([i * count + at for at in range(count)])
            return carry

        lax.fori_loop(low, high, body, 0)

    steps = nsub // count

    def loop(stage, between):
        over(0, (steps + 1) // 2, stage)
        between()
        over((steps + 1) // 2, steps, stage)

    def span(bb, s):
        at = lanes()
        return (at >= tab[bb, T_LO + s]) & (at < tab[bb, T_HI + s])

    def fill(ref, bb, s, inside, value):
        before = jnp.where(tab[bb, T_ZK + s] == 1, ref[s - 1], 0.0)
        ref[s] = jnp.where(inside, value, before)

    def corrections_mid(layer, bb):
        @pl.when(edge)
        def _():
            for s in range(1, segs):
                pair = hs[layer, bb, tab[bb, T_C + s]]
                slot = tab[bb, T_CS + s]
                value = dot16(left3(sm["fwd_mat"][slot]), cat(three(pair))) + wide(sm["fwd_add"][slot], SUB)
                fill(sm["zm"].at[bb], bb, s, span(bb, s), value)

    def corrections_back(layer, bb):
        @pl.when(edge)
        def _():
            for s in range(1, segs):
                cell, slot, inside = tab[bb, T_C + s], tab[bb, T_CS + s], span(bb, s)
                pairs = kvs[layer, bb, cell]
                e_k = dot16(left3(sm["key_mat"][slot]), cat(three(pairs, 2 * D))) + wide(sm["key_add"][slot], SUB)
                e_v = dot16(left3(sm["val_mat"][slot]), cat(three(pairs))) + wide(sm["val_add"][slot], SUB)
                e_d = dot16(left3(sm["back_mat"][layer, bb, slot]), cat(three(dms[bb, cell])))
                fill(sm["zk"], bb, s, inside, e_k)
                fill(sm["zv"], bb, s, inside, e_v)
                fill(sm["zm"].at[bb], bb, s, inside, e_d)

    def corrections_moments(layer, bb):
        @pl.when(edge)
        def _():
            for s in range(1, segs):
                cell, inside = tab[bb, T_C + s], span(bb, s)
                pairs = kvs[layer, bb, cell]
                product = outer16_sums(pairs[: 2 * D], pairs[2 * D :] * inside.astype(BF16))
                sm["corr_c"][s] = moment_rows(product)
                keys = pairs[: 2 * D].astype(F32)
                sm["corr_n"][s] = fold(jnp.where(inside, keys[:D] + keys[D:], 0.0))

    def corrections_grams(layer, bb):
        @pl.when(edge)
        def _():
            for s in range(1, segs):
                cell, inside = tab[bb, T_C + s], span(bb, s)
                q_pair = dms[bb, cell] * inside.astype(BF16)
                sm["corr_g"][s] = outer16_sums(hs[layer, bb, cell], q_pair)

    stats, own_c, own_d, vec, vec_c = sm["stats"], sm["own_c"], sm["own_d"], sm["vec"], sm["vec_c"]

    def total_of(name, bb, j):
        return sm["acc_" + name][tab[bb, T_LAST + j]] + sm["corr_" + name][tab[bb, T_CIDX + j]]

    def shifts(layer):
        return 1.0 + wvec[layer, 4], wvec[layer, 5], 1.0 + wvec[layer, 6], wvec[layer, 7]

    def moments_of(layer, bb, j):
        key_gain, key_shift, value_gain, value_shift = shifts(layer)
        gain_c, shift_c = sm["packed"][layer, 0], sm["packed"][layer, 1]
        rows_c = total_of("c", bb, j)
        product, values = rows_c[:group], rows_c[group : group + 1]
        keys = compact(jnp.broadcast_to(jnp.sum(total_of("n", bb, j), axis=1, keepdims=True), (D, 128)))
        stats[layer, bb, j] = cat([product, keys, rows_c[group:]])
        local = tab[bb, T_NLOC + j].astype(F32)
        from_values = values * value_gain + local * value_shift
        return gain_c * (product * value_gain + keys * value_shift) + shift_c * from_values

    def mixing_of(layer, bb, slots, moments):
        packs = []
        for j, moment in zip(slots, moments):
            pack = pack2((expand(moment) / tab[bb, T_CNT + j].astype(F32)).T)
            sm["mt"][layer, bb, j] = pack
            packs.append(left3(pack))
        mixed = dot16(cat(packs), sm["wq_right"][layer])
        rights = [right3(mixed[D * at : D * (at + 1)]) for at in range(len(slots))]
        through = dot16(sm["w3_t"][layer], cat(rights, 1))
        eye = (
            lax.broadcasted_iota(jnp.int32, (D, D), 0) == lax.broadcasted_iota(jnp.int32, (D, D), 1)
        ).astype(F32)
        for at, j in enumerate(slots):
            forward = through[:, 2 * D * at : 2 * D * at + D] + eye
            sm["fwd_mat"][j] = pack2(forward)
            sm["fwd_add"][j] = through[:, 2 * D * at + D : 2 * D * (at + 1)] + tables[layer, 3]
            sm["back_mat"][layer, bb, j] = pack2(forward.T)

    def grams_of(layer, bb, slots):
        grams = [total_of("g", bb, j) for j in slots]
        tall = D + 16
        onto = dot16(cat([pack3(gram) for gram in grams]), sm["w3_right"][layer])
        ontos = [onto[tall * at : tall * (at + 1)] for at in range(len(slots))]
        rights = [right3(cat([one[:D], gram[:D]], 1)) for one, gram in zip(ontos, grams)]
        both = dot16(sm["wq_t"][layer], cat(rights, 1))
        query_bias = tables[layer, 0]
        d_moments, throughs = [], []
        for at, (one, gram) in enumerate(zip(ontos, grams)):
            d_moments.append(compact(both[:, 2 * D * at : 2 * D * at + D] + query_bias * one[D : D + 1]))
            throughs.append(both[:, 2 * D * at + D : 2 * D * (at + 1)] + query_bias * gram[D : D + 1])
        return d_moments, ontos, throughs, grams

    def projections_of(layer, bb, slots, ontos, throughs, grams):
        mts = [sm["mt"][layer, bb, j] for j in slots]
        right = [part for mt in mts for part in (mt[:, :D], mt[:, D:], mt[:, :D])]
        d_query = dot16(cat([pack3(one) for one in ontos], 1), cat(right))
        gb[layer, R_Q : R_Q + D] += d_query[:D]
        gb[layer, R_3 : R_3 + D] += dot16(cat([left3(mt) for mt in mts], 1), cat([right3(through) for through in throughs]))
        vec[layer, 0] += d_query[D : D + 8]
        sums = grams[0][D : D + 8]
        for gram in grams[1:]:
            sums = sums + gram[D : D + 8]
        vec[layer, 1] += sums

    def back_of(layer, bb, slots, d_moments):
        key_gain, key_shift, value_gain, value_shift = shifts(layer)
        gain_c, shift_c, value_gain_c = (sm["packed"][layer, at] for at in range(3))

        def across(packed):
            return jnp.broadcast_to(jnp.sum(expand(centred(packed)), axis=1, keepdims=True), (D, 128))

        for j, d_moment in zip(slots, d_moments):
            d = d_moment / tab[bb, T_CNT + j].astype(F32)
            d_t = compact(expand(d).T)
            sm["key_mat"][j] = pack2(expand(centred(gain_c * d * value_gain)))
            sm["key_add"][j] = across(gain_c * d * value_shift)
            sm["val_mat"][j] = pack2(expand(centred(value_gain_c * d_t * key_gain)))
            sm["val_add"][j] = across(value_gain_c * d_t * key_shift)
            held = stats[layer, bb, j]
            product, keys, values = held[:group], held[group : 2 * group], held[2 * group : 2 * group + 1]
            local = tab[bb, T_NLOC + j].astype(F32)
            vec_c[layer, 0] += d * (product * value_gain + keys * value_shift)
            vec_c[layer, 1] += d * (values * value_gain + local * value_shift)
            vec_c[layer, 2] += d * (gain_c * product + shift_c * values)
            vec_c[layer, 3] += d * (gain_c * keys + shift_c * local)

    small = list(range(1, segs))

    def key_of(stage, bb):
        return stage * per + bb

    def moments_out(layer, bb, k):
        corrections_moments(layer, bb)
        ar_launch(k, 0, moments_of(layer, bb, 0))

        @pl.when(edge)
        def _():
            for j in small:
                own_c[layer, bb, j] = moments_of(layer, bb, j)

    def mixing_in(layer, bb, k):
        @pl.when(edge)
        def _():
            mixing_of(layer, bb, small, [own_c[layer, bb, j] for j in small])

        mixing_of(layer, bb, [0], [ar_finish(k)])
        corrections_mid(layer, bb)

    def grams_out(layer, bb, k):
        corrections_grams(layer, bb)
        d_moments, *rest = grams_of(layer, bb, [0])
        ar_launch(k, 0, d_moments[0])
        projections_of(layer, bb, [0], *rest)

        @pl.when(edge)
        def _():
            d_moments, *rest = grams_of(layer, bb, small)
            for j, d_moment in zip(small, d_moments):
                own_d[bb, j] = d_moment
            projections_of(layer, bb, small, *rest)

    def grams_in(layer, bb, k):
        @pl.when(edge)
        def _():
            back_of(layer, bb, small, [own_d[bb, j] for j in small])

        back_of(layer, bb, [0], [ar_finish(k)])
        corrections_back(layer, bb)

    vec[...] = jnp.zeros(vec.shape, F32)
    vec_c[...] = jnp.zeros(vec_c.shape, F32)

    targets = (act_hbm, grd_hbm)

    def kept(kind, layer, bb):
        return pltpu.make_async_copy(
            stage.at[layer, bb], targets[kind].at[c * per + bb], sm["o_local"].at[kind, bb]
        )

    def sent(kind, layer, bb):
        return pltpu.make_async_remote_copy(
            src_ref=stage.at[layer, bb], dst_ref=targets[kind].at[c * per + bb], send_sem=sm["o_send"].at[kind, bb],
            recv_sem=sm["o_recv"].at[kind, bb], device_id={"section": other}, device_id_type=MESH,
        )

    def came(kind, layer, bb):
        return pltpu.make_async_remote_copy(
            src_ref=stage.at[layer, bb], dst_ref=targets[kind].at[other * per + bb], send_sem=sm["o_send"].at[kind, bb],
            recv_sem=sm["o_recv"].at[kind, bb], device_id={"section": other}, device_id_type=MESH,
        )

    def ship(kind, layer, bb):
        @pl.when(c == layer)
        def _():
            kept(kind, layer, bb).start()

        @pl.when(c != layer)
        def _():
            sent(kind, layer, bb).start()

    def shipped(kind, layer, bb):
        @pl.when(c == layer)
        def _():
            kept(kind, layer, bb).wait()

        @pl.when(c != layer)
        def _():
            sent(kind, layer, bb).wait_send()

    def load_t(layer, bb, subs):
        return cat([stage[layer, bb, sub].T for sub in subs], 1)

    def save_t(layer, bb, subs, value):
        for at, sub in enumerate(subs):
            stage[layer, bb, sub] = part(value, at).T

    def start_stage(bb, subs):
        high, low = split(load_t(0, bb, subs))
        pair = cat([high, low])
        save(hs, (0, bb), subs, pair)
        keys_and_values(0, bb, subs, pair)

    def first_stage(bb, subs):
        out, mid_pair, hid_pair, slope = feed_forward(0, bb, subs)
        save(mids, (bb,), subs, mid_pair)
        save(hids, (bb,), subs, hid_pair)
        save(gps, (bb,), subs, slope)
        save_t(0, bb, subs, out)
        high, low = split(out)
        pair = cat([high, low])
        save(hs, (1, bb), subs, pair)
        keys_and_values(1, bb, subs, pair)

    def second_stage(bb, subs):
        out, mid_pair, hid_pair, slope = feed_forward(1, bb, subs)
        upstream = load_t(1, bb, subs)
        save_t(1, bb, subs, out)
        feed_back(1, bb, subs, upstream, mid_pair, hid_pair, slope)

    def third_stage(bb, subs):
        upstream = input_back(1, bb, subs, norm_back(1, bb, subs))
        save_t(1, bb, subs, upstream)
        held = [load(ref, (bb,), subs) for ref in (mids, hids, gps)]
        feed_back(0, bb, subs, upstream, *held)

    def fifth_stage(bb, subs):
        save(kvs, (0, bb), subs, norm_back(0, bb, subs))

    def sixth_stage(bb, subs):
        save_t(0, bb, subs, input_back(0, bb, subs, load(kvs, (0, bb), subs)))

    og = sm["og"]
    summed, widened = digits[:2], digits[2:]
    sizes = []
    for kind in range(2):
        sizes.append([parts_rows[kind]])
        for _, radix in summed:
            sizes[-1].append(sizes[-1][-1] // radix)
    g_send, g_recv = sm["g_send"], sm["g_recv"]

    def early_rows(layer):
        gb[layer, R_O : R_O + FF] = sm["d_outer"][layer]
        d_inner = sm["d_inner"][layer]
        for at in range(0, FF, D):
            gb[layer, R_I + at : R_I + at + D] = d_inner[at : at + D].T

    def late_rows(layer):
        d_kv = sm["d_kv"][layer]
        gb[layer, R_K : R_K + D] = d_kv[:D].T
        gb[layer, R_V : R_V + D] = d_kv[D:].T
        s_dz = mm_nt(ones8, sm["s_dz"][layer])
        s_du = mm_nt(ones8, sm["s_du"][layer])
        s_g = mm_nt(ones8, sm["s_g"][layer])
        lines = [vec[layer, 0], s_dz[:, :D], s_dz[:, D:], vec[layer, 1]]
        lines += [mm_nt(ones8, expand(vec_c[layer, at])) for at in (0, 1)]
        lines += [jnp.sum(vec_c[layer, at], axis=0, keepdims=True) for at in (2, 3)]
        lines += [s_g, s_du[:, :D], s_du[:, D:]]
        block = jnp.zeros((16, D), F32)
        row16 = lax.broadcasted_iota(jnp.int32, (16, D), 0)
        for at, line in enumerate(lines):
            block = jnp.where(row16 == at, line[0:1], block)
        gb[layer, R_VEC : R_VEC + 16] = block

    def block_of(kind, depth, at=None):
        low = 0 if kind == 0 else parts_rows[0]
        for digit in range(depth):
            offset = at if (at is not None and digit == depth - 1) else 0
            low = low + digit_at(digit, offset) * sizes[kind][digit + 1]
        return pl.ds(low if depth == 0 else pl.multiple_of(low, 8), sizes[kind][depth])

    def landing(kind, digit):
        return sm["rb%d%d" % (kind, digit)]

    def scatter_first(layer, kind, offset, far):
        radix = summed[0][1]
        slot = radix - 1 + offset if far else offset - 1
        target = {"section": other, "pts": partner(0, offset)} if far else {"pts": partner(0, offset)}
        return pltpu.make_async_remote_copy(
            src_ref=gb.at[layer, block_of(kind, 1, offset)], dst_ref=landing(kind, 0).at[slot],
            send_sem=g_send.at[kind, 0, 0, slot], recv_sem=g_recv.at[kind, 0, 0, slot],
            device_id=target, device_id_type=MESH,
        )

    def scatter_next(layer, kind, digit, offset):
        return pltpu.make_async_remote_copy(
            src_ref=gb.at[layer, block_of(kind, digit + 1, offset)], dst_ref=landing(kind, digit).at[offset - 1],
            send_sem=g_send.at[kind, 0, digit, offset - 1], recv_sem=g_recv.at[kind, 0, digit, offset - 1],
            device_id={"pts": partner(digit, offset)}, device_id_type=MESH,
        )

    def gather(kind, digit, offset, at):
        spot = og.at[block_of(kind, digit + 1, at)]
        return pltpu.make_async_remote_copy(
            src_ref=spot, dst_ref=spot,
            send_sem=g_send.at[kind, 1, digit, offset - 1], recv_sem=g_recv.at[kind, 1, digit, offset - 1],
            device_id={"pts": partner(digit, offset)}, device_id_type=MESH,
        )

    def exchange(kind, at, offset, back=0):
        digit = len(summed) + at
        spot = sm["wide%d" % kind].at[at, digit_at(digit, back)]
        return pltpu.make_async_remote_copy(
            src_ref=spot, dst_ref=spot,
            send_sem=g_send.at[kind, 0, digit, offset - 1], recv_sem=g_recv.at[kind, 0, digit, offset - 1],
            device_id={"pts": partner(digit, offset)}, device_id_type=MESH,
        )

    def gradient_step(layer, kind, step):
        last = len(summed)
        if step == 0:
            @pl.when(c == layer)
            def _():
                for offset in range(1, summed[0][1]):
                    scatter_first(layer, kind, offset, False).start()

            @pl.when(c != layer)
            def _():
                for offset in range(summed[0][1]):
                    scatter_first(layer, kind, offset, True).start()

        elif step <= last:
            digit = step - 1
            radix = summed[digit][1]

            @pl.when(c == layer)
            def _():
                total = gb[layer, block_of(kind, digit + 1)]
                for offset in range(1, radix):
                    if digit == 0:
                        scatter_first(layer, kind, offset, False).wait_recv()
                    else:
                        scatter_next(layer, kind, digit, offset).wait_recv()
                    total = total + landing(kind, digit)[offset - 1]
                if digit == 0:
                    for offset in range(radix):
                        scatter_first(layer, kind, offset, True).wait_recv()
                        total = total + landing(kind, 0)[radix - 1 + offset]
                if step < last:
                    gb[layer, block_of(kind, digit + 1)] = total
                    for offset in range(1, summed[step][1]):
                        scatter_next(layer, kind, step, offset).start()
                else:
                    for at, (_, wide_radix) in enumerate(widened):
                        digit_now = last + at
                        sm["wide%d" % kind][at, digit_at(digit_now)] = total
                        for offset in range(1, wide_radix):
                            exchange(kind, at, offset).start()
                        for offset in range(1, wide_radix):
                            exchange(kind, at, offset, wide_radix - offset).wait_recv()
                        total = sm["wide%d" % kind][at, 0]
                        for other_at in range(1, wide_radix):
                            total = total + sm["wide%d" % kind][at, other_at]
                    og[block_of(kind, last)] = total
                    for offset in range(1, radix):
                        gather(kind, digit, offset, 0).start()

        elif step <= 2 * last:
            digit = 2 * last - step

            @pl.when(c == layer)
            def _():
                radix = summed[digit][1]
                for offset in range(1, radix):
                    gather(kind, digit, offset, radix - offset).wait_recv()
                if digit > 0:
                    for offset in range(1, summed[digit - 1][1]):
                        gather(kind, digit - 1, offset, 0).start()

    def drain_gradients():
        for layer in range(2):
            @pl.when(c == layer)
            def _():
                for kind in range(2):
                    for offset in range(1, summed[0][1]):
                        scatter_first(layer, kind, offset, False).wait_send()
                    for digit in range(1, len(summed)):
                        for offset in range(1, summed[digit][1]):
                            scatter_next(layer, kind, digit, offset).wait_send()
                    for at, (_, wide_radix) in enumerate(widened):
                        for offset in range(1, wide_radix):
                            exchange(kind, at, offset).wait_send()
                    for digit in range(len(summed)):
                        for offset in range(1, summed[digit][1]):
                            gather(kind, digit, offset, 0).wait_send()

            @pl.when(c != layer)
            def _():
                for kind in range(2):
                    for offset in range(summed[0][1]):
                        scatter_first(layer, kind, offset, True).wait_send()

    EARLY, LATE = 0, 1

    def together(*actions):
        def run():
            for action in actions:
                action()

        return run

    def grad(layer, kind, step):
        return functools.partial(gradient_step, layer, kind, step)

    prepare_projections(0)
    for bb in range(per):
        x_copy(bb).wait()
        loop(functools.partial(start_stage, bb), lambda bb=bb: ar_step(key_of(0, bb - 1), 1) if bb > 0 else None)
        moments_out(0, bb, key_of(0, bb))
        if bb == 0:
            prepare(0)
    prepare_projections(1)
    prepare(1)
    gb[...] = jnp.zeros(gb.shape, F32)
    ar_step(key_of(0, per - 1), 1)

    def in_flight(stage, bb):
        if bb > 0:
            return lambda: ar_step(key_of(stage, bb - 1), 1)
        return lambda: None

    def late(stage):
        ar_step(key_of(stage, per - 1), 1)

    for bb in range(per):
        mixing_in(0, bb, key_of(0, bb))
        loop(functools.partial(first_stage, bb), in_flight(1, bb))
        ship(0, 0, bb)
        moments_out(1, bb, key_of(1, bb))
    for bb in range(per):
        cot_copy(bb).wait()
        mixing_in(1, bb, key_of(1, bb))
        loop(functools.partial(second_stage, bb), in_flight(2, bb) if bb > 0 else lambda: late(1))
        ship(0, 1, bb)
        grams_out(1, bb, key_of(2, bb))
    early_rows(1)
    gradient_step(1, EARLY, 0)
    for bb in range(per):
        grams_in(1, bb, key_of(2, bb))
        shipped(0, 1, bb)
        beside = together(in_flight(3, bb), grad(1, EARLY, 2)) if bb > 0 else together(functools.partial(late, 2), grad(1, EARLY, 1))
        loop(functools.partial(third_stage, bb), beside)
        ship(1, 1, bb)
        grams_out(0, bb, key_of(3, bb))
    early_rows(0)
    late_rows(1)
    gradient_step(0, EARLY, 0)
    gradient_step(1, LATE, 0)
    gradient_step(1, EARLY, 3)
    for bb in range(per):
        grams_in(0, bb, key_of(3, bb))
        shipped(0, 0, bb)
        if bb == 0:
            beside = together(functools.partial(late, 3), grad(0, EARLY, 1), grad(1, LATE, 1), grad(1, EARLY, 4))
        elif bb == 1:
            beside = together(grad(0, EARLY, 2), grad(1, LATE, 2))
        else:
            beside = lambda: None
        loop(functools.partial(fifth_stage, bb), beside)
    late_rows(0)
    gradient_step(0, LATE, 0)
    gradient_step(0, EARLY, 3)
    gradient_step(1, LATE, 3)
    for bb in range(per):
        loop(functools.partial(sixth_stage, bb), grad(0, LATE, 2) if bb == 1 else lambda: None)
        ship(1, 0, bb)
        if bb == 0:
            gradient_step(0, LATE, 1)
            gradient_step(0, EARLY, 4)
            gradient_step(1, LATE, 4)
    gradient_step(0, LATE, 3)
    gradient_step(0, LATE, 4)

    out_copy = pltpu.make_async_copy(og, gsum_hbm, dma_in.at[0])
    out_copy.start()

    drain_gradients()
    for k in range(4):
        weight_send(k).wait_send()
    for k in range(4 * per):
        ar_drain(k)
    for bb in range(per):
        for layer in range(2):
            shipped(1, layer, bb)
        for layer in range(2):
            @pl.when(c == layer)
            def _():
                came(0, layer, bb).wait_recv()
                came(1, layer, bb).wait_recv()
    out_copy.wait()


def finishing(scale, D, FF, first, act, grd, gsum_hbm, *refs):
    sources, results = refs[:12], refs[12:30]
    gsum, held, made, through, sem_large, sem_in, sem_out = refs[30], refs[31:43], refs[43:59], *refs[59:]
    large, onward = [], []
    for kind, (source, target) in enumerate(((act, results[0]), (grd, results[1]))):
        for part in range(source.shape[0]):
            spot = through.at[kind, part]
            large.append(pltpu.make_async_copy(source.at[part], spot, sem_large.at[0, kind, part]))
            onward.append(pltpu.make_async_copy(spot, target.at[part], sem_large.at[1, kind, part]))
    loads = [pltpu.make_async_copy(gsum_hbm, gsum, sem_in.at[12])]
    loads += [pltpu.make_async_copy(sources[at], held[at], sem_in.at[at]) for at in range(12)]
    for copy in loads:
        copy.start()
    for copy in large:
        copy.start()
    rate = plan()

    def step(weight, gradient, momentum, variance):
        average = gradient * scale
        new_momentum = 0.9 * momentum + 0.1 * average
        new_variance = 0.999 * variance + 0.001 * average * average
        mean = new_momentum / (1.0 - 0.9**STEP)
        square = new_variance / (1.0 - 0.999**STEP)
        updated = weight - rate * (mean / (jnp.sqrt(square) + 1e-08) + 0.01 * weight)
        return gradient, new_momentum, new_variance, updated

    parts = [first[name] for name in ("q", "k", "v", "o")]
    inner, outer, late = first["inner"], first["outer"], first["vec"]
    places = [
        [((0, at), slice(low, low + D)) for at, low in enumerate(parts)],
        [((0, slice(None), slice(at, at + D)), slice(inner + at, inner + at + D)) for at in range(0, FF, D)],
        [((0,), slice(outer, outer + FF))],
        [((line,), slice(late + line, late + line + 1)) for line in range(held[3].shape[0])],
    ]
    for copy, after in zip(large, onward):
        copy.wait()
        after.start()
    loads[0].wait()
    stores = []
    for kind in range(4):
        for at in (kind, 4 + 2 * kind, 5 + 2 * kind):
            loads[1 + at].wait()
        weight, momentum, variance = held[kind], held[4 + 2 * kind], held[5 + 2 * kind]
        for index, lines in places[kind]:
            values = step(weight[index], gsum[lines], momentum[index], variance[index])
            for ref, value in zip(made[4 * kind : 4 * kind + 4], values):
                ref[index] = value
        for at in range(4 * kind, 4 * kind + 4):
            stores.append(pltpu.make_async_copy(made[at], results[2 + at], sem_out.at[at]))
            stores[-1].start()
    for copy in onward + stores:
        copy.wait()


def per_device(
    node_features, cotangent, lengths, attention_weight, inner_weight, outer_weight, vectors,
    momentum_attention, variance_attention, momentum_inner, variance_inner,
    momentum_outer, variance_outer, momentum_vectors, variance_vectors,
):
    places = lax.axis_size("pts")
    micro, rows, D = node_features.shape
    FF = inner_weight.shape[-1]
    segs = lengths.shape[1]
    lines = vectors.shape[1]
    nsub = rows // SUB
    per = micro // 2
    digits = digits_of(places)
    group = D // HEADS
    first, parts_rows = gradient_rows(D, FF, digits)
    total_rows = sum(parts_rows)
    nar = 4 * per

    def f32(*shape):
        return pltpu.VMEM(shape, F32)

    def b16(*shape):
        return pltpu.VMEM(shape, BF16)

    def dma(*shape):
        return pltpu.SemaphoreType.DMA(shape)

    scratch = dict(
        watt=f32(2, 4, D, D), winn=f32(2, D, FF), wout=f32(2, FF, D), wvec=f32(2, lines, 1, D),
        tab=pltpu.SMEM((per, 4 * nsub + 12 * segs), jnp.int32),
        tables=f32(2, 7, D, 128), packed=f32(2, 3, group, D),
        wq_t=b16(2, D, 3 * D), w3_t=b16(2, D, 3 * D), wq_right=b16(2, 3 * D, 2 * D), w3_right=b16(2, 3 * D, D),
        kvw=b16(2, 2 * D, 2 * D), kvw_back=b16(2, D, 4 * D),
        inn_t=b16(2, FF, 2 * D), inn=b16(2, D, 2 * FF), out_t=b16(2, D, 2 * FF), out=b16(2, FF, 2 * D),
        hs=b16(2, per, nsub, 2 * D, SUB), kvs=b16(2, per, nsub, 4 * D, SUB),
        rst=f32(2, per, nsub, 2 * HEADS, SUB), dms=b16(per, nsub, 2 * D, SUB),
        mids=b16(per, nsub, 2 * D, SUB), hids=b16(per, nsub, 2 * FF, SUB), gps=f32(per, nsub, FF, SUB),
                stage=f32(2, per, nsub, SUB, D),
        zm=f32(per, segs, D, SUB), zk=f32(segs, D, SUB), zv=f32(segs, D, SUB),
        acc_c=f32(nsub + 1, group + 8, D), acc_n=f32(nsub + 1, D, 128), acc_g=f32(nsub + 1, D + 16, D),
        corr_c=f32(segs, group + 8, D), corr_n=f32(segs, D, 128), corr_g=f32(segs, D + 16, D),
        stats=f32(2, per, segs, 2 * group + 8, D), own_c=f32(2, per, segs, group, D), own_d=f32(per, segs, group, D),
        mt=b16(2, per, segs, D, 2 * D), vec_c=f32(2, 4, group, D),
        fwd_mat=b16(segs, D, 2 * D), fwd_add=f32(segs, D, 128), back_mat=b16(2, per, segs, D, 2 * D),
        key_mat=b16(segs, D, 2 * D), key_add=f32(segs, D, 128),
        val_mat=b16(segs, D, 2 * D), val_add=f32(segs, D, 128),
        d_outer=f32(2, FF, D), d_inner=f32(2, FF, D), d_kv=f32(2, 2 * D, D),
        s_du=f32(2, FF, 128), s_g=f32(2, D, 128), s_dz=f32(2, 2 * D, 128),
        vec=f32(2, 2, 8, D), gb=f32(2, total_rows, D), og=f32(total_rows, D),
        ar=f32(nar, len(digits), 4, group, D),
        dma_in=dma(2 * per + 4), w_send=dma(4), w_recv=dma(4),
        ar_send=dma(nar, len(digits), 3), ar_recv=dma(nar, len(digits), 3),
        o_local=dma(2, per), o_send=dma(2, per), o_recv=dma(2, per),
        g_send=dma(2, 2, len(digits), 7), g_recv=dma(2, 2, len(digits), 7),
    )
    for kind, size in enumerate(parts_rows):
        for digit, (_, radix) in enumerate(digits[:2]):
            size //= radix
            scratch["rb%d%d" % (kind, digit)] = f32(2 * radix - 1 if digit == 0 else radix - 1, size, D)
        if len(digits) > 2:
            scratch["wide%d" % kind] = f32(len(digits) - 2, 4, size, D)
    cfg = dict(names=list(scratch), places=places, segs=segs, micro=micro, nsub=nsub, D=D, FF=FF)

    def lined(piece):
        return jnp.transpose(piece, (1, 0, 2))

    anywhere = pl.BlockSpec(memory_space=pl.ANY)
    tiled = (micro, nsub, SUB, D)
    act, grd, gsum = pl.pallas_call(
        functools.partial(mega, cfg),
        out_shape=(
            jax.ShapeDtypeStruct(tiled, F32), jax.ShapeDtypeStruct(tiled, F32),
            jax.ShapeDtypeStruct((total_rows, D), F32),
        ),
        in_specs=[anywhere, anywhere, pl.BlockSpec(memory_space=pltpu.SMEM)] + [anywhere] * 4,
        out_specs=(anywhere, anywhere, anywhere),
        scratch_shapes=list(scratch.values()),
        compiler_params=pltpu.CompilerParams(
            collective_id=0, has_side_effects=True, vmem_limit_bytes=255 * 2**18
        ),
        name="layers",
    )(
        node_features.reshape(tiled), cotangent.reshape(tiled), lengths,
        attention_weight, inner_weight, outer_weight, lined(vectors),
    )
    scale = 1.0 / (micro * rows * places)
    held = [attention_weight, inner_weight, outer_weight, vectors]
    moments = [
        momentum_attention, variance_attention, momentum_inner, variance_inner,
        momentum_outer, variance_outer, momentum_vectors, variance_vectors,
    ]
    held[3] = lined(vectors)
    moments[6:] = [lined(momentum_vectors), lined(variance_vectors)]
    shapes = [jax.ShapeDtypeStruct(piece.shape, F32) for piece in held for _ in range(4)]
    results = pl.pallas_call(
        functools.partial(finishing, scale, D, FF, first),
        out_shape=tuple([jax.ShapeDtypeStruct(tiled, F32)] * 2 + shapes),
        in_specs=[pl.BlockSpec(memory_space=pltpu.HBM)] * 15,
        out_specs=tuple([pl.BlockSpec(memory_space=pltpu.HBM)] * 18),
        scratch_shapes=[f32(total_rows, D)] + [f32(*piece.shape) for piece in held + moments]
        + [f32(*shape.shape) for shape in shapes] + [f32(2, *tiled), dma(2, 2, micro), dma(13), dma(16)],
        compiler_params=pltpu.CompilerParams(vmem_limit_bytes=60 * 2**20),
        name="adamw",
    )(act, grd, gsum, *held, *moments)
    whole = (1, micro, rows, D)
    lines_back = tuple(lined(piece) for piece in results[14:])
    return (results[0].reshape(whole), results[1].reshape(whole)) + tuple(results[2:14]) + lines_back


def solution(mesh):
    first = P("section", None, None)
    attention = P("section", None, None, None)
    nodes = P(None, "pts", None)
    return jax.shard_map(
        per_device,
        mesh=mesh,
        in_specs=(nodes, nodes, P(), attention, first, first, first, attention, attention) + (first,) * 6,
        out_specs=(P("section", None, "pts", None),) * 2 + (attention,) * 4 + (first,) * 12,
        check_vma=False,
    )
```

```python
import functools
import math

import jax
import jax.numpy as jnp
from jax import lax
from jax.experimental import pallas as pl
from jax.experimental.pallas import tpu as pltpu
from jax.sharding import PartitionSpec as P

HEADS = 4
STEP = 1200
TOTAL_STEPS = 4000
EPS_NORM = 1e-05
SUB = 256
TILE = 1024

MESH = pl.DeviceIdType.MESH
HIGHEST = lax.Precision.HIGHEST
F32 = jnp.float32
BF16 = jnp.bfloat16


def plan():
    warm = 0.3 * TOTAL_STEPS
    top = 0.001
    start = top / 25.0
    low = start / 10000.0
    if STEP <= warm:
        return start + (top - start) * (1.0 - math.cos(math.pi * STEP / warm)) / 2.0
    return low + (top - low) * (1.0 + math.cos(math.pi * (STEP - warm) / (TOTAL_STEPS - warm))) / 2.0


def cat(parts, axis=0):
    return jnp.concatenate(parts, axis=axis)


def split(value):
    high = value.astype(BF16)
    return high, (value - high.astype(F32)).astype(BF16)


def pack3(weight):
    high, low = split(weight)
    return cat([high, high, low], 1)


def pack2(weight):
    return cat(list(split(weight)), 1)


def left3(pack):
    size = pack.shape[1] // 2
    return cat([pack[:, :size], pack], 1)


def right3(value):
    high, low = split(value)
    return cat([high, low, high])


def dot16(left, right):
    return jnp.dot(left, right, preferred_element_type=F32)


def outer16(left, right):
    full = lax.dot_general(left, right, (((1,), (1,)), ((), ())), preferred_element_type=F32)
    m, n = full.shape[0] // 2, full.shape[1] // 2
    return full[:m, :n] + full[m:, :n] + full[:m, n:]


def outer16_sums(left, right):
    ones = jnp.ones((16, left.shape[1]), BF16)
    full = lax.dot_general(cat([left, ones]), right, (((1,), (1,)), ((), ())), preferred_element_type=F32)
    m, n = left.shape[0] // 2, full.shape[1] // 2
    return cat([full[:m, :n] + full[m : 2 * m, :n] + full[:m, n:], full[2 * m :, :n] + full[2 * m :, n:]])


def mm_nt(left, right, precision=HIGHEST):
    return lax.dot_general(left, right, (((1,), (1,)), ((), ())), precision=precision, preferred_element_type=F32)


def wide(table, width):
    return cat([table] * (width // 128), 1)


def fold(value):
    total = value[:, :128]
    for at in range(128, value.shape[1], 128):
        total = total + value[:, at : at + 128]
    return total


def digits_of(places):
    found, stride = [], 1
    while stride < places:
        radix = 4 if (places // stride) % 4 == 0 else 2
        found.append((stride, radix))
        stride *= radix
    return found


def scattered_digits(digits):
    return min(2, len(digits)), 1


def gradient_rows(D, FF, digits):
    sizes = []
    for count, least in zip(scattered_digits(digits), (2 * FF + 2 * D, 2 * D + 16)):
        unit = 8
        for _, radix in digits[:count]:
            unit *= radix
        sizes.append(-(-least // unit) * unit)
    early = sizes[0]
    first = dict(outer=0, inner=FF, q=2 * FF, o=2 * FF + D, k=early, v=early + D, vec=early + 2 * D)
    return first, sizes


def mega(cfg, x_hbm, cot_hbm, len_s, att_hbm, inn_hbm, out_hbm, vec_hbm, act_hbm, grd_hbm, gsum_hbm, *scratch):
    sm = dict(zip(cfg["names"], scratch))
    places, segs, micro, nsub = cfg["places"], cfg["segs"], cfg["micro"], cfg["nsub"]
    rows = nsub * SUB
    tokens = rows * places
    per = micro // 2
    D = cfg["D"]
    FF = cfg["FF"]
    group = D // HEADS
    digits = digits_of(places)
    c = lax.axis_index("section")
    place = lax.axis_index("pts")
    other = 1 - c

    stage = sm["stage"]

    dma_in = sm["dma_in"]
    watt, winn, wout, wvec = sm["watt"], sm["winn"], sm["wout"], sm["wvec"]

    def x_copy(bb):
        return pltpu.make_async_copy(x_hbm.at[c * per + bb], stage.at[0, bb], dma_in.at[bb])

    def cot_copy(bb):
        return pltpu.make_async_copy(cot_hbm.at[c * per + bb], stage.at[1, bb], dma_in.at[per + bb])

    weights = [(att_hbm.at[0], watt), (inn_hbm.at[0], winn), (out_hbm.at[0], wout), (vec_hbm, wvec)]

    def weight_copy(k):
        source, held = weights[k]
        return pltpu.make_async_copy(source, held.at[c], dma_in.at[2 * per + k])

    def weight_send(k):
        source, held = weights[k]
        return pltpu.make_async_remote_copy(
            src_ref=source, dst_ref=held.at[c], send_sem=sm["w_send"].at[k], recv_sem=sm["w_recv"].at[k],
            device_id={"section": other}, device_id_type=MESH,
        )

    def weight_arrival(k):
        source, held = weights[k]
        return pltpu.make_async_remote_copy(
            src_ref=source, dst_ref=held.at[other], send_sem=sm["w_send"].at[k], recv_sem=sm["w_recv"].at[k],
            device_id={"section": other}, device_id_type=MESH,
        )

    x_copy(0).start()
    for k in (0, 3, 1, 2):
        weight_copy(k).start()
    for bb in range(1, per):
        x_copy(bb).start()
    for bb in range(per):
        cot_copy(bb).start()

    def partner(digit, offset):
        stride, radix = digits[digit]
        mine = (place // stride) % radix
        theirs = (mine + offset) % radix
        return place + (theirs - mine) * stride

    def digit_at(digit, offset=0):
        stride, radix = digits[digit]
        return ((place // stride) % radix + offset) % radix

    barrier = pltpu.get_barrier_semaphore()
    greeted = 1
    pl.semaphore_signal(barrier, inc=1, device_id={"section": other}, device_id_type=MESH)
    for digit, (stride, radix) in enumerate(digits):
        for offset in range(1, radix):
            pl.semaphore_signal(barrier, inc=1, device_id={"pts": partner(digit, offset)}, device_id_type=MESH)
            greeted += 1

    for offset in range(1, digits[0][1]):
        pl.semaphore_signal(
            barrier, inc=1, device_id={"section": other, "pts": partner(0, offset)}, device_id_type=MESH
        )
        greeted += 1

    tab = sm["tab"]
    T_SLOT, T_END, T_ZI, T_KEEP = 0, nsub, 2 * nsub, 3 * nsub
    T_C, T_LO, T_HI, T_CS, T_ZK, T_LAST, T_CIDX, T_NLOC, T_CNT, T_LS, T_LE, T_OK = (
        4 * nsub + at * segs for at in range(12)
    )
    base = place * rows
    zero = jnp.int32(0)

    for bb in range(per):
        batch = c * per + bb
        lens = [len_s[batch, s] for s in range(segs)]
        ends, run = [], zero
        for s in range(segs):
            run = run + lens[s]
            ends.append(run)
        starts = [zero] + ends[:-1]
        big = zero
        for s in range(1, segs):
            big = big + jnp.where(starts[s] <= rows - 1, 1, 0)
        before = zero
        for s in range(segs):
            before = before + jnp.where(ends[s] <= tokens - rows, 1, 0)
        big = jnp.minimum(big, before)
        local_start = [jnp.clip(starts[s] - base, -1, rows) for s in range(segs)]
        local_end = [jnp.clip(ends[s] - base, 0, rows) for s in range(segs)]
        cells, valid = [zero], [zero]
        tab[bb, T_C] = zero
        tab[bb, T_OK] = zero
        for s in range(segs):
            tab[bb, T_LS + s] = local_start[s]
            tab[bb, T_LE + s] = local_end[s]
            slot = jnp.where(s == big, 0, jnp.where(s < big, s + 1, s))
            tab[bb, T_CS + s] = slot
            if s > 0:
                at = local_start[s]
                inside = jnp.maximum(at, 0)
                cell = jnp.minimum(inside // SUB, nsub - 1)
                low = inside - cell * SUB
                ok = jnp.where((at > 0) & (at < rows) & (low > 0), 1, 0)
                cells.append(cell)
                valid.append(ok)
                tab[bb, T_C + s] = cell
                tab[bb, T_OK + s] = ok
                tab[bb, T_LO + s] = jnp.where(ok == 1, low, SUB)
                tab[bb, T_HI + s] = jnp.where(ok == 1, jnp.minimum(local_end[s] - cell * SUB, SUB), 0)
                tab[bb, T_ZK + s] = ok * valid[s - 1] * jnp.where(cell == cells[s - 1], 1, 0)
        past = None
        for sub in range(nsub):
            row = sub * SUB
            first, final = zero, zero
            for s in range(segs - 1):
                first = first + jnp.where(local_end[s] <= row, 1, 0)
                final = final + jnp.where(local_end[s] <= row + SUB - 1, 1, 0)
            tab[bb, T_SLOT + sub] = tab[bb, T_CS + first]
            tab[bb, T_END + sub] = jnp.minimum(tab[bb, T_LE + first] - row, SUB)
            tab[bb, T_KEEP + sub] = zero if past is None else jnp.where(first == past, 1, 0)
            tab[bb, T_ZI + sub] = jnp.where(final == first, 0, final)
            past = first
        for j in range(segs):
            s = big if j == 0 else jnp.where(j - 1 < big, j - 1, j)
            low, high = tab[bb, T_LS + s], tab[bb, T_LE + s]
            cell = jnp.maximum(high - 1, 0) // SUB
            tab[bb, T_LAST + j] = jnp.where((high > 0) & (low < rows) & (cell * SUB >= low), cell, nsub)
            tab[bb, T_CIDX + j] = jnp.where(tab[bb, T_OK + s] == 1, s, 0)
            tab[bb, T_NLOC + j] = high - jnp.maximum(low, 0)
            tab[bb, T_CNT + j] = len_s[batch, s]

    lane_head = lax.broadcasted_iota(jnp.int32, (group, D), 1) // group
    block_mask = (
        lax.broadcasted_iota(jnp.int32, (D, D), 0) // group == lax.broadcasted_iota(jnp.int32, (D, D), 1) // group
    ).astype(F32)
    ones8 = jnp.ones((8, 128), F32)
    row8 = lax.broadcasted_iota(jnp.int32, (8, D), 0)

    def lanes():
        return lax.broadcasted_iota(jnp.int32, (1, SUB), 1)

    def compact(square):
        total = None
        for j in range(HEADS):
            piece = jnp.where(lane_head == j, square[group * j : group * (j + 1), :], 0.0)
            total = piece if total is None else total + piece
        return total

    def moment_rows(product):
        return cat([compact(product[:D]), product[D : D + 8]])

    def expand(packed):
        return cat([packed] * HEADS, 0) * block_mask

    def centred(matrix):
        grouped = matrix.reshape(matrix.shape[0] // group, group, matrix.shape[1])
        return (grouped - jnp.mean(grouped, axis=1, keepdims=True)).reshape(matrix.shape)

    for bb in range(per):
        sm["zm"][bb, 0] = jnp.zeros((D, SUB), F32)
    for name in ("zk", "zv", "corr_c", "corr_n", "corr_g"):
        sm[name][0] = jnp.zeros(sm[name].shape[1:], F32)
    for name in ("acc_c", "acc_n", "acc_g"):
        sm[name][nsub] = jnp.zeros(sm[name].shape[1:], F32)
    for name in ("d_outer", "d_inner", "d_kv", "s_du", "s_g", "s_dz"):
        sm[name][...] = jnp.zeros(sm[name].shape, F32)
    gb = sm["gb"]
    first, parts_rows = gradient_rows(D, FF, digits)
    R_Q, R_K, R_V, R_3, R_I, R_O, R_VEC = (first[name] for name in ("q", "k", "v", "o", "inner", "outer", "vec"))

    pl.semaphore_wait(barrier, greeted)
    for k in (0, 3, 1, 2):
        weight_send(k).start()

    tables = sm["tables"]

    def arrived(layer, k):
        @pl.when(c == layer)
        def _():
            weight_copy(k).wait()

        @pl.when(c != layer)
        def _():
            weight_arrival(k).wait_recv()

    def column(layer, row):
        return jnp.broadcast_to(wvec[layer, row], (128, D)).T

    def prepare_projections(layer):
        arrived(layer, 0)
        arrived(layer, 3)
        for row in (1, 2):
            tables[layer, row] = centred(column(layer, row))
        packed = sm["packed"]
        packed[layer, 0] = compact(1.0 + column(layer, 4))
        packed[layer, 1] = compact(column(layer, 5))
        packed[layer, 2] = compact(1.0 + column(layer, 6))
        sm["kvw"][layer] = pack2(cat([centred(watt[layer, 1].T), centred(watt[layer, 2].T)], 0))

    def prepare(layer):
        arrived(layer, 1)
        arrived(layer, 2)

        for at, row in ((0, 0), (3, 3), (4, 8), (5, 9), (6, 10)):
            tables[layer, at] = column(layer, row)
        query_t, output_t = watt[layer, 0].T, watt[layer, 3].T
        sm["wq_t"][layer] = pack2(query_t)
        sm["w3_t"][layer] = pack2(output_t)
        sm["wq_right"][layer] = right3(cat([query_t, tables[layer, 0]], 1))
        sm["w3_right"][layer] = right3(output_t)
        sm["kvw_back"][layer] = cat([pack2(watt[layer, 1]), pack2(watt[layer, 2])], 1)
        inner = winn[layer]
        sm["inn_t"][layer] = pack2(cat([inner[:, at : at + D].T for at in range(0, FF, D)], 0))
        sm["inn"][layer] = pack2(inner)
        outer = wout[layer]
        sm["out_t"][layer] = pack2(cat([outer[at : at + D, :].T for at in range(0, FF, D)], 1))
        sm["out"][layer] = pack2(outer)

    ar = sm["ar"]

    def ar_copy(k, digit, offset):
        spot = ar.at[k, digit, digit_at(digit)]
        return pltpu.make_async_remote_copy(
            src_ref=spot, dst_ref=spot, send_sem=sm["ar_send"].at[k, digit, offset - 1],
            recv_sem=sm["ar_recv"].at[k, digit, offset - 1],
            device_id={"pts": partner(digit, offset)}, device_id_type=MESH,
        )

    def ar_arrival(k, digit, offset):
        radix = digits[digit][1]
        spot = ar.at[k, digit, digit_at(digit, radix - offset)]
        return pltpu.make_async_remote_copy(
            src_ref=spot, dst_ref=spot, send_sem=sm["ar_send"].at[k, digit, offset - 1],
            recv_sem=sm["ar_recv"].at[k, digit, offset - 1],
            device_id={"pts": partner(digit, offset)}, device_id_type=MESH,
        )

    def ar_launch(k, digit, payload):
        ar[k, digit, digit_at(digit)] = payload
        for offset in range(1, digits[digit][1]):
            ar_copy(k, digit, offset).start()

    def ar_land(k, digit):
        radix = digits[digit][1]
        for offset in range(1, radix):
            ar_arrival(k, digit, offset).wait_recv()
        total = ar[k, digit, 0]
        for at in range(1, radix):
            total = total + ar[k, digit, at]
        return total

    def ar_step(k, digit):
        if digit < len(digits):
            ar_launch(k, digit, ar_land(k, digit - 1))

    def ar_finish(k):
        for digit in range(2, len(digits)):
            ar_step(k, digit)
        return ar_land(k, len(digits) - 1)

    def ar_drain(k):
        for digit in range(len(digits)):
            for offset in range(1, digits[digit][1]):
                ar_copy(k, digit, offset).wait_send()

    hs, kvs, rst, dms = sm["hs"], sm["kvs"], sm["rst"], sm["dms"]
    mids, hids, gps = sm["mids"], sm["hids"], sm["gps"]

    def three(pair, at=0, size=D):
        high = pair[at : at + size]
        return [high, pair[at + size : at + 2 * size], high]

    def joined(pairs):
        whole = pairs.astype(F32)
        return cat([whole[:D] + whole[D : 2 * D], whole[2 * D : 3 * D] + whole[3 * D :]])

    def load(ref, lead, subs):
        return cat([ref[(*lead, sub)] for sub in subs], 1)

    def save(ref, lead, subs, value):
        for at, sub in enumerate(subs):
            ref[(*lead, sub)] = value[:, SUB * at : SUB * (at + 1)]

    def part(value, at):
        return value[:, SUB * at : SUB * (at + 1)]

    def inside_of(bb, sub):
        return lanes() < tab[bb, T_END + sub]

    def keys_and_values(layer, bb, subs, pair):
        width = SUB * len(subs)
        bias = cat([wide(tables[layer, 1], width), wide(tables[layer, 2], width)], 0)
        field = dot16(left3(sm["kvw"][layer]), cat(three(pair))) + bias
        grouped = field.reshape(2 * HEADS, group, width)
        spread = jnp.mean(grouped * grouped, axis=1, keepdims=True)
        scale = lax.rsqrt(spread + EPS_NORM)
        normed = (grouped * scale).reshape(2 * D, width)
        save(rst, (layer, bb), subs, scale.reshape(2 * HEADS, width))
        k_high, k_low = split(normed[:D])
        v_high, v_low = split(normed[D:])
        keys, values = cat([k_high, k_low]), cat([v_high, v_low])
        save(kvs, (layer, bb), subs, cat([keys, values]))
        for at, sub in enumerate(subs):
            inside = inside_of(bb, sub)
            product = moment_rows(outer16_sums(part(keys, at), part(values, at) * inside.astype(BF16)))
            sums = fold(jnp.where(inside, part(normed, at)[:D], 0.0))
            keep = tab[bb, T_KEEP + sub] == 1
            past = jnp.maximum(sub - 1, 0)
            sm["acc_c"][sub] = product + jnp.where(keep, sm["acc_c"][past], 0.0)
            sm["acc_n"][sub] = sums + jnp.where(keep, sm["acc_n"][past], 0.0)

    def feed_forward(layer, bb, subs):
        width = SUB * len(subs)
        middles = []
        for sub in subs:
            slot = tab[bb, T_SLOT + sub]
            value = dot16(left3(sm["mat_a"][bb, slot]), cat(three(hs[layer, bb, sub]))) + wide(sm["add_a"][bb, slot], SUB)
            middles.append(jnp.where(inside_of(bb, sub), value, sm["zm"][bb, tab[bb, T_ZI + sub]]))
        middle = cat(middles, 1)
        m_high, m_low = split(middle)
        mid_pair = cat([m_high, m_low])
        u = dot16(left3(sm["inn_t"][layer]), cat(three(mid_pair)))
        u = u + cat([wide(tables[layer, 5], width), wide(tables[layer, 6], width)], 0)
        k0 = 0.7978845608
        square = u * u
        t = jnp.tanh(u * (k0 + (k0 * 0.044715) * square))
        half = 0.5 + 0.5 * t
        hidden = u * half
        slope = half + hidden * (1.0 - t) * (k0 + (3.0 * k0 * 0.044715) * square)
        h_high, h_low = split(hidden)
        hid_pair = cat([h_high, h_low])
        out = middle + dot16(left3(sm["out_t"][layer]), cat(three(hid_pair, 0, FF))) + wide(tables[layer, 4], width)
        return out, mid_pair, hid_pair, slope

    def feed_back(layer, bb, subs, upstream, mid_pair, hid_pair, slope):
        g_high, g_low = split(upstream)
        g_pair = cat([g_high, g_low])
        du = dot16(left3(sm["out"][layer]), cat(three(g_pair))) * slope
        u_high, u_low = split(du)
        u_pair = cat([u_high, u_low])
        d_mid = upstream + dot16(left3(sm["inn"][layer]), cat(three(u_pair, 0, FF)))
        q_high, q_low = split(d_mid)
        q_pair = cat([q_high, q_low])
        save(dms, (bb,), subs, q_pair)
        for at, sub in enumerate(subs):
            q_inside = part(q_pair, at) * inside_of(bb, sub).astype(BF16)
            product = outer16_sums(hs[layer, bb, sub], q_inside)
            keep = tab[bb, T_KEEP + sub] == 1
            past = jnp.maximum(sub - 1, 0)
            sm["acc_g"][sub] = product + jnp.where(keep, sm["acc_g"][past], 0.0)
        sm["d_outer"][layer] += outer16(hid_pair, g_pair)
        sm["d_inner"][layer] += outer16(u_pair, mid_pair)
        sm["s_du"][layer] += fold(du)
        sm["s_g"][layer] += fold(upstream)

    def norm_back(layer, bb, subs):
        width = SUB * len(subs)
        pairs = load(kvs, (layer, bb), subs)
        normed = joined(pairs)
        e_ks, e_vs = [], []
        for at, sub in enumerate(subs):
            slot, zi, inside = tab[bb, T_SLOT + sub], tab[bb, T_ZI + sub], inside_of(bb, sub)
            own = part(pairs, at)
            e_k = dot16(left3(sm["mat_a"][bb, slot]), cat(three(own, 2 * D))) + wide(sm["add_a"][bb, slot], SUB)
            e_v = dot16(left3(sm["mat_b"][bb, slot]), cat(three(own))) + wide(sm["add_b"][bb, slot], SUB)
            e_ks.append(jnp.where(inside, e_k, sm["zk"][zi]))
            e_vs.append(jnp.where(inside, e_v, sm["zv"][zi]))
        e = cat([cat(e_ks, 1), cat(e_vs, 1)])
        shape = (2 * HEADS, group, width)
        e3, n3 = e.reshape(shape), normed.reshape(shape)
        scale = load(rst, (layer, bb), subs).reshape(2 * HEADS, 1, width)
        along = jnp.mean(e3 * n3, axis=1, keepdims=True)
        dz = ((e3 - n3 * along) * scale).reshape(2 * D, width)
        z_high, z_low = split(dz)
        z_pair = cat([z_high, z_low])
        sm["d_kv"][layer] += outer16(z_pair, load(hs, (layer, bb), subs))
        sm["s_dz"][layer] += fold(dz)
        return z_pair

    def input_back(layer, bb, subs, z_pair):
        z_high, z_low = z_pair[: 2 * D], z_pair[2 * D :]
        through = [z_high[:D], z_low[:D], z_high[:D], z_high[D:], z_low[D:], z_high[D:]]
        backs = []
        back = sm["kvw_back"][layer]
        for at, sub in enumerate(subs):
            slot, zi = tab[bb, T_SLOT + sub], tab[bb, T_ZI + sub]
            left = cat([left3(sm["back_mat"][layer, bb, slot]), left3(back[:, : 2 * D]), left3(back[:, 2 * D :])], 1)
            right = three(dms[bb, sub] * inside_of(bb, sub).astype(BF16)) + [part(one, at) for one in through]
            backs.append(dot16(left, cat(right)) + sm["zm"][bb, zi])
        return cat(backs, 1)

    count = TILE // SUB

    def over(low, high, stage):
        def body(i, carry):
            stage([i * count + at for at in range(count)])
            return carry

        if high - low == 1:
            body(low, 0)
        else:
            lax.fori_loop(low, high, body, 0)

    steps = nsub // count

    def loop(stage, between=lambda: None, beside=lambda: None, ahead=lambda: None):
        over(0, (steps + 1) // 2, stage)
        ahead()
        between()
        over((steps + 1) // 2, steps, stage)
        beside()

    def span(bb, s):
        at = lanes()
        return (at >= tab[bb, T_LO + s]) & (at < tab[bb, T_HI + s])

    def fill(ref, bb, s, inside, value):
        before = jnp.where(tab[bb, T_ZK + s] == 1, ref[s - 1], 0.0)
        ref[s] = jnp.where(inside, value, before)

    def corrections_mid(layer, bb):
        for s in range(1, segs):
            pair = hs[layer, bb, tab[bb, T_C + s]]
            slot = tab[bb, T_CS + s]
            value = dot16(left3(sm["mat_a"][bb, slot]), cat(three(pair))) + wide(sm["add_a"][bb, slot], SUB)
            fill(sm["zm"].at[bb], bb, s, span(bb, s), value)

    def corrections_back(layer, bb):
        for s in range(1, segs):
            cell, slot, inside = tab[bb, T_C + s], tab[bb, T_CS + s], span(bb, s)
            pairs = kvs[layer, bb, cell]
            e_k = dot16(left3(sm["mat_a"][bb, slot]), cat(three(pairs, 2 * D))) + wide(sm["add_a"][bb, slot], SUB)
            e_v = dot16(left3(sm["mat_b"][bb, slot]), cat(three(pairs))) + wide(sm["add_b"][bb, slot], SUB)
            e_d = dot16(left3(sm["back_mat"][layer, bb, slot]), cat(three(dms[bb, cell])))
            fill(sm["zk"], bb, s, inside, e_k)
            fill(sm["zv"], bb, s, inside, e_v)
            fill(sm["zm"].at[bb], bb, s, inside, e_d)

    def corrections_moments(layer, bb):
        for s in range(1, segs):
            cell, inside = tab[bb, T_C + s], span(bb, s)
            pairs = kvs[layer, bb, cell]
            product = outer16_sums(pairs[: 2 * D], pairs[2 * D :] * inside.astype(BF16))
            sm["corr_c"][s] = moment_rows(product)
            keys = pairs[: 2 * D].astype(F32)
            sm["corr_n"][s] = fold(jnp.where(inside, keys[:D] + keys[D:], 0.0))

    def corrections_grams(layer, bb):
        for s in range(1, segs):
            cell, inside = tab[bb, T_C + s], span(bb, s)
            q_pair = dms[bb, cell] * inside.astype(BF16)
            sm["corr_g"][s] = outer16_sums(hs[layer, bb, cell], q_pair)

    stats, own_c, own_sums, vec, vec_c = sm["stats"], sm["own_c"], sm["own_sums"], sm["vec"], sm["vec_c"]

    def total_of(name, bb, j):
        return sm["acc_" + name][tab[bb, T_LAST + j]] + sm["corr_" + name][tab[bb, T_CIDX + j]]

    def shifts(layer):
        return 1.0 + wvec[layer, 4], wvec[layer, 5], 1.0 + wvec[layer, 6], wvec[layer, 7]

    def moments_of(layer, bb, j):
        key_gain, key_shift, value_gain, value_shift = shifts(layer)
        gain_c, shift_c = sm["packed"][layer, 0], sm["packed"][layer, 1]
        rows_c = total_of("c", bb, j)
        product, values = rows_c[:group], rows_c[group : group + 1]
        keys = compact(jnp.broadcast_to(jnp.sum(total_of("n", bb, j), axis=1, keepdims=True), (D, 128)))
        stats[layer, bb, j] = cat([product, keys, rows_c[group:]])
        local = tab[bb, T_NLOC + j].astype(F32)
        from_values = values * value_gain + local * value_shift
        return gain_c * (product * value_gain + keys * value_shift) + shift_c * from_values

    def mixing_of(layer, bb, slots, moments):
        packs = []
        for j, moment in zip(slots, moments):
            pack = pack2((expand(moment) / tab[bb, T_CNT + j].astype(F32)).T)
            sm["mt"][layer, bb, j] = pack
            packs.append(left3(pack))
        mixed = dot16(cat(packs), sm["wq_right"][layer])
        rights = [right3(mixed[D * at : D * (at + 1)]) for at in range(len(slots))]
        through = dot16(left3(sm["w3_t"][layer]), cat(rights, 1))
        eye = (
            lax.broadcasted_iota(jnp.int32, (D, D), 0) == lax.broadcasted_iota(jnp.int32, (D, D), 1)
        ).astype(F32)
        for at, j in enumerate(slots):
            forward = through[:, 2 * D * at : 2 * D * at + D] + eye
            sm["mat_a"][bb, j] = pack2(forward)
            sm["add_a"][bb, j] = through[:, 2 * D * at + D : 2 * D * (at + 1)] + tables[layer, 3]
            sm["back_mat"][layer, bb, j] = pack2(forward.T)

    def grams_of(layer, grams):
        tall = D + 16
        onto = dot16(cat([pack3(gram) for gram in grams]), sm["w3_right"][layer])
        ontos = [onto[tall * at : tall * (at + 1)] for at in range(len(grams))]
        rights = [right3(cat([one[:D], gram[:D]], 1)) for one, gram in zip(ontos, grams)]
        both = dot16(left3(sm["wq_t"][layer]), cat(rights, 1))
        query_bias = tables[layer, 0]
        d_moments, throughs = [], []
        for at, (one, gram) in enumerate(zip(ontos, grams)):
            d_moments.append(compact(both[:, 2 * D * at : 2 * D * at + D] + query_bias * one[D : D + 1]))
            throughs.append(both[:, 2 * D * at + D : 2 * D * (at + 1)] + query_bias * gram[D : D + 1])
        return d_moments, ontos, throughs

    def projections_of(layer, bb, slots, ontos, throughs, grams):
        mts = [sm["mt"][layer, bb, j] for j in slots]
        right = [part for mt in mts for part in (mt[:, :D], mt[:, D:], mt[:, :D])]
        d_query = dot16(cat([pack3(one) for one in ontos], 1), cat(right))
        gb[layer, R_Q : R_Q + D] += d_query[:D]
        gb[layer, R_3 : R_3 + D] += dot16(cat([left3(mt) for mt in mts], 1), cat([right3(through) for through in throughs]))
        vec[layer, 0] += d_query[D : D + 8]
        sums = grams[0][D : D + 8]
        for gram in grams[1:]:
            sums = sums + gram[D : D + 8]
        vec[layer, 1] += sums

    def back_of(layer, bb, slots, d_moments):
        key_gain, key_shift, value_gain, value_shift = shifts(layer)
        gain_c, shift_c, value_gain_c = (sm["packed"][layer, at] for at in range(3))

        def across(packed):
            return jnp.broadcast_to(jnp.sum(expand(centred(packed)), axis=1, keepdims=True), (D, 128))

        for j, d_moment in zip(slots, d_moments):
            d = d_moment / tab[bb, T_CNT + j].astype(F32)
            d_t = compact(expand(d).T)
            sm["mat_a"][bb, j] = pack2(expand(centred(gain_c * d * value_gain)))
            sm["add_a"][bb, j] = across(gain_c * d * value_shift)
            sm["mat_b"][bb, j] = pack2(expand(centred(value_gain_c * d_t * key_gain)))
            sm["add_b"][bb, j] = across(value_gain_c * d_t * key_shift)
            held = stats[layer, bb, j]
            product, keys, values = held[:group], held[group : 2 * group], held[2 * group : 2 * group + 1]
            local = tab[bb, T_NLOC + j].astype(F32)
            vec_c[layer, 0] += d * (product * value_gain + keys * value_shift)
            vec_c[layer, 1] += d * (values * value_gain + local * value_shift)
            vec_c[layer, 2] += d * (gain_c * product + shift_c * values)
            vec_c[layer, 3] += d * (gain_c * keys + shift_c * local)

    small = list(range(1, segs))

    def key_of(stage, bb):
        return stage * per + bb

    def moments_out(layer, bb, k):
        corrections_moments(layer, bb)
        ar_launch(k, 0, moments_of(layer, bb, 0))
        for j in small:
            own_c[bb, j] = moments_of(layer, bb, j)

    def small_mixing(layer, bb):
        mixing_of(layer, bb, small, [own_c[bb, j] for j in small])

    def mixing_in(layer, bb, k):
        mixing_of(layer, bb, [0], [ar_finish(k)])
        corrections_mid(layer, bb)

    def spot_of(j):
        return watt.at[j // 4, j % 4]

    def grams_out(layer, bb, k):
        corrections_grams(layer, bb)
        grams = [total_of("g", bb, 0)]
        d_moments, *rest = grams_of(layer, grams)
        ar_launch(k, 0, d_moments[0])
        projections_of(layer, bb, [0], *rest, grams)
        for j in small:
            gram = total_of("g", bb, j)
            spot_of(j)[...] = gram[:D]
            own_sums[j] = gram[D:]

    def small_back(layer, bb):
        grams = [cat([spot_of(j)[...], own_sums[j]]) for j in small]
        d_moments, *rest = grams_of(layer, grams)
        projections_of(layer, bb, small, *rest, grams)
        back_of(layer, bb, small, d_moments)

    def grams_in(layer, bb, k):
        back_of(layer, bb, [0], [ar_finish(k)])
        corrections_back(layer, bb)

    vec[...] = jnp.zeros(vec.shape, F32)
    vec_c[...] = jnp.zeros(vec_c.shape, F32)

    targets = (act_hbm, grd_hbm)

    def kept(kind, layer, bb):
        return pltpu.make_async_copy(
            stage.at[layer, bb], targets[kind].at[c * per + bb], sm["o_local"].at[kind, bb]
        )

    def sent(kind, layer, bb):
        return pltpu.make_async_remote_copy(
            src_ref=stage.at[layer, bb], dst_ref=targets[kind].at[c * per + bb], send_sem=sm["o_send"].at[kind, bb],
            recv_sem=sm["o_recv"].at[kind, bb], device_id={"section": other}, device_id_type=MESH,
        )

    def came(kind, layer, bb):
        return pltpu.make_async_remote_copy(
            src_ref=stage.at[layer, bb], dst_ref=targets[kind].at[other * per + bb], send_sem=sm["o_send"].at[kind, bb],
            recv_sem=sm["o_recv"].at[kind, bb], device_id={"section": other}, device_id_type=MESH,
        )

    def ship(kind, layer, bb):
        @pl.when(c == layer)
        def _():
            kept(kind, layer, bb).start()

        @pl.when(c != layer)
        def _():
            sent(kind, layer, bb).start()

    def shipped(kind, layer, bb):
        @pl.when(c == layer)
        def _():
            kept(kind, layer, bb).wait()

        @pl.when(c != layer)
        def _():
            sent(kind, layer, bb).wait_send()

    def load_t(layer, bb, subs):
        return cat([stage[layer, bb, sub].T for sub in subs], 1)

    def save_t(layer, bb, subs, value):
        for at, sub in enumerate(subs):
            stage[layer, bb, sub] = part(value, at).T

    def start_stage(bb, subs):
        high, low = split(load_t(0, bb, subs))
        pair = cat([high, low])
        save(hs, (0, bb), subs, pair)
        keys_and_values(0, bb, subs, pair)

    def first_stage(bb, subs):
        out, mid_pair, hid_pair, slope = feed_forward(0, bb, subs)
        save(mids, (bb,), subs, mid_pair)
        save(hids, (bb,), subs, hid_pair)
        save(gps, (bb,), subs, slope)
        save_t(0, bb, subs, out)
        high, low = split(out)
        pair = cat([high, low])
        save(hs, (1, bb), subs, pair)
        keys_and_values(1, bb, subs, pair)

    def second_stage(bb, subs):
        out, mid_pair, hid_pair, slope = feed_forward(1, bb, subs)
        upstream = load_t(1, bb, subs)
        save_t(1, bb, subs, out)
        feed_back(1, bb, subs, upstream, mid_pair, hid_pair, slope)

    def third_stage(bb, subs):
        upstream = input_back(1, bb, subs, norm_back(1, bb, subs))
        save_t(1, bb, subs, upstream)
        held = [load(ref, (bb,), subs) for ref in (mids, hids, gps)]
        feed_back(0, bb, subs, upstream, *held)

    def fifth_stage(bb, subs):
        save(kvs, (0, bb), subs, norm_back(0, bb, subs))

    def sixth_stage(bb, subs):
        save_t(0, bb, subs, input_back(0, bb, subs, load(kvs, (0, bb), subs)))

    og = sm["og"]
    scattered = scattered_digits(digits)
    sizes, phases = [], []
    for kind, deep in enumerate(scattered):
        sizes.append([parts_rows[kind]])
        for _, radix in digits[:deep]:
            sizes[-1].append(sizes[-1][-1] // radix)
        phases.append(
            [("scatter", digit) for digit in range(deep)]
            + [("exchange", digit) for digit in range(deep, len(digits))]
            + [("gather", digit) for digit in reversed(range(deep))]
        )
    g_send, g_recv = sm["g_send"], sm["g_recv"]

    def early_rows(layer):
        gb[layer, R_O : R_O + FF] = sm["d_outer"][layer]
        d_inner = sm["d_inner"][layer]
        for at in range(0, FF, D):
            gb[layer, R_I + at : R_I + at + D] = d_inner[at : at + D].T

    def late_rows(layer):
        d_kv = sm["d_kv"][layer]
        gb[layer, R_K : R_K + D] = d_kv[:D].T
        gb[layer, R_V : R_V + D] = d_kv[D:].T
        s_dz = mm_nt(ones8, sm["s_dz"][layer])
        s_du = mm_nt(ones8, sm["s_du"][layer])
        s_g = mm_nt(ones8, sm["s_g"][layer])
        lines = [vec[layer, 0], s_dz[:, :D], s_dz[:, D:], vec[layer, 1]]
        lines += [mm_nt(ones8, expand(vec_c[layer, at])) for at in (0, 1)]
        lines += [jnp.sum(vec_c[layer, at], axis=0, keepdims=True) for at in (2, 3)]
        lines += [s_g, s_du[:, :D], s_du[:, D:]]
        block = jnp.zeros((16, D), F32)
        row16 = lax.broadcasted_iota(jnp.int32, (16, D), 0)
        for at, line in enumerate(lines):
            block = jnp.where(row16 == at, line[0:1], block)
        gb[layer, R_VEC : R_VEC + 16] = block

    def block_of(kind, depth, at=None):
        low = 0 if kind == 0 else parts_rows[0]
        for digit in range(depth):
            offset = at if (at is not None and digit == depth - 1) else 0
            low = low + digit_at(digit, offset) * sizes[kind][digit + 1]
        return pl.ds(low if depth == 0 else pl.multiple_of(low, 8), sizes[kind][depth])

    def landing(kind, digit):
        return sm["rb%d%d" % (kind, digit)]

    def scatter_first(layer, kind, offset, far):
        radix = digits[0][1]
        slot = radix - 1 + offset if far else offset - 1
        target = {"section": other, "pts": partner(0, offset)} if far else {"pts": partner(0, offset)}
        return pltpu.make_async_remote_copy(
            src_ref=gb.at[layer, block_of(kind, 1, offset)], dst_ref=landing(kind, 0).at[slot],
            send_sem=g_send.at[kind, 0, 0, slot], recv_sem=g_recv.at[kind, 0, 0, slot],
            device_id=target, device_id_type=MESH,
        )

    def scatter_next(layer, kind, digit, offset):
        return pltpu.make_async_remote_copy(
            src_ref=gb.at[layer, block_of(kind, digit + 1, offset)], dst_ref=landing(kind, digit).at[offset - 1],
            send_sem=g_send.at[kind, 0, digit, offset - 1], recv_sem=g_recv.at[kind, 0, digit, offset - 1],
            device_id={"pts": partner(digit, offset)}, device_id_type=MESH,
        )

    def gather(kind, digit, offset, at):
        spot = og.at[block_of(kind, digit + 1, at)]
        return pltpu.make_async_remote_copy(
            src_ref=spot, dst_ref=spot,
            send_sem=g_send.at[kind, 1, digit, offset - 1], recv_sem=g_recv.at[kind, 1, digit, offset - 1],
            device_id={"pts": partner(digit, offset)}, device_id_type=MESH,
        )

    def exchange(kind, digit, offset, back=0):
        spot = sm["wide%d" % kind].at[digit - scattered[kind], digit_at(digit, back)]
        return pltpu.make_async_remote_copy(
            src_ref=spot, dst_ref=spot,
            send_sem=g_send.at[kind, 0, digit, offset - 1], recv_sem=g_recv.at[kind, 0, digit, offset - 1],
            device_id={"pts": partner(digit, offset)}, device_id_type=MESH,
        )

    def outgoing(layer, kind, phase, far=False):
        name, digit = phase
        offsets = range(0 if far else 1, digits[digit][1])
        if name == "scatter" and digit == 0:
            return [scatter_first(layer, kind, offset, far) for offset in offsets]
        if far:
            return []
        if name == "scatter":
            return [scatter_next(layer, kind, digit, offset) for offset in offsets]
        if name == "exchange":
            return [exchange(kind, digit, offset) for offset in offsets]
        return [gather(kind, digit, offset, 0) for offset in offsets]

    def land(layer, kind, phase):
        name, digit = phase
        radix = digits[digit][1]
        if name == "gather":
            for offset in range(1, radix):
                gather(kind, digit, offset, radix - offset).wait_recv()
            return None
        if name == "exchange":
            for offset in range(1, radix):
                exchange(kind, digit, offset, radix - offset).wait_recv()
            held = sm["wide%d" % kind]
            total = held[digit - scattered[kind], 0]
            for at in range(1, radix):
                total = total + held[digit - scattered[kind], at]
            return total
        total = gb[layer, block_of(kind, digit + 1)]
        for copy in outgoing(layer, kind, phase):
            copy.wait_recv()
        for at in range(radix - 1):
            total = total + landing(kind, digit)[at]
        if digit == 0:
            for copy in outgoing(layer, kind, phase, True):
                copy.wait_recv()
            for at in range(radix):
                total = total + landing(kind, 0)[radix - 1 + at]
        return total

    def gradient_step(layer, kind, step):
        todo = phases[kind]
        if step == 0:
            @pl.when(c != layer)
            def _():
                for copy in outgoing(layer, kind, todo[0], True):
                    copy.start()

        if step <= len(todo):
            @pl.when(c == layer)
            def _():
                total = None if step == 0 else land(layer, kind, todo[step - 1])
                if step == len(todo):
                    return
                name, digit = todo[step]
                if total is not None:
                    if name == "scatter":
                        gb[layer, block_of(kind, digit)] = total
                    elif name == "exchange":
                        sm["wide%d" % kind][digit - scattered[kind], digit_at(digit)] = total
                    else:
                        og[block_of(kind, digit + 1)] = total
                for copy in outgoing(layer, kind, todo[step]):
                    copy.start()

    def gradient_rest(layer, kind, step):
        for left in range(step, len(phases[kind]) + 1):
            gradient_step(layer, kind, left)

    def drain_gradients():
        for layer in range(2):
            for kind in range(2):
                @pl.when(c == layer)
                def _():
                    for phase in phases[kind]:
                        for copy in outgoing(layer, kind, phase):
                            copy.wait_send()

                @pl.when(c != layer)
                def _():
                    for copy in outgoing(layer, kind, phases[kind][0], True):
                        copy.wait_send()

    EARLY, LATE = 0, 1

    def together(*actions):
        def run():
            for action in actions:
                action()

        return run

    def grad(layer, kind, step):
        return functools.partial(gradient_step, layer, kind, step)

    call = functools.partial
    prepare_projections(0)
    for bb in range(per):
        x_copy(bb).wait()
        if bb == 0:
            loop(call(start_stage, bb))
        else:
            loop(call(start_stage, bb), call(ar_step, key_of(0, bb - 1), 1), call(small_mixing, 0, bb - 1))
        moments_out(0, bb, key_of(0, bb))
        if bb == 0:
            prepare(0)
    prepare_projections(1)
    prepare(1)
    gb[...] = jnp.zeros(gb.shape, F32)
    ar_step(key_of(0, per - 1), 1)

    def step_of(stage, bb):
        if bb > 0:
            return call(ar_step, key_of(stage, bb - 1), 1)
        return (lambda: None) if stage == 1 else call(ar_step, key_of(stage - 1, per - 1), 1)

    for bb in range(per):
        mixing_in(0, bb, key_of(0, bb))
        filler = call(small_mixing, 0, per - 1) if bb == 0 else call(small_mixing, 1, bb - 1)
        loop(call(first_stage, bb), step_of(1, bb), filler)
        ship(0, 0, bb)
        moments_out(1, bb, key_of(1, bb))
    for bb in range(per):
        cot_copy(bb).wait()
        mixing_in(1, bb, key_of(1, bb))
        filler = call(small_mixing, 1, per - 1) if bb == 0 else call(small_back, 1, bb - 1)
        loop(call(second_stage, bb), step_of(2, bb), filler)
        ship(0, 1, bb)
        grams_out(1, bb, key_of(2, bb))
    early_rows(1)
    for bb in range(per):
        grams_in(1, bb, key_of(2, bb))
        shipped(0, 1, bb)
        filler = call(small_back, 1, per - 1) if bb == 0 else call(small_back, 0, bb - 1)
        beside = [step_of(3, bb)] + ([grad(1, EARLY, 1)] if bb == 1 else [])
        loop(call(third_stage, bb), together(*beside), filler)
        ship(1, 1, bb)
        if bb == 0:
            gradient_step(1, EARLY, 0)
        grams_out(0, bb, key_of(3, bb))
    early_rows(0)
    late_rows(1)
    gradient_step(1, LATE, 0)
    gradient_step(1, EARLY, 2)
    for bb in range(per):
        grams_in(0, bb, key_of(3, bb))
        shipped(0, 0, bb)
        if bb == 0:
            beside = [step_of(4, bb), grad(0, EARLY, 0), grad(1, LATE, 1), grad(1, EARLY, 3)]
            loop(call(fifth_stage, bb), together(*beside), ahead=call(small_back, 0, per - 1))
        elif bb == 1:
            loop(call(fifth_stage, bb), together(grad(0, EARLY, 1), grad(1, LATE, 2), grad(1, EARLY, 4)))
        else:
            loop(call(fifth_stage, bb))
    late_rows(0)
    gradient_step(0, LATE, 0)
    gradient_step(0, EARLY, 2)
    gradient_rest(1, EARLY, 5)
    gradient_rest(1, LATE, 3)
    for bb in range(per):
        loop(call(sixth_stage, bb))
        ship(1, 0, bb)
        if bb == 0:
            gradient_step(0, LATE, 1)
            gradient_step(0, EARLY, 3)
    gradient_step(0, LATE, 2)
    gradient_rest(0, EARLY, 4)
    gradient_rest(0, LATE, 3)

    out_copy = pltpu.make_async_copy(og, gsum_hbm, dma_in.at[0])
    out_copy.start()

    drain_gradients()
    for k in range(4):
        weight_send(k).wait_send()
    for k in range(4 * per):
        ar_drain(k)
    for bb in range(per):
        for layer in range(2):
            shipped(1, layer, bb)
        for layer in range(2):
            @pl.when(c == layer)
            def _():
                came(0, layer, bb).wait_recv()
                came(1, layer, bb).wait_recv()
    out_copy.wait()


def finishing(scale, D, FF, first, act, grd, gsum_hbm, *refs):
    sources, results = refs[:12], refs[12:30]
    gsum, held, made, through, sem_large, sem_in, sem_out = refs[30], refs[31:43], refs[43:59], *refs[59:]
    micro, nsub = act.shape[:2]
    half = nsub // 2
    large, onward = [], []
    for kind, (source, target) in enumerate(((act, results[0]), (grd, results[1]))):
        for part in range(2 * micro):
            rows = (part // 2, pl.ds(part % 2 * half, half))
            spot = through.at[(kind, *rows)]
            large.append(pltpu.make_async_copy(source.at[rows], spot, sem_large.at[0, kind, part]))
            onward.append(pltpu.make_async_copy(spot, target.at[rows], sem_large.at[1, kind, part]))
    loads = [pltpu.make_async_copy(gsum_hbm, gsum, sem_in.at[12])]
    loads += [pltpu.make_async_copy(sources[at], held[at], sem_in.at[at]) for at in range(12)]
    ahead = 4
    for copy in large[:ahead] + loads:
        copy.start()

    def pass_on(low, high):
        for at in range(low, high):
            large[at].wait()
            onward[at].start()
            if at + ahead < len(large):
                large[at + ahead].start()

    pass_on(0, micro)
    rate = plan()

    def step(weight, gradient, momentum, variance):
        average = gradient * scale
        new_momentum = 0.9 * momentum + 0.1 * average
        new_variance = 0.999 * variance + 0.001 * average * average
        mean = new_momentum / (1.0 - 0.9**STEP)
        square = new_variance / (1.0 - 0.999**STEP)
        updated = weight - rate * (mean / (jnp.sqrt(square) + 1e-08) + 0.01 * weight)
        return gradient, new_momentum, new_variance, updated

    parts = [first[name] for name in ("q", "k", "v", "o")]
    inner, outer, late = first["inner"], first["outer"], first["vec"]
    places = [
        [((0, at), slice(low, low + D)) for at, low in enumerate(parts)],
        [((0, slice(None), slice(at, at + D)), slice(inner + at, inner + at + D)) for at in range(0, FF, D)],
        [((0,), slice(outer, outer + FF))],
        [((line,), slice(late + line, late + line + 1)) for line in range(held[3].shape[0])],
    ]
    loads[0].wait()
    stores = []
    for kind in range(4):
        for at in (kind, 4 + 2 * kind, 5 + 2 * kind):
            loads[1 + at].wait()
        weight, momentum, variance = held[kind], held[4 + 2 * kind], held[5 + 2 * kind]
        for index, lines in places[kind]:
            values = step(weight[index], gsum[lines], momentum[index], variance[index])
            for ref, value in zip(made[4 * kind : 4 * kind + 4], values):
                ref[index] = value
        for at in range(4 * kind, 4 * kind + 4):
            stores.append(pltpu.make_async_copy(made[at], results[2 + at], sem_out.at[at]))
            stores[-1].start()
    pass_on(micro, len(large))
    for copy in onward + stores:
        copy.wait()


def per_device(
    node_features, cotangent, lengths, attention_weight, inner_weight, outer_weight, vectors,
    momentum_attention, variance_attention, momentum_inner, variance_inner,
    momentum_outer, variance_outer, momentum_vectors, variance_vectors,
):
    places = lax.axis_size("pts")
    micro, rows, D = node_features.shape
    FF = inner_weight.shape[-1]
    segs = lengths.shape[1]
    lines = vectors.shape[1]
    nsub = rows // SUB
    per = micro // 2
    digits = digits_of(places)
    group = D // HEADS
    first, parts_rows = gradient_rows(D, FF, digits)
    total_rows = sum(parts_rows)
    nar = 4 * per

    def f32(*shape):
        return pltpu.VMEM(shape, F32)

    def b16(*shape):
        return pltpu.VMEM(shape, BF16)

    def dma(*shape):
        return pltpu.SemaphoreType.DMA(shape)

    scratch = dict(
        watt=f32(2, 4, D, D), winn=f32(2, D, FF), wout=f32(2, FF, D), wvec=f32(2, lines, 1, D),
        tab=pltpu.SMEM((per, 4 * nsub + 12 * segs), jnp.int32),
        tables=f32(2, 7, D, 128), packed=f32(2, 3, group, D),
        wq_t=b16(2, D, 2 * D), w3_t=b16(2, D, 2 * D), wq_right=b16(2, 3 * D, 2 * D), w3_right=b16(2, 3 * D, D),
        kvw=b16(2, 2 * D, 2 * D), kvw_back=b16(2, D, 4 * D),
        inn_t=b16(2, FF, 2 * D), inn=b16(2, D, 2 * FF), out_t=b16(2, D, 2 * FF), out=b16(2, FF, 2 * D),
        hs=b16(2, per, nsub, 2 * D, SUB), kvs=b16(2, per, nsub, 4 * D, SUB),
        rst=f32(2, per, nsub, 2 * HEADS, SUB), dms=b16(per, nsub, 2 * D, SUB),
        mids=b16(per, nsub, 2 * D, SUB), hids=b16(per, nsub, 2 * FF, SUB), gps=f32(per, nsub, FF, SUB),
                stage=f32(2, per, nsub, SUB, D),
        zm=f32(per, segs, D, SUB), zk=f32(segs, D, SUB), zv=f32(segs, D, SUB),
        acc_c=f32(nsub + 1, group + 8, D), acc_n=f32(nsub + 1, D, 128), acc_g=f32(nsub + 1, D + 16, D),
        corr_c=f32(segs, group + 8, D), corr_n=f32(segs, D, 128), corr_g=f32(segs, D + 16, D),
        stats=f32(2, per, segs, 2 * group + 8, D), own_c=f32(per, segs, group, D), own_sums=f32(segs, 16, D),
        mt=b16(2, per, segs, D, 2 * D), vec_c=f32(2, 4, group, D),
        mat_a=b16(per, segs, D, 2 * D), add_a=f32(per, segs, D, 128), back_mat=b16(2, per, segs, D, 2 * D),
        mat_b=b16(per, segs, D, 2 * D), add_b=f32(per, segs, D, 128),
        d_outer=f32(2, FF, D), d_inner=f32(2, FF, D), d_kv=f32(2, 2 * D, D),
        s_du=f32(2, FF, 128), s_g=f32(2, D, 128), s_dz=f32(2, 2 * D, 128),
        vec=f32(2, 2, 8, D), gb=f32(2, total_rows, D), og=f32(total_rows, D),
        ar=f32(nar, len(digits), 4, group, D),
        dma_in=dma(2 * per + 4), w_send=dma(4), w_recv=dma(4),
        ar_send=dma(nar, len(digits), 3), ar_recv=dma(nar, len(digits), 3),
        o_local=dma(2, per), o_send=dma(2, per), o_recv=dma(2, per),
        g_send=dma(2, 2, len(digits), 7), g_recv=dma(2, 2, len(digits), 7),
    )
    for kind, (size, count) in enumerate(zip(parts_rows, scattered_digits(digits))):
        for digit, (_, radix) in enumerate(digits[:count]):
            size //= radix
            scratch["rb%d%d" % (kind, digit)] = f32(2 * radix - 1 if digit == 0 else radix - 1, size, D)
        if len(digits) > count:
            scratch["wide%d" % kind] = f32(len(digits) - count, 4, size, D)
    cfg = dict(names=list(scratch), places=places, segs=segs, micro=micro, nsub=nsub, D=D, FF=FF)

    def lined(piece):
        return jnp.transpose(piece, (1, 0, 2))

    anywhere = pl.BlockSpec(memory_space=pl.ANY)
    tiled = (micro, nsub, SUB, D)
    act, grd, gsum = pl.pallas_call(
        functools.partial(mega, cfg),
        out_shape=(
            jax.ShapeDtypeStruct(tiled, F32), jax.ShapeDtypeStruct(tiled, F32),
            jax.ShapeDtypeStruct((total_rows, D), F32),
        ),
        in_specs=[anywhere, anywhere, pl.BlockSpec(memory_space=pltpu.SMEM)] + [anywhere] * 4,
        out_specs=(anywhere, anywhere, anywhere),
        scratch_shapes=list(scratch.values()),
        compiler_params=pltpu.CompilerParams(
            collective_id=0, has_side_effects=True, vmem_limit_bytes=255 * 2**18
        ),
        name="layers",
    )(
        node_features.reshape(tiled), cotangent.reshape(tiled), lengths,
        attention_weight, inner_weight, outer_weight, lined(vectors),
    )
    scale = 1.0 / (micro * rows * places)
    held = [attention_weight, inner_weight, outer_weight, vectors]
    moments = [
        momentum_attention, variance_attention, momentum_inner, variance_inner,
        momentum_outer, variance_outer, momentum_vectors, variance_vectors,
    ]
    held[3] = lined(vectors)
    moments[6:] = [lined(momentum_vectors), lined(variance_vectors)]
    shapes = [jax.ShapeDtypeStruct(piece.shape, F32) for piece in held for _ in range(4)]
    results = pl.pallas_call(
        functools.partial(finishing, scale, D, FF, first),
        out_shape=tuple([jax.ShapeDtypeStruct(tiled, F32)] * 2 + shapes),
        in_specs=[pl.BlockSpec(memory_space=pltpu.HBM)] * 15,
        out_specs=tuple([pl.BlockSpec(memory_space=pltpu.HBM)] * 18),
        scratch_shapes=[f32(total_rows, D)] + [f32(*piece.shape) for piece in held + moments]
        + [f32(*shape.shape) for shape in shapes] + [f32(2, *tiled), dma(2, 2, 2 * micro), dma(13), dma(16)],
        compiler_params=pltpu.CompilerParams(vmem_limit_bytes=60 * 2**20),
        name="adamw",
    )(act, grd, gsum, *held, *moments)
    whole = (1, micro, rows, D)
    lines_back = tuple(lined(piece) for piece in results[14:])
    return (results[0].reshape(whole), results[1].reshape(whole)) + tuple(results[2:14]) + lines_back


def solution(mesh):
    first = P("section", None, None)
    attention = P("section", None, None, None)
    nodes = P(None, "pts", None)
    return jax.shard_map(
        per_device,
        mesh=mesh,
        in_specs=(nodes, nodes, P(), attention, first, first, first, attention, attention) + (first,) * 6,
        out_specs=(P("section", None, "pts", None),) * 2 + (attention,) * 4 + (first,) * 12,
        check_vma=False,
    )
```

```python
import functools
import math

import jax
import jax.numpy as jnp
from jax import lax
from jax.experimental import pallas as pl
from jax.experimental.pallas import tpu as pltpu
from jax.sharding import PartitionSpec as P

HEADS = 4
STEP = 1200
TOTAL_STEPS = 4000
EPS_NORM = 1e-05
SUB = 256
TILE = 1024

MESH = pl.DeviceIdType.MESH
HIGHEST = lax.Precision.HIGHEST
F32 = jnp.float32
BF16 = jnp.bfloat16


def plan():
    warm = 0.3 * TOTAL_STEPS
    top = 0.001
    start = top / 25.0
    low = start / 10000.0
    if STEP <= warm:
        return start + (top - start) * (1.0 - math.cos(math.pi * STEP / warm)) / 2.0
    return low + (top - low) * (1.0 + math.cos(math.pi * (STEP - warm) / (TOTAL_STEPS - warm))) / 2.0


def cat(parts, axis=0):
    return jnp.concatenate(parts, axis=axis)


def split(value):
    high = value.astype(BF16)
    return high, (value - high.astype(F32)).astype(BF16)


def pack3(weight):
    high, low = split(weight)
    return cat([high, high, low], 1)


def pack2(weight):
    return cat(list(split(weight)), 1)


def left3(pack):
    size = pack.shape[1] // 2
    return cat([pack[:, :size], pack], 1)


def right3(value):
    high, low = split(value)
    return cat([high, low, high])


def dot16(left, right):
    return jnp.dot(left, right, preferred_element_type=F32)


def outer16(left, right):
    full = lax.dot_general(left, right, (((1,), (1,)), ((), ())), preferred_element_type=F32)
    m, n = full.shape[0] // 2, full.shape[1] // 2
    return full[:m, :n] + full[m:, :n] + full[:m, n:]


def outer16_sums(left, right):
    ones = jnp.ones((16, left.shape[1]), BF16)
    full = lax.dot_general(cat([left, ones]), right, (((1,), (1,)), ((), ())), preferred_element_type=F32)
    m, n = left.shape[0] // 2, full.shape[1] // 2
    return cat([full[:m, :n] + full[m : 2 * m, :n] + full[:m, n:], full[2 * m :, :n] + full[2 * m :, n:]])


def mm_nt(left, right, precision=HIGHEST):
    return lax.dot_general(left, right, (((1,), (1,)), ((), ())), precision=precision, preferred_element_type=F32)


def wide(table, width):
    return cat([table] * (width // 128), 1)


def fold(value):
    total = value[:, :128]
    for at in range(128, value.shape[1], 128):
        total = total + value[:, at : at + 128]
    return total


def digits_of(places):
    found, stride = [], 1
    while stride < places:
        radix = 4 if (places // stride) % 4 == 0 else 2
        found.append((stride, radix))
        stride *= radix
    return found


def scattered_digits(digits):
    return min(2, len(digits)), 1


def gradient_rows(D, FF, digits):
    sizes = []
    for count, least in zip(scattered_digits(digits), (2 * FF + 2 * D, 2 * D + 16)):
        unit = 8
        for _, radix in digits[:count]:
            unit *= radix
        sizes.append(-(-least // unit) * unit)
    early = sizes[0]
    first = dict(outer=0, inner=FF, q=2 * FF, o=2 * FF + D, k=early, v=early + D, vec=early + 2 * D)
    return first, sizes


def mega(cfg, x_hbm, cot_hbm, len_s, att_hbm, inn_hbm, out_hbm, vec_hbm, act_hbm, grd_hbm, gsum_hbm, *scratch):
    sm = dict(zip(cfg["names"], scratch))
    places, segs, micro, nsub = cfg["places"], cfg["segs"], cfg["micro"], cfg["nsub"]
    rows = nsub * SUB
    tokens = rows * places
    per = micro // 2
    D = cfg["D"]
    FF = cfg["FF"]
    group = D // HEADS
    digits = digits_of(places)
    c = lax.axis_index("section")
    place = lax.axis_index("pts")
    other = 1 - c

    stage = sm["stage"]

    dma_in = sm["dma_in"]
    watt, winn, wout, wvec = sm["watt"], sm["winn"], sm["wout"], sm["wvec"]

    def x_copy(bb):
        return pltpu.make_async_copy(x_hbm.at[c * per + bb], stage.at[0, bb], dma_in.at[bb])

    def cot_copy(bb):
        return pltpu.make_async_copy(cot_hbm.at[c * per + bb], stage.at[1, bb], dma_in.at[per + bb])

    weights = [(att_hbm.at[0], watt), (inn_hbm.at[0], winn), (out_hbm.at[0], wout), (vec_hbm, wvec)]

    def weight_copy(k):
        source, held = weights[k]
        return pltpu.make_async_copy(source, held.at[c], dma_in.at[2 * per + k])

    def weight_send(k):
        source, held = weights[k]
        return pltpu.make_async_remote_copy(
            src_ref=source, dst_ref=held.at[c], send_sem=sm["w_send"].at[k], recv_sem=sm["w_recv"].at[k],
            device_id={"section": other}, device_id_type=MESH,
        )

    def weight_arrival(k):
        source, held = weights[k]
        return pltpu.make_async_remote_copy(
            src_ref=source, dst_ref=held.at[other], send_sem=sm["w_send"].at[k], recv_sem=sm["w_recv"].at[k],
            device_id={"section": other}, device_id_type=MESH,
        )

    x_copy(0).start()
    for k in (0, 3, 1, 2):
        weight_copy(k).start()
    for bb in range(1, per):
        x_copy(bb).start()
    for bb in range(per):
        cot_copy(bb).start()

    def partner(digit, offset):
        stride, radix = digits[digit]
        mine = (place // stride) % radix
        theirs = (mine + offset) % radix
        return place + (theirs - mine) * stride

    def digit_at(digit, offset=0):
        stride, radix = digits[digit]
        return ((place // stride) % radix + offset) % radix

    barrier = pltpu.get_barrier_semaphore()
    greeted = 1
    pl.semaphore_signal(barrier, inc=1, device_id={"section": other}, device_id_type=MESH)
    for digit, (stride, radix) in enumerate(digits):
        for offset in range(1, radix):
            pl.semaphore_signal(barrier, inc=1, device_id={"pts": partner(digit, offset)}, device_id_type=MESH)
            greeted += 1

    for offset in range(1, digits[0][1]):
        pl.semaphore_signal(
            barrier, inc=1, device_id={"section": other, "pts": partner(0, offset)}, device_id_type=MESH
        )
        greeted += 1

    tab = sm["tab"]
    T_SLOT, T_END, T_ZI, T_KEEP = 0, nsub, 2 * nsub, 3 * nsub
    T_C, T_LO, T_HI, T_CS, T_ZK, T_LAST, T_CIDX, T_NLOC, T_CNT, T_LS, T_LE, T_OK = (
        4 * nsub + at * segs for at in range(12)
    )
    base = place * rows
    zero = jnp.int32(0)

    for bb in range(per):
        batch = c * per + bb
        lens = [len_s[batch, s] for s in range(segs)]
        ends, run = [], zero
        for s in range(segs):
            run = run + lens[s]
            ends.append(run)
        starts = [zero] + ends[:-1]
        big = zero
        for s in range(1, segs):
            big = big + jnp.where(starts[s] <= rows - 1, 1, 0)
        before = zero
        for s in range(segs):
            before = before + jnp.where(ends[s] <= tokens - rows, 1, 0)
        big = jnp.minimum(big, before)
        local_start = [jnp.clip(starts[s] - base, -1, rows) for s in range(segs)]
        local_end = [jnp.clip(ends[s] - base, 0, rows) for s in range(segs)]
        cells, valid = [zero], [zero]
        tab[bb, T_C] = zero
        tab[bb, T_OK] = zero
        for s in range(segs):
            tab[bb, T_LS + s] = local_start[s]
            tab[bb, T_LE + s] = local_end[s]
            slot = jnp.where(s == big, 0, jnp.where(s < big, s + 1, s))
            tab[bb, T_CS + s] = slot
            if s > 0:
                at = local_start[s]
                inside = jnp.maximum(at, 0)
                cell = jnp.minimum(inside // SUB, nsub - 1)
                low = inside - cell * SUB
                ok = jnp.where((at > 0) & (at < rows) & (low > 0), 1, 0)
                cells.append(cell)
                valid.append(ok)
                tab[bb, T_C + s] = cell
                tab[bb, T_OK + s] = ok
                tab[bb, T_LO + s] = jnp.where(ok == 1, low, SUB)
                tab[bb, T_HI + s] = jnp.where(ok == 1, jnp.minimum(local_end[s] - cell * SUB, SUB), 0)
                tab[bb, T_ZK + s] = ok * valid[s - 1] * jnp.where(cell == cells[s - 1], 1, 0)
        past = None
        for sub in range(nsub):
            row = sub * SUB
            first, final = zero, zero
            for s in range(segs - 1):
                first = first + jnp.where(local_end[s] <= row, 1, 0)
                final = final + jnp.where(local_end[s] <= row + SUB - 1, 1, 0)
            tab[bb, T_SLOT + sub] = tab[bb, T_CS + first]
            tab[bb, T_END + sub] = jnp.minimum(tab[bb, T_LE + first] - row, SUB)
            tab[bb, T_KEEP + sub] = zero if past is None else jnp.where(first == past, 1, 0)
            tab[bb, T_ZI + sub] = jnp.where(final == first, 0, final)
            past = first
        for j in range(segs):
            s = big if j == 0 else jnp.where(j - 1 < big, j - 1, j)
            low, high = tab[bb, T_LS + s], tab[bb, T_LE + s]
            cell = jnp.maximum(high - 1, 0) // SUB
            tab[bb, T_LAST + j] = jnp.where((high > 0) & (low < rows) & (cell * SUB >= low), cell, nsub)
            tab[bb, T_CIDX + j] = jnp.where(tab[bb, T_OK + s] == 1, s, 0)
            tab[bb, T_NLOC + j] = high - jnp.maximum(low, 0)
            tab[bb, T_CNT + j] = len_s[batch, s]

    lane_head = lax.broadcasted_iota(jnp.int32, (group, D), 1) // group
    block_mask = (
        lax.broadcasted_iota(jnp.int32, (D, D), 0) // group == lax.broadcasted_iota(jnp.int32, (D, D), 1) // group
    ).astype(F32)
    ones8 = jnp.ones((8, 128), F32)
    row8 = lax.broadcasted_iota(jnp.int32, (8, D), 0)

    def lanes():
        return lax.broadcasted_iota(jnp.int32, (1, SUB), 1)

    def compact(square):
        total = None
        for j in range(HEADS):
            piece = jnp.where(lane_head == j, square[group * j : group * (j + 1), :], 0.0)
            total = piece if total is None else total + piece
        return total

    def moment_rows(product):
        return cat([compact(product[:D]), product[D : D + 8]])

    def expand(packed):
        return cat([packed] * HEADS, 0) * block_mask

    def centred(matrix):
        grouped = matrix.reshape(matrix.shape[0] // group, group, matrix.shape[1])
        return (grouped - jnp.mean(grouped, axis=1, keepdims=True)).reshape(matrix.shape)

    for bb in range(per):
        sm["zm"][bb, 0] = jnp.zeros((D, SUB), F32)
    for name in ("zk", "zv", "corr_c", "corr_n", "corr_g"):
        sm[name][0] = jnp.zeros(sm[name].shape[1:], F32)
    for name in ("acc_c", "acc_n", "acc_g"):
        sm[name][nsub] = jnp.zeros(sm[name].shape[1:], F32)
    for name in ("d_outer", "d_inner", "d_kv", "s_du", "s_g", "s_dz"):
        sm[name][...] = jnp.zeros(sm[name].shape, F32)
    gb = sm["gb"]
    first, parts_rows = gradient_rows(D, FF, digits)
    R_Q, R_K, R_V, R_3, R_I, R_O, R_VEC = (first[name] for name in ("q", "k", "v", "o", "inner", "outer", "vec"))

    pl.semaphore_wait(barrier, greeted)
    for k in (0, 3, 1, 2):
        weight_send(k).start()

    tables = sm["tables"]

    def arrived(layer, k):
        @pl.when(c == layer)
        def _():
            weight_copy(k).wait()

        @pl.when(c != layer)
        def _():
            weight_arrival(k).wait_recv()

    def column(layer, row):
        return jnp.broadcast_to(wvec[layer, row], (128, D)).T

    def prepare_projections(layer):
        arrived(layer, 0)
        arrived(layer, 3)
        for row in (1, 2):
            tables[layer, row] = centred(column(layer, row))
        packed = sm["packed"]
        packed[layer, 0] = compact(1.0 + column(layer, 4))
        packed[layer, 1] = compact(column(layer, 5))
        packed[layer, 2] = compact(1.0 + column(layer, 6))
        sm["kvw"][layer] = pack2(cat([centred(watt[layer, 1].T), centred(watt[layer, 2].T)], 0))

    def prepare(layer):
        arrived(layer, 1)
        arrived(layer, 2)

        for at, row in ((0, 0), (3, 3), (4, 8), (5, 9), (6, 10)):
            tables[layer, at] = column(layer, row)
        query_t, output_t = watt[layer, 0].T, watt[layer, 3].T
        sm["wq_t"][layer] = pack2(query_t)
        sm["w3_t"][layer] = pack2(output_t)
        sm["wq_right"][layer] = right3(cat([query_t, tables[layer, 0]], 1))
        sm["w3_right"][layer] = right3(output_t)
        sm["kvw_back"][layer] = cat([pack2(watt[layer, 1]), pack2(watt[layer, 2])], 1)
        inner = winn[layer]
        sm["inn_t"][layer] = pack2(cat([inner[:, at : at + D].T for at in range(0, FF, D)], 0))
        sm["inn"][layer] = pack2(inner)
        outer = wout[layer]
        sm["out_t"][layer] = pack2(cat([outer[at : at + D, :].T for at in range(0, FF, D)], 1))
        sm["out"][layer] = pack2(outer)

    ar = sm["ar"]

    def ar_copy(k, digit, offset):
        spot = ar.at[k, digit, digit_at(digit)]
        return pltpu.make_async_remote_copy(
            src_ref=spot, dst_ref=spot, send_sem=sm["ar_send"].at[k, digit, offset - 1],
            recv_sem=sm["ar_recv"].at[k, digit, offset - 1],
            device_id={"pts": partner(digit, offset)}, device_id_type=MESH,
        )

    def ar_arrival(k, digit, offset):
        radix = digits[digit][1]
        spot = ar.at[k, digit, digit_at(digit, radix - offset)]
        return pltpu.make_async_remote_copy(
            src_ref=spot, dst_ref=spot, send_sem=sm["ar_send"].at[k, digit, offset - 1],
            recv_sem=sm["ar_recv"].at[k, digit, offset - 1],
            device_id={"pts": partner(digit, offset)}, device_id_type=MESH,
        )

    def ar_launch(k, digit, payload):
        ar[k, digit, digit_at(digit)] = payload
        for offset in range(1, digits[digit][1]):
            ar_copy(k, digit, offset).start()

    def ar_land(k, digit):
        radix = digits[digit][1]
        for offset in range(1, radix):
            ar_arrival(k, digit, offset).wait_recv()
        total = ar[k, digit, 0]
        for at in range(1, radix):
            total = total + ar[k, digit, at]
        return total

    def ar_step(k, digit):
        if digit < len(digits):
            ar_launch(k, digit, ar_land(k, digit - 1))

    def ar_finish(k):
        for digit in range(2, len(digits)):
            ar_step(k, digit)
        return ar_land(k, len(digits) - 1)

    def ar_drain(k):
        for digit in range(len(digits)):
            for offset in range(1, digits[digit][1]):
                ar_copy(k, digit, offset).wait_send()

    hs, kvs, rst, dms = sm["hs"], sm["kvs"], sm["rst"], sm["dms"]
    mids, hids, gps = sm["mids"], sm["hids"], sm["gps"]

    def three(pair, at=0, size=D):
        high = pair[at : at + size]
        return [high, pair[at + size : at + 2 * size], high]

    def joined(pairs):
        whole = pairs.astype(F32)
        return cat([whole[:D] + whole[D : 2 * D], whole[2 * D : 3 * D] + whole[3 * D :]])

    def load(ref, lead, subs):
        return cat([ref[(*lead, sub)] for sub in subs], 1)

    def save(ref, lead, subs, value):
        for at, sub in enumerate(subs):
            ref[(*lead, sub)] = value[:, SUB * at : SUB * (at + 1)]

    def part(value, at):
        return value[:, SUB * at : SUB * (at + 1)]

    def inside_of(bb, sub):
        return lanes() < tab[bb, T_END + sub]

    def keys_and_values(layer, bb, subs, pair):
        width = SUB * len(subs)
        bias = cat([wide(tables[layer, 1], width), wide(tables[layer, 2], width)], 0)
        field = dot16(left3(sm["kvw"][layer]), cat(three(pair))) + bias
        grouped = field.reshape(2 * HEADS, group, width)
        spread = jnp.mean(grouped * grouped, axis=1, keepdims=True)
        scale = lax.rsqrt(spread + EPS_NORM)
        normed = (grouped * scale).reshape(2 * D, width)
        save(rst, (layer, bb), subs, scale.reshape(2 * HEADS, width))
        k_high, k_low = split(normed[:D])
        v_high, v_low = split(normed[D:])
        keys, values = cat([k_high, k_low]), cat([v_high, v_low])
        save(kvs, (layer, bb), subs, cat([keys, values]))
        for at, sub in enumerate(subs):
            inside = inside_of(bb, sub)
            product = moment_rows(outer16_sums(part(keys, at), part(values, at) * inside.astype(BF16)))
            sums = fold(jnp.where(inside, part(normed, at)[:D], 0.0))
            keep = tab[bb, T_KEEP + sub] == 1
            past = jnp.maximum(sub - 1, 0)
            sm["acc_c"][sub] = product + jnp.where(keep, sm["acc_c"][past], 0.0)
            sm["acc_n"][sub] = sums + jnp.where(keep, sm["acc_n"][past], 0.0)

    def feed_forward(layer, bb, subs):
        width = SUB * len(subs)
        middles = []
        for sub in subs:
            slot = tab[bb, T_SLOT + sub]
            value = dot16(left3(sm["mat_a"][bb, slot]), cat(three(hs[layer, bb, sub]))) + wide(sm["add_a"][bb, slot], SUB)
            middles.append(jnp.where(inside_of(bb, sub), value, sm["zm"][bb, tab[bb, T_ZI + sub]]))
        middle = cat(middles, 1)
        m_high, m_low = split(middle)
        mid_pair = cat([m_high, m_low])
        u = dot16(left3(sm["inn_t"][layer]), cat(three(mid_pair)))
        u = u + cat([wide(tables[layer, 5], width), wide(tables[layer, 6], width)], 0)
        k0 = 0.7978845608
        square = u * u
        t = jnp.tanh(u * (k0 + (k0 * 0.044715) * square))
        half = 0.5 + 0.5 * t
        hidden = u * half
        slope = half + hidden * (1.0 - t) * (k0 + (3.0 * k0 * 0.044715) * square)
        h_high, h_low = split(hidden)
        hid_pair = cat([h_high, h_low])
        out = middle + dot16(left3(sm["out_t"][layer]), cat(three(hid_pair, 0, FF))) + wide(tables[layer, 4], width)
        return out, mid_pair, hid_pair, slope

    def feed_back(layer, bb, subs, upstream, mid_pair, hid_pair, slope):
        g_high, g_low = split(upstream)
        g_pair = cat([g_high, g_low])
        du = dot16(left3(sm["out"][layer]), cat(three(g_pair))) * slope
        u_high, u_low = split(du)
        u_pair = cat([u_high, u_low])
        d_mid = upstream + dot16(left3(sm["inn"][layer]), cat(three(u_pair, 0, FF)))
        q_high, q_low = split(d_mid)
        q_pair = cat([q_high, q_low])
        save(dms, (bb,), subs, q_pair)
        for at, sub in enumerate(subs):
            q_inside = part(q_pair, at) * inside_of(bb, sub).astype(BF16)
            product = outer16_sums(hs[layer, bb, sub], q_inside)
            keep = tab[bb, T_KEEP + sub] == 1
            past = jnp.maximum(sub - 1, 0)
            sm["acc_g"][sub] = product + jnp.where(keep, sm["acc_g"][past], 0.0)
        sm["d_outer"][layer] += outer16(hid_pair, g_pair)
        sm["d_inner"][layer] += outer16(u_pair, mid_pair)
        sm["s_du"][layer] += fold(du)
        sm["s_g"][layer] += fold(upstream)

    def norm_back(layer, bb, subs):
        width = SUB * len(subs)
        pairs = load(kvs, (layer, bb), subs)
        normed = joined(pairs)
        e_ks, e_vs = [], []
        for at, sub in enumerate(subs):
            slot, zi, inside = tab[bb, T_SLOT + sub], tab[bb, T_ZI + sub], inside_of(bb, sub)
            own = part(pairs, at)
            e_k = dot16(left3(sm["mat_a"][bb, slot]), cat(three(own, 2 * D))) + wide(sm["add_a"][bb, slot], SUB)
            e_v = dot16(left3(sm["mat_b"][bb, slot]), cat(three(own))) + wide(sm["add_b"][bb, slot], SUB)
            e_ks.append(jnp.where(inside, e_k, sm["zk"][zi]))
            e_vs.append(jnp.where(inside, e_v, sm["zv"][zi]))
        e = cat([cat(e_ks, 1), cat(e_vs, 1)])
        shape = (2 * HEADS, group, width)
        e3, n3 = e.reshape(shape), normed.reshape(shape)
        scale = load(rst, (layer, bb), subs).reshape(2 * HEADS, 1, width)
        along = jnp.mean(e3 * n3, axis=1, keepdims=True)
        dz = ((e3 - n3 * along) * scale).reshape(2 * D, width)
        z_high, z_low = split(dz)
        z_pair = cat([z_high, z_low])
        sm["d_kv"][layer] += outer16(z_pair, load(hs, (layer, bb), subs))
        sm["s_dz"][layer] += fold(dz)
        return z_pair

    def input_back(layer, bb, subs, z_pair):
        z_high, z_low = z_pair[: 2 * D], z_pair[2 * D :]
        through = [z_high[:D], z_low[:D], z_high[:D], z_high[D:], z_low[D:], z_high[D:]]
        backs = []
        back = sm["kvw_back"][layer]
        for at, sub in enumerate(subs):
            slot, zi = tab[bb, T_SLOT + sub], tab[bb, T_ZI + sub]
            left = cat([left3(sm["back_mat"][layer, bb, slot]), left3(back[:, : 2 * D]), left3(back[:, 2 * D :])], 1)
            right = three(dms[bb, sub] * inside_of(bb, sub).astype(BF16)) + [part(one, at) for one in through]
            backs.append(dot16(left, cat(right)) + sm["zm"][bb, zi])
        return cat(backs, 1)

    count = TILE // SUB

    def over(low, high, stage):
        def body(i, carry):
            stage([i * count + at for at in range(count)])
            return carry

        if high - low == 1:
            body(low, 0)
        else:
            lax.fori_loop(low, high, body, 0)

    steps = nsub // count

    def loop(stage, between=lambda: None, beside=lambda: None, ahead=lambda: None):
        over(0, (steps + 1) // 2, stage)
        ahead()
        between()
        over((steps + 1) // 2, steps, stage)
        beside()

    def span(bb, s):
        at = lanes()
        return (at >= tab[bb, T_LO + s]) & (at < tab[bb, T_HI + s])

    def fill(ref, bb, s, inside, value):
        before = jnp.where(tab[bb, T_ZK + s] == 1, ref[s - 1], 0.0)
        ref[s] = jnp.where(inside, value, before)

    def corrections_mid(layer, bb):
        for s in range(1, segs):
            pair = hs[layer, bb, tab[bb, T_C + s]]
            slot = tab[bb, T_CS + s]
            value = dot16(left3(sm["mat_a"][bb, slot]), cat(three(pair))) + wide(sm["add_a"][bb, slot], SUB)
            fill(sm["zm"].at[bb], bb, s, span(bb, s), value)

    def corrections_back(layer, bb):
        for s in range(1, segs):
            cell, slot, inside = tab[bb, T_C + s], tab[bb, T_CS + s], span(bb, s)
            pairs = kvs[layer, bb, cell]
            e_k = dot16(left3(sm["mat_a"][bb, slot]), cat(three(pairs, 2 * D))) + wide(sm["add_a"][bb, slot], SUB)
            e_v = dot16(left3(sm["mat_b"][bb, slot]), cat(three(pairs))) + wide(sm["add_b"][bb, slot], SUB)
            e_d = dot16(left3(sm["back_mat"][layer, bb, slot]), cat(three(dms[bb, cell])))
            fill(sm["zk"], bb, s, inside, e_k)
            fill(sm["zv"], bb, s, inside, e_v)
            fill(sm["zm"].at[bb], bb, s, inside, e_d)

    def corrections_moments(layer, bb):
        for s in range(1, segs):
            cell, inside = tab[bb, T_C + s], span(bb, s)
            pairs = kvs[layer, bb, cell]
            product = outer16_sums(pairs[: 2 * D], pairs[2 * D :] * inside.astype(BF16))
            sm["corr_c"][s] = moment_rows(product)
            keys = pairs[: 2 * D].astype(F32)
            sm["corr_n"][s] = fold(jnp.where(inside, keys[:D] + keys[D:], 0.0))

    def corrections_grams(layer, bb):
        for s in range(1, segs):
            cell, inside = tab[bb, T_C + s], span(bb, s)
            q_pair = dms[bb, cell] * inside.astype(BF16)
            sm["corr_g"][s] = outer16_sums(hs[layer, bb, cell], q_pair)

    stats, own_c, own_sums, vec, vec_c = sm["stats"], sm["own_c"], sm["own_sums"], sm["vec"], sm["vec_c"]

    def total_of(name, bb, j):
        return sm["acc_" + name][tab[bb, T_LAST + j]] + sm["corr_" + name][tab[bb, T_CIDX + j]]

    def shifts(layer):
        return 1.0 + wvec[layer, 4], wvec[layer, 5], 1.0 + wvec[layer, 6], wvec[layer, 7]

    def moments_of(layer, bb, j):
        key_gain, key_shift, value_gain, value_shift = shifts(layer)
        gain_c, shift_c = sm["packed"][layer, 0], sm["packed"][layer, 1]
        rows_c = total_of("c", bb, j)
        product, values = rows_c[:group], rows_c[group : group + 1]
        keys = compact(jnp.broadcast_to(jnp.sum(total_of("n", bb, j), axis=1, keepdims=True), (D, 128)))
        stats[layer, bb, j] = cat([product, keys, rows_c[group:]])
        local = tab[bb, T_NLOC + j].astype(F32)
        from_values = values * value_gain + local * value_shift
        return gain_c * (product * value_gain + keys * value_shift) + shift_c * from_values

    def mixing_of(layer, bb, slots, moments):
        packs = []
        for j, moment in zip(slots, moments):
            pack = pack2((expand(moment) / tab[bb, T_CNT + j].astype(F32)).T)
            sm["mt"][layer, bb, j] = pack
            packs.append(left3(pack))
        mixed = dot16(cat(packs), sm["wq_right"][layer])
        rights = [right3(mixed[D * at : D * (at + 1)]) for at in range(len(slots))]
        through = dot16(left3(sm["w3_t"][layer]), cat(rights, 1))
        eye = (
            lax.broadcasted_iota(jnp.int32, (D, D), 0) == lax.broadcasted_iota(jnp.int32, (D, D), 1)
        ).astype(F32)
        for at, j in enumerate(slots):
            forward = through[:, 2 * D * at : 2 * D * at + D] + eye
            sm["mat_a"][bb, j] = pack2(forward)
            sm["add_a"][bb, j] = through[:, 2 * D * at + D : 2 * D * (at + 1)] + tables[layer, 3]
            sm["back_mat"][layer, bb, j] = pack2(forward.T)

    def grams_of(layer, grams):
        tall = D + 16
        onto = dot16(cat([pack3(gram) for gram in grams]), sm["w3_right"][layer])
        ontos = [onto[tall * at : tall * (at + 1)] for at in range(len(grams))]
        rights = [right3(cat([one[:D], gram[:D]], 1)) for one, gram in zip(ontos, grams)]
        both = dot16(left3(sm["wq_t"][layer]), cat(rights, 1))
        query_bias = tables[layer, 0]
        d_moments, throughs = [], []
        for at, (one, gram) in enumerate(zip(ontos, grams)):
            d_moments.append(compact(both[:, 2 * D * at : 2 * D * at + D] + query_bias * one[D : D + 1]))
            throughs.append(both[:, 2 * D * at + D : 2 * D * (at + 1)] + query_bias * gram[D : D + 1])
        return d_moments, ontos, throughs

    def projections_of(layer, bb, slots, ontos, throughs, grams):
        mts = [sm["mt"][layer, bb, j] for j in slots]
        right = [part for mt in mts for part in (mt[:, :D], mt[:, D:], mt[:, :D])]
        d_query = dot16(cat([pack3(one) for one in ontos], 1), cat(right))
        gb[layer, R_Q : R_Q + D] += d_query[:D]
        gb[layer, R_3 : R_3 + D] += dot16(cat([left3(mt) for mt in mts], 1), cat([right3(through) for through in throughs]))
        vec[layer, 0] += d_query[D : D + 8]
        sums = grams[0][D : D + 8]
        for gram in grams[1:]:
            sums = sums + gram[D : D + 8]
        vec[layer, 1] += sums

    def back_of(layer, bb, slots, d_moments):
        key_gain, key_shift, value_gain, value_shift = shifts(layer)
        gain_c, shift_c, value_gain_c = (sm["packed"][layer, at] for at in range(3))

        def across(packed):
            return jnp.broadcast_to(jnp.sum(expand(centred(packed)), axis=1, keepdims=True), (D, 128))

        for j, d_moment in zip(slots, d_moments):
            d = d_moment / tab[bb, T_CNT + j].astype(F32)
            d_t = compact(expand(d).T)
            sm["mat_a"][bb, j] = pack2(expand(centred(gain_c * d * value_gain)))
            sm["add_a"][bb, j] = across(gain_c * d * value_shift)
            sm["mat_b"][bb, j] = pack2(expand(centred(value_gain_c * d_t * key_gain)))
            sm["add_b"][bb, j] = across(value_gain_c * d_t * key_shift)
            held = stats[layer, bb, j]
            product, keys, values = held[:group], held[group : 2 * group], held[2 * group : 2 * group + 1]
            local = tab[bb, T_NLOC + j].astype(F32)
            vec_c[layer, 0] += d * (product * value_gain + keys * value_shift)
            vec_c[layer, 1] += d * (values * value_gain + local * value_shift)
            vec_c[layer, 2] += d * (gain_c * product + shift_c * values)
            vec_c[layer, 3] += d * (gain_c * keys + shift_c * local)

    small = list(range(1, segs))

    def key_of(stage, bb):
        return stage * per + bb

    def moments_out(layer, bb, k):
        corrections_moments(layer, bb)
        ar_launch(k, 0, moments_of(layer, bb, 0))
        for j in small:
            own_c[bb, j] = moments_of(layer, bb, j)

    def small_mixing(layer, bb):
        mixing_of(layer, bb, small, [own_c[bb, j] for j in small])

    def mixing_in(layer, bb, k):
        mixing_of(layer, bb, [0], [ar_finish(k)])
        corrections_mid(layer, bb)

    def spot_of(j):
        return watt.at[j // 4, j % 4]

    def grams_out(layer, bb, k):
        corrections_grams(layer, bb)
        grams = [total_of("g", bb, 0)]
        d_moments, *rest = grams_of(layer, grams)
        ar_launch(k, 0, d_moments[0])
        projections_of(layer, bb, [0], *rest, grams)
        for j in small:
            gram = total_of("g", bb, j)
            spot_of(j)[...] = gram[:D]
            own_sums[j] = gram[D:]

    def small_back(layer, bb):
        grams = [cat([spot_of(j)[...], own_sums[j]]) for j in small]
        d_moments, *rest = grams_of(layer, grams)
        projections_of(layer, bb, small, *rest, grams)
        back_of(layer, bb, small, d_moments)

    def grams_in(layer, bb, k):
        back_of(layer, bb, [0], [ar_finish(k)])
        corrections_back(layer, bb)

    vec[...] = jnp.zeros(vec.shape, F32)
    vec_c[...] = jnp.zeros(vec_c.shape, F32)

    targets = (act_hbm, grd_hbm)

    def kept(kind, layer, bb):
        return pltpu.make_async_copy(
            stage.at[layer, bb], targets[kind].at[c * per + bb], sm["o_local"].at[kind, bb]
        )

    def sent(kind, layer, bb):
        return pltpu.make_async_remote_copy(
            src_ref=stage.at[layer, bb], dst_ref=targets[kind].at[c * per + bb], send_sem=sm["o_send"].at[kind, bb],
            recv_sem=sm["o_recv"].at[kind, bb], device_id={"section": other}, device_id_type=MESH,
        )

    def came(kind, layer, bb):
        return pltpu.make_async_remote_copy(
            src_ref=stage.at[layer, bb], dst_ref=targets[kind].at[other * per + bb], send_sem=sm["o_send"].at[kind, bb],
            recv_sem=sm["o_recv"].at[kind, bb], device_id={"section": other}, device_id_type=MESH,
        )

    def ship(kind, layer, bb):
        @pl.when(c == layer)
        def _():
            kept(kind, layer, bb).start()

        @pl.when(c != layer)
        def _():
            sent(kind, layer, bb).start()

    def shipped(kind, layer, bb):
        @pl.when(c == layer)
        def _():
            kept(kind, layer, bb).wait()

        @pl.when(c != layer)
        def _():
            sent(kind, layer, bb).wait_send()

    def load_t(layer, bb, subs):
        return cat([stage[layer, bb, sub].T for sub in subs], 1)

    def save_t(layer, bb, subs, value):
        for at, sub in enumerate(subs):
            stage[layer, bb, sub] = part(value, at).T

    def start_stage(bb, subs):
        high, low = split(load_t(0, bb, subs))
        pair = cat([high, low])
        save(hs, (0, bb), subs, pair)
        keys_and_values(0, bb, subs, pair)

    def first_stage(bb, subs):
        out, mid_pair, hid_pair, slope = feed_forward(0, bb, subs)
        save(mids, (bb,), subs, mid_pair)
        save(hids, (bb,), subs, hid_pair)
        save(gps, (bb,), subs, slope)
        save_t(0, bb, subs, out)
        high, low = split(out)
        pair = cat([high, low])
        save(hs, (1, bb), subs, pair)
        keys_and_values(1, bb, subs, pair)

    def second_stage(bb, subs):
        out, mid_pair, hid_pair, slope = feed_forward(1, bb, subs)
        upstream = load_t(1, bb, subs)
        save_t(1, bb, subs, out)
        feed_back(1, bb, subs, upstream, mid_pair, hid_pair, slope)

    def third_stage(bb, subs):
        upstream = input_back(1, bb, subs, norm_back(1, bb, subs))
        save_t(1, bb, subs, upstream)
        held = [load(ref, (bb,), subs) for ref in (mids, hids, gps)]
        feed_back(0, bb, subs, upstream, *held)

    def fifth_stage(bb, subs):
        save(kvs, (0, bb), subs, norm_back(0, bb, subs))

    def sixth_stage(bb, subs):
        save_t(0, bb, subs, input_back(0, bb, subs, load(kvs, (0, bb), subs)))

    scattered = scattered_digits(digits)
    sizes, phases = [], []
    for kind, deep in enumerate(scattered):
        sizes.append([parts_rows[kind]])
        for _, radix in digits[:deep]:
            sizes[-1].append(sizes[-1][-1] // radix)
        phases.append(
            [("scatter", digit) for digit in range(deep)]
            + [("exchange", digit) for digit in range(deep, len(digits))]
            + [("gather", digit) for digit in reversed(range(deep))]
        )
    g_send, g_recv = sm["g_send"], sm["g_recv"]

    def early_rows(layer):
        gb[layer, R_O : R_O + FF] = sm["d_outer"][layer]
        d_inner = sm["d_inner"][layer]
        for at in range(0, FF, D):
            gb[layer, R_I + at : R_I + at + D] = d_inner[at : at + D].T

    def late_lines(layer):
        s_du = mm_nt(ones8, sm["s_du"][layer])
        s_g = mm_nt(ones8, sm["s_g"][layer])
        lines = [vec[layer, 0], None, None, vec[layer, 1]]
        lines += [mm_nt(ones8, expand(vec_c[layer, at])) for at in (0, 1)]
        lines += [jnp.sum(vec_c[layer, at], axis=0, keepdims=True) for at in (2, 3)]
        lines += [s_g, s_du[:, :D], s_du[:, D:]]
        block = jnp.zeros((16, D), F32)
        row16 = lax.broadcasted_iota(jnp.int32, (16, D), 0)
        for at, line in enumerate(lines):
            if line is not None:
                block = jnp.where(row16 == at, line[0:1], block)
        gb[layer, R_VEC : R_VEC + 16] = block

    def late_rows(layer):
        d_kv = sm["d_kv"][layer]
        gb[layer, R_K : R_K + D] = d_kv[:D].T
        gb[layer, R_V : R_V + D] = d_kv[D:].T
        s_dz = mm_nt(ones8, sm["s_dz"][layer])
        gb[layer, R_VEC + 1 : R_VEC + 2] = s_dz[0:1, :D]
        gb[layer, R_VEC + 2 : R_VEC + 3] = s_dz[0:1, D:]

    def block_of(kind, depth, at=None):
        low = 0 if kind == 0 else parts_rows[0]
        for digit in range(depth):
            offset = at if (at is not None and digit == depth - 1) else 0
            low = low + digit_at(digit, offset) * sizes[kind][digit + 1]
        return pl.ds(low if depth == 0 else pl.multiple_of(low, 8), sizes[kind][depth])

    def landing(kind, digit):
        return sm["rb%d%d" % (kind, digit)]

    def scatter_first(layer, kind, offset, far):
        radix = digits[0][1]
        slot = radix - 1 + offset if far else offset - 1
        target = {"section": other, "pts": partner(0, offset)} if far else {"pts": partner(0, offset)}
        return pltpu.make_async_remote_copy(
            src_ref=gb.at[layer, block_of(kind, 1, offset)], dst_ref=landing(kind, 0).at[slot],
            send_sem=g_send.at[kind, 0, 0, slot], recv_sem=g_recv.at[kind, 0, 0, slot],
            device_id=target, device_id_type=MESH,
        )

    def scatter_next(layer, kind, digit, offset):
        return pltpu.make_async_remote_copy(
            src_ref=gb.at[layer, block_of(kind, digit + 1, offset)], dst_ref=landing(kind, digit).at[offset - 1],
            send_sem=g_send.at[kind, 0, digit, offset - 1], recv_sem=g_recv.at[kind, 0, digit, offset - 1],
            device_id={"pts": partner(digit, offset)}, device_id_type=MESH,
        )

    def gather(kind, digit, offset, at):
        spot = gsum_hbm.at[block_of(kind, digit + 1, at)]
        made_here = at == 0 and digit == scattered[kind] - 1
        return pltpu.make_async_remote_copy(
            src_ref=sm["done%d" % kind] if made_here else spot, dst_ref=spot,
            send_sem=g_send.at[kind, 1, digit, offset - 1], recv_sem=g_recv.at[kind, 1, digit, offset - 1],
            device_id={"pts": partner(digit, offset)}, device_id_type=MESH,
        )

    def keep_done(kind):
        spot = gsum_hbm.at[block_of(kind, scattered[kind])]
        return pltpu.make_async_copy(sm["done%d" % kind], spot, sm["done_sem"].at[kind])

    def exchange(kind, digit, offset, back=0):
        spot = sm["wide%d" % kind].at[digit - scattered[kind], digit_at(digit, back)]
        return pltpu.make_async_remote_copy(
            src_ref=spot, dst_ref=spot,
            send_sem=g_send.at[kind, 0, digit, offset - 1], recv_sem=g_recv.at[kind, 0, digit, offset - 1],
            device_id={"pts": partner(digit, offset)}, device_id_type=MESH,
        )

    def outgoing(layer, kind, phase, far=False):
        name, digit = phase
        offsets = range(0 if far else 1, digits[digit][1])
        if name == "scatter" and digit == 0:
            return [scatter_first(layer, kind, offset, far) for offset in offsets]
        if far:
            return []
        if name == "scatter":
            return [scatter_next(layer, kind, digit, offset) for offset in offsets]
        if name == "exchange":
            return [exchange(kind, digit, offset) for offset in offsets]
        return [gather(kind, digit, offset, 0) for offset in offsets]

    def land(layer, kind, phase):
        name, digit = phase
        radix = digits[digit][1]
        if name == "gather":
            for offset in range(1, radix):
                gather(kind, digit, offset, radix - offset).wait_recv()
            return None
        if name == "exchange":
            for offset in range(1, radix):
                exchange(kind, digit, offset, radix - offset).wait_recv()
            held = sm["wide%d" % kind]
            total = held[digit - scattered[kind], 0]
            for at in range(1, radix):
                total = total + held[digit - scattered[kind], at]
            return total
        total = gb[layer, block_of(kind, digit + 1)]
        for copy in outgoing(layer, kind, phase):
            copy.wait_recv()
        for at in range(radix - 1):
            total = total + landing(kind, digit)[at]
        if digit == 0:
            for copy in outgoing(layer, kind, phase, True):
                copy.wait_recv()
            for at in range(radix):
                total = total + landing(kind, 0)[radix - 1 + at]
        return total

    def gradient_step(layer, kind, step):
        todo = phases[kind]
        if step == 0:
            @pl.when(c != layer)
            def _():
                for copy in outgoing(layer, kind, todo[0], True):
                    copy.start()

        if step <= len(todo):
            @pl.when(c == layer)
            def _():
                total = None if step == 0 else land(layer, kind, todo[step - 1])
                if step == len(todo):
                    return
                name, digit = todo[step]
                if total is not None:
                    if name == "scatter":
                        gb[layer, block_of(kind, digit)] = total
                    elif name == "exchange":
                        sm["wide%d" % kind][digit - scattered[kind], digit_at(digit)] = total
                    else:
                        sm["done%d" % kind][...] = total
                        keep_done(kind).start()
                elif name == "gather" and digit == scattered[kind] - 2:
                    keep_done(kind).wait()
                for copy in outgoing(layer, kind, todo[step]):
                    copy.start()

    def gradient_rest(layer, kind, step):
        for left in range(step, len(phases[kind]) + 1):
            gradient_step(layer, kind, left)

    def drain_gradients():
        for layer in range(2):
            for kind in range(2):
                @pl.when(c == layer)
                def _():
                    for phase in phases[kind]:
                        for copy in outgoing(layer, kind, phase):
                            copy.wait_send()
                    if scattered[kind] == 1:
                        keep_done(kind).wait()

                @pl.when(c != layer)
                def _():
                    for copy in outgoing(layer, kind, phases[kind][0], True):
                        copy.wait_send()

    EARLY, LATE = 0, 1

    def together(*actions):
        def run():
            for action in actions:
                action()

        return run

    def grad(layer, kind, step):
        return functools.partial(gradient_step, layer, kind, step)

    call = functools.partial
    prepare_projections(0)
    for bb in range(per):
        x_copy(bb).wait()
        if bb == 0:
            loop(call(start_stage, bb))
        else:
            loop(call(start_stage, bb), call(ar_step, key_of(0, bb - 1), 1), call(small_mixing, 0, bb - 1))
        moments_out(0, bb, key_of(0, bb))
        if bb == 0:
            prepare(0)
    prepare_projections(1)
    prepare(1)
    gb[...] = jnp.zeros(gb.shape, F32)
    ar_step(key_of(0, per - 1), 1)

    def step_of(stage, bb):
        if bb > 0:
            return call(ar_step, key_of(stage, bb - 1), 1)
        return (lambda: None) if stage == 1 else call(ar_step, key_of(stage - 1, per - 1), 1)

    for bb in range(per):
        mixing_in(0, bb, key_of(0, bb))
        filler = call(small_mixing, 0, per - 1) if bb == 0 else call(small_mixing, 1, bb - 1)
        loop(call(first_stage, bb), step_of(1, bb), filler)
        ship(0, 0, bb)
        moments_out(1, bb, key_of(1, bb))
    for bb in range(per):
        cot_copy(bb).wait()
        mixing_in(1, bb, key_of(1, bb))
        filler = call(small_mixing, 1, per - 1) if bb == 0 else call(small_back, 1, bb - 1)
        loop(call(second_stage, bb), step_of(2, bb), filler)
        ship(0, 1, bb)
        grams_out(1, bb, key_of(2, bb))
    early_rows(1)
    for bb in range(per):
        grams_in(1, bb, key_of(2, bb))
        shipped(0, 1, bb)
        filler = call(small_back, 1, per - 1) if bb == 0 else call(small_back, 0, bb - 1)
        beside = [step_of(3, bb)] + ([grad(1, EARLY, 1)] if bb == 1 else [])
        loop(call(third_stage, bb), together(*beside), filler)
        ship(1, 1, bb)
        if bb == 0:
            gradient_step(1, EARLY, 0)
        grams_out(0, bb, key_of(3, bb))
    early_rows(0)
    late_lines(1)
    late_rows(1)
    gradient_step(1, LATE, 0)
    gradient_step(1, EARLY, 2)
    for bb in range(per):
        grams_in(0, bb, key_of(3, bb))
        shipped(0, 0, bb)
        if bb == 0:
            beside = [step_of(4, bb), grad(0, EARLY, 0), grad(1, LATE, 1), grad(1, EARLY, 3)]
            loop(call(fifth_stage, bb), together(*beside), ahead=call(small_back, 0, per - 1))
        elif bb == 1:
            late_lines(0)
            loop(call(fifth_stage, bb), together(grad(0, EARLY, 1), grad(1, LATE, 2), grad(1, EARLY, 4)))
        else:
            loop(call(fifth_stage, bb))
    late_rows(0)
    gradient_step(0, LATE, 0)
    gradient_step(0, EARLY, 2)
    gradient_rest(1, EARLY, 5)
    gradient_rest(1, LATE, 3)
    for bb in range(per):
        loop(call(sixth_stage, bb))
        ship(1, 0, bb)
        if bb == 0:
            gradient_step(0, LATE, 1)
            gradient_step(0, EARLY, 3)
    for k in range(4):
        weight_send(k).wait_send()
    for k in range(4 * per):
        ar_drain(k)
    gradient_step(0, LATE, 2)
    gradient_rest(0, EARLY, 4)
    gradient_rest(0, LATE, 3)

    drain_gradients()
    for bb in range(per):
        for layer in range(2):
            shipped(1, layer, bb)
        for layer in range(2):
            @pl.when(c == layer)
            def _():
                came(0, layer, bb).wait_recv()
                came(1, layer, bb).wait_recv()


def finishing(scale, D, FF, first, act, grd, gsum_hbm, *refs):
    sources, results = refs[:12], refs[12:30]
    gsum, held, made, through, sem_large, sem_in, sem_out = refs[30], refs[31:43], refs[43:59], *refs[59:]
    large, onward = [], []
    for kind, (source, target) in enumerate(((act, results[0]), (grd, results[1]))):
        for part in range(source.shape[0]):
            spot = through.at[kind, part]
            large.append(pltpu.make_async_copy(source.at[part], spot, sem_large.at[0, kind, part]))
            onward.append(pltpu.make_async_copy(spot, target.at[part], sem_large.at[1, kind, part]))
    loads = [pltpu.make_async_copy(gsum_hbm, gsum, sem_in.at[12])]
    loads += [pltpu.make_async_copy(sources[at], held[at], sem_in.at[at]) for at in range(12)]
    for copy in loads:
        copy.start()
    for copy in large:
        copy.start()
    rate = plan()

    def step(weight, gradient, momentum, variance):
        average = gradient * scale
        new_momentum = 0.9 * momentum + 0.1 * average
        new_variance = 0.999 * variance + 0.001 * average * average
        mean = new_momentum / (1.0 - 0.9**STEP)
        square = new_variance / (1.0 - 0.999**STEP)
        updated = weight - rate * (mean / (jnp.sqrt(square) + 1e-08) + 0.01 * weight)
        return gradient, new_momentum, new_variance, updated

    parts = [first[name] for name in ("q", "k", "v", "o")]
    inner, outer, late = first["inner"], first["outer"], first["vec"]
    places = [
        [((0, at), slice(low, low + D)) for at, low in enumerate(parts)],
        [((0, slice(None), slice(at, at + D)), slice(inner + at, inner + at + D)) for at in range(0, FF, D)],
        [((0,), slice(outer, outer + FF))],
        [((line,), slice(late + line, late + line + 1)) for line in range(held[3].shape[0])],
    ]
    for copy, after in zip(large, onward):
        copy.wait()
        after.start()
    loads[0].wait()
    stores = []
    for kind in range(4):
        for at in (kind, 4 + 2 * kind, 5 + 2 * kind):
            loads[1 + at].wait()
        weight, momentum, variance = held[kind], held[4 + 2 * kind], held[5 + 2 * kind]
        for index, lines in places[kind]:
            values = step(weight[index], gsum[lines], momentum[index], variance[index])
            for ref, value in zip(made[4 * kind : 4 * kind + 4], values):
                ref[index] = value
        for at in range(4 * kind, 4 * kind + 4):
            stores.append(pltpu.make_async_copy(made[at], results[2 + at], sem_out.at[at]))
            stores[-1].start()
    for copy in onward + stores:
        copy.wait()


def per_device(
    node_features, cotangent, lengths, attention_weight, inner_weight, outer_weight, vectors,
    momentum_attention, variance_attention, momentum_inner, variance_inner,
    momentum_outer, variance_outer, momentum_vectors, variance_vectors,
):
    places = lax.axis_size("pts")
    micro, rows, D = node_features.shape
    FF = inner_weight.shape[-1]
    segs = lengths.shape[1]
    lines = vectors.shape[1]
    nsub = rows // SUB
    per = micro // 2
    digits = digits_of(places)
    group = D // HEADS
    first, parts_rows = gradient_rows(D, FF, digits)
    total_rows = sum(parts_rows)
    nar = 4 * per

    def f32(*shape):
        return pltpu.VMEM(shape, F32)

    def b16(*shape):
        return pltpu.VMEM(shape, BF16)

    def dma(*shape):
        return pltpu.SemaphoreType.DMA(shape)

    scratch = dict(
        watt=f32(2, 4, D, D), winn=f32(2, D, FF), wout=f32(2, FF, D), wvec=f32(2, lines, 1, D),
        tab=pltpu.SMEM((per, 4 * nsub + 12 * segs), jnp.int32),
        tables=f32(2, 7, D, 128), packed=f32(2, 3, group, D),
        wq_t=b16(2, D, 2 * D), w3_t=b16(2, D, 2 * D), wq_right=b16(2, 3 * D, 2 * D), w3_right=b16(2, 3 * D, D),
        kvw=b16(2, 2 * D, 2 * D), kvw_back=b16(2, D, 4 * D),
        inn_t=b16(2, FF, 2 * D), inn=b16(2, D, 2 * FF), out_t=b16(2, D, 2 * FF), out=b16(2, FF, 2 * D),
        hs=b16(2, per, nsub, 2 * D, SUB), kvs=b16(2, per, nsub, 4 * D, SUB),
        rst=f32(2, per, nsub, 2 * HEADS, SUB), dms=b16(per, nsub, 2 * D, SUB),
        mids=b16(per, nsub, 2 * D, SUB), hids=b16(per, nsub, 2 * FF, SUB), gps=f32(per, nsub, FF, SUB),
                stage=f32(2, per, nsub, SUB, D),
        zm=f32(per, segs, D, SUB), zk=f32(segs, D, SUB), zv=f32(segs, D, SUB),
        acc_c=f32(nsub + 1, group + 8, D), acc_n=f32(nsub + 1, D, 128), acc_g=f32(nsub + 1, D + 16, D),
        corr_c=f32(segs, group + 8, D), corr_n=f32(segs, D, 128), corr_g=f32(segs, D + 16, D),
        stats=f32(2, per, segs, 2 * group + 8, D), own_c=f32(per, segs, group, D), own_sums=f32(segs, 16, D),
        mt=b16(2, per, segs, D, 2 * D), vec_c=f32(2, 4, group, D),
        mat_a=b16(per, segs, D, 2 * D), add_a=f32(per, segs, D, 128), back_mat=b16(2, per, segs, D, 2 * D),
        mat_b=b16(per, segs, D, 2 * D), add_b=f32(per, segs, D, 128),
        d_outer=f32(2, FF, D), d_inner=f32(2, FF, D), d_kv=f32(2, 2 * D, D),
        s_du=f32(2, FF, 128), s_g=f32(2, D, 128), s_dz=f32(2, 2 * D, 128),
        vec=f32(2, 2, 8, D), gb=f32(2, total_rows, D),
        ar=f32(nar, len(digits), 4, group, D),
        dma_in=dma(2 * per + 4), w_send=dma(4), w_recv=dma(4),
        ar_send=dma(nar, len(digits), 3), ar_recv=dma(nar, len(digits), 3),
        o_local=dma(2, per), done_sem=dma(2), o_send=dma(2, per), o_recv=dma(2, per),
        g_send=dma(2, 2, len(digits), 7), g_recv=dma(2, 2, len(digits), 7),
    )
    for kind, (size, count) in enumerate(zip(parts_rows, scattered_digits(digits))):
        for digit, (_, radix) in enumerate(digits[:count]):
            size //= radix
            scratch["done%d" % kind] = f32(size, D)
            scratch["rb%d%d" % (kind, digit)] = f32(2 * radix - 1 if digit == 0 else radix - 1, size, D)
        if len(digits) > count:
            scratch["wide%d" % kind] = f32(len(digits) - count, 4, size, D)
    cfg = dict(names=list(scratch), places=places, segs=segs, micro=micro, nsub=nsub, D=D, FF=FF)

    def lined(piece):
        return jnp.transpose(piece, (1, 0, 2))

    anywhere = pl.BlockSpec(memory_space=pl.ANY)
    tiled = (micro, nsub, SUB, D)
    act, grd, gsum = pl.pallas_call(
        functools.partial(mega, cfg),
        out_shape=(
            jax.ShapeDtypeStruct(tiled, F32), jax.ShapeDtypeStruct(tiled, F32),
            jax.ShapeDtypeStruct((total_rows, D), F32),
        ),
        in_specs=[anywhere, anywhere, pl.BlockSpec(memory_space=pltpu.SMEM)] + [anywhere] * 4,
        out_specs=(anywhere, anywhere, anywhere),
        scratch_shapes=list(scratch.values()),
        compiler_params=pltpu.CompilerParams(
            collective_id=0, has_side_effects=True, vmem_limit_bytes=255 * 2**18
        ),
        name="layers",
    )(
        node_features.reshape(tiled), cotangent.reshape(tiled), lengths,
        attention_weight, inner_weight, outer_weight, lined(vectors),
    )
    scale = 1.0 / (micro * rows * places)
    held = [attention_weight, inner_weight, outer_weight, vectors]
    moments = [
        momentum_attention, variance_attention, momentum_inner, variance_inner,
        momentum_outer, variance_outer, momentum_vectors, variance_vectors,
    ]
    held[3] = lined(vectors)
    moments[6:] = [lined(momentum_vectors), lined(variance_vectors)]
    shapes = [jax.ShapeDtypeStruct(piece.shape, F32) for piece in held for _ in range(4)]
    results = pl.pallas_call(
        functools.partial(finishing, scale, D, FF, first),
        out_shape=tuple([jax.ShapeDtypeStruct(tiled, F32)] * 2 + shapes),
        in_specs=[pl.BlockSpec(memory_space=pltpu.HBM)] * 15,
        out_specs=tuple([pl.BlockSpec(memory_space=pltpu.HBM)] * 18),
        scratch_shapes=[f32(total_rows, D)] + [f32(*piece.shape) for piece in held + moments]
        + [f32(*shape.shape) for shape in shapes] + [f32(2, *tiled), dma(2, 2, micro), dma(13), dma(16)],
        compiler_params=pltpu.CompilerParams(vmem_limit_bytes=60 * 2**20),
        name="adamw",
    )(act, grd, gsum, *held, *moments)
    whole = (1, micro, rows, D)
    lines_back = tuple(lined(piece) for piece in results[14:])
    return (results[0].reshape(whole), results[1].reshape(whole)) + tuple(results[2:14]) + lines_back


def solution(mesh):
    first = P("section", None, None)
    attention = P("section", None, None, None)
    nodes = P(None, "pts", None)
    return jax.shard_map(
        per_device,
        mesh=mesh,
        in_specs=(nodes, nodes, P(), attention, first, first, first, attention, attention) + (first,) * 6,
        out_specs=(P("section", None, "pts", None),) * 2 + (attention,) * 4 + (first,) * 12,
        check_vma=False,
    )
```

```python
import functools
import math

import jax
import jax.numpy as jnp
from jax import lax
from jax.experimental import pallas as pl
from jax.experimental.pallas import tpu as pltpu
from jax.sharding import PartitionSpec as P

HEADS = 4
STEP = 1200
TOTAL_STEPS = 4000
EPS_NORM = 1e-05
SUB = 256
TILE = 1024

MESH = pl.DeviceIdType.MESH
HIGHEST = lax.Precision.HIGHEST
F32 = jnp.float32
BF16 = jnp.bfloat16


def plan():
    warm = 0.3 * TOTAL_STEPS
    top = 0.001
    start = top / 25.0
    low = start / 10000.0
    if STEP <= warm:
        return start + (top - start) * (1.0 - math.cos(math.pi * STEP / warm)) / 2.0
    return low + (top - low) * (1.0 + math.cos(math.pi * (STEP - warm) / (TOTAL_STEPS - warm))) / 2.0


def cat(parts, axis=0):
    return jnp.concatenate(parts, axis=axis)


def split(value):
    high = value.astype(BF16)
    return high, (value - high.astype(F32)).astype(BF16)


def pack3(weight):
    high, low = split(weight)
    return cat([high, high, low], 1)


def pack2(weight):
    return cat(list(split(weight)), 1)


def left3(pack):
    size = pack.shape[1] // 2
    return cat([pack[:, :size], pack], 1)


def right3(value):
    high, low = split(value)
    return cat([high, low, high])


def dot16(left, right):
    return jnp.dot(left, right, preferred_element_type=F32)


def outer16(left, right):
    full = lax.dot_general(left, right, (((1,), (1,)), ((), ())), preferred_element_type=F32)
    m, n = full.shape[0] // 2, full.shape[1] // 2
    return full[:m, :n] + full[m:, :n] + full[:m, n:]


def outer16_sums(left, right):
    ones = jnp.ones((16, left.shape[1]), BF16)
    full = lax.dot_general(cat([left, ones]), right, (((1,), (1,)), ((), ())), preferred_element_type=F32)
    m, n = left.shape[0] // 2, full.shape[1] // 2
    return cat([full[:m, :n] + full[m : 2 * m, :n] + full[:m, n:], full[2 * m :, :n] + full[2 * m :, n:]])


def mm_nt(left, right, precision=HIGHEST):
    return lax.dot_general(left, right, (((1,), (1,)), ((), ())), precision=precision, preferred_element_type=F32)


def wide(table, width):
    return cat([table] * (width // 128), 1)


def fold(value):
    total = value[:, :128]
    for at in range(128, value.shape[1], 128):
        total = total + value[:, at : at + 128]
    return total


def digits_of(places):
    found, stride = [], 1
    while stride < places:
        radix = 4 if (places // stride) % 4 == 0 else 2
        found.append((stride, radix))
        stride *= radix
    return found


def scattered_digits(digits):
    return min(2, len(digits)), 1


def gradient_rows(D, FF, digits):
    sizes = []
    for count, least in zip(scattered_digits(digits), (2 * FF + 2 * D, 2 * D + 16)):
        unit = 8
        for _, radix in digits[:count]:
            unit *= radix
        sizes.append(-(-least // unit) * unit)
    early = sizes[0]
    first = dict(outer=0, inner=FF, q=2 * FF, o=2 * FF + D, k=early, v=early + D, vec=early + 2 * D)
    return first, sizes


def mega(cfg, x_hbm, cot_hbm, len_s, att_hbm, inn_hbm, out_hbm, vec_hbm, act_hbm, grd_hbm, gsum_hbm, *scratch):
    sm = dict(zip(cfg["names"], scratch))
    places, segs, micro, nsub = cfg["places"], cfg["segs"], cfg["micro"], cfg["nsub"]
    rows = nsub * SUB
    tokens = rows * places
    per = micro // 2
    D = cfg["D"]
    FF = cfg["FF"]
    group = D // HEADS
    digits = digits_of(places)
    c = lax.axis_index("section")
    place = lax.axis_index("pts")
    other = 1 - c

    stage = sm["stage"]

    dma_in = sm["dma_in"]
    watt, winn, wout, wvec = sm["watt"], sm["winn"], sm["wout"], sm["wvec"]

    def x_copy(bb):
        return pltpu.make_async_copy(x_hbm.at[c * per + bb], stage.at[0, bb], dma_in.at[bb])

    def cot_copy(bb):
        return pltpu.make_async_copy(cot_hbm.at[c * per + bb], stage.at[1, bb], dma_in.at[per + bb])

    weights = [(att_hbm.at[0], watt), (inn_hbm.at[0], winn), (out_hbm.at[0], wout), (vec_hbm, wvec)]

    def weight_copy(k):
        source, held = weights[k]
        return pltpu.make_async_copy(source, held.at[c], dma_in.at[2 * per + k])

    def weight_send(k):
        source, held = weights[k]
        return pltpu.make_async_remote_copy(
            src_ref=source, dst_ref=held.at[c], send_sem=sm["w_send"].at[k], recv_sem=sm["w_recv"].at[k],
            device_id={"section": other}, device_id_type=MESH,
        )

    def weight_arrival(k):
        source, held = weights[k]
        return pltpu.make_async_remote_copy(
            src_ref=source, dst_ref=held.at[other], send_sem=sm["w_send"].at[k], recv_sem=sm["w_recv"].at[k],
            device_id={"section": other}, device_id_type=MESH,
        )

    x_copy(0).start()
    for k in (0, 3, 1, 2):
        weight_copy(k).start()
    for bb in range(1, per):
        x_copy(bb).start()
    for bb in range(per):
        cot_copy(bb).start()

    def partner(digit, offset):
        stride, radix = digits[digit]
        mine = (place // stride) % radix
        theirs = (mine + offset) % radix
        return place + (theirs - mine) * stride

    def digit_at(digit, offset=0):
        stride, radix = digits[digit]
        return ((place // stride) % radix + offset) % radix

    barrier = pltpu.get_barrier_semaphore()
    greeted = 1
    pl.semaphore_signal(barrier, inc=1, device_id={"section": other}, device_id_type=MESH)
    for digit, (stride, radix) in enumerate(digits):
        for offset in range(1, radix):
            pl.semaphore_signal(barrier, inc=1, device_id={"pts": partner(digit, offset)}, device_id_type=MESH)
            greeted += 1

    for offset in range(1, digits[0][1]):
        pl.semaphore_signal(
            barrier, inc=1, device_id={"section": other, "pts": partner(0, offset)}, device_id_type=MESH
        )
        greeted += 1

    tab = sm["tab"]
    T_SLOT, T_END, T_ZI, T_KEEP = 0, nsub, 2 * nsub, 3 * nsub
    T_C, T_LO, T_HI, T_CS, T_ZK, T_LAST, T_CIDX, T_NLOC, T_CNT, T_LS, T_LE, T_OK = (
        4 * nsub + at * segs for at in range(12)
    )
    base = place * rows
    zero = jnp.int32(0)

    for bb in range(per):
        batch = c * per + bb
        lens = [len_s[batch, s] for s in range(segs)]
        ends, run = [], zero
        for s in range(segs):
            run = run + lens[s]
            ends.append(run)
        starts = [zero] + ends[:-1]
        big = zero
        for s in range(1, segs):
            big = big + jnp.where(starts[s] <= rows - 1, 1, 0)
        before = zero
        for s in range(segs):
            before = before + jnp.where(ends[s] <= tokens - rows, 1, 0)
        big = jnp.minimum(big, before)
        local_start = [jnp.clip(starts[s] - base, -1, rows) for s in range(segs)]
        local_end = [jnp.clip(ends[s] - base, 0, rows) for s in range(segs)]
        cells, valid = [zero], [zero]
        tab[bb, T_C] = zero
        tab[bb, T_OK] = zero
        for s in range(segs):
            tab[bb, T_LS + s] = local_start[s]
            tab[bb, T_LE + s] = local_end[s]
            slot = jnp.where(s == big, 0, jnp.where(s < big, s + 1, s))
            tab[bb, T_CS + s] = slot
            if s > 0:
                at = local_start[s]
                inside = jnp.maximum(at, 0)
                cell = jnp.minimum(inside // SUB, nsub - 1)
                low = inside - cell * SUB
                ok = jnp.where((at > 0) & (at < rows) & (low > 0), 1, 0)
                cells.append(cell)
                valid.append(ok)
                tab[bb, T_C + s] = cell
                tab[bb, T_OK + s] = ok
                tab[bb, T_LO + s] = jnp.where(ok == 1, low, SUB)
                tab[bb, T_HI + s] = jnp.where(ok == 1, jnp.minimum(local_end[s] - cell * SUB, SUB), 0)
                tab[bb, T_ZK + s] = ok * valid[s - 1] * jnp.where(cell == cells[s - 1], 1, 0)
        past = None
        for sub in range(nsub):
            row = sub * SUB
            first, final = zero, zero
            for s in range(segs - 1):
                first = first + jnp.where(local_end[s] <= row, 1, 0)
                final = final + jnp.where(local_end[s] <= row + SUB - 1, 1, 0)
            tab[bb, T_SLOT + sub] = tab[bb, T_CS + first]
            tab[bb, T_END + sub] = jnp.minimum(tab[bb, T_LE + first] - row, SUB)
            tab[bb, T_KEEP + sub] = zero if past is None else jnp.where(first == past, 1, 0)
            tab[bb, T_ZI + sub] = jnp.where(final == first, 0, final)
            past = first
        for j in range(segs):
            s = big if j == 0 else jnp.where(j - 1 < big, j - 1, j)
            low, high = tab[bb, T_LS + s], tab[bb, T_LE + s]
            cell = jnp.maximum(high - 1, 0) // SUB
            tab[bb, T_LAST + j] = jnp.where((high > 0) & (low < rows) & (cell * SUB >= low), cell, nsub)
            tab[bb, T_CIDX + j] = jnp.where(tab[bb, T_OK + s] == 1, s, 0)
            tab[bb, T_NLOC + j] = high - jnp.maximum(low, 0)
            tab[bb, T_CNT + j] = len_s[batch, s]

    lane_head = lax.broadcasted_iota(jnp.int32, (group, D), 1) // group
    block_mask = (
        lax.broadcasted_iota(jnp.int32, (D, D), 0) // group == lax.broadcasted_iota(jnp.int32, (D, D), 1) // group
    ).astype(F32)
    ones8 = jnp.ones((8, 128), F32)
    row8 = lax.broadcasted_iota(jnp.int32, (8, D), 0)

    def lanes():
        return lax.broadcasted_iota(jnp.int32, (1, SUB), 1)

    def compact(square):
        total = None
        for j in range(HEADS):
            piece = jnp.where(lane_head == j, square[group * j : group * (j + 1), :], 0.0)
            total = piece if total is None else total + piece
        return total

    def moment_rows(product):
        return cat([compact(product[:D]), product[D : D + 8]])

    def expand(packed):
        return cat([packed] * HEADS, 0) * block_mask

    def centred(matrix):
        grouped = matrix.reshape(matrix.shape[0] // group, group, matrix.shape[1])
        return (grouped - jnp.mean(grouped, axis=1, keepdims=True)).reshape(matrix.shape)

    for bb in range(per):
        sm["zm"][bb, 0] = jnp.zeros((D, SUB), F32)
    for name in ("zk", "zv", "corr_c", "corr_n", "corr_g"):
        sm[name][0] = jnp.zeros(sm[name].shape[1:], F32)
    for name in ("acc_c", "acc_n", "acc_g"):
        sm[name][nsub] = jnp.zeros(sm[name].shape[1:], F32)
    for name in ("d_outer", "d_inner", "d_kv", "s_du", "s_g", "s_dz"):
        sm[name][...] = jnp.zeros(sm[name].shape, F32)
    gb = sm["gb"]
    first, parts_rows = gradient_rows(D, FF, digits)
    R_Q, R_K, R_V, R_3, R_I, R_O, R_VEC = (first[name] for name in ("q", "k", "v", "o", "inner", "outer", "vec"))

    pl.semaphore_wait(barrier, greeted)
    for k in (0, 3, 1, 2):
        weight_send(k).start()

    tables = sm["tables"]

    def arrived(layer, k):
        @pl.when(c == layer)
        def _():
            weight_copy(k).wait()

        @pl.when(c != layer)
        def _():
            weight_arrival(k).wait_recv()

    def column(layer, row):
        return jnp.broadcast_to(wvec[layer, row], (128, D)).T

    def prepare_projections(layer):
        arrived(layer, 0)
        arrived(layer, 3)
        for row in (1, 2):
            tables[layer, row] = centred(column(layer, row))
        packed = sm["packed"]
        packed[layer, 0] = compact(1.0 + column(layer, 4))
        packed[layer, 1] = compact(column(layer, 5))
        packed[layer, 2] = compact(1.0 + column(layer, 6))
        sm["kvw"][layer] = pack2(cat([centred(watt[layer, 1].T), centred(watt[layer, 2].T)], 0))

    def prepare(layer):
        arrived(layer, 1)
        arrived(layer, 2)

        for at, row in ((0, 0), (3, 3), (4, 8), (5, 9), (6, 10)):
            tables[layer, at] = column(layer, row)
        query_t, output_t = watt[layer, 0].T, watt[layer, 3].T
        sm["wq_t"][layer] = pack2(query_t)
        sm["w3_t"][layer] = pack2(output_t)
        sm["wq_right"][layer] = right3(cat([query_t, tables[layer, 0]], 1))
        sm["w3_right"][layer] = right3(output_t)
        sm["kvw_back"][layer] = cat([pack2(watt[layer, 1]), pack2(watt[layer, 2])], 1)
        inner = winn[layer]
        sm["inn_t"][layer] = pack2(cat([inner[:, at : at + D].T for at in range(0, FF, D)], 0))
        sm["inn"][layer] = pack2(inner)
        outer = wout[layer]
        sm["out_t"][layer] = pack2(cat([outer[at : at + D, :].T for at in range(0, FF, D)], 1))
        sm["out"][layer] = pack2(outer)

    ar = sm["ar"]

    def ar_copy(k, digit, offset):
        spot = ar.at[k, digit, digit_at(digit)]
        return pltpu.make_async_remote_copy(
            src_ref=spot, dst_ref=spot, send_sem=sm["ar_send"].at[k, digit, offset - 1],
            recv_sem=sm["ar_recv"].at[k, digit, offset - 1],
            device_id={"pts": partner(digit, offset)}, device_id_type=MESH,
        )

    def ar_arrival(k, digit, offset):
        radix = digits[digit][1]
        spot = ar.at[k, digit, digit_at(digit, radix - offset)]
        return pltpu.make_async_remote_copy(
            src_ref=spot, dst_ref=spot, send_sem=sm["ar_send"].at[k, digit, offset - 1],
            recv_sem=sm["ar_recv"].at[k, digit, offset - 1],
            device_id={"pts": partner(digit, offset)}, device_id_type=MESH,
        )

    def ar_launch(k, digit, payload):
        ar[k, digit, digit_at(digit)] = payload
        for offset in range(1, digits[digit][1]):
            ar_copy(k, digit, offset).start()

    def ar_land(k, digit):
        radix = digits[digit][1]
        for offset in range(1, radix):
            ar_arrival(k, digit, offset).wait_recv()
        total = ar[k, digit, 0]
        for at in range(1, radix):
            total = total + ar[k, digit, at]
        return total

    def ar_step(k, digit):
        if digit < len(digits):
            ar_launch(k, digit, ar_land(k, digit - 1))

    def ar_finish(k):
        for digit in range(2, len(digits)):
            ar_step(k, digit)
        return ar_land(k, len(digits) - 1)

    def ar_drain(k):
        for digit in range(len(digits)):
            for offset in range(1, digits[digit][1]):
                ar_copy(k, digit, offset).wait_send()

    hs, kvs, rst, dms = sm["hs"], sm["kvs"], sm["rst"], sm["dms"]
    mids, hids, gps = sm["mids"], sm["hids"], sm["gps"]

    def three(pair, at=0, size=D):
        high = pair[at : at + size]
        return [high, pair[at + size : at + 2 * size], high]

    def joined(pairs):
        whole = pairs.astype(F32)
        return cat([whole[:D] + whole[D : 2 * D], whole[2 * D : 3 * D] + whole[3 * D :]])

    def load(ref, lead, subs):
        return cat([ref[(*lead, sub)] for sub in subs], 1)

    def save(ref, lead, subs, value):
        for at, sub in enumerate(subs):
            ref[(*lead, sub)] = value[:, SUB * at : SUB * (at + 1)]

    def part(value, at):
        return value[:, SUB * at : SUB * (at + 1)]

    def inside_of(bb, sub):
        return lanes() < tab[bb, T_END + sub]

    def keys_and_values(layer, bb, subs, pair):
        width = SUB * len(subs)
        bias = cat([wide(tables[layer, 1], width), wide(tables[layer, 2], width)], 0)
        field = dot16(left3(sm["kvw"][layer]), cat(three(pair))) + bias
        grouped = field.reshape(2 * HEADS, group, width)
        spread = jnp.mean(grouped * grouped, axis=1, keepdims=True)
        scale = lax.rsqrt(spread + EPS_NORM)
        normed = (grouped * scale).reshape(2 * D, width)
        save(rst, (layer, bb), subs, scale.reshape(2 * HEADS, width))
        k_high, k_low = split(normed[:D])
        v_high, v_low = split(normed[D:])
        keys, values = cat([k_high, k_low]), cat([v_high, v_low])
        save(kvs, (layer, bb), subs, cat([keys, values]))
        for at, sub in enumerate(subs):
            inside = inside_of(bb, sub)
            product = moment_rows(outer16_sums(part(keys, at), part(values, at) * inside.astype(BF16)))
            sums = fold(jnp.where(inside, part(normed, at)[:D], 0.0))
            keep = tab[bb, T_KEEP + sub] == 1
            past = jnp.maximum(sub - 1, 0)
            sm["acc_c"][sub] = product + jnp.where(keep, sm["acc_c"][past], 0.0)
            sm["acc_n"][sub] = sums + jnp.where(keep, sm["acc_n"][past], 0.0)

    def feed_forward(layer, bb, subs):
        width = SUB * len(subs)
        middles = []
        for sub in subs:
            slot = tab[bb, T_SLOT + sub]
            value = dot16(left3(sm["mat_a"][bb, slot]), cat(three(hs[layer, bb, sub]))) + wide(sm["add_a"][bb, slot], SUB)
            middles.append(jnp.where(inside_of(bb, sub), value, sm["zm"][bb, tab[bb, T_ZI + sub]]))
        middle = cat(middles, 1)
        m_high, m_low = split(middle)
        mid_pair = cat([m_high, m_low])
        u = dot16(left3(sm["inn_t"][layer]), cat(three(mid_pair)))
        u = u + cat([wide(tables[layer, 5], width), wide(tables[layer, 6], width)], 0)
        k0 = 0.7978845608
        square = u * u
        t = jnp.tanh(u * (k0 + (k0 * 0.044715) * square))
        half = 0.5 + 0.5 * t
        hidden = u * half
        slope = half + hidden * (1.0 - t) * (k0 + (3.0 * k0 * 0.044715) * square)
        h_high, h_low = split(hidden)
        hid_pair = cat([h_high, h_low])
        out = middle + dot16(left3(sm["out_t"][layer]), cat(three(hid_pair, 0, FF))) + wide(tables[layer, 4], width)
        return out, mid_pair, hid_pair, slope

    def feed_back(layer, bb, subs, upstream, mid_pair, hid_pair, slope):
        g_high, g_low = split(upstream)
        g_pair = cat([g_high, g_low])
        du = dot16(left3(sm["out"][layer]), cat(three(g_pair))) * slope
        u_high, u_low = split(du)
        u_pair = cat([u_high, u_low])
        d_mid = upstream + dot16(left3(sm["inn"][layer]), cat(three(u_pair, 0, FF)))
        q_high, q_low = split(d_mid)
        q_pair = cat([q_high, q_low])
        save(dms, (bb,), subs, q_pair)
        for at, sub in enumerate(subs):
            q_inside = part(q_pair, at) * inside_of(bb, sub).astype(BF16)
            product = outer16_sums(hs[layer, bb, sub], q_inside)
            keep = tab[bb, T_KEEP + sub] == 1
            past = jnp.maximum(sub - 1, 0)
            sm["acc_g"][sub] = product + jnp.where(keep, sm["acc_g"][past], 0.0)
        sm["d_outer"][layer] += outer16(hid_pair, g_pair)
        sm["d_inner"][layer] += outer16(u_pair, mid_pair)
        sm["s_du"][layer] += fold(du)
        sm["s_g"][layer] += fold(upstream)

    def norm_back(layer, bb, subs):
        width = SUB * len(subs)
        pairs = load(kvs, (layer, bb), subs)
        normed = joined(pairs)
        e_ks, e_vs = [], []
        for at, sub in enumerate(subs):
            slot, zi, inside = tab[bb, T_SLOT + sub], tab[bb, T_ZI + sub], inside_of(bb, sub)
            own = part(pairs, at)
            e_k = dot16(left3(sm["mat_a"][bb, slot]), cat(three(own, 2 * D))) + wide(sm["add_a"][bb, slot], SUB)
            e_v = dot16(left3(sm["mat_b"][bb, slot]), cat(three(own))) + wide(sm["add_b"][bb, slot], SUB)
            e_ks.append(jnp.where(inside, e_k, sm["zk"][zi]))
            e_vs.append(jnp.where(inside, e_v, sm["zv"][zi]))
        e = cat([cat(e_ks, 1), cat(e_vs, 1)])
        shape = (2 * HEADS, group, width)
        e3, n3 = e.reshape(shape), normed.reshape(shape)
        scale = load(rst, (layer, bb), subs).reshape(2 * HEADS, 1, width)
        along = jnp.mean(e3 * n3, axis=1, keepdims=True)
        dz = ((e3 - n3 * along) * scale).reshape(2 * D, width)
        z_high, z_low = split(dz)
        z_pair = cat([z_high, z_low])
        sm["d_kv"][layer] += outer16(z_pair, load(hs, (layer, bb), subs))
        sm["s_dz"][layer] += fold(dz)
        return z_pair

    def input_back(layer, bb, subs, z_pair):
        z_high, z_low = z_pair[: 2 * D], z_pair[2 * D :]
        through = [z_high[:D], z_low[:D], z_high[:D], z_high[D:], z_low[D:], z_high[D:]]
        backs = []
        back = sm["kvw_back"][layer]
        for at, sub in enumerate(subs):
            slot, zi = tab[bb, T_SLOT + sub], tab[bb, T_ZI + sub]
            left = cat([left3(sm["back_mat"][layer, bb, slot]), left3(back[:, : 2 * D]), left3(back[:, 2 * D :])], 1)
            right = three(dms[bb, sub] * inside_of(bb, sub).astype(BF16)) + [part(one, at) for one in through]
            backs.append(dot16(left, cat(right)) + sm["zm"][bb, zi])
        return cat(backs, 1)

    count = TILE // SUB

    def over(low, high, stage):
        def body(i, carry):
            stage([i * count + at for at in range(count)])
            return carry

        if high - low == 1:
            body(low, 0)
        else:
            lax.fori_loop(low, high, body, 0)

    steps = nsub // count

    def loop(stage, between=lambda: None, beside=lambda: None, ahead=lambda: None):
        over(0, (steps + 1) // 2, stage)
        ahead()
        between()
        over((steps + 1) // 2, steps, stage)
        beside()

    def span(bb, s):
        at = lanes()
        return (at >= tab[bb, T_LO + s]) & (at < tab[bb, T_HI + s])

    def fill(ref, bb, s, inside, value):
        before = jnp.where(tab[bb, T_ZK + s] == 1, ref[s - 1], 0.0)
        ref[s] = jnp.where(inside, value, before)

    def corrections_mid(layer, bb):
        for s in range(1, segs):
            pair = hs[layer, bb, tab[bb, T_C + s]]
            slot = tab[bb, T_CS + s]
            value = dot16(left3(sm["mat_a"][bb, slot]), cat(three(pair))) + wide(sm["add_a"][bb, slot], SUB)
            fill(sm["zm"].at[bb], bb, s, span(bb, s), value)

    def corrections_back(layer, bb):
        for s in range(1, segs):
            cell, slot, inside = tab[bb, T_C + s], tab[bb, T_CS + s], span(bb, s)
            pairs = kvs[layer, bb, cell]
            e_k = dot16(left3(sm["mat_a"][bb, slot]), cat(three(pairs, 2 * D))) + wide(sm["add_a"][bb, slot], SUB)
            e_v = dot16(left3(sm["mat_b"][bb, slot]), cat(three(pairs))) + wide(sm["add_b"][bb, slot], SUB)
            e_d = dot16(left3(sm["back_mat"][layer, bb, slot]), cat(three(dms[bb, cell])))
            fill(sm["zk"], bb, s, inside, e_k)
            fill(sm["zv"], bb, s, inside, e_v)
            fill(sm["zm"].at[bb], bb, s, inside, e_d)

    def corrections_moments(layer, bb):
        for s in range(1, segs):
            cell, inside = tab[bb, T_C + s], span(bb, s)
            pairs = kvs[layer, bb, cell]
            product = outer16_sums(pairs[: 2 * D], pairs[2 * D :] * inside.astype(BF16))
            sm["corr_c"][s] = moment_rows(product)
            keys = pairs[: 2 * D].astype(F32)
            sm["corr_n"][s] = fold(jnp.where(inside, keys[:D] + keys[D:], 0.0))

    def corrections_grams(layer, bb):
        for s in range(1, segs):
            cell, inside = tab[bb, T_C + s], span(bb, s)
            q_pair = dms[bb, cell] * inside.astype(BF16)
            sm["corr_g"][s] = outer16_sums(hs[layer, bb, cell], q_pair)

    stats, own_c, own_sums, vec, vec_c = sm["stats"], sm["own_c"], sm["own_sums"], sm["vec"], sm["vec_c"]

    def total_of(name, bb, j):
        return sm["acc_" + name][tab[bb, T_LAST + j]] + sm["corr_" + name][tab[bb, T_CIDX + j]]

    def shifts(layer):
        return 1.0 + wvec[layer, 4], wvec[layer, 5], 1.0 + wvec[layer, 6], wvec[layer, 7]

    def moments_of(layer, bb, j):
        key_gain, key_shift, value_gain, value_shift = shifts(layer)
        gain_c, shift_c = sm["packed"][layer, 0], sm["packed"][layer, 1]
        rows_c = total_of("c", bb, j)
        product, values = rows_c[:group], rows_c[group : group + 1]
        keys = compact(jnp.broadcast_to(jnp.sum(total_of("n", bb, j), axis=1, keepdims=True), (D, 128)))
        stats[layer, bb, j] = cat([product, keys, rows_c[group:]])
        local = tab[bb, T_NLOC + j].astype(F32)
        from_values = values * value_gain + local * value_shift
        return gain_c * (product * value_gain + keys * value_shift) + shift_c * from_values

    def mixing_of(layer, bb, slots, moments):
        packs = []
        for j, moment in zip(slots, moments):
            pack = pack2((expand(moment) / tab[bb, T_CNT + j].astype(F32)).T)
            sm["mt"][layer, bb, j] = pack
            packs.append(left3(pack))
        mixed = dot16(cat(packs), sm["wq_right"][layer])
        rights = [right3(mixed[D * at : D * (at + 1)]) for at in range(len(slots))]
        through = dot16(left3(sm["w3_t"][layer]), cat(rights, 1))
        eye = (
            lax.broadcasted_iota(jnp.int32, (D, D), 0) == lax.broadcasted_iota(jnp.int32, (D, D), 1)
        ).astype(F32)
        for at, j in enumerate(slots):
            forward = through[:, 2 * D * at : 2 * D * at + D] + eye
            sm["mat_a"][bb, j] = pack2(forward)
            sm["add_a"][bb, j] = through[:, 2 * D * at + D : 2 * D * (at + 1)] + tables[layer, 3]
            sm["back_mat"][layer, bb, j] = pack2(forward.T)

    def grams_of(layer, grams):
        tall = D + 16
        onto = dot16(cat([pack3(gram) for gram in grams]), sm["w3_right"][layer])
        ontos = [onto[tall * at : tall * (at + 1)] for at in range(len(grams))]
        rights = [right3(cat([one[:D], gram[:D]], 1)) for one, gram in zip(ontos, grams)]
        both = dot16(left3(sm["wq_t"][layer]), cat(rights, 1))
        query_bias = tables[layer, 0]
        d_moments, throughs = [], []
        for at, (one, gram) in enumerate(zip(ontos, grams)):
            d_moments.append(compact(both[:, 2 * D * at : 2 * D * at + D] + query_bias * one[D : D + 1]))
            throughs.append(both[:, 2 * D * at + D : 2 * D * (at + 1)] + query_bias * gram[D : D + 1])
        return d_moments, ontos, throughs

    def projections_of(layer, bb, slots, ontos, throughs, grams):
        mts = [sm["mt"][layer, bb, j] for j in slots]
        right = [part for mt in mts for part in (mt[:, :D], mt[:, D:], mt[:, :D])]
        d_query = dot16(cat([pack3(one) for one in ontos], 1), cat(right))
        gb[layer, R_Q : R_Q + D] += d_query[:D]
        gb[layer, R_3 : R_3 + D] += dot16(cat([left3(mt) for mt in mts], 1), cat([right3(through) for through in throughs]))
        vec[layer, 0] += d_query[D : D + 8]
        sums = grams[0][D : D + 8]
        for gram in grams[1:]:
            sums = sums + gram[D : D + 8]
        vec[layer, 1] += sums

    def back_of(layer, bb, slots, d_moments):
        key_gain, key_shift, value_gain, value_shift = shifts(layer)
        gain_c, shift_c, value_gain_c = (sm["packed"][layer, at] for at in range(3))

        def across(packed):
            return jnp.broadcast_to(jnp.sum(expand(centred(packed)), axis=1, keepdims=True), (D, 128))

        for j, d_moment in zip(slots, d_moments):
            d = d_moment / tab[bb, T_CNT + j].astype(F32)
            d_t = compact(expand(d).T)
            sm["mat_a"][bb, j] = pack2(expand(centred(gain_c * d * value_gain)))
            sm["add_a"][bb, j] = across(gain_c * d * value_shift)
            sm["mat_b"][bb, j] = pack2(expand(centred(value_gain_c * d_t * key_gain)))
            sm["add_b"][bb, j] = across(value_gain_c * d_t * key_shift)
            held = stats[layer, bb, j]
            product, keys, values = held[:group], held[group : 2 * group], held[2 * group : 2 * group + 1]
            local = tab[bb, T_NLOC + j].astype(F32)
            vec_c[layer, 0] += d * (product * value_gain + keys * value_shift)
            vec_c[layer, 1] += d * (values * value_gain + local * value_shift)
            vec_c[layer, 2] += d * (gain_c * product + shift_c * values)
            vec_c[layer, 3] += d * (gain_c * keys + shift_c * local)

    small = list(range(1, segs))

    def key_of(stage, bb):
        return stage * per + bb

    def moments_out(layer, bb, k):
        corrections_moments(layer, bb)
        ar_launch(k, 0, moments_of(layer, bb, 0))
        for j in small:
            own_c[bb, j] = moments_of(layer, bb, j)

    def small_mixing(layer, bb):
        mixing_of(layer, bb, small, [own_c[bb, j] for j in small])

    def mixing_in(layer, bb, k):
        mixing_of(layer, bb, [0], [ar_finish(k)])
        corrections_mid(layer, bb)

    def spot_of(j):
        return watt.at[j // 4, j % 4]

    def grams_out(layer, bb, k):
        corrections_grams(layer, bb)
        grams = [total_of("g", bb, 0)]
        d_moments, *rest = grams_of(layer, grams)
        ar_launch(k, 0, d_moments[0])
        projections_of(layer, bb, [0], *rest, grams)
        for j in small:
            gram = total_of("g", bb, j)
            spot_of(j)[...] = gram[:D]
            own_sums[j] = gram[D:]

    def small_back(layer, bb):
        grams = [cat([spot_of(j)[...], own_sums[j]]) for j in small]
        d_moments, *rest = grams_of(layer, grams)
        projections_of(layer, bb, small, *rest, grams)
        back_of(layer, bb, small, d_moments)

    def grams_in(layer, bb, k):
        back_of(layer, bb, [0], [ar_finish(k)])
        corrections_back(layer, bb)

    vec[...] = jnp.zeros(vec.shape, F32)
    vec_c[...] = jnp.zeros(vec_c.shape, F32)

    targets = (act_hbm, grd_hbm)

    def kept(kind, layer, bb):
        return pltpu.make_async_copy(
            stage.at[layer, bb], targets[kind].at[c * per + bb], sm["o_local"].at[kind, bb]
        )

    def sent(kind, layer, bb):
        return pltpu.make_async_remote_copy(
            src_ref=stage.at[layer, bb], dst_ref=targets[kind].at[c * per + bb], send_sem=sm["o_send"].at[kind, bb],
            recv_sem=sm["o_recv"].at[kind, bb], device_id={"section": other}, device_id_type=MESH,
        )

    def came(kind, layer, bb):
        return pltpu.make_async_remote_copy(
            src_ref=stage.at[layer, bb], dst_ref=targets[kind].at[other * per + bb], send_sem=sm["o_send"].at[kind, bb],
            recv_sem=sm["o_recv"].at[kind, bb], device_id={"section": other}, device_id_type=MESH,
        )

    def ship(kind, layer, bb):
        @pl.when(c == layer)
        def _():
            kept(kind, layer, bb).start()

        @pl.when(c != layer)
        def _():
            sent(kind, layer, bb).start()

    def shipped(kind, layer, bb):
        @pl.when(c == layer)
        def _():
            kept(kind, layer, bb).wait()

        @pl.when(c != layer)
        def _():
            sent(kind, layer, bb).wait_send()

    def load_t(layer, bb, subs):
        return cat([stage[layer, bb, sub].T for sub in subs], 1)

    def save_t(layer, bb, subs, value):
        for at, sub in enumerate(subs):
            stage[layer, bb, sub] = part(value, at).T

    def start_stage(bb, subs):
        high, low = split(load_t(0, bb, subs))
        pair = cat([high, low])
        save(hs, (0, bb), subs, pair)
        keys_and_values(0, bb, subs, pair)

    def first_stage(bb, subs):
        out, mid_pair, hid_pair, slope = feed_forward(0, bb, subs)
        save(mids, (bb,), subs, mid_pair)
        save(hids, (bb,), subs, hid_pair)
        save(gps, (bb,), subs, slope)
        save_t(0, bb, subs, out)
        high, low = split(out)
        pair = cat([high, low])
        save(hs, (1, bb), subs, pair)
        keys_and_values(1, bb, subs, pair)

    def second_stage(bb, subs):
        out, mid_pair, hid_pair, slope = feed_forward(1, bb, subs)
        upstream = load_t(1, bb, subs)
        save_t(1, bb, subs, out)
        feed_back(1, bb, subs, upstream, mid_pair, hid_pair, slope)

    def third_stage(bb, subs):
        upstream = input_back(1, bb, subs, norm_back(1, bb, subs))
        save_t(1, bb, subs, upstream)
        held = [load(ref, (bb,), subs) for ref in (mids, hids, gps)]
        feed_back(0, bb, subs, upstream, *held)

    def fifth_stage(bb, subs):
        save(kvs, (0, bb), subs, norm_back(0, bb, subs))

    def sixth_stage(bb, subs):
        save_t(0, bb, subs, input_back(0, bb, subs, load(kvs, (0, bb), subs)))

    scattered = scattered_digits(digits)
    sizes, phases = [], []
    for kind, deep in enumerate(scattered):
        sizes.append([parts_rows[kind]])
        for _, radix in digits[:deep]:
            sizes[-1].append(sizes[-1][-1] // radix)
        phases.append(
            [("scatter", digit) for digit in range(deep)]
            + [("exchange", digit) for digit in range(deep, len(digits))]
            + [("gather", digit) for digit in reversed(range(deep))]
        )
    g_send, g_recv, og = sm["g_send"], sm["g_recv"], sm["og"]
    EARLY, LATE = 0, 1

    def early_rows(layer):
        gb[layer, R_O : R_O + FF] = sm["d_outer"][layer]
        d_inner = sm["d_inner"][layer]
        for at in range(0, FF, D):
            gb[layer, R_I + at : R_I + at + D] = d_inner[at : at + D].T

    def late_lines(layer):
        s_du = mm_nt(ones8, sm["s_du"][layer])
        s_g = mm_nt(ones8, sm["s_g"][layer])
        lines = [vec[layer, 0], None, None, vec[layer, 1]]
        lines += [mm_nt(ones8, expand(vec_c[layer, at])) for at in (0, 1)]
        lines += [jnp.sum(vec_c[layer, at], axis=0, keepdims=True) for at in (2, 3)]
        lines += [s_g, s_du[:, :D], s_du[:, D:]]
        block = jnp.zeros((16, D), F32)
        row16 = lax.broadcasted_iota(jnp.int32, (16, D), 0)
        for at, line in enumerate(lines):
            if line is not None:
                block = jnp.where(row16 == at, line[0:1], block)
        gb[layer, R_VEC : R_VEC + 16] = block

    def late_rows(layer):
        d_kv = sm["d_kv"][layer]
        gb[layer, R_K : R_K + D] = d_kv[:D].T
        gb[layer, R_V : R_V + D] = d_kv[D:].T
        s_dz = mm_nt(ones8, sm["s_dz"][layer])
        gb[layer, R_VEC + 1 : R_VEC + 2] = s_dz[0:1, :D]
        gb[layer, R_VEC + 2 : R_VEC + 3] = s_dz[0:1, D:]

    def block_of(kind, depth, at=None):
        low = 0 if kind == 0 else parts_rows[0]
        for digit in range(depth):
            offset = at if (at is not None and digit == depth - 1) else 0
            low = low + digit_at(digit, offset) * sizes[kind][digit + 1]
        return pl.ds(low if depth == 0 else pl.multiple_of(low, 8), sizes[kind][depth])

    def landing(kind, digit):
        return sm["rb%d%d" % (kind, digit)]

    def scatter_first(layer, kind, offset, far):
        radix = digits[0][1]
        slot = radix - 1 + offset if far else offset - 1
        target = {"section": other, "pts": partner(0, offset)} if far else {"pts": partner(0, offset)}
        return pltpu.make_async_remote_copy(
            src_ref=gb.at[layer, block_of(kind, 1, offset)], dst_ref=landing(kind, 0).at[slot],
            send_sem=g_send.at[kind, 0, 0, slot], recv_sem=g_recv.at[kind, 0, 0, slot],
            device_id=target, device_id_type=MESH,
        )

    def scatter_next(layer, kind, digit, offset):
        return pltpu.make_async_remote_copy(
            src_ref=gb.at[layer, block_of(kind, digit + 1, offset)], dst_ref=landing(kind, digit).at[offset - 1],
            send_sem=g_send.at[kind, 0, digit, offset - 1], recv_sem=g_recv.at[kind, 0, digit, offset - 1],
            device_id={"pts": partner(digit, offset)}, device_id_type=MESH,
        )

    def gather(kind, digit, offset, at):
        rows_of = block_of(kind, digit + 1, at)
        spot = og.at[rows_of] if kind == EARLY else gsum_hbm.at[rows_of]
        return pltpu.make_async_remote_copy(
            src_ref=sm["done"] if kind == LATE and at == 0 else spot, dst_ref=spot,
            send_sem=g_send.at[kind, 1, digit, offset - 1], recv_sem=g_recv.at[kind, 1, digit, offset - 1],
            device_id={"pts": partner(digit, offset)}, device_id_type=MESH,
        )

    def keep_done(kind):
        if kind == EARLY:
            source, spot = og, gsum_hbm.at[pl.ds(0, parts_rows[0])]
        else:
            source, spot = sm["done"], gsum_hbm.at[block_of(kind, scattered[kind])]
        return pltpu.make_async_copy(source, spot, sm["done_sem"].at[kind])

    def exchange(kind, digit, offset, back=0):
        spot = sm["wide%d" % kind].at[digit - scattered[kind], digit_at(digit, back)]
        return pltpu.make_async_remote_copy(
            src_ref=spot, dst_ref=spot,
            send_sem=g_send.at[kind, 0, digit, offset - 1], recv_sem=g_recv.at[kind, 0, digit, offset - 1],
            device_id={"pts": partner(digit, offset)}, device_id_type=MESH,
        )

    def outgoing(layer, kind, phase, far=False):
        name, digit = phase
        offsets = range(0 if far else 1, digits[digit][1])
        if name == "scatter" and digit == 0:
            return [scatter_first(layer, kind, offset, far) for offset in offsets]
        if far:
            return []
        if name == "scatter":
            return [scatter_next(layer, kind, digit, offset) for offset in offsets]
        if name == "exchange":
            return [exchange(kind, digit, offset) for offset in offsets]
        return [gather(kind, digit, offset, 0) for offset in offsets]

    def land(layer, kind, phase):
        name, digit = phase
        radix = digits[digit][1]
        if name == "gather":
            for offset in range(1, radix):
                gather(kind, digit, offset, radix - offset).wait_recv()
            return None
        if name == "exchange":
            for offset in range(1, radix):
                exchange(kind, digit, offset, radix - offset).wait_recv()
            held = sm["wide%d" % kind]
            total = held[digit - scattered[kind], 0]
            for at in range(1, radix):
                total = total + held[digit - scattered[kind], at]
            return total
        total = gb[layer, block_of(kind, digit + 1)]
        for copy in outgoing(layer, kind, phase):
            copy.wait_recv()
        for at in range(radix - 1):
            total = total + landing(kind, digit)[at]
        if digit == 0:
            for copy in outgoing(layer, kind, phase, True):
                copy.wait_recv()
            for at in range(radix):
                total = total + landing(kind, 0)[radix - 1 + at]
        return total

    def gradient_step(layer, kind, step):
        todo = phases[kind]
        if step == 0:
            @pl.when(c != layer)
            def _():
                for copy in outgoing(layer, kind, todo[0], True):
                    copy.start()

        if step <= len(todo):
            @pl.when(c == layer)
            def _():
                total = None if step == 0 else land(layer, kind, todo[step - 1])
                if step == len(todo):
                    if kind == EARLY:
                        keep_done(kind).start()
                    return
                name, digit = todo[step]
                if total is not None:
                    if name == "scatter":
                        gb[layer, block_of(kind, digit)] = total
                    elif name == "exchange":
                        sm["wide%d" % kind][digit - scattered[kind], digit_at(digit)] = total
                    elif kind == EARLY:
                        og[block_of(kind, digit + 1)] = total
                    else:
                        sm["done"][...] = total
                        keep_done(kind).start()
                for copy in outgoing(layer, kind, todo[step]):
                    copy.start()

    def gradient_rest(layer, kind, step):
        for left in range(step, len(phases[kind]) + 1):
            gradient_step(layer, kind, left)

    def drain_gradients():
        for layer in range(2):
            for kind in range(2):
                @pl.when(c == layer)
                def _():
                    for phase in phases[kind]:
                        for copy in outgoing(layer, kind, phase):
                            copy.wait_send()
                    keep_done(kind).wait()

                @pl.when(c != layer)
                def _():
                    for copy in outgoing(layer, kind, phases[kind][0], True):
                        copy.wait_send()

    def together(*actions):
        def run():
            for action in actions:
                action()

        return run

    def grad(layer, kind, step):
        return functools.partial(gradient_step, layer, kind, step)

    call = functools.partial
    prepare_projections(0)
    for bb in range(per):
        x_copy(bb).wait()
        if bb == 0:
            loop(call(start_stage, bb))
        else:
            loop(call(start_stage, bb), call(ar_step, key_of(0, bb - 1), 1), call(small_mixing, 0, bb - 1))
        moments_out(0, bb, key_of(0, bb))
        if bb == 0:
            prepare(0)
    prepare_projections(1)
    prepare(1)
    gb[...] = jnp.zeros(gb.shape, F32)
    ar_step(key_of(0, per - 1), 1)

    def step_of(stage, bb):
        if bb > 0:
            return call(ar_step, key_of(stage, bb - 1), 1)
        return (lambda: None) if stage == 1 else call(ar_step, key_of(stage - 1, per - 1), 1)

    for bb in range(per):
        mixing_in(0, bb, key_of(0, bb))
        filler = call(small_mixing, 0, per - 1) if bb == 0 else call(small_mixing, 1, bb - 1)
        loop(call(first_stage, bb), step_of(1, bb), filler)
        ship(0, 0, bb)
        moments_out(1, bb, key_of(1, bb))
    for bb in range(per):
        cot_copy(bb).wait()
        mixing_in(1, bb, key_of(1, bb))
        filler = call(small_mixing, 1, per - 1) if bb == 0 else call(small_back, 1, bb - 1)
        loop(call(second_stage, bb), step_of(2, bb), filler)
        ship(0, 1, bb)
        grams_out(1, bb, key_of(2, bb))
    early_rows(1)
    for bb in range(per):
        grams_in(1, bb, key_of(2, bb))
        shipped(0, 1, bb)
        filler = call(small_back, 1, per - 1) if bb == 0 else call(small_back, 0, bb - 1)
        beside = [step_of(3, bb)] + ([grad(1, EARLY, 1)] if bb == 1 else [])
        loop(call(third_stage, bb), together(*beside), filler)
        ship(1, 1, bb)
        if bb == 0:
            gradient_step(1, EARLY, 0)
        grams_out(0, bb, key_of(3, bb))
    early_rows(0)
    late_lines(1)
    late_rows(1)
    gradient_step(1, LATE, 0)
    gradient_step(1, EARLY, 2)
    for bb in range(per):
        grams_in(0, bb, key_of(3, bb))
        shipped(0, 0, bb)
        if bb == 0:
            beside = [step_of(4, bb), grad(0, EARLY, 0), grad(1, LATE, 1), grad(1, EARLY, 3)]
            loop(call(fifth_stage, bb), together(*beside), ahead=call(small_back, 0, per - 1))
        elif bb == 1:
            late_lines(0)
            loop(call(fifth_stage, bb), together(grad(0, EARLY, 1), grad(1, LATE, 2), grad(1, EARLY, 4)))
        else:
            loop(call(fifth_stage, bb))
    late_rows(0)
    gradient_step(0, LATE, 0)
    gradient_step(0, EARLY, 2)
    gradient_rest(1, EARLY, 5)
    gradient_rest(1, LATE, 3)
    for bb in range(per):
        loop(call(sixth_stage, bb))
        ship(1, 0, bb)
        if bb == 0:
            gradient_step(0, LATE, 1)
            gradient_step(0, EARLY, 3)
    for k in range(4):
        weight_send(k).wait_send()
    for k in range(4 * per):
        ar_drain(k)
    gradient_step(0, LATE, 2)
    gradient_rest(0, EARLY, 4)
    gradient_rest(0, LATE, 3)

    drain_gradients()
    for bb in range(per):
        for layer in range(2):
            shipped(1, layer, bb)
        for layer in range(2):
            @pl.when(c == layer)
            def _():
                came(0, layer, bb).wait_recv()
                came(1, layer, bb).wait_recv()


def finishing(scale, D, FF, first, act, grd, gsum_hbm, *refs):
    sources, results = refs[:12], refs[12:30]
    gsum, held, made, through, sem_large, sem_in, sem_out = refs[30], refs[31:43], refs[43:59], *refs[59:]
    large, onward = [], []
    for kind, (source, target) in enumerate(((act, results[0]), (grd, results[1]))):
        for part in range(source.shape[0]):
            spot = through.at[kind, part]
            large.append(pltpu.make_async_copy(source.at[part], spot, sem_large.at[0, kind, part]))
            onward.append(pltpu.make_async_copy(spot, target.at[part], sem_large.at[1, kind, part]))
    loads = [pltpu.make_async_copy(gsum_hbm, gsum, sem_in.at[12])]
    loads += [pltpu.make_async_copy(sources[at], held[at], sem_in.at[at]) for at in range(12)]
    for copy in loads:
        copy.start()
    for copy in large:
        copy.start()
    rate = plan()

    def step(weight, gradient, momentum, variance):
        average = gradient * scale
        new_momentum = 0.9 * momentum + 0.1 * average
        new_variance = 0.999 * variance + 0.001 * average * average
        mean = new_momentum / (1.0 - 0.9**STEP)
        square = new_variance / (1.0 - 0.999**STEP)
        updated = weight - rate * (mean / (jnp.sqrt(square) + 1e-08) + 0.01 * weight)
        return gradient, new_momentum, new_variance, updated

    parts = [first[name] for name in ("q", "k", "v", "o")]
    inner, outer, late = first["inner"], first["outer"], first["vec"]
    places = [
        [((0, at), slice(low, low + D)) for at, low in enumerate(parts)],
        [((0, slice(None), slice(at, at + D)), slice(inner + at, inner + at + D)) for at in range(0, FF, D)],
        [((0,), slice(outer, outer + FF))],
        [((line,), slice(late + line, late + line + 1)) for line in range(held[3].shape[0])],
    ]
    for copy, after in zip(large, onward):
        copy.wait()
        after.start()
    loads[0].wait()
    stores = []
    for kind in range(4):
        for at in (kind, 4 + 2 * kind, 5 + 2 * kind):
            loads[1 + at].wait()
        weight, momentum, variance = held[kind], held[4 + 2 * kind], held[5 + 2 * kind]
        for index, lines in places[kind]:
            values = step(weight[index], gsum[lines], momentum[index], variance[index])
            for ref, value in zip(made[4 * kind : 4 * kind + 4], values):
                ref[index] = value
        for at in range(4 * kind, 4 * kind + 4):
            stores.append(pltpu.make_async_copy(made[at], results[2 + at], sem_out.at[at]))
            stores[-1].start()
    for copy in onward + stores:
        copy.wait()


def per_device(
    node_features, cotangent, lengths, attention_weight, inner_weight, outer_weight, vectors,
    momentum_attention, variance_attention, momentum_inner, variance_inner,
    momentum_outer, variance_outer, momentum_vectors, variance_vectors,
):
    places = lax.axis_size("pts")
    micro, rows, D = node_features.shape
    FF = inner_weight.shape[-1]
    segs = lengths.shape[1]
    lines = vectors.shape[1]
    nsub = rows // SUB
    per = micro // 2
    digits = digits_of(places)
    group = D // HEADS
    first, parts_rows = gradient_rows(D, FF, digits)
    total_rows = sum(parts_rows)
    nar = 4 * per

    def f32(*shape):
        return pltpu.VMEM(shape, F32)

    def b16(*shape):
        return pltpu.VMEM(shape, BF16)

    def dma(*shape):
        return pltpu.SemaphoreType.DMA(shape)

    scratch = dict(
        watt=f32(2, 4, D, D), winn=f32(2, D, FF), wout=f32(2, FF, D), wvec=f32(2, lines, 1, D),
        tab=pltpu.SMEM((per, 4 * nsub + 12 * segs), jnp.int32),
        tables=f32(2, 7, D, 128), packed=f32(2, 3, group, D),
        wq_t=b16(2, D, 2 * D), w3_t=b16(2, D, 2 * D), wq_right=b16(2, 3 * D, 2 * D), w3_right=b16(2, 3 * D, D),
        kvw=b16(2, 2 * D, 2 * D), kvw_back=b16(2, D, 4 * D),
        inn_t=b16(2, FF, 2 * D), inn=b16(2, D, 2 * FF), out_t=b16(2, D, 2 * FF), out=b16(2, FF, 2 * D),
        hs=b16(2, per, nsub, 2 * D, SUB), kvs=b16(2, per, nsub, 4 * D, SUB),
        rst=f32(2, per, nsub, 2 * HEADS, SUB), dms=b16(per, nsub, 2 * D, SUB),
        mids=b16(per, nsub, 2 * D, SUB), hids=b16(per, nsub, 2 * FF, SUB), gps=f32(per, nsub, FF, SUB),
                stage=f32(2, per, nsub, SUB, D),
        zm=f32(per, segs, D, SUB), zk=f32(segs, D, SUB), zv=f32(segs, D, SUB),
        acc_c=f32(nsub + 1, group + 8, D), acc_n=f32(nsub + 1, D, 128), acc_g=f32(nsub + 1, D + 16, D),
        corr_c=f32(segs, group + 8, D), corr_n=f32(segs, D, 128), corr_g=f32(segs, D + 16, D),
        stats=f32(2, per, segs, 2 * group + 8, D), own_c=f32(per, segs, group, D), own_sums=f32(segs, 16, D),
        mt=b16(2, per, segs, D, 2 * D), vec_c=f32(2, 4, group, D),
        mat_a=b16(per, segs, D, 2 * D), add_a=f32(per, segs, D, 128), back_mat=b16(2, per, segs, D, 2 * D),
        mat_b=b16(per, segs, D, 2 * D), add_b=f32(per, segs, D, 128),
        d_outer=f32(2, FF, D), d_inner=f32(2, FF, D), d_kv=f32(2, 2 * D, D),
        s_du=f32(2, FF, 128), s_g=f32(2, D, 128), s_dz=f32(2, 2 * D, 128),
        vec=f32(2, 2, 8, D), gb=f32(2, total_rows, D), og=f32(parts_rows[0], D), done=f32(parts_rows[1] // digits[0][1], D),
        ar=f32(nar, len(digits), 4, group, D),
        dma_in=dma(2 * per + 4), w_send=dma(4), w_recv=dma(4),
        ar_send=dma(nar, len(digits), 3), ar_recv=dma(nar, len(digits), 3),
        o_local=dma(2, per), done_sem=dma(2), o_send=dma(2, per), o_recv=dma(2, per),
        g_send=dma(2, 2, len(digits), 7), g_recv=dma(2, 2, len(digits), 7),
    )
    for kind, (size, count) in enumerate(zip(parts_rows, scattered_digits(digits))):
        for digit, (_, radix) in enumerate(digits[:count]):
            size //= radix
            scratch["rb%d%d" % (kind, digit)] = f32(2 * radix - 1 if digit == 0 else radix - 1, size, D)
        if len(digits) > count:
            scratch["wide%d" % kind] = f32(len(digits) - count, 4, size, D)
    cfg = dict(names=list(scratch), places=places, segs=segs, micro=micro, nsub=nsub, D=D, FF=FF)

    def lined(piece):
        return jnp.transpose(piece, (1, 0, 2))

    anywhere = pl.BlockSpec(memory_space=pl.ANY)
    tiled = (micro, nsub, SUB, D)
    act, grd, gsum = pl.pallas_call(
        functools.partial(mega, cfg),
        out_shape=(
            jax.ShapeDtypeStruct(tiled, F32), jax.ShapeDtypeStruct(tiled, F32),
            jax.ShapeDtypeStruct((total_rows, D), F32),
        ),
        in_specs=[anywhere, anywhere, pl.BlockSpec(memory_space=pltpu.SMEM)] + [anywhere] * 4,
        out_specs=(anywhere, anywhere, anywhere),
        scratch_shapes=list(scratch.values()),
        compiler_params=pltpu.CompilerParams(
            collective_id=0, has_side_effects=True, vmem_limit_bytes=255 * 2**18
        ),
        name="layers",
    )(
        node_features.reshape(tiled), cotangent.reshape(tiled), lengths,
        attention_weight, inner_weight, outer_weight, lined(vectors),
    )
    scale = 1.0 / (micro * rows * places)
    held = [attention_weight, inner_weight, outer_weight, vectors]
    moments = [
        momentum_attention, variance_attention, momentum_inner, variance_inner,
        momentum_outer, variance_outer, momentum_vectors, variance_vectors,
    ]
    held[3] = lined(vectors)
    moments[6:] = [lined(momentum_vectors), lined(variance_vectors)]
    shapes = [jax.ShapeDtypeStruct(piece.shape, F32) for piece in held for _ in range(4)]
    results = pl.pallas_call(
        functools.partial(finishing, scale, D, FF, first),
        out_shape=tuple([jax.ShapeDtypeStruct(tiled, F32)] * 2 + shapes),
        in_specs=[pl.BlockSpec(memory_space=pltpu.HBM)] * 15,
        out_specs=tuple([pl.BlockSpec(memory_space=pltpu.HBM)] * 18),
        scratch_shapes=[f32(total_rows, D)] + [f32(*piece.shape) for piece in held + moments]
        + [f32(*shape.shape) for shape in shapes] + [f32(2, *tiled), dma(2, 2, micro), dma(13), dma(16)],
        compiler_params=pltpu.CompilerParams(vmem_limit_bytes=60 * 2**20),
        name="adamw",
    )(act, grd, gsum, *held, *moments)
    whole = (1, micro, rows, D)
    lines_back = tuple(lined(piece) for piece in results[14:])
    return (results[0].reshape(whole), results[1].reshape(whole)) + tuple(results[2:14]) + lines_back


def solution(mesh):
    first = P("section", None, None)
    attention = P("section", None, None, None)
    nodes = P(None, "pts", None)
    return jax.shard_map(
        per_device,
        mesh=mesh,
        in_specs=(nodes, nodes, P(), attention, first, first, first, attention, attention) + (first,) * 6,
        out_specs=(P("section", None, "pts", None),) * 2 + (attention,) * 4 + (first,) * 12,
        check_vma=False,
    )
```
